32 devices in a mesh: seq: 8 (over z, y), batch: 4 (over x, core).
Axes of the slice: x: 2, y: 2, z: 4, core: 2. Of those that a mesh axis runs over, the one named last changes fastest.
Arguments:
- inputs: bfloat16 [32, 1024, 512], P('batch', 'seq'), may hold values from -6 to 6
- cotangent: bfloat16 [32, 1024, 512], P('batch', 'seq'), may hold values from -6 to 6
- lengths: int32 [32], P('batch'), may hold values from 256 to 1024, as said below
- norm1_gain: float32 [512], replicated, may hold values from 0.25 to 1.75
- norm1_bias: float32 [512], replicated, may hold values from -4 to 4
- qkv_weight: bfloat16 [512, 1536], replicated, may hold values from -0.25 to 0.25
- blend_weights: float32 [3, 8], replicated, may hold values from 0.5 to 4
- out_weight: bfloat16 [512, 512], replicated, may hold values from -1 to 1
- norm2_gain: float32 [512], replicated, may hold values from 0.25 to 1.75
- norm2_bias: float32 [512], replicated, may hold values from -4 to 4
- in_weight: bfloat16 [512, 2048], replicated, may hold values from -0.25 to 0.25
- in_bias: float32 [2048], replicated, may hold values from -4 to 4
- down_weight: bfloat16 [2048, 512], replicated, may hold values from -0.125 to 0.125
- down_bias: float32 [512], replicated, may hold values from -4 to 4
Outputs:
- output: bfloat16 [32, 1024, 512], P('batch', 'seq')
- input_grad: bfloat16 [32, 1024, 512], P('batch', 'seq')
- norm1_gain_grad: float32 [512], replicated
- norm1_bias_grad: float32 [512], replicated
- qkv_weight_grad: float32 [512, 1536], replicated
- blend_grad: float32 [3, 8], replicated
- out_weight_grad: float32 [512, 512], replicated
- norm2_gain_grad: float32 [512], replicated
- norm2_bias_grad: float32 [512], replicated
- in_weight_grad: float32 [512, 2048], replicated
- in_bias_grad: float32 [2048], replicated
- down_weight_grad: float32 [2048, 512], replicated
- down_bias_grad: float32 [512], replicated
The draws below stay inside these ranges and needn't reach their ends.
Inputs may be any that keep to these rules, and one draw needn't show every extreme that they name: `lengths`: in each aligned group of 8 sequences one, drawn from the seed, has length 1024.
All inputs are finite; a program needn't handle non-finite values.
Results may differ from the reference program's by a relative error of at most 0.009.
Values may be sent and summed in bfloat16 or wider, within the bound.
No kernel may reach another device: no remote copies, remote signals or barrier semaphores. Data moves between devices by JAX's collectives and lax.ppermute only.
A program may use at most 320 MiB of HBM per device.

```python
import math
import jax
import jax.numpy as jnp
from jax import lax

D = 512
HEADS = 8
HEAD = 64
FF = 2048
WINDOW = 30
SPAN = 128
SEQS_DEV = 8
SEQS = 32
LENGTH = 1024


def draw_lengths(key, part):
    key = jax.random.fold_in(key, 11)
    first_key, second_key = jax.random.split(key)
    drawn = jax.random.randint(first_key, (SEQS,), LENGTH // 4, LENGTH + 1)
    chosen = jax.random.randint(second_key, (SEQS // SEQS_DEV,), 0, SEQS_DEV)
    places = jnp.arange(SEQS, dtype=jnp.int32) % SEQS_DEV
    full_length = places == jnp.repeat(chosen, SEQS_DEV)
    return jnp.where(full_length, LENGTH, drawn).astype(jnp.int32)


def block_scale(key, shape, cuts, low, largest):
    loudness = 1.0
    for axis_at, blocks in cuts:
        steps = jax.random.uniform(jax.random.fold_in(jax.random.fold_in(key, 6), axis_at), (blocks,), jnp.float32, low / len(cuts), largest / len(cuts))
        loudness = loudness * jnp.repeat(jnp.exp(steps), shape[axis_at] // blocks).reshape((-1,) + (1,) * (len(shape) - 1 - axis_at))
    return loudness


def scatter_about(stream_key, dims, scale, reach, cuts=(), kind=jnp.bfloat16):
    values = jax.random.normal(stream_key, dims, jnp.float32) * scale
    if len(cuts) > 0:
        values = block_scale(stream_key, dims, cuts, -0.22, 0.18) * values
    return jnp.clip(values, min=-reach, max=reach).astype(kind)


def setup_inputs(seed: int = 0) -> dict:
    streams_of = jax.random.split(jax.random.key(seed), 15)
    inputs = scatter_about(streams_of[0], (SEQS, LENGTH, D), 1.0, 6.0, ((0, 4), (1, 8)))
    cotangent = scatter_about(streams_of[1], (SEQS, LENGTH, D), 1.0, 6.0, ((0, 4), (1, 8)))
    lengths = draw_lengths(jax.random.fold_in(streams_of[14], 71), 0)
    norm1_gain = jnp.clip(1.0 + 0.15 * jax.random.normal(streams_of[3], (D,), jnp.float32), 0.25, 1.75)
    norm1_bias = scatter_about(streams_of[4], (D,), 0.3, 4.0, (), jnp.float32)
    qkv_weight = scatter_about(streams_of[5], (D, 3 * D), D ** -0.5, 0.25)
    blend_weights = jnp.clip(jnp.exp(jax.random.uniform(streams_of[6], (3, HEADS), jnp.float32, math.log(0.5), math.log(4.0))), 0.5, 4.0)
    out_weight = scatter_about(streams_of[7], (D, D), (D // 16) ** -0.5, 1.0)
    norm2_gain = jnp.clip(1.0 + 0.15 * jax.random.normal(streams_of[8], (D,), jnp.float32), 0.25, 1.75)
    norm2_bias = scatter_about(streams_of[9], (D,), 0.3, 4.0, (), jnp.float32)
    in_weight = scatter_about(streams_of[10], (D, FF), D ** -0.5, 0.25)
    in_bias = scatter_about(streams_of[11], (FF,), 0.3, 4.0, (), jnp.float32)
    down_weight = scatter_about(streams_of[12], (FF, D), FF ** -0.5, 0.125)
    down_bias = scatter_about(streams_of[13], (D,), 0.3, 4.0, (), jnp.float32)
    return dict(inputs=inputs, cotangent=cotangent, lengths=lengths, norm1_gain=norm1_gain, norm1_bias=norm1_bias, qkv_weight=qkv_weight, blend_weights=blend_weights, out_weight=out_weight, norm2_gain=norm2_gain, norm2_bias=norm2_bias, in_weight=in_weight, in_bias=in_bias, down_weight=down_weight, down_bias=down_bias)


EPS = 1e-05
NEG = -1e+30
HIGH = lax.Precision.HIGHEST

@jax.custom_vjp
def low(v):
    return lax.optimization_barrier(v.astype(jnp.bfloat16)).astype(jnp.float32)

@jax.custom_vjp
def low_back(v):
    return v

def low_keep(v):
    return (low(v), None)

def low_pass(kept, grad):
    return (grad,)

def back_keep(v):
    return (v, None)

def back_low(kept, grad):
    return (low(grad),)
low.defvjp(low_keep, low_pass)
low_back.defvjp(back_keep, back_low)

def layer_norm(field, gain, shift):
    center = field - lax.optimization_barrier(jnp.mean(field, axis=-1, keepdims=True))
    spread = lax.optimization_barrier(jnp.mean(center * center, axis=-1, keepdims=True))
    return center * lax.rsqrt(spread + EPS) * gain + shift

def feature_elu(field):
    return jax.nn.elu(field) + 1.0

def feature_tanh(field):
    return 1.0 + jnp.tanh(field)

def sequence_forward(tokens, length, params):
    gain_one, bias_one, qkv_w, blend, out_w, gain_two, bias_two, in_w, in_b, down_w, down_b = params
    normed = low(layer_norm(tokens, gain_one, bias_one))
    qkv_rows = low_back(low(jnp.dot(normed, qkv_w, precision=HIGH)))
    queries = qkv_rows[:, :D].reshape(LENGTH, HEADS, HEAD)
    key_rows = qkv_rows[:, D:2 * D].reshape(LENGTH, HEADS, HEAD)
    value_rows = qkv_rows[:, 2 * D:].reshape(LENGTH, HEADS, HEAD)
    front = jnp.zeros((WINDOW, HEADS, HEAD), jnp.float32)
    key_pad = jnp.concatenate([front, key_rows], 0)
    value_pad = jnp.concatenate([front, value_rows], 0)
    positions = jnp.arange(LENGTH, dtype=jnp.int32)
    key_valid = (positions < length).astype(jnp.float32)[:, None, None]
    feat_q = [low(feature_elu(queries)), low(feature_tanh(queries))]
    feat_k = [low(feature_elu(key_rows)) * key_valid, low(feature_tanh(key_rows)) * key_valid]
    local_pos = jnp.arange(SPAN, dtype=jnp.int32)
    causal = (local_pos[None, :] <= local_pos[:, None]).astype(jnp.float32)

    def block_step(carry, number):
        offset = number * SPAN
        q_block = lax.dynamic_slice_in_dim(queries, offset, SPAN, 0)
        k_wide = lax.dynamic_slice_in_dim(key_pad, offset, SPAN + WINDOW, 0)
        v_wide = lax.dynamic_slice_in_dim(value_pad, offset, SPAN + WINDOW, 0)
        v_block = lax.dynamic_slice_in_dim(value_rows, offset, SPAN, 0)
        row_pos = offset + local_pos
        col_pos = offset - WINDOW + jnp.arange(SPAN + WINDOW, dtype=jnp.int32)
        row_b = row_pos[:, None]
        col_b = col_pos[None, :]
        allowed = (col_b >= row_b - WINDOW) & (col_b <= row_b) & (col_b >= 0) & ((col_b < length) | (col_b == row_b))
        scores = low_back(jnp.einsum('rhd,thd->hrt', q_block, k_wide, precision=HIGH) * 0.125)
        masked = jnp.where(allowed[None], scores, NEG)
        row_max = lax.optimization_barrier(jnp.max(masked, axis=-1, keepdims=True))
        weights = jnp.where(allowed[None], jnp.exp(masked - row_max), 0.0)
        probs = weights / lax.optimization_barrier(jnp.sum(weights, axis=-1, keepdims=True))
        near_out = low_back(jnp.einsum('hrt,thd->rhd', low(probs), v_wide, precision=HIGH))
        mixture = blend[0][None, :, None] * near_out
        new_carry = []
        for branch_id in range(2):
            state_sum = carry[2 * branch_id]
            norm_sum = carry[2 * branch_id + 1]
            fq_block = lax.dynamic_slice_in_dim(feat_q[branch_id], offset, SPAN, 0)
            fk_block = lax.dynamic_slice_in_dim(feat_k[branch_id], offset, SPAN, 0)
            affinity = low_back(jnp.einsum('rhd,thd->hrt', fq_block, fk_block, precision=HIGH)) * causal[None]
            numerator = jnp.einsum('hrt,thd->rhd', low(affinity), v_block, precision=HIGH)
            numerator = numerator + jnp.einsum('rhd,hde->rhe', fq_block, low(state_sum), precision=HIGH)
            numerator = low_back(numerator)
            denominator = jnp.transpose(lax.optimization_barrier(jnp.sum(affinity, axis=-1))) + jnp.einsum('rhd,hd->rh', fq_block, norm_sum, precision=HIGH)
            mixture = mixture + blend[branch_id + 1][None, :, None] * numerator / denominator[:, :, None]
            block_term = low_back(jnp.einsum('thd,the->hde', fk_block, v_block, precision=HIGH))
            new_carry.append(state_sum + block_term)
            new_carry.append(norm_sum + lax.optimization_barrier(jnp.sum(fk_block, axis=0)))
        return (tuple(new_carry), mixture)
    state_zero = jnp.zeros((HEADS, HEAD, HEAD), jnp.float32)
    sum_zero = jnp.zeros((HEADS, HEAD), jnp.float32)
    blocks = LENGTH // SPAN
    carry_end, mixed_blocks = lax.scan(jax.checkpoint(block_step), (state_zero, sum_zero, state_zero, sum_zero), jnp.arange(blocks, dtype=jnp.int32))
    attended = low(mixed_blocks.reshape(LENGTH, D))
    first = tokens + low_back(jnp.dot(attended, out_w, precision=HIGH))
    second = low(layer_norm(first, gain_two, bias_two))
    hidden = low(jax.nn.gelu(low_back(jnp.dot(second, in_w, precision=HIGH) + in_b)))
    return first + low_back(jnp.dot(hidden, down_w, precision=HIGH) + down_b)

def reference(inputs, cotangent, lengths, norm1_gain, norm1_bias, qkv_weight, blend_weights, out_weight, norm2_gain, norm2_bias, in_weight, in_bias, down_weight, down_bias):
    params = (norm1_gain, norm1_bias, qkv_weight.astype(jnp.float32), blend_weights, out_weight.astype(jnp.float32), norm2_gain, norm2_bias, in_weight.astype(jnp.float32), in_bias, down_weight.astype(jnp.float32), down_bias)
    zeros = jax.tree.map(jnp.zeros_like, params)

    def one_sequence(totals, sample):
        tokens, direction, length = sample

        def forward(token_rows, weights):
            return sequence_forward(token_rows, length, weights)
        result, pullback = jax.vjp(forward, tokens.astype(jnp.float32), params)
        grad_tokens, grad_params = pullback(direction.astype(jnp.float32))
        totals = jax.tree.map(jnp.add, totals, grad_params)
        return (totals, (result.astype(jnp.bfloat16), grad_tokens.astype(jnp.bfloat16)))
    totals, (outputs, grads) = lax.scan(one_sequence, zeros, (inputs, cotangent, lengths))
    return (outputs, grads, totals[0], totals[1], totals[2], totals[3], totals[4], totals[5], totals[6], totals[7], totals[8], totals[9], totals[10])
```

```python
import functools

import jax
import jax.numpy as jnp
from jax import lax
from jax.experimental import pallas as pl
from jax.experimental.pallas import tpu as pltpu
from jax.sharding import PartitionSpec as P

WINDOW = 30
HEAD = 64
PAIR = 2 * HEAD
TILE = 64
EPS = 1e-05
NEG = -1e30
BF16 = jnp.bfloat16
F32 = jnp.float32


def layer_norm(field, gain, shift):
    center = field - jnp.mean(field, axis=-1, keepdims=True)
    spread = jnp.mean(center * center, axis=-1, keepdims=True)
    return center * lax.rsqrt(spread + EPS) * gain + shift


def rows_product(left, right):
    return lax.dot_general(
        left, right, (((0,), (0,)), ((), ())), preferred_element_type=F32
    )


def times_transposed(left, right):
    return lax.dot_general(
        left, right, (((1,), (1,)), ((), ())), preferred_element_type=F32
    )


def times(left, right):
    return lax.dot_general(
        left, right, (((1,), (0,)), ((), ())), preferred_element_type=F32
    )


def split_heads(block):
    lane = lax.broadcasted_iota(jnp.int32, block.shape, 1)
    zero = jnp.zeros_like(block)
    return jnp.concatenate(
        [jnp.where(lane < HEAD, block, zero), jnp.where(lane < HEAD, zero, block)], 0
    )


def same_head(rows, lanes):
    row = lax.broadcasted_iota(jnp.int32, (rows, lanes), 0) % PAIR
    lane = lax.broadcasted_iota(jnp.int32, (rows, lanes), 1) % PAIR
    return (row // HEAD) == (lane // HEAD)


def elu_feature(field):
    return jnp.where(field > 0, field + 1.0, jnp.exp(jnp.minimum(field, 0.0)))


def tanh_feature(field):
    return 1.0 + jnp.tanh(field)


def fill_features(meta_ref, qkv_ref, halo_ref, kpad, vpad, fq, fk, rows, width):
    chunk = 2 * TILE
    zero = jnp.zeros((TILE, width), BF16)
    kpad[:TILE, :] = halo_ref[:, :width] * 0.125
    vpad[:TILE, :] = halo_ref[:, width:]
    for c in range(2):
        fk[c, :TILE, :] = zero
    length, offset = meta_ref[0], meta_ref[1]

    def fill(step, carry):
        at = pl.multiple_of(step * chunk, chunk)
        here, there = pl.ds(at, chunk), pl.ds(at + TILE, chunk)
        q = qkv_ref[here, :width].astype(F32)
        k_low = qkv_ref[here, width : 2 * width]
        k = k_low.astype(F32)
        position = offset + at + lax.broadcasted_iota(jnp.int32, (chunk, width), 0)
        valid = position < length
        kpad[there, :] = k_low * 0.125
        vpad[there, :] = qkv_ref[here, 2 * width :]
        for c, feature in enumerate((elu_feature, tanh_feature)):
            fq[c, here, :] = feature(q).astype(BF16)
            fk[c, there, :] = jnp.where(valid, feature(k), 0.0).astype(BF16)
        return carry

    lax.fori_loop(0, rows // chunk, fill, 0)


def tile_masks(meta_ref, tile):
    shape = (TILE, 2 * PAIR)
    row = lax.broadcasted_iota(jnp.int32, shape, 0)
    lane = lax.broadcasted_iota(jnp.int32, shape, 1) % PAIR
    back = row + TILE - lane
    key = meta_ref[1] + (tile - 1) * TILE + lane
    known = (key >= 0) & (key < meta_ref[0])
    near = (back >= 0) & (back <= WINDOW) & (known | (back == 0))
    return near, back >= 0


def tile_scores(q, keys, fq, fks, near_mask, far_mask):
    scores = jnp.where(near_mask, times_transposed(q, keys), NEG)
    halves = []
    for h in range(2):
        part = scores[:, h * PAIR : (h + 1) * PAIR]
        part = jnp.exp(part - jnp.max(part, axis=1, keepdims=True))
        halves.append(part / jnp.sum(part, axis=1, keepdims=True))
    probs = jnp.concatenate(halves, 1)
    far = [jnp.where(far_mask, times_transposed(fq[c], fks[c]), 0.0) for c in range(2)]
    return probs, far[0], far[1]


def attend_kernel(
    rows, width, meta_ref, blend_ref, qkv_ref, halo_ref, state_ref, att_ref, total_ref,
    kpad, vpad, fq, fk, state,
):
    pairs = width // PAIR
    fill_features(meta_ref, qkv_ref, halo_ref, kpad, vpad, fq, fk, rows, width)
    state[...] = state_ref[...]
    ones = same_head(2 * PAIR, PAIR)
    ones = jnp.where(
        (lax.broadcasted_iota(jnp.int32, (2 * PAIR, PAIR), 0) // PAIR)
        == (lax.broadcasted_iota(jnp.int32, (2 * PAIR, PAIR), 1) // HEAD),
        1.0,
        0.0,
    ).astype(BF16)
    block = same_head(PAIR, 2 * PAIR)
    plain_ones = jnp.ones((TILE, PAIR), BF16)

    def step(tile, carry):
        at = pl.multiple_of(tile * TILE, TILE)
        here, window = pl.ds(at, TILE), pl.ds(at, 2 * TILE)
        near_mask, far_mask = tile_masks(meta_ref, tile)
        for p in range(pairs):
            lanes = slice(p * PAIR, (p + 1) * PAIR)
            q = qkv_ref[here, lanes]
            keys = split_heads(kpad[window, lanes])
            values = vpad[window, lanes]
            wide = jnp.concatenate([split_heads(values), ones], 1)
            feats = [fq[c, here, lanes] for c in range(2)]
            fkw = [fk[c, window, lanes] for c in range(2)]
            probs, far1, far2 = tile_scores(
                q, keys, feats, [split_heads(f) for f in fkw], near_mask, far_mask
            )
            stack = jnp.concatenate([probs, far1, far2], 0).astype(BF16)
            sums = times(stack, wide)
            mixed = blend_ref[0:1, lanes] * sums[:TILE, :PAIR]
            for c in range(2):
                mine = sums[(c + 1) * TILE : (c + 2) * TILE]
                mine = mine + times(feats[c], state[c, p].astype(BF16))
                mixed = mixed + blend_ref[c + 1 : c + 2, lanes] * (
                    mine[:, :PAIR] / mine[:, PAIR:]
                )
                gone = rows_product(
                    fkw[c][:TILE], jnp.concatenate([values[:TILE], plain_ones], 1)
                )
                state[c, p] = state[c, p] + jnp.where(block, gone, 0.0)
            att_ref[here, lanes] = mixed.astype(BF16)
        return carry

    lax.fori_loop(0, rows // TILE, step, 0)
    for p in range(pairs):
        lanes = slice(p * PAIR, (p + 1) * PAIR)
        for c in range(2):
            last = rows_product(
                fk[c, rows:, lanes], jnp.concatenate([vpad[rows:, lanes], plain_ones], 1)
            )
            total_ref[c, p] = state[c, p] + jnp.where(block, last, 0.0)


def attend_back_kernel(
    rows, width, meta_ref, blend_ref, qkv_ref, halo_ref, state_ref, later_ref, go_ref,
    gqkv_ref, ghalo_ref, mix_ref, total_ref,
    kpad, vpad, fq, fk, state, gk, gv, gfk, gon,
):
    pairs = width // PAIR
    tiles = rows // TILE
    fill_features(meta_ref, qkv_ref, halo_ref, kpad, vpad, fq, fk, rows, width)
    state[...] = state_ref[...]
    mix_ref[...] = jnp.zeros_like(mix_ref)
    gk[...] = jnp.zeros_like(gk)
    gv[...] = jnp.zeros_like(gv)
    gfk[...] = jnp.zeros_like(gfk)
    ones = jnp.where(
        (lax.broadcasted_iota(jnp.int32, (2 * PAIR, PAIR), 0) // PAIR)
        == (lax.broadcasted_iota(jnp.int32, (2 * PAIR, PAIR), 1) // HEAD),
        1.0,
        0.0,
    ).astype(BF16)
    block = same_head(PAIR, 2 * PAIR)
    heads = jnp.where(same_head(2 * PAIR, PAIR), 1.0, 0.0).astype(BF16)
    plain_ones = jnp.ones((TILE, PAIR), BF16)
    high = (lax.broadcasted_iota(jnp.int32, (TILE, PAIR), 1) % HEAD) < HEAD // 2

    def step(tile, carry):
        at = pl.multiple_of(tile * TILE, TILE)
        here, window = pl.ds(at, TILE), pl.ds(at, 2 * TILE)
        near_mask, far_mask = tile_masks(meta_ref, tile)
        for p in range(pairs):
            lanes = slice(p * PAIR, (p + 1) * PAIR)
            q = qkv_ref[here, lanes]
            keys = split_heads(kpad[window, lanes])
            values = vpad[window, lanes]
            wide = jnp.concatenate([split_heads(values), ones], 1)
            feats = [fq[c, here, lanes] for c in range(2)]
            fkw = [fk[c, window, lanes] for c in range(2)]
            fks = [split_heads(f) for f in fkw]
            scores = tile_scores(q, keys, feats, fks, near_mask, far_mask)
            stack = jnp.concatenate(scores, 0).astype(BF16)
            sums = times(stack, wide)
            past = [state[c, p].astype(BF16) for c in range(2)]
            go = go_ref[here, lanes]
            outs = [sums[:TILE, :PAIR]]
            scales = [jnp.broadcast_to(blend_ref[0:1, lanes], (TILE, PAIR))]
            for c in range(2):
                mine = sums[(c + 1) * TILE : (c + 2) * TILE] + times(feats[c], past[c])
                inverse = 1.0 / mine[:, PAIR:]
                outs.append(mine[:, :PAIR] * inverse)
                scales.append(blend_ref[c + 1 : c + 2, lanes] * inverse)
            prods = [go * out for out in outs]
            for c in range(3):
                mix_ref[c : c + 1, lanes] += jnp.sum(prods[c], axis=0, keepdims=True)
            prod = jnp.concatenate(prods, 0)
            prod_low = prod.astype(BF16)
            rest = (prod - prod_low.astype(F32)).astype(BF16)
            deltas = times(jnp.concatenate([prod_low, rest], 1), heads)
            grads = []
            for c in range(3):
                delta = scales[c] * deltas[c * TILE : (c + 1) * TILE] * (-2.0 / HEAD)
                delta_low = delta.astype(BF16).astype(F32)
                delta = jnp.where(high, delta_low, delta - delta_low)
                grads.append(jnp.concatenate([scales[c] * go, delta], 1).astype(BF16))
            back = times_transposed(jnp.concatenate(grads, 0), wide)
            ds = (scores[0] * back[:TILE]).astype(BF16)
            gas = [
                jnp.where(far_mask, back[(c + 1) * TILE : (c + 2) * TILE], 0.0).astype(BF16)
                for c in range(2)
            ]
            q32 = q.astype(F32)
            small = jnp.exp(jnp.minimum(q32, 0.0))
            bent = jnp.tanh(q32)
            slopes = [jnp.where(q32 > 0, 1.0, small), 1.0 - bent * bent]
            gq = times(ds, keys)
            for c in range(2):
                gq = gq + slopes[c] * (
                    times(gas[c], fks[c]) + times_transposed(grads[c + 1], past[c])
                )
            gqkv_ref[here, lanes] = gq.astype(BF16)

            def tall(block):
                return jnp.concatenate([block[:, :PAIR], block[:, PAIR:]], 0)

            gk[window, lanes] += rows_product(tall(ds), split_heads(q * 0.125))
            for c in range(2):
                gfk[c, window, lanes] += rows_product(tall(gas[c]), split_heads(feats[c]))
            gv[window, lanes] += rows_product(
                jnp.concatenate([tall(stack[c * TILE : (c + 1) * TILE]) for c in range(3)], 0),
                jnp.concatenate([split_heads(g[:, :PAIR]) for g in grads], 0),
            )
            for c in range(2):
                gon[c, here, p * 2 * PAIR : (p + 1) * 2 * PAIR] = grads[c + 1]
                gone = rows_product(
                    fkw[c][:TILE], jnp.concatenate([values[:TILE], plain_ones], 1)
                )
                state[c, p] = state[c, p] + jnp.where(block, gone, 0.0)
        return carry

    lax.fori_loop(0, tiles, step, 0)
    ghalo_ref[:, :width] = gk[:TILE, :].astype(BF16)
    ghalo_ref[:, width:] = gv[:TILE, :].astype(BF16)
    state[...] = later_ref[...]
    length, offset = meta_ref[0], meta_ref[1]

    def add_later(at):
        here = pl.ds(at, TILE)
        for p in range(pairs):
            lanes = slice(p * PAIR, (p + 1) * PAIR)
            for c in range(2):
                come = rows_product(
                    fq[c, here, lanes], gon[c, here, p * 2 * PAIR : (p + 1) * 2 * PAIR]
                )
                state[c, p] = state[c, p] + jnp.where(block, come, 0.0)

    def back_step(step, carry):
        tile = tiles - 1 - step

        @pl.when(step >= 2)
        def _():
            add_later(pl.multiple_of((tile + 2) * TILE, TILE))

        at = pl.multiple_of(tile * TILE, TILE)
        here, there = pl.ds(at, TILE), pl.ds(at + TILE, TILE)
        position = offset + at + lax.broadcasted_iota(jnp.int32, (TILE, PAIR), 0)
        valid = position < length
        for p in range(pairs):
            lanes = slice(p * PAIR, (p + 1) * PAIR)
            values = vpad[there, lanes]
            wide = jnp.concatenate([values, plain_ones], 1)
            k32 = qkv_ref[here, width + p * PAIR : width + (p + 1) * PAIR].astype(F32)
            small = jnp.exp(jnp.minimum(k32, 0.0))
            bent = jnp.tanh(k32)
            slopes = [jnp.where(k32 > 0, 1.0, small), 1.0 - bent * bent]
            grad_k = gk[there, lanes]
            grad_v = gv[there, lanes]
            for c in range(2):
                later = state[c, p].astype(BF16)
                grad_f = gfk[c, there, lanes] + times_transposed(wide, later)
                grad_k = grad_k + jnp.where(valid, slopes[c] * grad_f, 0.0)
                grad_v = grad_v + times(fk[c, there, lanes], later[:, :PAIR])
            gqkv_ref[here, width + p * PAIR : width + (p + 1) * PAIR] = grad_k.astype(BF16)
            gqkv_ref[here, 2 * width + p * PAIR : 2 * width + (p + 1) * PAIR] = grad_v.astype(BF16)
        return carry

    lax.fori_loop(0, tiles, back_step, 0)
    add_later(TILE)
    add_later(0)
    total_ref[...] = state[...]


def attention_specs(rows, width):
    smem = pl.BlockSpec(memory_space=pltpu.SMEM)
    vmem = pl.BlockSpec(memory_space=pltpu.VMEM)
    scratch = [
        pltpu.VMEM((rows + TILE, width), BF16),
        pltpu.VMEM((rows + TILE, width), BF16),
        pltpu.VMEM((2, rows, width), BF16),
        pltpu.VMEM((2, rows + TILE, width), BF16),
        pltpu.VMEM((2, width // PAIR, PAIR, 2 * PAIR), F32),
    ]
    return smem, vmem, scratch


def attend(meta, blend, qkv, halo, state):
    rows, width = qkv.shape[0], qkv.shape[1] // 3
    smem, vmem, scratch = attention_specs(rows, width)
    return pl.pallas_call(
        functools.partial(attend_kernel, rows, width),
        out_shape=(
            jax.ShapeDtypeStruct((rows, width), BF16),
            jax.ShapeDtypeStruct(state.shape, F32),
        ),
        in_specs=[smem] + [vmem] * 4,
        out_specs=(vmem, vmem),
        scratch_shapes=scratch,
        compiler_params=pltpu.CompilerParams(vmem_limit_bytes=48 * 2**20),
        cost_estimate=pl.CostEstimate(
            flops=rows * width * 2 * 1024, bytes_accessed=rows * width * 8, transcendentals=0
        ),
    )(meta, blend, qkv, halo, state)


def attend_back(meta, blend, qkv, halo, state, later, go):
    rows, width = qkv.shape[0], qkv.shape[1] // 3
    smem, vmem, scratch = attention_specs(rows, width)
    return pl.pallas_call(
        functools.partial(attend_back_kernel, rows, width),
        out_shape=(
            jax.ShapeDtypeStruct((rows, 3 * width), BF16),
            jax.ShapeDtypeStruct((TILE, 2 * width), BF16),
            jax.ShapeDtypeStruct((3, width), F32),
            jax.ShapeDtypeStruct(state.shape, F32),
        ),
        in_specs=[smem] + [vmem] * 6,
        out_specs=(vmem,) * 4,
        scratch_shapes=scratch
        + [
            pltpu.VMEM((rows + TILE, width), F32),
            pltpu.VMEM((rows + TILE, width), F32),
            pltpu.VMEM((2, rows + TILE, width), F32),
            pltpu.VMEM((2, rows, 2 * width), BF16),
        ],
        compiler_params=pltpu.CompilerParams(vmem_limit_bytes=56 * 2**20),
        cost_estimate=pl.CostEstimate(
            flops=rows * width * 2 * 4096, bytes_accessed=rows * width * 16, transcendentals=0
        ),
    )(meta, blend, qkv, halo, state, later, go)


def to_sequences(block, axis, groups):
    return lax.all_to_all(block, axis, 0, 0, axis_index_groups=groups)


def from_parts(total, axis, parts, stride, forward):
    size = lax.axis_size(axis)
    low = total.astype(BF16)
    result = jnp.zeros_like(total)
    for hop in range(1, parts):
        distance = hop * stride
        route = [
            (i, i + distance) if forward else (i + distance, i) for i in range(size - distance)
        ]
        result = result + lax.ppermute(low, axis, route).astype(F32)
    return result


def local(
    inputs,
    cotangent,
    lengths,
    norm1_gain,
    norm1_bias,
    qkv_weight,
    blend_weights,
    out_weight,
    norm2_gain,
    norm2_bias,
    in_weight,
    in_bias,
    down_weight,
    down_bias,
):
    seqs, span, width = inputs.shape
    heads = blend_weights.shape[1]
    devices = lax.axis_size("seq")
    parts = devices // seqs
    rows = seqs * span
    index = lax.axis_index("seq")
    groups = None
    if parts > 1:
        groups = [[r * seqs + s for s in range(seqs)] for r in range(parts)]
    mine, part = index % seqs, index // seqs
    meta = jnp.stack([lax.dynamic_index_in_dim(lengths, mine, 0, False), part * rows])
    blend = jnp.repeat(blend_weights, width // heads, axis=1)

    x = to_sequences(inputs, "seq", groups).reshape(rows, width).astype(F32)
    grad_out = to_sequences(cotangent, "seq", groups).reshape(rows, width)

    normed, norm1_back = jax.vjp(layer_norm, x, norm1_gain, norm1_bias)
    normed_low = normed.astype(BF16)
    qkv = times(normed_low, qkv_weight).astype(BF16)
    halo = jnp.zeros((TILE, 2 * width), BF16)
    state = jnp.zeros((2, width // PAIR, PAIR, 2 * PAIR), F32)
    later = state
    if parts > 1:
        onward = [(i, i + seqs) for i in range(devices - seqs)]
        halo = lax.ppermute(qkv[rows - TILE :, width:], "seq", onward)
        total = attend(meta, blend, qkv, halo, state)[1]
        state = from_parts(total, "seq", parts, seqs, True)
    attended = attend(meta, blend, qkv, halo, state)[0]
    first = x + times(attended, out_weight)
    second, norm2_back = jax.vjp(layer_norm, first, norm2_gain, norm2_bias)
    second_low = second.astype(BF16)
    pre = times(second_low, in_weight) + in_bias
    hidden, gelu_back = jax.vjp(jax.nn.gelu, pre)
    hidden_low = hidden.astype(BF16)
    result = (first + times(hidden_low, down_weight) + down_bias).astype(BF16)
    output = to_sequences(result.reshape(seqs, span, width), "seq", groups)

    grad_out_f = grad_out.astype(F32)
    grad_down_w = rows_product(hidden_low, grad_out)
    grad_down_b = jnp.sum(grad_out_f, axis=0)
    (grad_pre,) = gelu_back(times_transposed(grad_out, down_weight))
    grad_pre_low = grad_pre.astype(BF16)
    grad_in_b = jnp.sum(grad_pre_low.astype(F32), axis=0)
    grad_in_w = rows_product(second_low, grad_pre_low)
    grad_first_part, grad_gain2, grad_bias2 = norm2_back(times_transposed(grad_pre_low, in_weight))
    grad_first = grad_out_f + grad_first_part
    grad_att_low = grad_first.astype(BF16)
    grad_out_w = rows_product(attended, grad_att_low)
    grad_o = times_transposed(grad_att_low, out_weight)

    if parts > 1:
        total = attend_back(meta, blend, qkv, halo, state, later, grad_o)[3]
        later = from_parts(total, "seq", parts, seqs, False)
    grad_qkv, grad_halo, mix, _ = attend_back(meta, blend, qkv, halo, state, later, grad_o)
    if parts > 1:
        homeward = [(i + seqs, i) for i in range(devices - seqs)]
        back = lax.ppermute(grad_halo, "seq", homeward)
        tail = grad_qkv[rows - TILE :, width:].astype(F32) + back.astype(F32)
        grad_qkv = grad_qkv.at[rows - TILE :, width:].set(tail.astype(BF16))
    grad_blend = jnp.sum(mix.reshape(3, heads, width // heads), axis=-1)
    grad_qkv_w = rows_product(normed_low, grad_qkv)
    grad_x_part, grad_gain1, grad_bias1 = norm1_back(times_transposed(grad_qkv, qkv_weight))
    grad_x = (grad_first + grad_x_part).astype(BF16)
    input_grad = to_sequences(grad_x.reshape(seqs, span, width), "seq", groups)
    summed = lax.psum(
        (
            grad_gain1,
            grad_bias1,
            grad_qkv_w,
            grad_blend,
            grad_out_w,
            grad_gain2,
            grad_bias2,
            grad_in_w,
            grad_in_b,
            grad_down_w,
            grad_down_b,
        ),
        ("seq", "batch"),
    )
    return (output, input_grad) + tuple(summed)


def solution(mesh):
    rows = P("batch", "seq", None)
    return jax.shard_map(
        local,
        mesh=mesh,
        in_specs=(rows, rows, P("batch")) + (P(),) * 11,
        out_specs=(rows, rows) + (P(),) * 11,
        check_vma=False,
    )
```

```python
import functools

import jax
import jax.numpy as jnp
from jax import lax
from jax.experimental import pallas as pl
from jax.experimental.pallas import tpu as pltpu
from jax.sharding import PartitionSpec as P

WINDOW = 30
HEAD = 64
PAIR = 2 * HEAD
TILE = 64
EPS = 1e-05
NEG = -1e30
BF16 = jnp.bfloat16
F32 = jnp.float32


def layer_norm(field, gain, shift):
    center = field - jnp.mean(field, axis=-1, keepdims=True)
    spread = jnp.mean(center * center, axis=-1, keepdims=True)
    return center * lax.rsqrt(spread + EPS) * gain + shift


def rows_product(left, right):
    return lax.dot_general(
        left, right, (((0,), (0,)), ((), ())), preferred_element_type=F32
    )


def times_transposed(left, right):
    return lax.dot_general(
        left, right, (((1,), (1,)), ((), ())), preferred_element_type=F32
    )


def times(left, right):
    return lax.dot_general(
        left, right, (((1,), (0,)), ((), ())), preferred_element_type=F32
    )


def elu_feature(field):
    return jnp.where(field > 0, field + 1.0, jnp.exp(jnp.minimum(field, 0.0)))


def tanh_feature(field):
    return 1.0 + jnp.tanh(field)


def pair_lanes(p, part=0, width=PAIR):
    return slice(p * width + part * PAIR, p * width + (part + 1) * PAIR)


def store_split(ref, index, rows, block):
    lane = lax.broadcasted_iota(jnp.int32, (block.shape[0], PAIR), 1)
    for p in range(block.shape[1] // PAIR):
        pair = block[:, pair_lanes(p)]
        for h in range(2):
            mine = (lane < HEAD) if h == 0 else (lane >= HEAD)
            ref[index + (rows, pair_lanes(p, h, 2 * PAIR))] = jnp.where(mine, pair, 0.0).astype(
                BF16
            )


def load_split(ref, index, rows, p):
    return jnp.concatenate([ref[index + (rows, pair_lanes(p, h, 2 * PAIR))] for h in range(2)], 0)


def tall(block):
    return jnp.concatenate([block[:, :PAIR], block[:, PAIR:]], 0)


def fill_features(meta_ref, qkv_ref, halo_ref, keys, values, fq, fk, rows, width, split):
    chunk = 2 * TILE
    front = pl.ds(0, TILE)
    zero = jnp.zeros((TILE, width), F32)
    store_split(keys, (), front, halo_ref[:, :width].astype(F32) * 0.125)
    store_split(values, (), front, halo_ref[:, width:].astype(F32))
    for c in range(2):
        store_split(fk, (c,), front, zero)

    def fill(step, carry):
        at = pl.multiple_of(step * chunk, chunk)
        here, there = pl.ds(at, chunk), pl.ds(at + TILE, chunk)
        q = qkv_ref[here, :width].astype(F32)
        k = qkv_ref[here, width : 2 * width].astype(F32)
        store_split(keys, (), there, k * 0.125)
        store_split(values, (), there, qkv_ref[here, 2 * width :].astype(F32))
        position = meta_ref[1] + at + lax.broadcasted_iota(jnp.int32, (chunk, width), 0)
        valid = position < meta_ref[0]
        for c, feature in enumerate((elu_feature, tanh_feature)):
            if split:
                store_split(fq, (c,), here, feature(q))
            else:
                fq[c, here, :] = feature(q).astype(BF16)
            store_split(fk, (c,), there, jnp.where(valid, feature(k), 0.0))
        return carry

    lax.fori_loop(0, rows // chunk, fill, 0)


def tile_masks(meta_ref, tile):
    shape = (TILE, 2 * PAIR)
    row = lax.broadcasted_iota(jnp.int32, shape, 0)
    lane = lax.broadcasted_iota(jnp.int32, shape, 1) % PAIR
    back = row + TILE - lane
    key = meta_ref[1] + (tile - 1) * TILE + lane
    known = (key >= 0) & (key < meta_ref[0])
    near = (back >= 0) & (back <= WINDOW) & (known | (back == 0))
    return near, back >= 0


def softmax_pair(scores):
    halves = []
    for h in range(2):
        part = scores[:, h * PAIR : (h + 1) * PAIR]
        part = jnp.exp(part - jnp.max(part, axis=1, keepdims=True))
        halves.append(part * (1.0 / jnp.sum(part, axis=1, keepdims=True)))
    return jnp.concatenate(halves, 1)


def tile_constants():
    row = lax.broadcasted_iota(jnp.int32, (2 * PAIR, PAIR), 0)
    lane = lax.broadcasted_iota(jnp.int32, (2 * PAIR, PAIR), 1)
    ones = jnp.where(row // PAIR == lane // HEAD, 1.0, 0.0).astype(BF16)
    row = lax.broadcasted_iota(jnp.int32, (PAIR, 2 * PAIR), 0)
    lane = lax.broadcasted_iota(jnp.int32, (PAIR, 2 * PAIR), 1)
    return ones, row // HEAD == (lane % PAIR) // HEAD


def attend_kernel(
    rows, width, meta_ref, blend_ref, qkv_ref, halo_ref, state_ref, att_ref, total_ref,
    keys, values, fq, fk, state,
):
    pairs = range(width // PAIR)
    fill_features(meta_ref, qkv_ref, halo_ref, keys, values, fq, fk, rows, width, False)
    state[...] = state_ref[...]
    ones, block = tile_constants()
    plain_ones = jnp.ones((TILE, PAIR), BF16)

    def gone(past, values_past):
        fks, vs = past[:TILE] + past[TILE:], values_past[:TILE] + values_past[TILE:]
        return jnp.where(block, rows_product(fks, jnp.concatenate([vs, plain_ones], 1)), 0.0)

    def step(tile, carry):
        at = pl.multiple_of(tile * TILE, TILE)
        here, window, past = pl.ds(at, TILE), pl.ds(at, 2 * TILE), pl.ds(at, TILE)
        near_mask, far_mask = tile_masks(meta_ref, tile)
        q = [qkv_ref[here, pair_lanes(p)] for p in pairs]
        feats = [[fq[c, here, pair_lanes(p)] for c in range(2)] for p in pairs]
        held = [[state[c, p] for c in range(2)] for p in pairs]
        added = [
            [gone(load_split(fk, (c,), past, p), load_split(values, (), past, p)) for c in range(2)]
            for p in pairs
        ]
        near = [times_transposed(q[p], load_split(keys, (), window, p)) for p in pairs]
        far = [
            [times_transposed(feats[p][c], load_split(fk, (c,), window, p)) for c in range(2)]
            for p in pairs
        ]
        near = [softmax_pair(jnp.where(near_mask, n, NEG)) for n in near]
        far = [[jnp.where(far_mask, f, 0.0) for f in fs] for fs in far]
        stack = [jnp.concatenate([n] + fs, 0).astype(BF16) for n, fs in zip(near, far)]
        wide = [jnp.concatenate([load_split(values, (), window, p), ones], 1) for p in pairs]
        sums = [times(s, w) for s, w in zip(stack, wide)]
        old = [[times(feats[p][c], held[p][c].astype(BF16)) for c in range(2)] for p in pairs]
        for p in pairs:
            mixed = blend_ref[0:1, pair_lanes(p)] * sums[p][:TILE, :PAIR]
            for c in range(2):
                mine = sums[p][(c + 1) * TILE : (c + 2) * TILE] + old[p][c]
                mixed = mixed + blend_ref[c + 1 : c + 2, pair_lanes(p)] * (
                    mine[:, :PAIR] / mine[:, PAIR:]
                )
            att_ref[here, pair_lanes(p)] = mixed.astype(BF16)
        for p in pairs:
            for c in range(2):
                state[c, p] = held[p][c] + added[p][c]
        return carry

    lax.fori_loop(0, rows // TILE, step, 0)
    last = pl.ds(rows, TILE)
    for p in pairs:
        for c in range(2):
            total_ref[c, p] = state[c, p] + gone(
                load_split(fk, (c,), last, p), load_split(values, (), last, p)
            )


def attend_back_kernel(
    rows, width, meta_ref, blend_ref, qkv_ref, halo_ref, state_ref, later_ref, go_ref,
    gqkv_ref, ghalo_ref, mix_ref, total_ref,
    keys, values, fq, fk, state, gk, gv, gfk, gon,
):
    pairs = range(width // PAIR)
    tiles = rows // TILE
    fill_features(meta_ref, qkv_ref, halo_ref, keys, values, fq, fk, rows, width, True)
    state[...] = state_ref[...]
    mix_ref[...] = jnp.zeros_like(mix_ref)
    gk[:TILE, :] = jnp.zeros((TILE, width), F32)
    gv[:TILE, :] = jnp.zeros((TILE, width), F32)
    gfk[:, :TILE, :] = jnp.zeros((2, TILE, width), F32)
    ones, block = tile_constants()
    row = lax.broadcasted_iota(jnp.int32, (2 * PAIR, PAIR), 0) % PAIR
    lane = lax.broadcasted_iota(jnp.int32, (2 * PAIR, PAIR), 1)
    heads = jnp.where(row // HEAD == lane // HEAD, 1.0, 0.0).astype(BF16)
    plain_ones = jnp.ones((TILE, PAIR), BF16)
    high = (lax.broadcasted_iota(jnp.int32, (TILE, PAIR), 1) % HEAD) < HEAD // 2

    def gone(fks, vs):
        fks, vs = fks[:TILE] + fks[TILE:], vs[:TILE] + vs[TILE:]
        return jnp.where(block, rows_product(fks, jnp.concatenate([vs, plain_ones], 1)), 0.0)

    def slopes_of(field):
        small = jnp.exp(jnp.minimum(field, 0.0))
        bent = jnp.tanh(field)
        return [jnp.where(field > 0, 1.0, small), 1.0 - bent * bent]

    def step(tile, carry):
        at = pl.multiple_of(tile * TILE, TILE)
        here, window = pl.ds(at, TILE), pl.ds(at, 2 * TILE)
        before, after = pl.ds(at, TILE), pl.ds(at + TILE, TILE)
        near_mask, far_mask = tile_masks(meta_ref, tile)
        q = [qkv_ref[here, pair_lanes(p)] for p in pairs]
        go = [go_ref[here, pair_lanes(p)] for p in pairs]
        blend = [[blend_ref[c : c + 1, pair_lanes(p)] for c in range(3)] for p in pairs]
        fqs = [[load_split(fq, (c,), here, p) for c in range(2)] for p in pairs]
        feats = [[f[:TILE] + f[TILE:] for f in fs] for fs in fqs]
        held = [[state[c, p] for c in range(2)] for p in pairs]
        past = [[h.astype(BF16) for h in hs] for hs in held]
        ks = [load_split(keys, (), window, p) for p in pairs]
        fks = [[load_split(fk, (c,), window, p) for c in range(2)] for p in pairs]
        wide = [jnp.concatenate([load_split(values, (), window, p), ones], 1) for p in pairs]
        added = [
            [gone(load_split(fk, (c,), before, p), load_split(values, (), before, p)) for c in range(2)]
            for p in pairs
        ]
        old_gk = [gk[before, pair_lanes(p)] for p in pairs]
        old_gv = [gv[before, pair_lanes(p)] for p in pairs]
        old_gf = [[gfk[c, before, pair_lanes(p)] for c in range(2)] for p in pairs]

        near = [times_transposed(q[p], ks[p]) for p in pairs]
        far = [[times_transposed(feats[p][c], fks[p][c]) for c in range(2)] for p in pairs]
        old = [[times(feats[p][c], past[p][c]) for c in range(2)] for p in pairs]
        near = [softmax_pair(jnp.where(near_mask, n, NEG)) for n in near]
        far = [[jnp.where(far_mask, f, 0.0).astype(BF16) for f in fs] for fs in far]
        stack = [jnp.concatenate([n.astype(BF16)] + fs, 0) for n, fs in zip(near, far)]
        sums = [times(s, w) for s, w in zip(stack, wide)]
        scales, prods = [], []
        for p in pairs:
            outs = [sums[p][:TILE, :PAIR]]
            scale = [jnp.broadcast_to(blend[p][0], (TILE, PAIR))]
            for c in range(2):
                mine = sums[p][(c + 1) * TILE : (c + 2) * TILE] + old[p][c]
                inverse = 1.0 / mine[:, PAIR:]
                outs.append(mine[:, :PAIR] * inverse)
                scale.append(blend[p][c + 1] * inverse)
            scales.append(scale)
            prods.append(jnp.concatenate([go[p] * out for out in outs], 0))
        deltas = []
        for p in pairs:
            low = prods[p].astype(BF16)
            rest = (prods[p] - low.astype(F32)).astype(BF16)
            deltas.append(times(jnp.concatenate([low, rest], 1), heads))
        grads = []
        for p in pairs:
            mine = []
            for c in range(3):
                delta = scales[p][c] * deltas[p][c * TILE : (c + 1) * TILE] * (-2.0 / HEAD)
                delta_low = delta.astype(BF16).astype(F32)
                delta = jnp.where(high, delta_low, delta - delta_low)
                mine.append(jnp.concatenate([scales[p][c] * go[p], delta], 1).astype(BF16))
            grads.append(mine)
        back = [times_transposed(jnp.concatenate(grads[p], 0), wide[p]) for p in pairs]
        late = [[times_transposed(grads[p][c + 1], past[p][c]) for c in range(2)] for p in pairs]
        ds = [(near[p] * back[p][:TILE]).astype(BF16) for p in pairs]
        gas = [
            [
                jnp.where(far_mask, back[p][(c + 1) * TILE : (c + 2) * TILE], 0.0).astype(BF16)
                for c in range(2)
            ]
            for p in pairs
        ]
        gq_near = [times(ds[p], ks[p]) for p in pairs]
        gq_far = [[times(gas[p][c], fks[p][c]) + late[p][c] for c in range(2)] for p in pairs]
        lane = lax.broadcasted_iota(jnp.int32, (TILE, PAIR), 1)

        def split(block):
            zero = jnp.zeros_like(block)
            return jnp.concatenate(
                [jnp.where(lane < HEAD, block, zero), jnp.where(lane < HEAD, zero, block)], 0
            )

        new_k = [rows_product(tall(ds[p]), split(q[p] * 0.125)) for p in pairs]
        new_f = [[rows_product(tall(gas[p][c]), fqs[p][c]) for c in range(2)] for p in pairs]
        new_v = [
            rows_product(
                jnp.concatenate([tall(stack[p][c * TILE : (c + 1) * TILE]) for c in range(3)], 0),
                jnp.concatenate([split(g[:, :PAIR]) for g in grads[p]], 0),
            )
            for p in pairs
        ]
        for p in pairs:
            lanes = pair_lanes(p)
            slopes = slopes_of(q[p].astype(F32))
            gq = gq_near[p] + slopes[0] * gq_far[p][0] + slopes[1] * gq_far[p][1]
            gqkv_ref[here, lanes] = gq.astype(BF16)
            for c in range(3):
                mix_ref[c : c + 1, lanes] += jnp.sum(
                    prods[p][c * TILE : (c + 1) * TILE], axis=0, keepdims=True
                )
            gk[before, lanes] = old_gk[p] + new_k[p][:TILE]
            gk[after, lanes] = new_k[p][TILE:]
            gv[before, lanes] = old_gv[p] + new_v[p][:TILE]
            gv[after, lanes] = new_v[p][TILE:]
            for c in range(2):
                gfk[c, before, lanes] = old_gf[p][c] + new_f[p][c][:TILE]
                gfk[c, after, lanes] = new_f[p][c][TILE:]
                gon[c, here, p * 2 * PAIR : (p + 1) * 2 * PAIR] = grads[p][c + 1]
                state[c, p] = held[p][c] + added[p][c]
        return carry

    lax.fori_loop(0, tiles, step, 0)
    ghalo_ref[:, :width] = gk[:TILE, :].astype(BF16)
    ghalo_ref[:, width:] = gv[:TILE, :].astype(BF16)
    state[...] = later_ref[...]

    def come(at, c, p):
        here = pl.ds(at, TILE)
        f = load_split(fq, (c,), here, p)
        share = rows_product(f[:TILE] + f[TILE:], gon[c, here, p * 2 * PAIR : (p + 1) * 2 * PAIR])
        return jnp.where(block, share, 0.0)

    def back_step(step, carry):
        tile = tiles - 1 - step
        at = pl.multiple_of(tile * TILE, TILE)
        nearer = pl.multiple_of(jnp.minimum(tile + 2, tiles - 1) * TILE, TILE)
        here, there = pl.ds(at, TILE), pl.ds(at + TILE, TILE)
        position = meta_ref[1] + at + lax.broadcasted_iota(jnp.int32, (TILE, PAIR), 0)
        valid = position < meta_ref[0]
        share = [[come(nearer, c, p) for c in range(2)] for p in pairs]
        held = [
            [state[c, p] + jnp.where(step >= 2, share[p][c], 0.0) for c in range(2)] for p in pairs
        ]
        later = [[h.astype(BF16) for h in hs] for hs in held]
        vs = [load_split(values, (), there, p) for p in pairs]
        fks = [[load_split(fk, (c,), there, p) for c in range(2)] for p in pairs]
        wide = [jnp.concatenate([v[:TILE] + v[TILE:], plain_ones], 1) for v in vs]
        far_k = [[times_transposed(wide[p], later[p][c]) for c in range(2)] for p in pairs]
        far_v = [
            times(
                jnp.concatenate([f[:TILE] + f[TILE:] for f in fks[p]], 1),
                jnp.concatenate([g[:, :PAIR] for g in later[p]], 0),
            )
            for p in pairs
        ]
        for p in pairs:
            lanes = pair_lanes(p)
            k_lanes = slice(width + p * PAIR, width + (p + 1) * PAIR)
            v_lanes = slice(2 * width + p * PAIR, 2 * width + (p + 1) * PAIR)
            slopes = slopes_of(qkv_ref[here, k_lanes].astype(F32))
            grad_f = [gfk[c, there, lanes] + far_k[p][c] for c in range(2)]
            bent = slopes[0] * grad_f[0] + slopes[1] * grad_f[1]
            grad_k = gk[there, lanes] + jnp.where(valid, bent, 0.0)
            gqkv_ref[here, k_lanes] = grad_k.astype(BF16)
            gqkv_ref[here, v_lanes] = (gv[there, lanes] + far_v[p]).astype(BF16)
            for c in range(2):
                state[c, p] = held[p][c]
        return carry

    lax.fori_loop(0, tiles, back_step, 0)
    for p in pairs:
        for c in range(2):
            total_ref[c, p] = state[c, p] + come(0, c, p) + come(TILE, c, p)


def attention_specs(rows, width, split):
    smem = pl.BlockSpec(memory_space=pltpu.SMEM)
    vmem = pl.BlockSpec(memory_space=pltpu.VMEM)
    scratch = [
        pltpu.VMEM((rows + TILE, 2 * width), BF16),
        pltpu.VMEM((rows + TILE, 2 * width), BF16),
        pltpu.VMEM((2, rows, (2 if split else 1) * width), BF16),
        pltpu.VMEM((2, rows + TILE, 2 * width), BF16),
        pltpu.VMEM((2, width // PAIR, PAIR, 2 * PAIR), F32),
    ]
    return smem, vmem, scratch


def attend(meta, blend, qkv, halo, state):
    rows, width = qkv.shape[0], qkv.shape[1] // 3
    smem, vmem, scratch = attention_specs(rows, width, False)
    return pl.pallas_call(
        functools.partial(attend_kernel, rows, width),
        out_shape=(
            jax.ShapeDtypeStruct((rows, width), BF16),
            jax.ShapeDtypeStruct(state.shape, F32),
        ),
        in_specs=[smem] + [vmem] * 4,
        out_specs=(vmem, vmem),
        scratch_shapes=scratch,
        compiler_params=pltpu.CompilerParams(vmem_limit_bytes=48 * 2**20),
        cost_estimate=pl.CostEstimate(
            flops=rows * width * 2 * 1024, bytes_accessed=rows * width * 8, transcendentals=0
        ),
    )(meta, blend, qkv, halo, state)


def attend_back(meta, blend, qkv, halo, state, later, go):
    rows, width = qkv.shape[0], qkv.shape[1] // 3
    smem, vmem, scratch = attention_specs(rows, width, True)
    return pl.pallas_call(
        functools.partial(attend_back_kernel, rows, width),
        out_shape=(
            jax.ShapeDtypeStruct((rows, 3 * width), BF16),
            jax.ShapeDtypeStruct((TILE, 2 * width), BF16),
            jax.ShapeDtypeStruct((3, width), F32),
            jax.ShapeDtypeStruct(state.shape, F32),
        ),
        in_specs=[smem] + [vmem] * 6,
        out_specs=(vmem,) * 4,
        scratch_shapes=scratch
        + [
            pltpu.VMEM((rows + TILE, width), F32),
            pltpu.VMEM((rows + TILE, width), F32),
            pltpu.VMEM((2, rows + TILE, width), F32),
            pltpu.VMEM((2, rows, 2 * width), BF16),
        ],
        compiler_params=pltpu.CompilerParams(vmem_limit_bytes=56 * 2**20),
        cost_estimate=pl.CostEstimate(
            flops=rows * width * 2 * 4096, bytes_accessed=rows * width * 16, transcendentals=0
        ),
    )(meta, blend, qkv, halo, state, later, go)


def to_sequences(block, axis, groups):
    return lax.all_to_all(block, axis, 0, 0, axis_index_groups=groups)


def from_parts(total, axis, parts, stride, forward):
    size = lax.axis_size(axis)
    low = total.astype(BF16)
    result = jnp.zeros_like(total)
    for hop in range(1, parts):
        distance = hop * stride
        route = [
            (i, i + distance) if forward else (i + distance, i) for i in range(size - distance)
        ]
        result = result + lax.ppermute(low, axis, route).astype(F32)
    return result


class Ring:
    def __init__(self, batch, seq):
        self.batch, self.seq = batch, seq
        self.low = 2 ** ((seq.bit_length() - 1) // 2)
        self.sizes = {"core": 2, "near": batch // 2 * self.low, "far": seq // self.low}
        self.pieces = batch * seq

    def place(self, s, b):
        return {"core": b % 2, "near": b // 2 * self.low + s % self.low, "far": s // self.low}

    def device(self, place):
        s = place["far"] * self.low + place["near"] % self.low
        return s * self.batch + place["near"] // self.low * 2 + place["core"]

    def mine(self):
        return self.place(lax.axis_index("seq"), lax.axis_index("batch"))

    def swap(self, value, level, k):
        route = []
        for s in range(self.seq):
            for b in range(self.batch):
                place = self.place(s, b)
                place[level] ^= k
                route.append((s * self.batch + b, self.device(place)))
        return lax.ppermute(value, ("seq", "batch"), route)

    def scatter(self, value, level):
        size, me = self.sizes[level], self.mine()[level]
        value = value.reshape((size, value.shape[0] // size) + value.shape[1:])
        parts = [
            self.swap(lax.dynamic_index_in_dim(value, me ^ k, 0, False), level, k)
            for k in range(1, size)
        ]
        total = lax.dynamic_index_in_dim(value, me, 0, False).astype(F32)
        for part in parts:
            total = total + part.astype(F32)
        return total.astype(BF16)

    def gather(self, value, level):
        parts = [value] + [self.swap(value, level, k) for k in range(1, self.sizes[level])]
        return jnp.concatenate(parts, 0)

    def total(self, value):
        for level, size in self.sizes.items():
            parts = [value] + [self.swap(value, level, k) for k in range(1, size)]
            while len(parts) > 1:
                parts = [parts[i] + parts[i + 1] for i in range(0, len(parts), 2)]
            value = parts[0]
        return value

    def reduce(self, value):
        for level in ("core", "near", "far"):
            value = self.scatter(value, level)
        for level in ("far", "near"):
            value = self.gather(value, level)
        return value, self.swap(value, "core", 1)

    def order(self):
        me = self.mine()
        piece = jnp.arange(self.pieces, dtype=jnp.int32)
        far, near = self.sizes["far"], self.sizes["near"]
        core = (piece // (far * near)) ^ me["core"]
        near = ((piece // far) % near) ^ me["near"]
        return (core * self.sizes["near"] + near) * far + ((piece % far) ^ me["far"])


def to_pieces(matrix, pieces, lanes):
    rows, columns = matrix.shape
    matrix = matrix.reshape(pieces, rows // pieces, columns // lanes, lanes)
    return jnp.swapaxes(matrix, 1, 2).reshape(pieces, -1, lanes)


def unpack_kernel(shapes, order_ref, own_ref, other_ref, *out_refs):
    pieces, half = order_ref.shape[0], own_ref.shape[0]
    lanes = own_ref.shape[2]
    for piece in range(pieces):
        at = order_ref[piece]

        def write(source, at, piece=piece):
            below = 0
            for out, (rows, columns) in zip(out_refs, shapes):
                size = rows // pieces
                for block in range(columns // lanes):
                    out[piece * size : (piece + 1) * size, block * lanes : (block + 1) * lanes] = (
                        source[at, below : below + size, :].astype(F32)
                    )
                    below += size

        @pl.when(at < half)
        def _():
            write(own_ref, at)

        @pl.when(at >= half)
        def _():
            write(other_ref, at - half)


def unpack(order, own, other, shapes):
    vmem = pl.BlockSpec(memory_space=pltpu.VMEM)
    return pl.pallas_call(
        functools.partial(unpack_kernel, shapes),
        out_shape=[jax.ShapeDtypeStruct(shape, F32) for shape in shapes],
        in_specs=[pl.BlockSpec(memory_space=pltpu.SMEM), vmem, vmem],
        out_specs=[vmem] * len(shapes),
        compiler_params=pltpu.CompilerParams(vmem_limit_bytes=48 * 2**20),
        cost_estimate=pl.CostEstimate(flops=0, bytes_accessed=8 * own.size, transcendentals=0),
    )(order, own, other)


def sum_over_devices(ring, early, late, small):
    width = early[-1].shape[1]
    rows = min(matrix.shape[0] for matrix in early + late)
    if rows % (16 * ring.pieces):
        return lax.psum((early, late, small), ("seq", "batch"))
    order = ring.order()
    results = []
    for group in (early, late):
        packed = [to_pieces(matrix.astype(BF16), ring.pieces, width) for matrix in group]
        own, other = ring.reduce(jnp.concatenate(packed, 1))
        results.append(unpack(order, own, other, [matrix.shape for matrix in group]))
    sizes = [part.size for part in small]
    flat = jnp.concatenate([part.reshape(-1) for part in small])
    flat = jnp.pad(flat, (0, -flat.size % 1024)).reshape(-1, 128)
    flat = ring.total(flat).reshape(-1)
    vectors, at = [], 0
    for part, size in zip(small, sizes):
        vectors.append(flat[at : at + size].reshape(part.shape))
        at += size
    return tuple(results[0]), tuple(results[1]), tuple(vectors)


def local(
    inputs,
    cotangent,
    lengths,
    norm1_gain,
    norm1_bias,
    qkv_weight,
    blend_weights,
    out_weight,
    norm2_gain,
    norm2_bias,
    in_weight,
    in_bias,
    down_weight,
    down_bias,
):
    seqs, span, width = inputs.shape
    heads = blend_weights.shape[1]
    devices = lax.axis_size("seq")
    parts = devices // seqs
    rows = seqs * span
    index = lax.axis_index("seq")
    groups = None
    if parts > 1:
        groups = [[r * seqs + s for s in range(seqs)] for r in range(parts)]
    mine, part = index % seqs, index // seqs
    meta = jnp.stack([lax.dynamic_index_in_dim(lengths, mine, 0, False), part * rows])
    blend = jnp.repeat(blend_weights, width // heads, axis=1)

    x = to_sequences(inputs, "seq", groups).reshape(rows, width).astype(F32)
    grad_out = to_sequences(cotangent, "seq", groups).reshape(rows, width)

    normed, norm1_back = jax.vjp(layer_norm, x, norm1_gain, norm1_bias)
    normed_low = normed.astype(BF16)
    qkv = times(normed_low, qkv_weight).astype(BF16)
    halo = jnp.zeros((TILE, 2 * width), BF16)
    state = jnp.zeros((2, width // PAIR, PAIR, 2 * PAIR), F32)
    later = state
    if parts > 1:
        onward = [(i, i + seqs) for i in range(devices - seqs)]
        halo = lax.ppermute(qkv[rows - TILE :, width:], "seq", onward)
        total = attend(meta, blend, qkv, halo, state)[1]
        state = from_parts(total, "seq", parts, seqs, True)
    attended = attend(meta, blend, qkv, halo, state)[0]
    first = x + times(attended, out_weight)
    second, norm2_back = jax.vjp(layer_norm, first, norm2_gain, norm2_bias)
    second_low = second.astype(BF16)
    pre = times(second_low, in_weight) + in_bias
    hidden, gelu_back = jax.vjp(jax.nn.gelu, pre)
    hidden_low = hidden.astype(BF16)
    result = (first + times(hidden_low, down_weight) + down_bias).astype(BF16)
    output = to_sequences(result.reshape(seqs, span, width), "seq", groups)

    grad_out_f = grad_out.astype(F32)
    grad_down_w = rows_product(hidden_low, grad_out)
    grad_down_b = jnp.sum(grad_out_f, axis=0)
    (grad_pre,) = gelu_back(times_transposed(grad_out, down_weight))
    grad_pre_low = grad_pre.astype(BF16)
    grad_in_b = jnp.sum(grad_pre_low.astype(F32), axis=0)
    grad_in_w = rows_product(second_low, grad_pre_low)
    grad_first_part, grad_gain2, grad_bias2 = norm2_back(times_transposed(grad_pre_low, in_weight))
    grad_first = grad_out_f + grad_first_part
    grad_att_low = grad_first.astype(BF16)
    grad_out_w = rows_product(attended, grad_att_low)
    grad_o = times_transposed(grad_att_low, out_weight)

    if parts > 1:
        total = attend_back(meta, blend, qkv, halo, state, later, grad_o)[3]
        later = from_parts(total, "seq", parts, seqs, False)
    grad_qkv, grad_halo, mix, _ = attend_back(meta, blend, qkv, halo, state, later, grad_o)
    if parts > 1:
        homeward = [(i + seqs, i) for i in range(devices - seqs)]
        back = lax.ppermute(grad_halo, "seq", homeward)
        tail = grad_qkv[rows - TILE :, width:].astype(F32) + back.astype(F32)
        grad_qkv = grad_qkv.at[rows - TILE :, width:].set(tail.astype(BF16))
    grad_blend = jnp.sum(mix.reshape(3, heads, width // heads), axis=-1)
    grad_qkv_w = rows_product(normed_low, grad_qkv)
    grad_x_part, grad_gain1, grad_bias1 = norm1_back(times_transposed(grad_qkv, qkv_weight))
    grad_x = (grad_first + grad_x_part).astype(BF16)
    input_grad = to_sequences(grad_x.reshape(seqs, span, width), "seq", groups)
    ring = Ring(lax.axis_size("batch"), devices)
    early, late, small = sum_over_devices(
        ring,
        (grad_in_w, grad_down_w, grad_out_w),
        (grad_qkv_w,),
        (grad_gain1, grad_bias1, grad_blend, grad_gain2, grad_bias2, grad_in_b, grad_down_b),
    )
    grad_in_w, grad_down_w, grad_out_w = early
    grad_gain1, grad_bias1, grad_blend, grad_gain2, grad_bias2, grad_in_b, grad_down_b = small
    return (
        output,
        input_grad,
        grad_gain1,
        grad_bias1,
        late[0],
        grad_blend,
        grad_out_w,
        grad_gain2,
        grad_bias2,
        grad_in_w,
        grad_in_b,
        grad_down_w,
        grad_down_b,
    )


def solution(mesh):
    rows = P("batch", "seq", None)
    return jax.shard_map(
        local,
        mesh=mesh,
        in_specs=(rows, rows, P("batch")) + (P(),) * 11,
        out_specs=(rows, rows) + (P(),) * 11,
        check_vma=False,
    )
```

```python
import functools

import jax
import jax.numpy as jnp
from jax import lax
from jax.experimental import pallas as pl
from jax.experimental.pallas import tpu as pltpu
from jax.sharding import PartitionSpec as P

WINDOW = 30
HEAD = 64
PAIR = 2 * HEAD
TILE = 64
EPS = 1e-05
NEG = -1e30
BF16 = jnp.bfloat16
F32 = jnp.float32


def layer_norm(field, gain, shift):
    center = field - jnp.mean(field, axis=-1, keepdims=True)
    spread = jnp.mean(center * center, axis=-1, keepdims=True)
    return center * lax.rsqrt(spread + EPS) * gain + shift


def rows_product(left, right):
    return lax.dot_general(
        left, right, (((0,), (0,)), ((), ())), preferred_element_type=F32
    )


def times_transposed(left, right):
    return lax.dot_general(
        left, right, (((1,), (1,)), ((), ())), preferred_element_type=F32
    )


def times(left, right):
    return lax.dot_general(
        left, right, (((1,), (0,)), ((), ())), preferred_element_type=F32
    )


def elu_feature(field):
    return jnp.where(field > 0, field + 1.0, jnp.exp(jnp.minimum(field, 0.0)))


def tanh_feature(field):
    return 1.0 + jnp.tanh(field)


def pair_lanes(p, part=0, width=PAIR):
    return slice(p * width + part * PAIR, p * width + (part + 1) * PAIR)


def store_split(ref, index, rows, block):
    lane = lax.broadcasted_iota(jnp.int32, (block.shape[0], PAIR), 1)
    for p in range(block.shape[1] // PAIR):
        pair = block[:, pair_lanes(p)]
        for h in range(2):
            mine = (lane < HEAD) if h == 0 else (lane >= HEAD)
            ref[index + (rows, pair_lanes(p, h, 2 * PAIR))] = jnp.where(mine, pair, 0.0).astype(
                BF16
            )


def load_split(ref, index, rows, p):
    return jnp.concatenate([ref[index + (rows, pair_lanes(p, h, 2 * PAIR))] for h in range(2)], 0)


def tall(block):
    return jnp.concatenate([block[:, :PAIR], block[:, PAIR:]], 0)


def fill_features(meta_ref, q_ref, k_ref, v_ref, halo_k, halo_v, keys, values, fq, fk, split):
    rows, width = q_ref.shape
    chunk = 2 * TILE
    front = pl.ds(0, TILE)
    zero = jnp.zeros((TILE, width), F32)
    store_split(keys, (), front, halo_k[...].astype(F32) * 0.125)
    store_split(values, (), front, halo_v[...].astype(F32))
    for c in range(2):
        store_split(fk, (c,), front, zero)

    def fill(step, carry):
        at = pl.multiple_of(step * chunk, chunk)
        here, there = pl.ds(at, chunk), pl.ds(at + TILE, chunk)
        q = q_ref[here, :].astype(F32)
        k = k_ref[here, :].astype(F32)
        store_split(keys, (), there, k * 0.125)
        store_split(values, (), there, v_ref[here, :].astype(F32))
        position = meta_ref[1] + at + lax.broadcasted_iota(jnp.int32, (chunk, width), 0)
        valid = position < meta_ref[0]
        for c, feature in enumerate((elu_feature, tanh_feature)):
            if split:
                store_split(fq, (c,), here, feature(q))
            else:
                fq[c, here, :] = feature(q).astype(BF16)
            store_split(fk, (c,), there, jnp.where(valid, feature(k), 0.0))
        return carry

    lax.fori_loop(0, rows // chunk, fill, 0)


def tile_masks(meta_ref, tile):
    shape = (TILE, 2 * PAIR)
    row = lax.broadcasted_iota(jnp.int32, shape, 0)
    lane = lax.broadcasted_iota(jnp.int32, shape, 1) % PAIR
    back = row + TILE - lane
    key = meta_ref[1] + (tile - 1) * TILE + lane
    known = (key >= 0) & (key < meta_ref[0])
    near = (back >= 0) & (back <= WINDOW) & (known | (back == 0))
    return near, back >= 0


def softmax_pair(scores):
    halves = []
    for h in range(2):
        part = scores[:, h * PAIR : (h + 1) * PAIR]
        part = jnp.exp(part - jnp.max(part, axis=1, keepdims=True))
        halves.append(part * (1.0 / jnp.sum(part, axis=1, keepdims=True)))
    return jnp.concatenate(halves, 1)


def tile_constants():
    row = lax.broadcasted_iota(jnp.int32, (2 * PAIR, PAIR), 0)
    lane = lax.broadcasted_iota(jnp.int32, (2 * PAIR, PAIR), 1)
    ones = jnp.where(row // PAIR == lane // HEAD, 1.0, 0.0).astype(BF16)
    row = lax.broadcasted_iota(jnp.int32, (PAIR, 2 * PAIR), 0)
    lane = lax.broadcasted_iota(jnp.int32, (PAIR, 2 * PAIR), 1)
    return ones, row // HEAD == (lane % PAIR) // HEAD


def whole(split):
    half = split.shape[0] // 2
    return split[:half] + split[half:]


def state_share(block, fks, vs):
    ones = jnp.ones((TILE, PAIR), BF16)
    share = rows_product(whole(fks), jnp.concatenate([whole(vs), ones], 1))
    return jnp.where(block, share, 0.0)


def attend_kernel(
    meta_ref, blend_ref, q_ref, k_ref, v_ref, halo_k, halo_v, state_ref, att_ref, total_ref,
    keys, values, fq, fk, state,
):
    rows, width = q_ref.shape
    pairs = range(width // PAIR)
    fill_features(meta_ref, q_ref, k_ref, v_ref, halo_k, halo_v, keys, values, fq, fk, False)
    state[...] = state_ref[...]
    ones, block = tile_constants()

    def step(tile, carry):
        at = pl.multiple_of(tile * TILE, TILE)
        here, window, past = pl.ds(at, TILE), pl.ds(at, 2 * TILE), pl.ds(at, TILE)
        near_mask, far_mask = tile_masks(meta_ref, tile)
        q = [q_ref[here, pair_lanes(p)] for p in pairs]
        feats = [[fq[c, here, pair_lanes(p)] for c in range(2)] for p in pairs]
        held = [[state[c, p] for c in range(2)] for p in pairs]
        added = [
            [
                state_share(block, load_split(fk, (c,), past, p), load_split(values, (), past, p))
                for c in range(2)
            ]
            for p in pairs
        ]
        near = [times_transposed(q[p], load_split(keys, (), window, p)) for p in pairs]
        far = [
            [times_transposed(feats[p][c], load_split(fk, (c,), window, p)) for c in range(2)]
            for p in pairs
        ]
        near = [softmax_pair(jnp.where(near_mask, n, NEG)) for n in near]
        far = [[jnp.where(far_mask, f, 0.0) for f in fs] for fs in far]
        stack = [jnp.concatenate([n] + fs, 0).astype(BF16) for n, fs in zip(near, far)]
        wide = [jnp.concatenate([load_split(values, (), window, p), ones], 1) for p in pairs]
        sums = [times(s, w) for s, w in zip(stack, wide)]
        old = [[times(feats[p][c], held[p][c].astype(BF16)) for c in range(2)] for p in pairs]
        for p in pairs:
            mixed = blend_ref[0:1, pair_lanes(p)] * sums[p][:TILE, :PAIR]
            for c in range(2):
                mine = sums[p][(c + 1) * TILE : (c + 2) * TILE] + old[p][c]
                mixed = mixed + blend_ref[c + 1 : c + 2, pair_lanes(p)] * (
                    mine[:, :PAIR] / mine[:, PAIR:]
                )
            att_ref[here, pair_lanes(p)] = mixed.astype(BF16)
        for p in pairs:
            for c in range(2):
                state[c, p] = held[p][c] + added[p][c]
        return carry

    lax.fori_loop(0, rows // TILE, step, 0)
    last = pl.ds(rows, TILE)
    for p in pairs:
        for c in range(2):
            total_ref[c, p] = state[c, p] + state_share(
                block, load_split(fk, (c,), last, p), load_split(values, (), last, p)
            )


def slopes_of(field):
    small = jnp.exp(jnp.minimum(field, 0.0))
    bent = jnp.tanh(field)
    return [jnp.where(field > 0, 1.0, small), 1.0 - bent * bent]


def split_heads(block):
    lane = lax.broadcasted_iota(jnp.int32, block.shape, 1)
    zero = jnp.zeros_like(block)
    return jnp.concatenate(
        [jnp.where(lane < HEAD, block, zero), jnp.where(lane < HEAD, zero, block)], 0
    )


def attend_back_kernel(
    together, meta_ref, blend_ref, q_ref, k_ref, v_ref, halo_k, halo_v, state_ref, later_ref,
    go_ref, gq_ref, gk_ref, gv_ref, hk_ref, hv_ref, mix_ref, total_ref,
    keys, values, fq, fk, state, gk, gv, gfk, gon,
):
    rows, width = q_ref.shape
    pairs = range(width // PAIR)
    tiles = rows // TILE
    near_by = range(together)
    units = [(s, p) for s in near_by for p in pairs]
    fill_features(meta_ref, q_ref, k_ref, v_ref, halo_k, halo_v, keys, values, fq, fk, True)
    state[...] = state_ref[...]
    mix_ref[...] = jnp.zeros_like(mix_ref)
    gk[:TILE, :] = jnp.zeros((TILE, width), F32)
    gv[:TILE, :] = jnp.zeros((TILE, width), F32)
    gfk[:, :TILE, :] = jnp.zeros((2, TILE, width), F32)
    ones, block = tile_constants()
    row = lax.broadcasted_iota(jnp.int32, (2 * PAIR, PAIR), 0) % PAIR
    lane = lax.broadcasted_iota(jnp.int32, (2 * PAIR, PAIR), 1)
    heads = jnp.where(row // HEAD == lane // HEAD, 1.0, 0.0).astype(BF16)
    plain_ones = jnp.ones((TILE, PAIR), BF16)
    high = (lax.broadcasted_iota(jnp.int32, (TILE, PAIR), 1) % HEAD) < HEAD // 2

    def step(number, carry):
        first = number * together
        at = pl.multiple_of(first * TILE, TILE)
        here = [pl.ds(at + s * TILE, TILE) for s in range(together + 1)]
        window = [pl.ds(at + s * TILE, 2 * TILE) for s in near_by]
        masks = [tile_masks(meta_ref, first + s) for s in near_by]
        q = {(s, p): q_ref[here[s], pair_lanes(p)] for s, p in units}
        go = {(s, p): go_ref[here[s], pair_lanes(p)] for s, p in units}
        blend = [[blend_ref[c : c + 1, pair_lanes(p)] for c in range(3)] for p in pairs]
        fqs = {(s, p): [load_split(fq, (c,), here[s], p) for c in range(2)] for s, p in units}
        feats = {u: [whole(f) for f in fqs[u]] for u in units}
        ks = {(s, p): load_split(keys, (), window[s], p) for s, p in units}
        fks = {(s, p): [load_split(fk, (c,), window[s], p) for c in range(2)] for s, p in units}
        wide = {
            (s, p): jnp.concatenate([load_split(values, (), window[s], p), ones], 1)
            for s, p in units
        }
        held = {(0, p): [state[c, p] for c in range(2)] for p in pairs}
        for s, p in units:
            vs = load_split(values, (), here[s], p)
            held[s + 1, p] = [
                held[s, p][c] + state_share(block, load_split(fk, (c,), here[s], p), vs)
                for c in range(2)
            ]
        past = {u: [h.astype(BF16) for h in held[u]] for u in units}
        old_k = [gk[here[0], pair_lanes(p)] for p in pairs]
        old_v = [gv[here[0], pair_lanes(p)] for p in pairs]
        old_f = [[gfk[c, here[0], pair_lanes(p)] for c in range(2)] for p in pairs]

        near = {u: times_transposed(q[u], ks[u]) for u in units}
        far = {u: [times_transposed(feats[u][c], fks[u][c]) for c in range(2)] for u in units}
        old = {u: [times(feats[u][c], past[u][c]) for c in range(2)] for u in units}
        near = {u: softmax_pair(jnp.where(masks[u[0]][0], near[u], NEG)) for u in units}
        far = {u: [jnp.where(masks[u[0]][1], f, 0.0).astype(BF16) for f in far[u]] for u in units}
        stack = {u: jnp.concatenate([near[u].astype(BF16)] + far[u], 0) for u in units}
        sums = {u: times(stack[u], wide[u]) for u in units}
        scales, prods = {}, {}
        for u in units:
            outs = [sums[u][:TILE, :PAIR]]
            scales[u] = [jnp.broadcast_to(blend[u[1]][0], (TILE, PAIR))]
            for c in range(2):
                mine = sums[u][(c + 1) * TILE : (c + 2) * TILE] + old[u][c]
                inverse = 1.0 / mine[:, PAIR:]
                outs.append(mine[:, :PAIR] * inverse)
                scales[u].append(blend[u[1]][c + 1] * inverse)
            prods[u] = jnp.concatenate([go[u] * out for out in outs], 0)
        deltas = {}
        for u in units:
            low = prods[u].astype(BF16)
            rest = (prods[u] - low.astype(F32)).astype(BF16)
            deltas[u] = times(jnp.concatenate([low, rest], 1), heads)
        grads = {}
        for u in units:
            grads[u] = []
            for c in range(3):
                delta = scales[u][c] * deltas[u][c * TILE : (c + 1) * TILE] * (-2.0 / HEAD)
                delta_low = delta.astype(BF16).astype(F32)
                delta = jnp.where(high, delta_low, delta - delta_low)
                grads[u].append(jnp.concatenate([scales[u][c] * go[u], delta], 1).astype(BF16))
        back = {u: times_transposed(jnp.concatenate(grads[u], 0), wide[u]) for u in units}
        late = {u: [times_transposed(grads[u][c + 1], past[u][c]) for c in range(2)] for u in units}
        ds = {u: (near[u] * back[u][:TILE]).astype(BF16) for u in units}
        gas = {
            u: [
                jnp.where(masks[u[0]][1], back[u][(c + 1) * TILE : (c + 2) * TILE], 0.0).astype(BF16)
                for c in range(2)
            ]
            for u in units
        }
        gq_near = {u: times(ds[u], ks[u]) for u in units}
        gq_far = {u: [times(gas[u][c], fks[u][c]) + late[u][c] for c in range(2)] for u in units}
        new_k = {u: rows_product(tall(ds[u]), split_heads(q[u] * 0.125)) for u in units}
        new_f = {u: [rows_product(tall(gas[u][c]), fqs[u][c]) for c in range(2)] for u in units}
        new_v = {
            u: rows_product(
                jnp.concatenate([tall(stack[u][c * TILE : (c + 1) * TILE]) for c in range(3)], 0),
                jnp.concatenate([split_heads(g[:, :PAIR]) for g in grads[u]], 0),
            )
            for u in units
        }

        def overlap(old, new, p):
            parts = [old + new(0, p)[:TILE]]
            parts += [new(s, p)[TILE:] + new(s + 1, p)[:TILE] for s in range(together - 1)]
            return parts + [new(together - 1, p)[TILE:]]

        for s, p in units:
            u, lanes = (s, p), pair_lanes(p)
            slopes = slopes_of(q[u].astype(F32))
            gq = gq_near[u] + slopes[0] * gq_far[u][0] + slopes[1] * gq_far[u][1]
            gq_ref[here[s], lanes] = gq.astype(BF16)
            for c in range(2):
                gon[c, here[s], p * 2 * PAIR : (p + 1) * 2 * PAIR] = grads[u][c + 1]
        for p in pairs:
            lanes = pair_lanes(p)
            for c in range(3):
                mix_ref[c : c + 1, lanes] += sum(
                    jnp.sum(prods[s, p][c * TILE : (c + 1) * TILE], axis=0, keepdims=True)
                    for s in near_by
                )
            for rows_at, part in zip(here, overlap(old_k[p], lambda s, p: new_k[s, p], p)):
                gk[rows_at, lanes] = part
            for rows_at, part in zip(here, overlap(old_v[p], lambda s, p: new_v[s, p], p)):
                gv[rows_at, lanes] = part
            for c in range(2):
                parts = overlap(old_f[p][c], lambda s, p: new_f[s, p][c], p)
                for rows_at, part in zip(here, parts):
                    gfk[c, rows_at, lanes] = part
                state[c, p] = held[together, p][c]
        return carry

    lax.fori_loop(0, tiles // together, step, 0)
    hk_ref[...] = gk[:TILE, :].astype(BF16)
    hv_ref[...] = gv[:TILE, :].astype(BF16)
    state[...] = later_ref[...]

    def come(at, c, p):
        here = pl.ds(at, TILE)
        grads = gon[c, here, p * 2 * PAIR : (p + 1) * 2 * PAIR]
        share = rows_product(whole(load_split(fq, (c,), here, p)), grads)
        return jnp.where(block, share, 0.0)

    def back_step(number, carry):
        first = tiles - 1 - number * together
        at = [pl.multiple_of((first - s) * TILE, TILE) for s in near_by]
        here = [pl.ds(a, TILE) for a in at]
        there = [pl.ds(a + TILE, TILE) for a in at]
        held = {(-1, p): [state[c, p] for c in range(2)] for p in pairs}
        for s, p in units:
            tile = first - s + 2
            nearer = pl.multiple_of(jnp.minimum(tile, tiles - 1) * TILE, TILE)
            held[s, p] = [
                held[s - 1, p][c] + jnp.where(tile < tiles, come(nearer, c, p), 0.0)
                for c in range(2)
            ]
        later = {u: [h.astype(BF16) for h in held[u]] for u in units}
        vs = {(s, p): whole(load_split(values, (), there[s], p)) for s, p in units}
        fks = {
            (s, p): jnp.concatenate([whole(load_split(fk, (c,), there[s], p)) for c in range(2)], 1)
            for s, p in units
        }
        wide = {u: jnp.concatenate([vs[u], plain_ones], 1) for u in units}
        far_k = {u: [times_transposed(wide[u], later[u][c]) for c in range(2)] for u in units}
        far_v = {
            u: times(fks[u], jnp.concatenate([g[:, :PAIR] for g in later[u]], 0)) for u in units
        }
        for s, p in units:
            u, lanes = (s, p), pair_lanes(p)
            position = meta_ref[1] + at[s] + lax.broadcasted_iota(jnp.int32, (TILE, PAIR), 0)
            slopes = slopes_of(k_ref[here[s], lanes].astype(F32))
            grad_f = [gfk[c, there[s], lanes] + far_k[u][c] for c in range(2)]
            bent = slopes[0] * grad_f[0] + slopes[1] * grad_f[1]
            grad_k = gk[there[s], lanes] + jnp.where(position < meta_ref[0], bent, 0.0)
            gk_ref[here[s], lanes] = grad_k.astype(BF16)
            gv_ref[here[s], lanes] = (gv[there[s], lanes] + far_v[u]).astype(BF16)
        for p in pairs:
            for c in range(2):
                state[c, p] = held[together - 1, p][c]
        return carry

    lax.fori_loop(0, tiles // together, back_step, 0)
    for p in pairs:
        for c in range(2):
            total_ref[c, p] = state[c, p] + come(0, c, p) + come(TILE, c, p)


def attention_specs(rows, width, count, number, split):
    lanes, calls = width // count, count

    def columns(height, part):
        return pl.BlockSpec((height, lanes), lambda _: (0, part * calls + number))

    state = pl.BlockSpec(
        (2, lanes // PAIR, PAIR, 2 * PAIR), lambda _: (0, number, 0, 0)
    )
    ins = [pl.BlockSpec(memory_space=pltpu.SMEM), columns(3, 0)]
    ins += [columns(rows, part) for part in range(3)]
    ins += [columns(TILE, part) for part in range(2)]
    scratch = [
        pltpu.VMEM((rows + TILE, 2 * lanes), BF16),
        pltpu.VMEM((rows + TILE, 2 * lanes), BF16),
        pltpu.VMEM((2, rows, (2 if split else 1) * lanes), BF16),
        pltpu.VMEM((2, rows + TILE, 2 * lanes), BF16),
        pltpu.VMEM((2, lanes // PAIR, PAIR, 2 * PAIR), F32),
    ]
    return lanes, columns, ins, state, scratch


def outcome(shape, dtype):
    return jax.ShapeDtypeStruct(shape, dtype), pl.BlockSpec(shape, lambda _: (0,) * len(shape))


def attend(meta, blend, qkv, halo, state):
    rows, width = qkv.shape[0], qkv.shape[1] // 3
    _, _, ins, held, scratch = attention_specs(rows, width, 1, 0, False)
    shapes, blocks = zip(outcome((rows, width), BF16), outcome(state.shape, F32))
    return pl.pallas_call(
        attend_kernel,
        grid=(1,),
        out_shape=shapes,
        in_specs=ins + [held],
        out_specs=blocks,
        scratch_shapes=scratch,
        compiler_params=pltpu.CompilerParams(vmem_limit_bytes=48 * 2**20),
        cost_estimate=pl.CostEstimate(
            flops=rows * width * 48000, bytes_accessed=rows * width * 8, transcendentals=0
        ),
    )(meta, blend, qkv, qkv, qkv, halo, halo, state)


def attend_back(meta, blend, qkv, halo, state, later, go, calls, number):
    rows, width = qkv.shape[0], qkv.shape[1] // 3
    lanes, columns, ins, held, scratch = attention_specs(rows, width, calls, number, True)
    shapes, blocks = zip(
        *[outcome((rows, lanes), BF16)] * 3,
        *[outcome((TILE, lanes), BF16)] * 2,
        outcome((3, lanes), F32),
        outcome((2, lanes // PAIR, PAIR, 2 * PAIR), F32),
    )
    together = 4 * PAIR // lanes
    return pl.pallas_call(
        functools.partial(attend_back_kernel, together),
        grid=(1,),
        out_shape=shapes,
        in_specs=ins + [held, held, columns(rows, 0)],
        out_specs=blocks,
        scratch_shapes=scratch
        + [
            pltpu.VMEM((rows + TILE, lanes), F32),
            pltpu.VMEM((rows + TILE, lanes), F32),
            pltpu.VMEM((2, rows + TILE, lanes), F32),
            pltpu.VMEM((2, rows, 2 * lanes), BF16),
        ],
        compiler_params=pltpu.CompilerParams(vmem_limit_bytes=56 * 2**20),
        cost_estimate=pl.CostEstimate(
            flops=rows * lanes * 96000, bytes_accessed=rows * lanes * 16, transcendentals=0
        ),
    )(meta, blend, qkv, qkv, qkv, halo, halo, state, later, go)


CHUNK = 256
GELU_A, GELU_B = 0.7978845608028654, 0.044715


def normalized(field):
    center = field - jnp.mean(field, axis=-1, keepdims=True)
    scale = lax.rsqrt(jnp.mean(center * center, axis=-1, keepdims=True) + EPS)
    return center * scale, scale


def norm_back(grad, unit, scale):
    shared = jnp.mean(grad * unit, axis=-1, keepdims=True)
    return scale * (grad - jnp.mean(grad, axis=-1, keepdims=True) - unit * shared)


def gelu_pair(field):
    square = field * field
    bent = jnp.tanh(GELU_A * field * (1.0 + GELU_B * square))
    half = 0.5 + 0.5 * bent
    slope = half + 0.5 * field * (1.0 - bent * bent) * (GELU_A + 3.0 * GELU_A * GELU_B * square)
    return field * half, slope


def column_sum(block):
    return jnp.sum(block, axis=0, keepdims=True)


def feed_kernel(
    pieces, x_ref, att_ref, grad_ref, out_w, gain_ref, bias_ref, in_w, in_b, down_w, down_b,
    result_ref, first_ref, go_ref, packed_ref, small_ref, wide_ref,
    second, hidden, pre_low, att_low,
):
    rows, width = x_ref.shape
    inner = in_w.shape[1]
    small_ref[...] = jnp.zeros_like(small_ref)
    wide_ref[...] = jnp.zeros_like(wide_ref)

    def step(number, carry):
        here = pl.ds(pl.multiple_of(number * CHUNK, CHUNK), CHUNK)
        first = x_ref[here, :].astype(F32) + times(att_ref[here, :], out_w[...])
        unit, scale = normalized(first)
        low = (unit * gain_ref[...] + bias_ref[...]).astype(BF16)
        second[here, :] = low
        grad = grad_ref[here, :]
        grad_f = grad.astype(F32)
        result = first + down_b[...]
        back = jnp.zeros((CHUNK, width), F32)
        for at in range(0, inner, width):
            lanes = slice(at, at + width)
            act, slope = gelu_pair(times(low, in_w[:, lanes]) + in_b[:, lanes])
            act = act.astype(BF16)
            hidden[here, lanes] = act
            result = result + times(act, down_w[lanes, :])
            pre = (times_transposed(grad, down_w[lanes, :]) * slope).astype(BF16)
            pre_low[here, lanes] = pre
            wide_ref[:, lanes] += column_sum(pre.astype(F32))
            back = back + times_transposed(pre, in_w[:, lanes])
        result_ref[here, :] = result.astype(BF16)
        small_ref[0:1, :] += column_sum(back * unit)
        small_ref[1:2, :] += column_sum(back)
        small_ref[2:3, :] += column_sum(grad_f)
        grad_first = grad_f + norm_back(back * gain_ref[...], unit, scale)
        first_ref[here, :] = grad_first
        grad_att = grad_first.astype(BF16)
        att_low[here, :] = grad_att
        go_ref[here, :] = times_transposed(grad_att, out_w[...])
        return carry

    lax.fori_loop(0, rows // CHUNK, step, 0)
    for at in range(0, inner, width):
        lanes = slice(at, at + width)
        packed_ref[:, lanes] = rows_product(second[...], pre_low[:, lanes]).astype(BF16)
    packed_ref[:, inner : inner + width] = rows_product(att_ref[...], att_low[...]).astype(BF16)
    tall_rows, flat_rows = inner // pieces, width // pieces
    for at in range(0, inner, width):
        share = rows_product(hidden[:, at : at + width], grad_ref[...]).astype(BF16)
        for below in range(0, width, flat_rows):
            piece, block = divmod(at + below, tall_rows)
            lanes = inner + width + block // flat_rows * width
            packed_ref[piece * flat_rows : (piece + 1) * flat_rows, lanes : lanes + width] = share[
                below : below + flat_rows
            ]


def feed_forward(pieces, x, att, grad, out_w, gain, bias, in_w, in_b, down_w, down_b):
    rows, width = x.shape
    inner = in_w.shape[1]
    return pl.pallas_call(
        functools.partial(feed_kernel, pieces),
        out_shape=(
            jax.ShapeDtypeStruct((rows, width), BF16),
            jax.ShapeDtypeStruct((rows, width), F32),
            jax.ShapeDtypeStruct((rows, width), F32),
            jax.ShapeDtypeStruct((width, 2 * inner + width), BF16),
            jax.ShapeDtypeStruct((3, width), F32),
            jax.ShapeDtypeStruct((1, inner), F32),
        ),
        in_specs=[pl.BlockSpec(memory_space=pltpu.VMEM)] * 10,
        out_specs=(pl.BlockSpec(memory_space=pltpu.VMEM),) * 6,
        scratch_shapes=[
            pltpu.VMEM((rows, width), BF16),
            pltpu.VMEM((rows, inner), BF16),
            pltpu.VMEM((rows, inner), BF16),
            pltpu.VMEM((rows, width), BF16),
        ],
        compiler_params=pltpu.CompilerParams(vmem_limit_bytes=56 * 2**20),
        cost_estimate=pl.CostEstimate(
            flops=rows * width * inner * 24, bytes_accessed=rows * width * 20, transcendentals=0
        ),
    )(x, att, grad, out_w, gain[None], bias[None], in_w, in_b[None], down_w, down_b[None])


def project_back_kernel(
    calls, x_ref, first_ref, w_ref, gain_ref, bias_ref, mix_ref, small2_ref, wide_ref, *refs
):
    grads = refs[: 3 * calls]
    result_ref, packed_ref, normed, gathered, sums, rows_of = refs[3 * calls :]
    rows, width = x_ref.shape
    sums[...] = jnp.zeros_like(sums)

    def step(number, carry):
        here = pl.ds(pl.multiple_of(number * CHUNK, CHUNK), CHUNK)
        unit, scale = normalized(x_ref[here, :].astype(F32))
        normed[here, :] = (unit * gain_ref[...] + bias_ref[...]).astype(BF16)
        grad = jnp.concatenate([ref[here, :] for ref in grads], 1)
        gathered[here, :] = grad
        back = times_transposed(grad, w_ref[...])
        sums[0:1, :] += column_sum(back * unit)
        sums[1:2, :] += column_sum(back)
        grad_x = first_ref[here, :] + norm_back(back * gain_ref[...], unit, scale)
        result_ref[here, :] = grad_x.astype(BF16)
        return carry

    lax.fori_loop(0, rows // CHUNK, step, 0)
    for at in range(0, 3 * width, width):
        lanes = slice(at, at + width)
        packed_ref[:, lanes] = rows_product(normed[...], gathered[:, lanes]).astype(BF16)
    rows_of[...] = jnp.zeros_like(rows_of)
    at = 0
    for ref in (sums, small2_ref, mix_ref, wide_ref):
        for row in range(ref.shape[0]):
            for lane in range(0, ref.shape[1], PAIR):
                rows_of[at : at + 1, :] = ref[row : row + 1, lane : lane + PAIR]
                at += 1
    high = rows_of[...].astype(BF16)
    packed_ref[:, 3 * width : 3 * width + PAIR] = high
    packed_ref[:, 3 * width + PAIR :] = (rows_of[...] - high.astype(F32)).astype(BF16)


def project_back(x, grad_first, weight, gain, bias, mix, small2, wide, grads):
    rows, width = x.shape
    vmem = pl.BlockSpec(memory_space=pltpu.VMEM)
    return pl.pallas_call(
        functools.partial(project_back_kernel, len(grads) // 3),
        out_shape=(
            jax.ShapeDtypeStruct((rows, width), BF16),
            jax.ShapeDtypeStruct((width, 3 * width + 2 * PAIR), BF16),
        ),
        in_specs=[vmem] * (8 + len(grads)),
        out_specs=(vmem, vmem),
        scratch_shapes=[
            pltpu.VMEM((rows, width), BF16),
            pltpu.VMEM((rows, 3 * width), BF16),
            pltpu.VMEM((2, width), F32),
            pltpu.VMEM((width, PAIR), F32),
        ],
        compiler_params=pltpu.CompilerParams(vmem_limit_bytes=48 * 2**20),
        cost_estimate=pl.CostEstimate(
            flops=rows * width * width * 24, bytes_accessed=rows * width * 20, transcendentals=0
        ),
    )(x, grad_first, weight, gain[None], bias[None], mix, small2, wide, *grads)


def to_sequences(block, axis, groups):
    return lax.all_to_all(block, axis, 0, 0, axis_index_groups=groups)


def from_parts(total, axis, parts, stride, forward):
    size = lax.axis_size(axis)
    low = total.astype(BF16)
    result = jnp.zeros_like(total)
    for hop in range(1, parts):
        distance = hop * stride
        route = [
            (i, i + distance) if forward else (i + distance, i) for i in range(size - distance)
        ]
        result = result + lax.ppermute(low, axis, route).astype(F32)
    return result


class Ring:
    def __init__(self, batch, seq):
        self.batch, self.seq = batch, seq
        self.low = 2 ** ((seq.bit_length() - 1) // 2)
        self.sizes = {"core": 2, "near": batch // 2 * self.low, "far": seq // self.low}
        self.pieces = batch * seq

    def place(self, s, b):
        return {"core": b % 2, "near": b // 2 * self.low + s % self.low, "far": s // self.low}

    def device(self, place):
        s = place["far"] * self.low + place["near"] % self.low
        return s * self.batch + place["near"] // self.low * 2 + place["core"]

    def mine(self):
        return self.place(lax.axis_index("seq"), lax.axis_index("batch"))

    def swap(self, value, level, k):
        route = []
        for s in range(self.seq):
            for b in range(self.batch):
                place = self.place(s, b)
                place[level] ^= k
                route.append((s * self.batch + b, self.device(place)))
        return lax.ppermute(value, ("seq", "batch"), route)

    def scatter(self, value, level, fine):
        size, me = self.sizes[level], self.mine()[level]
        value = value.reshape((size, value.shape[0] // size) + value.shape[1:])
        parts = [
            self.swap(lax.dynamic_index_in_dim(value, me ^ k, 0, False), level, k)
            for k in range(1, size)
        ]
        total = lax.dynamic_index_in_dim(value, me, 0, False).astype(F32)
        for part in parts:
            total = total + part.astype(F32)
        if not fine:
            return total.astype(BF16)
        end = total.shape[-1] - 2 * fine
        exact = total[..., end : end + fine] + total[..., end + fine :]
        high = lax.reduce_precision(exact, 8, 7)
        return jnp.concatenate([total[..., :end], high, exact - high], -1).astype(BF16)

    def gather(self, value, level):
        parts = [value] + [self.swap(value, level, k) for k in range(1, self.sizes[level])]
        return jnp.concatenate(parts, 0)

    def reduce(self, value, fine=0):
        value = value.reshape(self.pieces, value.shape[0] // self.pieces, value.shape[1])
        for level in ("core", "near", "far"):
            value = self.scatter(value, level, fine)
        for level in ("far", "near"):
            value = self.gather(value, level)
        return value, self.swap(value, "core", 1)

    def order(self):
        me = self.mine()
        piece = jnp.arange(self.pieces, dtype=jnp.int32)
        far, near = self.sizes["far"], self.sizes["near"]
        core = (piece // (far * near)) ^ me["core"]
        near = ((piece // far) % near) ^ me["near"]
        return (core * self.sizes["near"] + near) * far + ((piece % far) ^ me["far"])


def unpack_kernel(write, order_ref, own_ref, other_ref, *out_refs):
    half = own_ref.shape[0]
    for piece in range(2 * half):
        at = order_ref[piece]

        @pl.when(at < half)
        def _(piece=piece, at=at):
            write(piece, own_ref[at].astype(F32), out_refs)

        @pl.when(at >= half)
        def _(piece=piece, at=at):
            write(piece, other_ref[at - half].astype(F32), out_refs)


def write_feed(piece, block, out_refs):
    in_ref, out_ref, down_ref = out_refs
    size, inner, width = block.shape[0], in_ref.shape[1], in_ref.shape[0]
    rows = slice(piece * size, (piece + 1) * size)
    in_ref[rows, :] = block[:, :inner]
    out_ref[rows, :] = block[:, inner : inner + width]
    tall_rows = inner // (width // size)
    for below in range(0, tall_rows, size):
        at = inner + width + below // size * width
        down_ref[piece * tall_rows + below : piece * tall_rows + below + size, :] = block[
            :, at : at + width
        ]


def write_project(piece, block, out_refs):
    w_ref, small_ref = out_refs
    size, end = block.shape[0], w_ref.shape[1]
    rows = slice(piece * size, (piece + 1) * size)
    w_ref[rows, :] = block[:, :end]
    small_ref[rows, :] = block[:, end : end + PAIR] + block[:, end + PAIR :]


def unpack(write, order, halves, shapes):
    vmem = pl.BlockSpec(memory_space=pltpu.VMEM)
    return pl.pallas_call(
        functools.partial(unpack_kernel, write),
        out_shape=[jax.ShapeDtypeStruct(shape, F32) for shape in shapes],
        in_specs=[pl.BlockSpec(memory_space=pltpu.SMEM), vmem, vmem],
        out_specs=[vmem] * len(shapes),
        compiler_params=pltpu.CompilerParams(vmem_limit_bytes=48 * 2**20),
        cost_estimate=pl.CostEstimate(
            flops=0, bytes_accessed=8 * halves[0].size, transcendentals=0
        ),
    )(order, *halves)


def local(
    inputs,
    cotangent,
    lengths,
    norm1_gain,
    norm1_bias,
    qkv_weight,
    blend_weights,
    out_weight,
    norm2_gain,
    norm2_bias,
    in_weight,
    in_bias,
    down_weight,
    down_bias,
):
    seqs, span, width = inputs.shape
    heads = blend_weights.shape[1]
    devices = lax.axis_size("seq")
    parts = devices // seqs
    rows = seqs * span
    index = lax.axis_index("seq")
    groups = None
    if parts > 1:
        groups = [[r * seqs + s for s in range(seqs)] for r in range(parts)]
    mine, part = index % seqs, index // seqs
    meta = jnp.stack([lax.dynamic_index_in_dim(lengths, mine, 0, False), part * rows])
    blend = jnp.repeat(blend_weights, width // heads, axis=1)

    ring = Ring(lax.axis_size("batch"), devices)
    by_ring = width % (16 * ring.pieces) == 0
    inner = in_weight.shape[1]

    x = to_sequences(inputs, "seq", groups).reshape(rows, width)
    grad_out = to_sequences(cotangent, "seq", groups).reshape(rows, width)

    normed = layer_norm(x.astype(F32), norm1_gain, norm1_bias).astype(BF16)
    qkv = times(normed, qkv_weight).astype(BF16)
    halo = jnp.zeros((TILE, 2 * width), BF16)
    state = jnp.zeros((2, width // PAIR, PAIR, 2 * PAIR), F32)
    later = state
    if parts > 1:
        onward = [(i, i + seqs) for i in range(devices - seqs)]
        halo = lax.ppermute(qkv[rows - TILE :, width:], "seq", onward)
        total = attend(meta, blend, qkv, halo, state)[1]
        state = from_parts(total, "seq", parts, seqs, True)
    attended = attend(meta, blend, qkv, halo, state)[0]

    result, grad_first, grad_o, feed_grads, small2, grad_in_b = feed_forward(
        ring.pieces if by_ring else 16,
        x, attended, grad_out, out_weight, norm2_gain, norm2_bias,
        in_weight, in_bias, down_weight, down_bias,
    )
    output = to_sequences(result.reshape(seqs, span, width), "seq", groups)
    if by_ring:
        feed_halves = ring.reduce(feed_grads)

    calls = 4

    def back(later):
        return [
            attend_back(meta, blend, qkv, halo, state, later, grad_o, calls, number)
            for number in range(calls)
        ]

    if parts > 1:
        total = jnp.concatenate([call[6] for call in back(later)], 1)
        later = from_parts(total, "seq", parts, seqs, False)
    backs = back(later)
    grads = [[call[part] for call in backs] for part in range(3)]
    if parts > 1:
        homeward = [(i + seqs, i) for i in range(devices - seqs)]
        for part in (1, 2):
            for number in range(calls):
                received = lax.ppermute(backs[number][part + 2], "seq", homeward)
                grad = grads[part][number]
                tail = grad[rows - TILE :].astype(F32) + received.astype(F32)
                grads[part][number] = grad.at[rows - TILE :].set(tail.astype(BF16))
    mix = jnp.concatenate([call[5] for call in backs], 1)
    grad_x, project_grads = project_back(
        x, grad_first, qkv_weight, norm1_gain, norm1_bias, mix, small2, grad_in_b,
        grads[0] + grads[1] + grads[2],
    )
    input_grad = to_sequences(grad_x.reshape(seqs, span, width), "seq", groups)

    if by_ring:
        order = ring.order()
        project_halves = ring.reduce(project_grads, PAIR)
    else:
        order = jnp.arange(16, dtype=jnp.int32)
        total = lax.psum((feed_grads.astype(F32), project_grads.astype(F32)), ("seq", "batch"))
        feed_halves, project_halves = [
            [half.reshape(8, width // 16, -1) for half in (t[: width // 2], t[width // 2 :])]
            for t in total
        ]
    grad_in_w, grad_out_w, grad_down_w = unpack(
        write_feed, order, feed_halves, [(width, inner), (width, width), (inner, width)]
    )
    grad_qkv_w, small = unpack(
        write_project, order, project_halves, [(width, 3 * width), (width, PAIR)]
    )
    vectors = small.reshape(-1)
    vector = [vectors[at : at + width] for at in range(0, 8 * width, width)]
    grad_blend = vectors[5 * width : 8 * width].reshape(3, heads, width // heads).sum(-1)
    return (
        output,
        input_grad,
        vector[0],
        vector[1],
        grad_qkv_w,
        grad_blend,
        grad_out_w,
        vector[2],
        vector[3],
        grad_in_w,
        vectors[8 * width : 8 * width + inner],
        grad_down_w,
        vector[4],
    )


def solution(mesh):
    rows = P("batch", "seq", None)
    return jax.shard_map(
        local,
        mesh=mesh,
        in_specs=(rows, rows, P("batch")) + (P(),) * 11,
        out_specs=(rows, rows) + (P(),) * 11,
        check_vma=False,
    )
```

```python
import functools

import jax
import jax.numpy as jnp
from jax import lax
from jax.experimental import pallas as pl
from jax.experimental.pallas import tpu as pltpu
from jax.sharding import PartitionSpec as P

WINDOW = 30
HEAD = 64
PAIR = 2 * HEAD
TILE = 64
EPS = 1e-05
NEG = -1e30
BF16 = jnp.bfloat16
F32 = jnp.float32


def layer_norm(field, gain, shift):
    center = field - jnp.mean(field, axis=-1, keepdims=True)
    spread = jnp.mean(center * center, axis=-1, keepdims=True)
    return center * lax.rsqrt(spread + EPS) * gain + shift


def rows_product(left, right):
    return lax.dot_general(
        left, right, (((0,), (0,)), ((), ())), preferred_element_type=F32
    )


def times_transposed(left, right):
    return lax.dot_general(
        left, right, (((1,), (1,)), ((), ())), preferred_element_type=F32
    )


def times(left, right):
    return lax.dot_general(
        left, right, (((1,), (0,)), ((), ())), preferred_element_type=F32
    )


def elu_feature(field):
    return jnp.where(field > 0, field + 1.0, jnp.exp(jnp.minimum(field, 0.0)))


def tanh_feature(field):
    return 1.0 + jnp.tanh(field)


def pair_lanes(p, part=0, width=PAIR):
    return slice(p * width + part * PAIR, p * width + (part + 1) * PAIR)


def store_split(ref, index, rows, block):
    lane = lax.broadcasted_iota(jnp.int32, (block.shape[0], PAIR), 1)
    for p in range(block.shape[1] // PAIR):
        pair = block[:, pair_lanes(p)]
        for h in range(2):
            mine = (lane < HEAD) if h == 0 else (lane >= HEAD)
            ref[index + (rows, pair_lanes(p, h, 2 * PAIR))] = jnp.where(mine, pair, 0.0).astype(
                BF16
            )


def load_split(ref, index, rows, p):
    return jnp.concatenate([ref[index + (rows, pair_lanes(p, h, 2 * PAIR))] for h in range(2)], 0)


def tall(block):
    return jnp.concatenate([block[:, :PAIR], block[:, PAIR:]], 0)


def fill_features(meta_ref, q_ref, k_ref, v_ref, halo_k, halo_v, keys, values, fq, fk, split):
    rows, width = q_ref.shape
    chunk = 2 * TILE
    front = pl.ds(0, TILE)
    zero = jnp.zeros((TILE, width), F32)
    store_split(keys, (), front, halo_k[...].astype(F32) * 0.125)
    store_split(values, (), front, halo_v[...].astype(F32))
    for c in range(2):
        store_split(fk, (c,), front, zero)

    def fill(step, carry):
        at = pl.multiple_of(step * chunk, chunk)
        here, there = pl.ds(at, chunk), pl.ds(at + TILE, chunk)
        q = q_ref[here, :].astype(F32)
        k = k_ref[here, :].astype(F32)
        store_split(keys, (), there, k * 0.125)
        store_split(values, (), there, v_ref[here, :].astype(F32))
        position = meta_ref[1] + at + lax.broadcasted_iota(jnp.int32, (chunk, width), 0)
        valid = position < meta_ref[0]
        for c, feature in enumerate((elu_feature, tanh_feature)):
            if split:
                store_split(fq, (c,), here, feature(q))
            else:
                fq[c, here, :] = feature(q).astype(BF16)
            store_split(fk, (c,), there, jnp.where(valid, feature(k), 0.0))
        return carry

    lax.fori_loop(0, rows // chunk, fill, 0)


def tile_masks(meta_ref, tile):
    shape = (TILE, 2 * PAIR)
    row = lax.broadcasted_iota(jnp.int32, shape, 0)
    lane = lax.broadcasted_iota(jnp.int32, shape, 1) % PAIR
    back = row + TILE - lane
    key = meta_ref[1] + (tile - 1) * TILE + lane
    known = (key >= 0) & (key < meta_ref[0])
    near = (back >= 0) & (back <= WINDOW) & (known | (back == 0))
    return near, back >= 0


def softmax_pair(scores):
    halves = []
    for h in range(2):
        part = scores[:, h * PAIR : (h + 1) * PAIR]
        part = jnp.exp(part - jnp.max(part, axis=1, keepdims=True))
        halves.append(part * (1.0 / jnp.sum(part, axis=1, keepdims=True)))
    return jnp.concatenate(halves, 1)


def tile_constants():
    row = lax.broadcasted_iota(jnp.int32, (2 * PAIR, PAIR), 0)
    lane = lax.broadcasted_iota(jnp.int32, (2 * PAIR, PAIR), 1)
    ones = jnp.where(row // PAIR == lane // HEAD, 1.0, 0.0).astype(BF16)
    row = lax.broadcasted_iota(jnp.int32, (PAIR, 2 * PAIR), 0)
    lane = lax.broadcasted_iota(jnp.int32, (PAIR, 2 * PAIR), 1)
    return ones, row // HEAD == (lane % PAIR) // HEAD


def whole(split):
    half = split.shape[0] // 2
    return split[:half] + split[half:]


def state_share(block, fks, vs):
    ones = jnp.ones((TILE, PAIR), BF16)
    share = rows_product(whole(fks), jnp.concatenate([whole(vs), ones], 1))
    return jnp.where(block, share, 0.0)


def attend_kernel(
    meta_ref, blend_ref, q_ref, k_ref, v_ref, halo_k, halo_v, state_ref, att_ref, total_ref,
    keys, values, fq, fk, state,
):
    rows, width = q_ref.shape
    pairs = range(width // PAIR)
    fill_features(meta_ref, q_ref, k_ref, v_ref, halo_k, halo_v, keys, values, fq, fk, False)
    state[...] = state_ref[...]
    ones, block = tile_constants()

    def step(tile, carry):
        at = pl.multiple_of(tile * TILE, TILE)
        here, window, past = pl.ds(at, TILE), pl.ds(at, 2 * TILE), pl.ds(at, TILE)
        near_mask, far_mask = tile_masks(meta_ref, tile)
        q = [q_ref[here, pair_lanes(p)] for p in pairs]
        feats = [[fq[c, here, pair_lanes(p)] for c in range(2)] for p in pairs]
        held = [[state[c, p] for c in range(2)] for p in pairs]
        added = [
            [
                state_share(block, load_split(fk, (c,), past, p), load_split(values, (), past, p))
                for c in range(2)
            ]
            for p in pairs
        ]
        near = [times_transposed(q[p], load_split(keys, (), window, p)) for p in pairs]
        far = [
            [times_transposed(feats[p][c], load_split(fk, (c,), window, p)) for c in range(2)]
            for p in pairs
        ]
        near = [softmax_pair(jnp.where(near_mask, n, NEG)) for n in near]
        far = [[jnp.where(far_mask, f, 0.0) for f in fs] for fs in far]
        stack = [jnp.concatenate([n] + fs, 0).astype(BF16) for n, fs in zip(near, far)]
        wide = [jnp.concatenate([load_split(values, (), window, p), ones], 1) for p in pairs]
        sums = [times(s, w) for s, w in zip(stack, wide)]
        old = [[times(feats[p][c], held[p][c].astype(BF16)) for c in range(2)] for p in pairs]
        for p in pairs:
            mixed = blend_ref[0:1, pair_lanes(p)] * sums[p][:TILE, :PAIR]
            for c in range(2):
                mine = sums[p][(c + 1) * TILE : (c + 2) * TILE] + old[p][c]
                mixed = mixed + blend_ref[c + 1 : c + 2, pair_lanes(p)] * (
                    mine[:, :PAIR] / mine[:, PAIR:]
                )
            att_ref[here, pair_lanes(p)] = mixed.astype(BF16)
        for p in pairs:
            for c in range(2):
                state[c, p] = held[p][c] + added[p][c]
        return carry

    lax.fori_loop(0, rows // TILE, step, 0)
    last = pl.ds(rows, TILE)
    for p in pairs:
        for c in range(2):
            total_ref[c, p] = state[c, p] + state_share(
                block, load_split(fk, (c,), last, p), load_split(values, (), last, p)
            )


def slopes_of(field):
    small = jnp.exp(jnp.minimum(field, 0.0))
    bent = jnp.tanh(field)
    return [jnp.where(field > 0, 1.0, small), 1.0 - bent * bent]


def split_heads(block):
    lane = lax.broadcasted_iota(jnp.int32, block.shape, 1)
    zero = jnp.zeros_like(block)
    return jnp.concatenate(
        [jnp.where(lane < HEAD, block, zero), jnp.where(lane < HEAD, zero, block)], 0
    )


def attend_back_kernel(
    together, meta_ref, blend_ref, q_ref, k_ref, v_ref, halo_k, halo_v, state_ref, later_ref,
    go_ref, gq_ref, gk_ref, gv_ref, hk_ref, hv_ref, mix_ref, total_ref,
    keys, values, fq, fk, state, gk, gv, gfk, gon,
):
    rows, width = q_ref.shape
    pairs = range(width // PAIR)
    tiles = rows // TILE
    near_by = range(together)
    units = [(s, p) for s in near_by for p in pairs]
    fill_features(meta_ref, q_ref, k_ref, v_ref, halo_k, halo_v, keys, values, fq, fk, True)
    state[...] = state_ref[...]
    mix_ref[...] = jnp.zeros_like(mix_ref)
    gk[:TILE, :] = jnp.zeros((TILE, width), F32)
    gv[:TILE, :] = jnp.zeros((TILE, width), F32)
    gfk[:, :TILE, :] = jnp.zeros((2, TILE, width), F32)
    ones, block = tile_constants()
    row = lax.broadcasted_iota(jnp.int32, (2 * PAIR, PAIR), 0) % PAIR
    lane = lax.broadcasted_iota(jnp.int32, (2 * PAIR, PAIR), 1)
    heads = jnp.where(row // HEAD == lane // HEAD, 1.0, 0.0).astype(BF16)
    plain_ones = jnp.ones((TILE, PAIR), BF16)
    high = (lax.broadcasted_iota(jnp.int32, (TILE, PAIR), 1) % HEAD) < HEAD // 2

    def step(number, carry):
        first = number * together
        at = pl.multiple_of(first * TILE, TILE)
        here = [pl.ds(at + s * TILE, TILE) for s in range(together + 1)]
        window = [pl.ds(at + s * TILE, 2 * TILE) for s in near_by]
        masks = [tile_masks(meta_ref, first + s) for s in near_by]
        q = {(s, p): q_ref[here[s], pair_lanes(p)] for s, p in units}
        go = {(s, p): go_ref[here[s], pair_lanes(p)] for s, p in units}
        blend = [[blend_ref[c : c + 1, pair_lanes(p)] for c in range(3)] for p in pairs]
        fqs = {(s, p): [load_split(fq, (c,), here[s], p) for c in range(2)] for s, p in units}
        feats = {u: [whole(f) for f in fqs[u]] for u in units}
        ks = {(s, p): load_split(keys, (), window[s], p) for s, p in units}
        fks = {(s, p): [load_split(fk, (c,), window[s], p) for c in range(2)] for s, p in units}
        wide = {
            (s, p): jnp.concatenate([load_split(values, (), window[s], p), ones], 1)
            for s, p in units
        }
        held = {(0, p): [state[c, p] for c in range(2)] for p in pairs}
        for s, p in units:
            vs = load_split(values, (), here[s], p)
            held[s + 1, p] = [
                held[s, p][c] + state_share(block, load_split(fk, (c,), here[s], p), vs)
                for c in range(2)
            ]
        past = {u: [h.astype(BF16) for h in held[u]] for u in units}
        old_k = [gk[here[0], pair_lanes(p)] for p in pairs]
        old_v = [gv[here[0], pair_lanes(p)] for p in pairs]
        old_f = [[gfk[c, here[0], pair_lanes(p)] for c in range(2)] for p in pairs]

        near = {u: times_transposed(q[u], ks[u]) for u in units}
        far = {u: [times_transposed(feats[u][c], fks[u][c]) for c in range(2)] for u in units}
        old = {u: [times(feats[u][c], past[u][c]) for c in range(2)] for u in units}
        near = {u: softmax_pair(jnp.where(masks[u[0]][0], near[u], NEG)) for u in units}
        far = {u: [jnp.where(masks[u[0]][1], f, 0.0).astype(BF16) for f in far[u]] for u in units}
        stack = {u: jnp.concatenate([near[u].astype(BF16)] + far[u], 0) for u in units}
        sums = {u: times(stack[u], wide[u]) for u in units}
        scales, prods = {}, {}
        for u in units:
            outs = [sums[u][:TILE, :PAIR]]
            scales[u] = [jnp.broadcast_to(blend[u[1]][0], (TILE, PAIR))]
            for c in range(2):
                mine = sums[u][(c + 1) * TILE : (c + 2) * TILE] + old[u][c]
                inverse = 1.0 / mine[:, PAIR:]
                outs.append(mine[:, :PAIR] * inverse)
                scales[u].append(blend[u[1]][c + 1] * inverse)
            prods[u] = jnp.concatenate([go[u] * out for out in outs], 0)
        deltas = {}
        for u in units:
            low = prods[u].astype(BF16)
            rest = (prods[u] - low.astype(F32)).astype(BF16)
            deltas[u] = times(jnp.concatenate([low, rest], 1), heads)
        grads = {}
        for u in units:
            grads[u] = []
            for c in range(3):
                delta = scales[u][c] * deltas[u][c * TILE : (c + 1) * TILE] * (-2.0 / HEAD)
                delta_low = delta.astype(BF16).astype(F32)
                delta = jnp.where(high, delta_low, delta - delta_low)
                grads[u].append(jnp.concatenate([scales[u][c] * go[u], delta], 1).astype(BF16))
        back = {u: times_transposed(jnp.concatenate(grads[u], 0), wide[u]) for u in units}
        late = {u: [times_transposed(grads[u][c + 1], past[u][c]) for c in range(2)] for u in units}
        ds = {u: (near[u] * back[u][:TILE]).astype(BF16) for u in units}
        gas = {
            u: [
                jnp.where(masks[u[0]][1], back[u][(c + 1) * TILE : (c + 2) * TILE], 0.0).astype(BF16)
                for c in range(2)
            ]
            for u in units
        }
        gq_near = {u: times(ds[u], ks[u]) for u in units}
        gq_far = {u: [times(gas[u][c], fks[u][c]) + late[u][c] for c in range(2)] for u in units}
        new_k = {u: rows_product(tall(ds[u]), split_heads(q[u] * 0.125)) for u in units}
        new_f = {u: [rows_product(tall(gas[u][c]), fqs[u][c]) for c in range(2)] for u in units}
        new_v = {
            u: rows_product(
                jnp.concatenate([tall(stack[u][c * TILE : (c + 1) * TILE]) for c in range(3)], 0),
                jnp.concatenate([split_heads(g[:, :PAIR]) for g in grads[u]], 0),
            )
            for u in units
        }

        def overlap(old, new, p):
            parts = [old + new(0, p)[:TILE]]
            parts += [new(s, p)[TILE:] + new(s + 1, p)[:TILE] for s in range(together - 1)]
            return parts + [new(together - 1, p)[TILE:]]

        for s, p in units:
            u, lanes = (s, p), pair_lanes(p)
            slopes = slopes_of(q[u].astype(F32))
            gq = gq_near[u] + slopes[0] * gq_far[u][0] + slopes[1] * gq_far[u][1]
            gq_ref[here[s], lanes] = gq.astype(BF16)
            for c in range(2):
                gon[c, here[s], p * 2 * PAIR : (p + 1) * 2 * PAIR] = grads[u][c + 1]
        for p in pairs:
            lanes = pair_lanes(p)
            for c in range(3):
                mix_ref[c : c + 1, lanes] += sum(
                    jnp.sum(prods[s, p][c * TILE : (c + 1) * TILE], axis=0, keepdims=True)
                    for s in near_by
                )
            for rows_at, part in zip(here, overlap(old_k[p], lambda s, p: new_k[s, p], p)):
                gk[rows_at, lanes] = part
            for rows_at, part in zip(here, overlap(old_v[p], lambda s, p: new_v[s, p], p)):
                gv[rows_at, lanes] = part
            for c in range(2):
                parts = overlap(old_f[p][c], lambda s, p: new_f[s, p][c], p)
                for rows_at, part in zip(here, parts):
                    gfk[c, rows_at, lanes] = part
                state[c, p] = held[together, p][c]
        return carry

    lax.fori_loop(0, tiles // together, step, 0)
    hk_ref[...] = gk[:TILE, :].astype(BF16)
    hv_ref[...] = gv[:TILE, :].astype(BF16)
    state[...] = later_ref[...]

    def come(at, c, p):
        here = pl.ds(at, TILE)
        grads = gon[c, here, p * 2 * PAIR : (p + 1) * 2 * PAIR]
        share = rows_product(whole(load_split(fq, (c,), here, p)), grads)
        return jnp.where(block, share, 0.0)

    def back_step(number, carry):
        first = tiles - 1 - number * together
        at = [pl.multiple_of((first - s) * TILE, TILE) for s in near_by]
        here = [pl.ds(a, TILE) for a in at]
        there = [pl.ds(a + TILE, TILE) for a in at]
        held = {(-1, p): [state[c, p] for c in range(2)] for p in pairs}
        for s, p in units:
            tile = first - s + 2
            nearer = pl.multiple_of(jnp.minimum(tile, tiles - 1) * TILE, TILE)
            held[s, p] = [
                held[s - 1, p][c] + jnp.where(tile < tiles, come(nearer, c, p), 0.0)
                for c in range(2)
            ]
        later = {u: [h.astype(BF16) for h in held[u]] for u in units}
        vs = {(s, p): whole(load_split(values, (), there[s], p)) for s, p in units}
        fks = {
            (s, p): jnp.concatenate([whole(load_split(fk, (c,), there[s], p)) for c in range(2)], 1)
            for s, p in units
        }
        wide = {u: jnp.concatenate([vs[u], plain_ones], 1) for u in units}
        far_k = {u: [times_transposed(wide[u], later[u][c]) for c in range(2)] for u in units}
        far_v = {
            u: times(fks[u], jnp.concatenate([g[:, :PAIR] for g in later[u]], 0)) for u in units
        }
        for s, p in units:
            u, lanes = (s, p), pair_lanes(p)
            position = meta_ref[1] + at[s] + lax.broadcasted_iota(jnp.int32, (TILE, PAIR), 0)
            slopes = slopes_of(k_ref[here[s], lanes].astype(F32))
            grad_f = [gfk[c, there[s], lanes] + far_k[u][c] for c in range(2)]
            bent = slopes[0] * grad_f[0] + slopes[1] * grad_f[1]
            grad_k = gk[there[s], lanes] + jnp.where(position < meta_ref[0], bent, 0.0)
            gk_ref[here[s], lanes] = grad_k.astype(BF16)
            gv_ref[here[s], lanes] = (gv[there[s], lanes] + far_v[u]).astype(BF16)
        for p in pairs:
            for c in range(2):
                state[c, p] = held[together - 1, p][c]
        return carry

    lax.fori_loop(0, tiles // together, back_step, 0)
    for p in pairs:
        for c in range(2):
            total_ref[c, p] = state[c, p] + come(0, c, p) + come(TILE, c, p)


def attention_specs(rows, width, count, number, split):
    lanes, calls = width // count, count

    def columns(height, part):
        return pl.BlockSpec((height, lanes), lambda _: (0, part * calls + number))

    state = pl.BlockSpec(
        (2, lanes // PAIR, PAIR, 2 * PAIR), lambda _: (0, number, 0, 0)
    )
    ins = [pl.BlockSpec(memory_space=pltpu.SMEM), columns(3, 0)]
    ins += [columns(rows, part) for part in range(3)]
    ins += [columns(TILE, part) for part in range(2)]
    scratch = [
        pltpu.VMEM((rows + TILE, 2 * lanes), BF16),
        pltpu.VMEM((rows + TILE, 2 * lanes), BF16),
        pltpu.VMEM((2, rows, (2 if split else 1) * lanes), BF16),
        pltpu.VMEM((2, rows + TILE, 2 * lanes), BF16),
        pltpu.VMEM((2, lanes // PAIR, PAIR, 2 * PAIR), F32),
    ]
    return lanes, columns, ins, state, scratch


def outcome(shape, dtype):
    return jax.ShapeDtypeStruct(shape, dtype), pl.BlockSpec(shape, lambda _: (0,) * len(shape))


def attend(meta, blend, qkv, halo, state):
    rows, width = qkv.shape[0], qkv.shape[1] // 3
    _, _, ins, held, scratch = attention_specs(rows, width, 1, 0, False)
    shapes, blocks = zip(outcome((rows, width), BF16), outcome(state.shape, F32))
    return pl.pallas_call(
        attend_kernel,
        grid=(1,),
        out_shape=shapes,
        in_specs=ins + [held],
        out_specs=blocks,
        scratch_shapes=scratch,
        compiler_params=pltpu.CompilerParams(vmem_limit_bytes=48 * 2**20),
        cost_estimate=pl.CostEstimate(
            flops=rows * width * 48000, bytes_accessed=rows * width * 8, transcendentals=0
        ),
    )(meta, blend, qkv, qkv, qkv, halo, halo, state)


def attend_back(meta, blend, qkv, halo, state, later, go, calls, number):
    rows, width = qkv.shape[0], qkv.shape[1] // 3
    lanes, columns, ins, held, scratch = attention_specs(rows, width, calls, number, True)
    shapes, blocks = zip(
        *[outcome((rows, lanes), BF16)] * 3,
        *[outcome((TILE, lanes), BF16)] * 2,
        outcome((3, lanes), F32),
        outcome((2, lanes // PAIR, PAIR, 2 * PAIR), F32),
    )
    together = 4 * PAIR // lanes
    return pl.pallas_call(
        functools.partial(attend_back_kernel, together),
        grid=(1,),
        out_shape=shapes,
        in_specs=ins + [held, held, columns(rows, 0)],
        out_specs=blocks,
        scratch_shapes=scratch
        + [
            pltpu.VMEM((rows + TILE, lanes), F32),
            pltpu.VMEM((rows + TILE, lanes), F32),
            pltpu.VMEM((2, rows + TILE, lanes), F32),
            pltpu.VMEM((2, rows, 2 * lanes), BF16),
        ],
        compiler_params=pltpu.CompilerParams(vmem_limit_bytes=56 * 2**20),
        cost_estimate=pl.CostEstimate(
            flops=rows * lanes * 96000, bytes_accessed=rows * lanes * 16, transcendentals=0
        ),
    )(meta, blend, qkv, qkv, qkv, halo, halo, state, later, go)


CHUNK = 256
GELU_A, GELU_B = 0.7978845608028654, 0.044715


def normalized(field):
    center = field - jnp.mean(field, axis=-1, keepdims=True)
    scale = lax.rsqrt(jnp.mean(center * center, axis=-1, keepdims=True) + EPS)
    return center * scale, scale


def norm_back(grad, unit, scale):
    shared = jnp.mean(grad * unit, axis=-1, keepdims=True)
    return scale * (grad - jnp.mean(grad, axis=-1, keepdims=True) - unit * shared)


def gelu_pair(field):
    square = field * field
    bent = jnp.tanh(GELU_A * field * (1.0 + GELU_B * square))
    half = 0.5 + 0.5 * bent
    slope = half + 0.5 * field * (1.0 - bent * bent) * (GELU_A + 3.0 * GELU_A * GELU_B * square)
    return field * half, slope


def column_sum(block):
    return jnp.sum(block, axis=0, keepdims=True)


def feed_kernel(
    pieces, x_ref, att_ref, grad_ref, out_w, gain_ref, bias_ref, in_w, in_b, down_w, down_b,
    result_ref, first_ref, go_ref, packed_ref, small_ref, wide_ref,
    second, hidden, pre_low, att_low,
):
    rows, width = x_ref.shape
    inner = in_w.shape[1]
    small_ref[...] = jnp.zeros_like(small_ref)
    wide_ref[...] = jnp.zeros_like(wide_ref)

    def step(number, carry):
        here = pl.ds(pl.multiple_of(number * CHUNK, CHUNK), CHUNK)
        first = x_ref[here, :].astype(F32) + times(att_ref[here, :], out_w[...])
        unit, scale = normalized(first)
        low = (unit * gain_ref[...] + bias_ref[...]).astype(BF16)
        second[here, :] = low
        grad = grad_ref[here, :]
        grad_f = grad.astype(F32)
        result = first + down_b[...]
        back = jnp.zeros((CHUNK, width), F32)
        for at in range(0, inner, width):
            lanes = slice(at, at + width)
            act, slope = gelu_pair(times(low, in_w[:, lanes]) + in_b[:, lanes])
            act = act.astype(BF16)
            hidden[here, lanes] = act
            result = result + times(act, down_w[lanes, :])
            pre = (times_transposed(grad, down_w[lanes, :]) * slope).astype(BF16)
            pre_low[here, lanes] = pre
            wide_ref[:, lanes] += column_sum(pre.astype(F32))
            back = back + times_transposed(pre, in_w[:, lanes])
        result_ref[here, :] = result.astype(BF16)
        small_ref[0:1, :] += column_sum(back * unit)
        small_ref[1:2, :] += column_sum(back)
        small_ref[2:3, :] += column_sum(grad_f)
        grad_first = grad_f + norm_back(back * gain_ref[...], unit, scale)
        first_ref[here, :] = grad_first
        grad_att = grad_first.astype(BF16)
        att_low[here, :] = grad_att
        go_ref[here, :] = times_transposed(grad_att, out_w[...])
        return carry

    lax.fori_loop(0, rows // CHUNK, step, 0)
    for at in range(0, inner, width):
        lanes = slice(at, at + width)
        packed_ref[:, lanes] = rows_product(second[...], pre_low[:, lanes]).astype(BF16)
    packed_ref[:, inner : inner + width] = rows_product(att_ref[...], att_low[...]).astype(BF16)
    tall_rows, flat_rows = inner // pieces, width // pieces
    for at in range(0, inner, width):
        share = rows_product(hidden[:, at : at + width], grad_ref[...]).astype(BF16)
        for below in range(0, width, flat_rows):
            piece, block = divmod(at + below, tall_rows)
            lanes = inner + width + block // flat_rows * width
            packed_ref[piece * flat_rows : (piece + 1) * flat_rows, lanes : lanes + width] = share[
                below : below + flat_rows
            ]


def feed_forward(pieces, x, att, grad, out_w, gain, bias, in_w, in_b, down_w, down_b):
    rows, width = x.shape
    inner = in_w.shape[1]
    return pl.pallas_call(
        functools.partial(feed_kernel, pieces),
        out_shape=(
            jax.ShapeDtypeStruct((rows, width), BF16),
            jax.ShapeDtypeStruct((rows, width), F32),
            jax.ShapeDtypeStruct((rows, width), F32),
            jax.ShapeDtypeStruct((width, 2 * inner + width), BF16),
            jax.ShapeDtypeStruct((3, width), F32),
            jax.ShapeDtypeStruct((1, inner), F32),
        ),
        in_specs=[pl.BlockSpec(memory_space=pltpu.VMEM)] * 10,
        out_specs=(pl.BlockSpec(memory_space=pltpu.VMEM),) * 6,
        scratch_shapes=[
            pltpu.VMEM((rows, width), BF16),
            pltpu.VMEM((rows, inner), BF16),
            pltpu.VMEM((rows, inner), BF16),
            pltpu.VMEM((rows, width), BF16),
        ],
        compiler_params=pltpu.CompilerParams(vmem_limit_bytes=56 * 2**20),
        cost_estimate=pl.CostEstimate(
            flops=rows * width * inner * 24, bytes_accessed=rows * width * 20, transcendentals=0
        ),
    )(x, att, grad, out_w, gain[None], bias[None], in_w, in_b[None], down_w, down_b[None])


def project_back_kernel(
    calls, x_ref, first_ref, w_ref, gain_ref, bias_ref, mix_ref, small2_ref, wide_ref, *refs
):
    grads = refs[: 3 * calls]
    result_ref, packed_ref, normed, gathered, sums, rows_of = refs[3 * calls :]
    rows, width = x_ref.shape
    sums[...] = jnp.zeros_like(sums)

    def step(number, carry):
        here = pl.ds(pl.multiple_of(number * CHUNK, CHUNK), CHUNK)
        unit, scale = normalized(x_ref[here, :].astype(F32))
        normed[here, :] = (unit * gain_ref[...] + bias_ref[...]).astype(BF16)
        grad = jnp.concatenate([ref[here, :] for ref in grads], 1)
        gathered[here, :] = grad
        back = times_transposed(grad, w_ref[...])
        sums[0:1, :] += column_sum(back * unit)
        sums[1:2, :] += column_sum(back)
        grad_x = first_ref[here, :] + norm_back(back * gain_ref[...], unit, scale)
        result_ref[here, :] = grad_x.astype(BF16)
        return carry

    lax.fori_loop(0, rows // CHUNK, step, 0)
    for at in range(0, 3 * width, width):
        lanes = slice(at, at + width)
        packed_ref[:, lanes] = rows_product(normed[...], gathered[:, lanes]).astype(BF16)
    rows_of[...] = jnp.zeros_like(rows_of)
    at = 0
    for ref in (sums, small2_ref, mix_ref, wide_ref):
        for row in range(ref.shape[0]):
            for lane in range(0, ref.shape[1], PAIR):
                rows_of[at : at + 1, :] = ref[row : row + 1, lane : lane + PAIR]
                at += 1
    high = rows_of[...].astype(BF16)
    packed_ref[:, 3 * width : 3 * width + PAIR] = high
    packed_ref[:, 3 * width + PAIR :] = (rows_of[...] - high.astype(F32)).astype(BF16)


def project_back(x, grad_first, weight, gain, bias, mix, small2, wide, grads):
    rows, width = x.shape
    vmem = pl.BlockSpec(memory_space=pltpu.VMEM)
    return pl.pallas_call(
        functools.partial(project_back_kernel, len(grads) // 3),
        out_shape=(
            jax.ShapeDtypeStruct((rows, width), BF16),
            jax.ShapeDtypeStruct((width, 3 * width + 2 * PAIR), BF16),
        ),
        in_specs=[vmem] * (8 + len(grads)),
        out_specs=(vmem, vmem),
        scratch_shapes=[
            pltpu.VMEM((rows, width), BF16),
            pltpu.VMEM((rows, 3 * width), BF16),
            pltpu.VMEM((2, width), F32),
            pltpu.VMEM((width, PAIR), F32),
        ],
        compiler_params=pltpu.CompilerParams(vmem_limit_bytes=48 * 2**20),
        cost_estimate=pl.CostEstimate(
            flops=rows * width * width * 24, bytes_accessed=rows * width * 20, transcendentals=0
        ),
    )(x, grad_first, weight, gain[None], bias[None], mix, small2, wide, *grads)


def to_sequences(block, axis, groups):
    return lax.all_to_all(block, axis, 0, 0, axis_index_groups=groups)


def after(value, *others):
    return lax.optimization_barrier((value,) + others)[0]


def from_parts(total, axis, parts, stride, forward):
    size = lax.axis_size(axis)
    low = total.astype(BF16)
    result = jnp.zeros_like(total)
    for hop in range(1, parts):
        distance = hop * stride
        route = [
            (i, i + distance) if forward else (i + distance, i) for i in range(size - distance)
        ]
        result = result + lax.ppermute(low, axis, route).astype(F32)
    return result


class Ring:
    def __init__(self, batch, seq):
        self.batch, self.seq = batch, seq
        self.low = 2 ** ((seq.bit_length() - 1) // 2)
        self.sizes = {"core": 2, "near": batch // 2 * self.low, "far": seq // self.low}
        self.pieces = batch * seq

    def place(self, s, b):
        return {"core": b % 2, "near": b // 2 * self.low + s % self.low, "far": s // self.low}

    def device(self, place):
        s = place["far"] * self.low + place["near"] % self.low
        return s * self.batch + place["near"] // self.low * 2 + place["core"]

    def mine(self):
        return self.place(lax.axis_index("seq"), lax.axis_index("batch"))

    def swap(self, value, level, k):
        route = []
        for s in range(self.seq):
            for b in range(self.batch):
                place = self.place(s, b)
                place[level] ^= k
                route.append((s * self.batch + b, self.device(place)))
        return lax.ppermute(value, ("seq", "batch"), route)

    def scatter(self, value, level, fine):
        size, me = self.sizes[level], self.mine()[level]
        value = value.reshape((size, value.shape[0] // size) + value.shape[1:])
        parts = [
            self.swap(lax.dynamic_index_in_dim(value, me ^ k, 0, False), level, k)
            for k in range(1, size)
        ]
        total = lax.dynamic_index_in_dim(value, me, 0, False).astype(F32)
        for part in parts:
            total = total + part.astype(F32)
        if not fine:
            return total.astype(BF16)
        end = total.shape[-1] - 2 * fine
        exact = total[..., end : end + fine] + total[..., end + fine :]
        high = lax.reduce_precision(exact, 8, 7)
        return jnp.concatenate([total[..., :end], high, exact - high], -1).astype(BF16)

    def gather(self, value, level):
        parts = [value] + [self.swap(value, level, k) for k in range(1, self.sizes[level])]
        return jnp.concatenate(parts, 0)

    def to_pieces(self, value):
        return value.reshape(self.pieces, value.shape[0] // self.pieces, value.shape[1])

    def halves(self, value):
        for level in ("far", "near"):
            value = self.gather(value, level)
        return value, self.swap(value, "core", 1)

    def reduce(self, value, fine=0):
        value = self.to_pieces(value)
        for level in ("core", "near", "far"):
            value = self.scatter(value, level, fine)
        return self.halves(value)

    def order(self):
        me = self.mine()
        piece = jnp.arange(self.pieces, dtype=jnp.int32)
        far, near = self.sizes["far"], self.sizes["near"]
        core = (piece // (far * near)) ^ me["core"]
        near = ((piece // far) % near) ^ me["near"]
        return (core * self.sizes["near"] + near) * far + ((piece % far) ^ me["far"])


def unpack_kernel(write, order_ref, own_ref, other_ref, *out_refs):
    half = own_ref.shape[0]
    for piece in range(2 * half):
        at = order_ref[piece]

        @pl.when(at < half)
        def _(piece=piece, at=at):
            write(piece, own_ref[at].astype(F32), out_refs)

        @pl.when(at >= half)
        def _(piece=piece, at=at):
            write(piece, other_ref[at - half].astype(F32), out_refs)


def write_feed(piece, block, out_refs):
    in_ref, out_ref, down_ref = out_refs
    size, inner, width = block.shape[0], in_ref.shape[1], in_ref.shape[0]
    rows = slice(piece * size, (piece + 1) * size)
    in_ref[rows, :] = block[:, :inner]
    out_ref[rows, :] = block[:, inner : inner + width]
    tall_rows = inner // (width // size)
    for below in range(0, tall_rows, size):
        at = inner + width + below // size * width
        down_ref[piece * tall_rows + below : piece * tall_rows + below + size, :] = block[
            :, at : at + width
        ]


def write_project(piece, block, out_refs):
    w_ref, small_ref = out_refs
    size, end = block.shape[0], w_ref.shape[1]
    rows = slice(piece * size, (piece + 1) * size)
    w_ref[rows, :] = block[:, :end]
    small_ref[rows, :] = block[:, end : end + PAIR] + block[:, end + PAIR :]


def unpack(write, order, halves, shapes):
    vmem = pl.BlockSpec(memory_space=pltpu.VMEM)
    return pl.pallas_call(
        functools.partial(unpack_kernel, write),
        out_shape=[jax.ShapeDtypeStruct(shape, F32) for shape in shapes],
        in_specs=[pl.BlockSpec(memory_space=pltpu.SMEM), vmem, vmem],
        out_specs=[vmem] * len(shapes),
        compiler_params=pltpu.CompilerParams(vmem_limit_bytes=48 * 2**20),
        cost_estimate=pl.CostEstimate(
            flops=0, bytes_accessed=8 * halves[0].size, transcendentals=0
        ),
    )(order, *halves)


def local(
    inputs,
    cotangent,
    lengths,
    norm1_gain,
    norm1_bias,
    qkv_weight,
    blend_weights,
    out_weight,
    norm2_gain,
    norm2_bias,
    in_weight,
    in_bias,
    down_weight,
    down_bias,
):
    seqs, span, width = inputs.shape
    heads = blend_weights.shape[1]
    devices = lax.axis_size("seq")
    parts = devices // seqs
    rows = seqs * span
    index = lax.axis_index("seq")
    groups = None
    if parts > 1:
        groups = [[r * seqs + s for s in range(seqs)] for r in range(parts)]
    mine, part = index % seqs, index // seqs
    meta = jnp.stack([lax.dynamic_index_in_dim(lengths, mine, 0, False), part * rows])
    blend = jnp.repeat(blend_weights, width // heads, axis=1)

    ring = Ring(lax.axis_size("batch"), devices)
    by_ring = width % (16 * ring.pieces) == 0
    inner = in_weight.shape[1]

    x = to_sequences(inputs, "seq", groups).reshape(rows, width)
    grad_out = to_sequences(cotangent, "seq", groups).reshape(rows, width)

    normed = layer_norm(x.astype(F32), norm1_gain, norm1_bias).astype(BF16)
    qkv = times(normed, qkv_weight).astype(BF16)
    halo = jnp.zeros((TILE, 2 * width), BF16)
    state = jnp.zeros((2, width // PAIR, PAIR, 2 * PAIR), F32)
    later = state
    if parts > 1:
        onward = [(i, i + seqs) for i in range(devices - seqs)]
        halo = lax.ppermute(qkv[rows - TILE :, width:], "seq", onward)
        total = attend(meta, blend, qkv, halo, state)[1]
        state = from_parts(total, "seq", parts, seqs, True)
    attended = attend(meta, blend, qkv, halo, state)[0]

    result, grad_first, grad_o, feed_grads, small2, grad_in_b = feed_forward(
        ring.pieces if by_ring else 16,
        x, attended, grad_out, out_weight, norm2_gain, norm2_bias,
        in_weight, in_bias, down_weight, down_bias,
    )
    output = to_sequences(result.reshape(seqs, span, width), "seq", groups)
    calls = 4

    def back(meta, number, later):
        return attend_back(meta, blend, qkv, halo, state, later, grad_o, calls, number)

    if parts > 1:
        total = jnp.concatenate([back(meta, number, later)[6] for number in range(calls)], 1)
        later = from_parts(total, "seq", parts, seqs, False)
    backs, turn = [], meta
    if by_ring:
        held = ring.to_pieces(feed_grads)
        rounds = {1: "core", 3: "near"}
        for number in range(calls):
            if number in rounds:
                held = ring.scatter(held, rounds[number], 0)
                turn = after(turn, held)
            backs.append(back(turn, number, later))
            turn = after(turn, backs[-1][5])
        held = ring.scatter(held, "far", 0)
        grad_first = after(grad_first, held, output)
        feed_halves = ring.halves(held)
    else:
        backs = [back(meta, number, later) for number in range(calls)]
    grads = [[call[part] for call in backs] for part in range(3)]
    if parts > 1:
        homeward = [(i + seqs, i) for i in range(devices - seqs)]
        for part in (1, 2):
            for number in range(calls):
                received = lax.ppermute(backs[number][part + 2], "seq", homeward)
                grad = grads[part][number]
                tail = grad[rows - TILE :].astype(F32) + received.astype(F32)
                grads[part][number] = grad.at[rows - TILE :].set(tail.astype(BF16))
    mix = jnp.concatenate([call[5] for call in backs], 1)
    grad_x, project_grads = project_back(
        x, grad_first, qkv_weight, norm1_gain, norm1_bias, mix, small2, grad_in_b,
        grads[0] + grads[1] + grads[2],
    )
    input_grad = to_sequences(grad_x.reshape(seqs, span, width), "seq", groups)

    if by_ring:
        order = ring.order()
        project_halves = ring.reduce(project_grads, PAIR)
    else:
        order = jnp.arange(16, dtype=jnp.int32)
        total = lax.psum((feed_grads.astype(F32), project_grads.astype(F32)), ("seq", "batch"))
        feed_halves, project_halves = [
            [half.reshape(8, width // 16, -1) for half in (t[: width // 2], t[width // 2 :])]
            for t in total
        ]
    grad_in_w, grad_out_w, grad_down_w = unpack(
        write_feed, order, feed_halves, [(width, inner), (width, width), (inner, width)]
    )
    grad_qkv_w, small = unpack(
        write_project, order, project_halves, [(width, 3 * width), (width, PAIR)]
    )
    vectors = small.reshape(-1)
    vector = [vectors[at : at + width] for at in range(0, 8 * width, width)]
    grad_blend = vectors[5 * width : 8 * width].reshape(3, heads, width // heads).sum(-1)
    return (
        output,
        input_grad,
        vector[0],
        vector[1],
        grad_qkv_w,
        grad_blend,
        grad_out_w,
        vector[2],
        vector[3],
        grad_in_w,
        vectors[8 * width : 8 * width + inner],
        grad_down_w,
        vector[4],
    )


def solution(mesh):
    rows = P("batch", "seq", None)
    return jax.shard_map(
        local,
        mesh=mesh,
        in_specs=(rows, rows, P("batch")) + (P(),) * 11,
        out_specs=(rows, rows) + (P(),) * 11,
        check_vma=False,
    )
```

```python
import functools

import jax
import jax.numpy as jnp
from jax import lax
from jax.experimental import pallas as pl
from jax.experimental.pallas import tpu as pltpu
from jax.sharding import PartitionSpec as P

WINDOW = 30
HEAD = 64
PAIR = 2 * HEAD
TILE = 64
EPS = 1e-05
NEG = -1e30
BF16 = jnp.bfloat16
F32 = jnp.float32


def layer_norm(field, gain, shift):
    center = field - jnp.mean(field, axis=-1, keepdims=True)
    spread = jnp.mean(center * center, axis=-1, keepdims=True)
    return center * lax.rsqrt(spread + EPS) * gain + shift


def rows_product(left, right):
    return lax.dot_general(
        left, right, (((0,), (0,)), ((), ())), preferred_element_type=F32
    )


def times_transposed(left, right):
    return lax.dot_general(
        left, right, (((1,), (1,)), ((), ())), preferred_element_type=F32
    )


def times(left, right):
    return lax.dot_general(
        left, right, (((1,), (0,)), ((), ())), preferred_element_type=F32
    )


def elu_feature(field):
    return jnp.where(field > 0, field + 1.0, jnp.exp(jnp.minimum(field, 0.0)))


def tanh_feature(field):
    return 1.0 + jnp.tanh(field)


def pair_lanes(p, part=0, width=PAIR):
    return slice(p * width + part * PAIR, p * width + (part + 1) * PAIR)


def store_split(ref, index, rows, block):
    lane = lax.broadcasted_iota(jnp.int32, (block.shape[0], PAIR), 1)
    for p in range(block.shape[1] // PAIR):
        pair = block[:, pair_lanes(p)]
        for h in range(2):
            mine = (lane < HEAD) if h == 0 else (lane >= HEAD)
            ref[index + (rows, pair_lanes(p, h, 2 * PAIR))] = jnp.where(mine, pair, 0.0).astype(
                BF16
            )


def load_split(ref, index, rows, p):
    return jnp.concatenate([ref[index + (rows, pair_lanes(p, h, 2 * PAIR))] for h in range(2)], 0)


def tall(block):
    return jnp.concatenate([block[:, :PAIR], block[:, PAIR:]], 0)


def fill_features(meta_ref, q_ref, k_ref, v_ref, halo_k, halo_v, keys, values, fq, fk, split):
    rows, width = q_ref.shape
    chunk = 2 * TILE
    front = pl.ds(0, TILE)
    zero = jnp.zeros((TILE, width), F32)
    store_split(keys, (), front, halo_k[...].astype(F32) * 0.125)
    store_split(values, (), front, halo_v[...].astype(F32))
    for c in range(2):
        store_split(fk, (c,), front, zero)

    def fill(step, carry):
        at = pl.multiple_of(step * chunk, chunk)
        here, there = pl.ds(at, chunk), pl.ds(at + TILE, chunk)
        q = q_ref[here, :].astype(F32)
        k = k_ref[here, :].astype(F32)
        store_split(keys, (), there, k * 0.125)
        store_split(values, (), there, v_ref[here, :].astype(F32))
        position = meta_ref[1] + at + lax.broadcasted_iota(jnp.int32, (chunk, width), 0)
        valid = position < meta_ref[0]
        for c, feature in enumerate((elu_feature, tanh_feature)):
            if split:
                store_split(fq, (c,), here, feature(q))
            else:
                fq[c, here, :] = feature(q).astype(BF16)
            store_split(fk, (c,), there, jnp.where(valid, feature(k), 0.0))
        return carry

    lax.fori_loop(0, rows // chunk, fill, 0)


def tile_masks(meta_ref, tile):
    shape = (TILE, 2 * PAIR)
    row = lax.broadcasted_iota(jnp.int32, shape, 0)
    lane = lax.broadcasted_iota(jnp.int32, shape, 1) % PAIR
    back = row + TILE - lane
    key = meta_ref[1] + (tile - 1) * TILE + lane
    known = (key >= 0) & (key < meta_ref[0])
    near = (back >= 0) & (back <= WINDOW) & (known | (back == 0))
    return near, back >= 0


def softmax_pair(scores):
    halves = []
    for h in range(2):
        part = scores[:, h * PAIR : (h + 1) * PAIR]
        part = jnp.exp(part - jnp.max(part, axis=1, keepdims=True))
        halves.append(part * (1.0 / jnp.sum(part, axis=1, keepdims=True)))
    return jnp.concatenate(halves, 1)


def tile_constants():
    row = lax.broadcasted_iota(jnp.int32, (2 * PAIR, PAIR), 0)
    lane = lax.broadcasted_iota(jnp.int32, (2 * PAIR, PAIR), 1)
    ones = jnp.where(row // PAIR == lane // HEAD, 1.0, 0.0).astype(BF16)
    row = lax.broadcasted_iota(jnp.int32, (PAIR, 2 * PAIR), 0)
    lane = lax.broadcasted_iota(jnp.int32, (PAIR, 2 * PAIR), 1)
    return ones, row // HEAD == (lane % PAIR) // HEAD


def whole(split):
    half = split.shape[0] // 2
    return split[:half] + split[half:]


def state_share(block, fks, vs):
    ones = jnp.ones((TILE, PAIR), BF16)
    share = rows_product(whole(fks), jnp.concatenate([whole(vs), ones], 1))
    return jnp.where(block, share, 0.0)


def attend_kernel(
    meta_ref, blend_ref, q_ref, k_ref, v_ref, halo_k, halo_v, state_ref, att_ref, total_ref,
    keys, values, fq, fk, state,
):
    rows, width = q_ref.shape
    pairs = range(width // PAIR)
    fill_features(meta_ref, q_ref, k_ref, v_ref, halo_k, halo_v, keys, values, fq, fk, False)
    state[...] = state_ref[...]
    ones, block = tile_constants()

    def step(tile, carry):
        at = pl.multiple_of(tile * TILE, TILE)
        here, window, past = pl.ds(at, TILE), pl.ds(at, 2 * TILE), pl.ds(at, TILE)
        near_mask, far_mask = tile_masks(meta_ref, tile)
        q = [q_ref[here, pair_lanes(p)] for p in pairs]
        feats = [[fq[c, here, pair_lanes(p)] for c in range(2)] for p in pairs]
        held = [[state[c, p] for c in range(2)] for p in pairs]
        added = [
            [
                state_share(block, load_split(fk, (c,), past, p), load_split(values, (), past, p))
                for c in range(2)
            ]
            for p in pairs
        ]
        near = [times_transposed(q[p], load_split(keys, (), window, p)) for p in pairs]
        far = [
            [times_transposed(feats[p][c], load_split(fk, (c,), window, p)) for c in range(2)]
            for p in pairs
        ]
        near = [softmax_pair(jnp.where(near_mask, n, NEG)) for n in near]
        far = [[jnp.where(far_mask, f, 0.0) for f in fs] for fs in far]
        stack = [jnp.concatenate([n] + fs, 0).astype(BF16) for n, fs in zip(near, far)]
        wide = [jnp.concatenate([load_split(values, (), window, p), ones], 1) for p in pairs]
        sums = [times(s, w) for s, w in zip(stack, wide)]
        old = [[times(feats[p][c], held[p][c].astype(BF16)) for c in range(2)] for p in pairs]
        for p in pairs:
            mixed = blend_ref[0:1, pair_lanes(p)] * sums[p][:TILE, :PAIR]
            for c in range(2):
                mine = sums[p][(c + 1) * TILE : (c + 2) * TILE] + old[p][c]
                mixed = mixed + blend_ref[c + 1 : c + 2, pair_lanes(p)] * (
                    mine[:, :PAIR] / mine[:, PAIR:]
                )
            att_ref[here, pair_lanes(p)] = mixed.astype(BF16)
        for p in pairs:
            for c in range(2):
                state[c, p] = held[p][c] + added[p][c]
        return carry

    lax.fori_loop(0, rows // TILE, step, 0)
    last = pl.ds(rows, TILE)
    for p in pairs:
        for c in range(2):
            total_ref[c, p] = state[c, p] + state_share(
                block, load_split(fk, (c,), last, p), load_split(values, (), last, p)
            )


def slopes_of(field):
    small = jnp.exp(jnp.minimum(field, 0.0))
    bent = jnp.tanh(field)
    return [jnp.where(field > 0, 1.0, small), 1.0 - bent * bent]


def split_heads(block):
    lane = lax.broadcasted_iota(jnp.int32, block.shape, 1)
    zero = jnp.zeros_like(block)
    return jnp.concatenate(
        [jnp.where(lane < HEAD, block, zero), jnp.where(lane < HEAD, zero, block)], 0
    )


def attend_back_kernel(
    together, meta_ref, blend_ref, q_ref, k_ref, v_ref, halo_k, halo_v, state_ref, later_ref,
    go_ref, gq_ref, gk_ref, gv_ref, hk_ref, hv_ref, mix_ref, total_ref,
    keys, values, fq, fk, state, gk, gv, gfk, gon,
):
    rows, width = q_ref.shape
    pairs = range(width // PAIR)
    tiles = rows // TILE
    near_by = range(together)
    units = [(s, p) for s in near_by for p in pairs]
    fill_features(meta_ref, q_ref, k_ref, v_ref, halo_k, halo_v, keys, values, fq, fk, True)
    state[...] = state_ref[...]
    mix_ref[...] = jnp.zeros_like(mix_ref)
    gk[:TILE, :] = jnp.zeros((TILE, width), F32)
    gv[:TILE, :] = jnp.zeros((TILE, width), F32)
    gfk[:, :TILE, :] = jnp.zeros((2, TILE, width), F32)
    ones, block = tile_constants()
    row = lax.broadcasted_iota(jnp.int32, (2 * PAIR, PAIR), 0) % PAIR
    lane = lax.broadcasted_iota(jnp.int32, (2 * PAIR, PAIR), 1)
    heads = jnp.where(row // HEAD == lane // HEAD, 1.0, 0.0).astype(BF16)
    plain_ones = jnp.ones((TILE, PAIR), BF16)
    high = (lax.broadcasted_iota(jnp.int32, (TILE, PAIR), 1) % HEAD) < HEAD // 2

    def step(number, carry):
        first = number * together
        at = pl.multiple_of(first * TILE, TILE)
        here = [pl.ds(at + s * TILE, TILE) for s in range(together + 1)]
        window = [pl.ds(at + s * TILE, 2 * TILE) for s in near_by]
        masks = [tile_masks(meta_ref, first + s) for s in near_by]
        q = {(s, p): q_ref[here[s], pair_lanes(p)] for s, p in units}
        go = {(s, p): go_ref[here[s], pair_lanes(p)] for s, p in units}
        blend = [[blend_ref[c : c + 1, pair_lanes(p)] for c in range(3)] for p in pairs]
        fqs = {(s, p): [load_split(fq, (c,), here[s], p) for c in range(2)] for s, p in units}
        feats = {u: [whole(f) for f in fqs[u]] for u in units}
        ks = {(s, p): load_split(keys, (), window[s], p) for s, p in units}
        fks = {(s, p): [load_split(fk, (c,), window[s], p) for c in range(2)] for s, p in units}
        wide = {
            (s, p): jnp.concatenate([load_split(values, (), window[s], p), ones], 1)
            for s, p in units
        }
        held = {(0, p): [state[c, p] for c in range(2)] for p in pairs}
        for s, p in units:
            vs = load_split(values, (), here[s], p)
            held[s + 1, p] = [
                held[s, p][c] + state_share(block, load_split(fk, (c,), here[s], p), vs)
                for c in range(2)
            ]
        past = {u: [h.astype(BF16) for h in held[u]] for u in units}
        old_k = [gk[here[0], pair_lanes(p)] for p in pairs]
        old_v = [gv[here[0], pair_lanes(p)] for p in pairs]
        old_f = [[gfk[c, here[0], pair_lanes(p)] for c in range(2)] for p in pairs]

        near = {u: times_transposed(q[u], ks[u]) for u in units}
        far = {u: [times_transposed(feats[u][c], fks[u][c]) for c in range(2)] for u in units}
        old = {u: [times(feats[u][c], past[u][c]) for c in range(2)] for u in units}
        near = {u: softmax_pair(jnp.where(masks[u[0]][0], near[u], NEG)) for u in units}
        far = {u: [jnp.where(masks[u[0]][1], f, 0.0).astype(BF16) for f in far[u]] for u in units}
        stack = {u: jnp.concatenate([near[u].astype(BF16)] + far[u], 0) for u in units}
        sums = {u: times(stack[u], wide[u]) for u in units}
        scales, prods = {}, {}
        for u in units:
            outs = [sums[u][:TILE, :PAIR]]
            scales[u] = [jnp.broadcast_to(blend[u[1]][0], (TILE, PAIR))]
            for c in range(2):
                mine = sums[u][(c + 1) * TILE : (c + 2) * TILE] + old[u][c]
                inverse = 1.0 / mine[:, PAIR:]
                outs.append(mine[:, :PAIR] * inverse)
                scales[u].append(blend[u[1]][c + 1] * inverse)
            prods[u] = jnp.concatenate([go[u] * out for out in outs], 0)
        deltas = {}
        for u in units:
            low = prods[u].astype(BF16)
            rest = (prods[u] - low.astype(F32)).astype(BF16)
            deltas[u] = times(jnp.concatenate([low, rest], 1), heads)
        grads = {}
        for u in units:
            grads[u] = []
            for c in range(3):
                delta = scales[u][c] * deltas[u][c * TILE : (c + 1) * TILE] * (-2.0 / HEAD)
                delta_low = delta.astype(BF16).astype(F32)
                delta = jnp.where(high, delta_low, delta - delta_low)
                grads[u].append(jnp.concatenate([scales[u][c] * go[u], delta], 1).astype(BF16))
        back = {u: times_transposed(jnp.concatenate(grads[u], 0), wide[u]) for u in units}
        late = {u: [times_transposed(grads[u][c + 1], past[u][c]) for c in range(2)] for u in units}
        ds = {u: (near[u] * back[u][:TILE]).astype(BF16) for u in units}
        gas = {
            u: [
                jnp.where(masks[u[0]][1], back[u][(c + 1) * TILE : (c + 2) * TILE], 0.0).astype(BF16)
                for c in range(2)
            ]
            for u in units
        }
        gq_near = {u: times(ds[u], ks[u]) for u in units}
        gq_far = {u: [times(gas[u][c], fks[u][c]) + late[u][c] for c in range(2)] for u in units}
        new_k = {u: rows_product(tall(ds[u]), split_heads(q[u] * 0.125)) for u in units}
        new_f = {u: [rows_product(tall(gas[u][c]), fqs[u][c]) for c in range(2)] for u in units}
        new_v = {
            u: rows_product(
                jnp.concatenate([tall(stack[u][c * TILE : (c + 1) * TILE]) for c in range(3)], 0),
                jnp.concatenate([split_heads(g[:, :PAIR]) for g in grads[u]], 0),
            )
            for u in units
        }

        def overlap(old, new, p):
            parts = [old + new(0, p)[:TILE]]
            parts += [new(s, p)[TILE:] + new(s + 1, p)[:TILE] for s in range(together - 1)]
            return parts + [new(together - 1, p)[TILE:]]

        for s, p in units:
            u, lanes = (s, p), pair_lanes(p)
            slopes = slopes_of(q[u].astype(F32))
            gq = gq_near[u] + slopes[0] * gq_far[u][0] + slopes[1] * gq_far[u][1]
            gq_ref[here[s], lanes] = gq.astype(BF16)
            for c in range(2):
                gon[c, here[s], p * 2 * PAIR : (p + 1) * 2 * PAIR] = grads[u][c + 1]
        for p in pairs:
            lanes = pair_lanes(p)
            for c in range(3):
                mix_ref[c : c + 1, lanes] += sum(
                    jnp.sum(prods[s, p][c * TILE : (c + 1) * TILE], axis=0, keepdims=True)
                    for s in near_by
                )
            for rows_at, part in zip(here, overlap(old_k[p], lambda s, p: new_k[s, p], p)):
                gk[rows_at, lanes] = part
            for rows_at, part in zip(here, overlap(old_v[p], lambda s, p: new_v[s, p], p)):
                gv[rows_at, lanes] = part
            for c in range(2):
                parts = overlap(old_f[p][c], lambda s, p: new_f[s, p][c], p)
                for rows_at, part in zip(here, parts):
                    gfk[c, rows_at, lanes] = part
                state[c, p] = held[together, p][c]
        return carry

    lax.fori_loop(0, tiles // together, step, 0)
    hk_ref[...] = gk[:TILE, :].astype(BF16)
    hv_ref[...] = gv[:TILE, :].astype(BF16)
    state[...] = later_ref[...]

    def come(at, c, p):
        here = pl.ds(at, TILE)
        grads = gon[c, here, p * 2 * PAIR : (p + 1) * 2 * PAIR]
        share = rows_product(whole(load_split(fq, (c,), here, p)), grads)
        return jnp.where(block, share, 0.0)

    def back_step(number, carry):
        first = tiles - 1 - number * together
        at = [pl.multiple_of((first - s) * TILE, TILE) for s in near_by]
        here = [pl.ds(a, TILE) for a in at]
        there = [pl.ds(a + TILE, TILE) for a in at]
        held = {(-1, p): [state[c, p] for c in range(2)] for p in pairs}
        for s, p in units:
            tile = first - s + 2
            nearer = pl.multiple_of(jnp.minimum(tile, tiles - 1) * TILE, TILE)
            held[s, p] = [
                held[s - 1, p][c] + jnp.where(tile < tiles, come(nearer, c, p), 0.0)
                for c in range(2)
            ]
        later = {u: [h.astype(BF16) for h in held[u]] for u in units}
        vs = {(s, p): whole(load_split(values, (), there[s], p)) for s, p in units}
        fks = {
            (s, p): jnp.concatenate([whole(load_split(fk, (c,), there[s], p)) for c in range(2)], 1)
            for s, p in units
        }
        wide = {u: jnp.concatenate([vs[u], plain_ones], 1) for u in units}
        far_k = {u: [times_transposed(wide[u], later[u][c]) for c in range(2)] for u in units}
        far_v = {
            u: times(fks[u], jnp.concatenate([g[:, :PAIR] for g in later[u]], 0)) for u in units
        }
        for s, p in units:
            u, lanes = (s, p), pair_lanes(p)
            position = meta_ref[1] + at[s] + lax.broadcasted_iota(jnp.int32, (TILE, PAIR), 0)
            slopes = slopes_of(k_ref[here[s], lanes].astype(F32))
            grad_f = [gfk[c, there[s], lanes] + far_k[u][c] for c in range(2)]
            bent = slopes[0] * grad_f[0] + slopes[1] * grad_f[1]
            grad_k = gk[there[s], lanes] + jnp.where(position < meta_ref[0], bent, 0.0)
            gk_ref[here[s], lanes] = grad_k.astype(BF16)
            gv_ref[here[s], lanes] = (gv[there[s], lanes] + far_v[u]).astype(BF16)
        for p in pairs:
            for c in range(2):
                state[c, p] = held[together - 1, p][c]
        return carry

    lax.fori_loop(0, tiles // together, back_step, 0)
    for p in pairs:
        for c in range(2):
            total_ref[c, p] = state[c, p] + come(0, c, p) + come(TILE, c, p)


def attention_specs(rows, width, count, number, split):
    lanes, calls = width // count, count

    def columns(height, part):
        return pl.BlockSpec((height, lanes), lambda _: (0, part * calls + number))

    state = pl.BlockSpec(
        (2, lanes // PAIR, PAIR, 2 * PAIR), lambda _: (0, number, 0, 0)
    )
    ins = [pl.BlockSpec(memory_space=pltpu.SMEM), columns(3, 0)]
    ins += [columns(rows, part) for part in range(3)]
    ins += [columns(TILE, part) for part in range(2)]
    scratch = [
        pltpu.VMEM((rows + TILE, 2 * lanes), BF16),
        pltpu.VMEM((rows + TILE, 2 * lanes), BF16),
        pltpu.VMEM((2, rows, (2 if split else 1) * lanes), BF16),
        pltpu.VMEM((2, rows + TILE, 2 * lanes), BF16),
        pltpu.VMEM((2, lanes // PAIR, PAIR, 2 * PAIR), F32),
    ]
    return lanes, columns, ins, state, scratch


def outcome(shape, dtype):
    return jax.ShapeDtypeStruct(shape, dtype), pl.BlockSpec(shape, lambda _: (0,) * len(shape))


def attend(meta, blend, qkv, halo, state):
    rows, width = qkv.shape[0], qkv.shape[1] // 3
    _, _, ins, held, scratch = attention_specs(rows, width, 1, 0, False)
    shapes, blocks = zip(outcome((rows, width), BF16), outcome(state.shape, F32))
    return pl.pallas_call(
        attend_kernel,
        grid=(1,),
        out_shape=shapes,
        in_specs=ins + [held],
        out_specs=blocks,
        scratch_shapes=scratch,
        compiler_params=pltpu.CompilerParams(vmem_limit_bytes=32 * 2**20),
        cost_estimate=pl.CostEstimate(
            flops=rows * width * 48000, bytes_accessed=rows * width * 8, transcendentals=0
        ),
    )(meta, blend, qkv, qkv, qkv, halo, halo, state)


def attend_back(meta, blend, qkv, halo, state, later, go, calls, number):
    rows, width = qkv.shape[0], qkv.shape[1] // 3
    lanes, columns, ins, held, scratch = attention_specs(rows, width, calls, number, True)
    shapes, blocks = zip(
        *[outcome((rows, lanes), BF16)] * 3,
        *[outcome((TILE, lanes), BF16)] * 2,
        outcome((3, lanes), F32),
        outcome((2, lanes // PAIR, PAIR, 2 * PAIR), F32),
    )
    together = 4 * PAIR // lanes
    return pl.pallas_call(
        functools.partial(attend_back_kernel, together),
        grid=(1,),
        out_shape=shapes,
        in_specs=ins + [held, held, columns(rows, 0)],
        out_specs=blocks,
        scratch_shapes=scratch
        + [
            pltpu.VMEM((rows + TILE, lanes), F32),
            pltpu.VMEM((rows + TILE, lanes), F32),
            pltpu.VMEM((2, rows + TILE, lanes), F32),
            pltpu.VMEM((2, rows, 2 * lanes), BF16),
        ],
        compiler_params=pltpu.CompilerParams(vmem_limit_bytes=20 * 2**20),
        cost_estimate=pl.CostEstimate(
            flops=rows * lanes * 96000, bytes_accessed=rows * lanes * 16, transcendentals=0
        ),
    )(meta, blend, qkv, qkv, qkv, halo, halo, state, later, go)


CHUNK = 512
GELU_A, GELU_B = 0.7978845608028654, 0.044715


def normalized(field):
    center = field - jnp.mean(field, axis=-1, keepdims=True)
    scale = lax.rsqrt(jnp.mean(center * center, axis=-1, keepdims=True) + EPS)
    return center * scale, scale


def norm_back(grad, unit, scale):
    shared = jnp.mean(grad * unit, axis=-1, keepdims=True)
    return scale * (grad - jnp.mean(grad, axis=-1, keepdims=True) - unit * shared)


def gelu_pair(field):
    square = field * field
    bent = jnp.tanh(GELU_A * field * (1.0 + GELU_B * square))
    half = 0.5 + 0.5 * bent
    slope = half + 0.5 * field * (1.0 - bent * bent) * (GELU_A + 3.0 * GELU_A * GELU_B * square)
    return field * half, slope


def column_sum(block):
    return jnp.sum(block, axis=0, keepdims=True)


def feed_kernel(
    pieces, x_ref, att_ref, grad_ref, out_w, gain_ref, bias_ref, in_w, in_b, down_w, down_b,
    result_ref, first_ref, go_ref, packed_ref, small_ref, wide_ref,
    second, hidden, pre_low, att_low,
):
    rows, width = x_ref.shape
    inner = in_w.shape[1]
    small_ref[...] = jnp.zeros_like(small_ref)
    wide_ref[...] = jnp.zeros_like(wide_ref)

    def step(number, carry):
        here = pl.ds(pl.multiple_of(number * CHUNK, CHUNK), CHUNK)
        first = x_ref[here, :].astype(F32) + times(att_ref[here, :], out_w[...])
        unit, scale = normalized(first)
        low = (unit * gain_ref[...] + bias_ref[...]).astype(BF16)
        second[here, :] = low
        grad = grad_ref[here, :]
        grad_f = grad.astype(F32)
        result = first + down_b[...]
        back = jnp.zeros((CHUNK, width), F32)
        for at in range(0, inner, width):
            lanes = slice(at, at + width)
            act, slope = gelu_pair(times(low, in_w[:, lanes]) + in_b[:, lanes])
            act = act.astype(BF16)
            hidden[here, lanes] = act
            result = result + times(act, down_w[lanes, :])
            pre = (times_transposed(grad, down_w[lanes, :]) * slope).astype(BF16)
            pre_low[here, lanes] = pre
            wide_ref[:, lanes] += column_sum(pre.astype(F32))
            back = back + times_transposed(pre, in_w[:, lanes])
        result_ref[here, :] = result.astype(BF16)
        small_ref[0:1, :] += column_sum(back * unit)
        small_ref[1:2, :] += column_sum(back)
        small_ref[2:3, :] += column_sum(grad_f)
        grad_first = grad_f + norm_back(back * gain_ref[...], unit, scale)
        first_ref[here, :] = grad_first
        grad_att = grad_first.astype(BF16)
        att_low[here, :] = grad_att
        go_ref[here, :] = times_transposed(grad_att, out_w[...])
        return carry

    lax.fori_loop(0, rows // CHUNK, step, 0)
    for at in range(0, inner, width):
        lanes = slice(at, at + width)
        packed_ref[:, lanes] = rows_product(second[...], pre_low[:, lanes]).astype(BF16)
    packed_ref[:, inner : inner + width] = rows_product(att_ref[...], att_low[...]).astype(BF16)
    tall_rows, flat_rows = inner // pieces, width // pieces
    for at in range(0, inner, width):
        share = rows_product(hidden[:, at : at + width], grad_ref[...]).astype(BF16)
        for below in range(0, width, flat_rows):
            piece, block = divmod(at + below, tall_rows)
            lanes = inner + width + block // flat_rows * width
            packed_ref[piece * flat_rows : (piece + 1) * flat_rows, lanes : lanes + width] = share[
                below : below + flat_rows
            ]


def feed_forward(pieces, x, att, grad, out_w, gain, bias, in_w, in_b, down_w, down_b):
    rows, width = x.shape
    inner = in_w.shape[1]
    return pl.pallas_call(
        functools.partial(feed_kernel, pieces),
        out_shape=(
            jax.ShapeDtypeStruct((rows, width), BF16),
            jax.ShapeDtypeStruct((rows, width), F32),
            jax.ShapeDtypeStruct((rows, width), F32),
            jax.ShapeDtypeStruct((width, 2 * inner + width), BF16),
            jax.ShapeDtypeStruct((3, width), F32),
            jax.ShapeDtypeStruct((1, inner), F32),
        ),
        in_specs=[pl.BlockSpec(memory_space=pltpu.VMEM)] * 10,
        out_specs=(pl.BlockSpec(memory_space=pltpu.VMEM),) * 6,
        scratch_shapes=[
            pltpu.VMEM((rows, width), BF16),
            pltpu.VMEM((rows, inner), BF16),
            pltpu.VMEM((rows, inner), BF16),
            pltpu.VMEM((rows, width), BF16),
        ],
        compiler_params=pltpu.CompilerParams(vmem_limit_bytes=40 * 2**20),
        cost_estimate=pl.CostEstimate(
            flops=rows * width * inner * 24, bytes_accessed=rows * width * 20, transcendentals=0
        ),
    )(x, att, grad, out_w, gain[None], bias[None], in_w, in_b[None], down_w, down_b[None])


def project_back_kernel(
    calls, x_ref, first_ref, w_ref, gain_ref, bias_ref, mix_ref, small2_ref, wide_ref, *refs
):
    grads = refs[: 3 * calls]
    result_ref, packed_ref, normed, gathered, sums, rows_of = refs[3 * calls :]
    rows, width = x_ref.shape
    sums[...] = jnp.zeros_like(sums)

    def step(number, carry):
        here = pl.ds(pl.multiple_of(number * CHUNK, CHUNK), CHUNK)
        unit, scale = normalized(x_ref[here, :].astype(F32))
        normed[here, :] = (unit * gain_ref[...] + bias_ref[...]).astype(BF16)
        grad = jnp.concatenate([ref[here, :] for ref in grads], 1)
        gathered[here, :] = grad
        back = times_transposed(grad, w_ref[...])
        sums[0:1, :] += column_sum(back * unit)
        sums[1:2, :] += column_sum(back)
        grad_x = first_ref[here, :] + norm_back(back * gain_ref[...], unit, scale)
        result_ref[here, :] = grad_x.astype(BF16)
        return carry

    lax.fori_loop(0, rows // CHUNK, step, 0)
    for at in range(0, 3 * width, width):
        lanes = slice(at, at + width)
        packed_ref[:, lanes] = rows_product(normed[...], gathered[:, lanes]).astype(BF16)
    rows_of[...] = jnp.zeros_like(rows_of)
    at = 0
    for ref in (sums, small2_ref, mix_ref, wide_ref):
        for row in range(ref.shape[0]):
            for lane in range(0, ref.shape[1], PAIR):
                rows_of[at : at + 1, :] = ref[row : row + 1, lane : lane + PAIR]
                at += 1
    high = rows_of[...].astype(BF16)
    packed_ref[:, 3 * width : 3 * width + PAIR] = high
    packed_ref[:, 3 * width + PAIR :] = (rows_of[...] - high.astype(F32)).astype(BF16)


def project_back(x, grad_first, weight, gain, bias, mix, small2, wide, grads):
    rows, width = x.shape
    vmem = pl.BlockSpec(memory_space=pltpu.VMEM)
    return pl.pallas_call(
        functools.partial(project_back_kernel, len(grads) // 3),
        out_shape=(
            jax.ShapeDtypeStruct((rows, width), BF16),
            jax.ShapeDtypeStruct((width, 3 * width + 2 * PAIR), BF16),
        ),
        in_specs=[vmem] * (8 + len(grads)),
        out_specs=(vmem, vmem),
        scratch_shapes=[
            pltpu.VMEM((rows, width), BF16),
            pltpu.VMEM((rows, 3 * width), BF16),
            pltpu.VMEM((2, width), F32),
            pltpu.VMEM((width, PAIR), F32),
        ],
        compiler_params=pltpu.CompilerParams(vmem_limit_bytes=24 * 2**20),
        cost_estimate=pl.CostEstimate(
            flops=rows * width * width * 24, bytes_accessed=rows * width * 20, transcendentals=0
        ),
    )(x, grad_first, weight, gain[None], bias[None], mix, small2, wide, *grads)


def to_sequences(block, axis, groups):
    return lax.all_to_all(block, axis, 0, 0, axis_index_groups=groups)


def after(value, *others):
    return lax.optimization_barrier((value,) + others)[0]


def settle_kernel(source_ref, out_ref):
    out_ref[...] = source_ref[...]


def settle(value):
    vmem = pl.BlockSpec(memory_space=pltpu.VMEM)
    return pl.pallas_call(
        settle_kernel,
        out_shape=jax.ShapeDtypeStruct(value.shape, value.dtype),
        in_specs=[vmem],
        out_specs=vmem,
        compiler_params=pltpu.CompilerParams(vmem_limit_bytes=8 * 2**20),
        cost_estimate=pl.CostEstimate(flops=0, bytes_accessed=4 * value.size, transcendentals=0),
    )(value)


def from_parts(total, axis, parts, stride, forward):
    size = lax.axis_size(axis)
    low = total.astype(BF16)
    result = jnp.zeros_like(total)
    for hop in range(1, parts):
        distance = hop * stride
        route = [
            (i, i + distance) if forward else (i + distance, i) for i in range(size - distance)
        ]
        result = result + lax.ppermute(low, axis, route).astype(F32)
    return result


class Ring:
    def __init__(self, batch, seq):
        self.batch, self.seq = batch, seq
        self.low = 2 ** ((seq.bit_length() - 1) // 2)
        self.sizes = {"core": 2, "near": batch // 2 * self.low, "far": seq // self.low}
        self.pieces = batch * seq

    def place(self, s, b):
        return {"core": b % 2, "near": b // 2 * self.low + s % self.low, "far": s // self.low}

    def device(self, place):
        s = place["far"] * self.low + place["near"] % self.low
        return s * self.batch + place["near"] // self.low * 2 + place["core"]

    def mine(self):
        return self.place(lax.axis_index("seq"), lax.axis_index("batch"))

    def swap(self, value, level, k):
        route = []
        for s in range(self.seq):
            for b in range(self.batch):
                place = self.place(s, b)
                place[level] ^= k
                route.append((s * self.batch + b, self.device(place)))
        return lax.ppermute(value, ("seq", "batch"), route)

    def scatter(self, value, level, fine=0, beside=()):
        size, me = self.sizes[level], self.mine()[level]
        value = value.reshape((size, value.shape[0] // size) + value.shape[1:])
        parts = [
            self.swap(lax.dynamic_index_in_dim(value, me ^ k, 0, False), level, k)
            for k in range(1, size)
        ]
        total = after(lax.dynamic_index_in_dim(value, me, 0, False), *beside).astype(F32)
        for part in parts:
            total = total + part.astype(F32)
        if not fine:
            return total.astype(BF16)
        end = total.shape[-1] - 2 * fine
        exact = total[..., end : end + fine] + total[..., end + fine :]
        high = lax.reduce_precision(exact, 8, 7)
        return jnp.concatenate([total[..., :end], high, exact - high], -1).astype(BF16)

    def gather(self, value, level, beside=()):
        parts = [self.swap(value, level, k) for k in range(1, self.sizes[level])]
        return jnp.concatenate([after(value, *beside)] + parts, 0)

    def to_pieces(self, value):
        return value.reshape(self.pieces, value.shape[0] // self.pieces, value.shape[1])

    def order(self):
        me = self.mine()
        piece = jnp.arange(self.pieces, dtype=jnp.int32)
        far, near = self.sizes["far"], self.sizes["near"]
        core = (piece // (far * near)) ^ me["core"]
        near = ((piece // far) % near) ^ me["near"]
        return (core * self.sizes["near"] + near) * far + ((piece % far) ^ me["far"])


def unpack_kernel(write, order_ref, own_ref, other_ref, *out_refs):
    half = own_ref.shape[0]
    for piece in range(2 * half):
        at = order_ref[piece]

        @pl.when(at < half)
        def _(piece=piece, at=at):
            write(piece, own_ref[at].astype(F32), out_refs)

        @pl.when(at >= half)
        def _(piece=piece, at=at):
            write(piece, other_ref[at - half].astype(F32), out_refs)


def write_feed(piece, block, out_refs):
    in_ref, out_ref, down_ref = out_refs
    size, inner, width = block.shape[0], in_ref.shape[1], in_ref.shape[0]
    rows = slice(piece * size, (piece + 1) * size)
    in_ref[rows, :] = block[:, :inner]
    out_ref[rows, :] = block[:, inner : inner + width]
    tall_rows = inner // (width // size)
    for below in range(0, tall_rows, size):
        at = inner + width + below // size * width
        down_ref[piece * tall_rows + below : piece * tall_rows + below + size, :] = block[
            :, at : at + width
        ]


def write_project(piece, block, out_refs):
    w_ref, small_ref = out_refs
    size, end = block.shape[0], w_ref.shape[1]
    rows = slice(piece * size, (piece + 1) * size)
    w_ref[rows, :] = block[:, :end]
    small_ref[rows, :] = block[:, end : end + PAIR] + block[:, end + PAIR :]


def unpack(write, order, halves, shapes):
    vmem = pl.BlockSpec(memory_space=pltpu.VMEM)
    return pl.pallas_call(
        functools.partial(unpack_kernel, write),
        out_shape=[jax.ShapeDtypeStruct(shape, F32) for shape in shapes],
        in_specs=[pl.BlockSpec(memory_space=pltpu.SMEM), vmem, vmem],
        out_specs=[vmem] * len(shapes),
        compiler_params=pltpu.CompilerParams(vmem_limit_bytes=20 * 2**20),
        cost_estimate=pl.CostEstimate(
            flops=0, bytes_accessed=8 * halves[0].size, transcendentals=0
        ),
    )(order, *halves)


def local(
    inputs,
    cotangent,
    lengths,
    norm1_gain,
    norm1_bias,
    qkv_weight,
    blend_weights,
    out_weight,
    norm2_gain,
    norm2_bias,
    in_weight,
    in_bias,
    down_weight,
    down_bias,
):
    seqs, span, width = inputs.shape
    heads = blend_weights.shape[1]
    devices = lax.axis_size("seq")
    parts = devices // seqs
    rows = seqs * span
    index = lax.axis_index("seq")
    groups = None
    if parts > 1:
        groups = [[r * seqs + s for s in range(seqs)] for r in range(parts)]
    mine, part = index % seqs, index // seqs
    meta = jnp.stack([lax.dynamic_index_in_dim(lengths, mine, 0, False), part * rows])
    blend = jnp.repeat(blend_weights, width // heads, axis=1)

    ring = Ring(lax.axis_size("batch"), devices)
    by_ring = width % (16 * ring.pieces) == 0
    inner = in_weight.shape[1]

    x = to_sequences(inputs, "seq", groups).reshape(rows, width)
    grad_out = to_sequences(cotangent, "seq", groups).reshape(rows, width)

    normed = layer_norm(x.astype(F32), norm1_gain, norm1_bias).astype(BF16)
    qkv = times(normed, qkv_weight).astype(BF16)
    halo = jnp.zeros((TILE, 2 * width), BF16)
    state = jnp.zeros((2, width // PAIR, PAIR, 2 * PAIR), F32)
    later = state
    if parts > 1:
        onward = [(i, i + seqs) for i in range(devices - seqs)]
        halo = lax.ppermute(qkv[rows - TILE :, width:], "seq", onward)
        total = attend(meta, blend, qkv, halo, state)[1]
        state = from_parts(total, "seq", parts, seqs, True)
    attended = attend(meta, blend, qkv, halo, state)[0]

    result, grad_first, grad_o, feed_grads, small2, grad_in_b = feed_forward(
        ring.pieces if by_ring else 16,
        x, attended, grad_out, out_weight, norm2_gain, norm2_bias,
        in_weight, in_bias, down_weight, down_bias,
    )
    output = to_sequences(result.reshape(seqs, span, width), "seq", groups)
    def unpack_feed(order, halves):
        shapes = [(width, inner), (width, width), (inner, width)]
        return unpack(write_feed, order, halves, shapes)

    calls = 4

    def back(meta, number, later):
        return attend_back(meta, blend, qkv, halo, state, later, grad_o, calls, number)

    if parts > 1:
        total = jnp.concatenate([back(meta, number, later)[6] for number in range(calls)], 1)
        later = from_parts(total, "seq", parts, seqs, False)
    backs, turn = [], meta
    if by_ring:
        held = ring.to_pieces(feed_grads)
        rounds = {1: "core", 3: "near"}
        for number in range(calls):
            if number in rounds:
                held = ring.scatter(held, rounds[number])
                turn = after(turn, held)
            backs.append(back(turn, number, later))
            turn = after(turn, backs[-1][5])
        held = ring.scatter(held, "far")
        output = settle(after(output, backs[1][5]))
        grad_first = after(grad_first, held, output)
    else:
        backs = [back(meta, number, later) for number in range(calls)]
    grads = [[call[part] for call in backs] for part in range(3)]
    if parts > 1:
        homeward = [(i + seqs, i) for i in range(devices - seqs)]
        for part in (1, 2):
            for number in range(calls):
                received = lax.ppermute(backs[number][part + 2], "seq", homeward)
                grad = grads[part][number]
                tail = grad[rows - TILE :].astype(F32) + received.astype(F32)
                grads[part][number] = grad.at[rows - TILE :].set(tail.astype(BF16))
    mix = jnp.concatenate([call[5] for call in backs], 1)
    grad_x, project_grads = project_back(
        x, grad_first, qkv_weight, norm1_gain, norm1_bias, mix, small2, grad_in_b,
        grads[0] + grads[1] + grads[2],
    )
    if by_ring:
        order = ring.order()
        late = ring.scatter(ring.to_pieces(project_grads), "core", PAIR)
        moved = to_sequences(after(grad_x, late).reshape(seqs, span, width), "seq", groups)
        held = ring.gather(held, "far")
        late = ring.scatter(late, "near", PAIR)
        held = ring.gather(held, "near", (late,))
        other = ring.swap(held, "core", 1)
        late = ring.scatter(late, "far", PAIR, (held,))
        grad_in_w, grad_out_w, grad_down_w = unpack_feed(order, (held, after(other, late)))
        late = ring.gather(late, "far", (grad_out_w,))
        input_grad = settle(after(moved, late))
        late = ring.gather(late, "near", (input_grad,))
        project_halves = late, ring.swap(late, "core", 1)
    else:
        input_grad = to_sequences(grad_x.reshape(seqs, span, width), "seq", groups)
        order = jnp.arange(16, dtype=jnp.int32)
        total = lax.psum((feed_grads.astype(F32), project_grads.astype(F32)), ("seq", "batch"))
        feed_halves, project_halves = [
            [half.reshape(8, width // 16, -1) for half in (t[: width // 2], t[width // 2 :])]
            for t in total
        ]
        grad_in_w, grad_out_w, grad_down_w = unpack_feed(order, feed_halves)
    grad_qkv_w, small = unpack(
        write_project, order, project_halves, [(width, 3 * width), (width, PAIR)]
    )
    vectors = small.reshape(-1)
    vector = [vectors[at : at + width] for at in range(0, 8 * width, width)]
    grad_blend = vectors[5 * width : 8 * width].reshape(3, heads, width // heads).sum(-1)
    return (
        output,
        input_grad,
        vector[0],
        vector[1],
        grad_qkv_w,
        grad_blend,
        grad_out_w,
        vector[2],
        vector[3],
        grad_in_w,
        vectors[8 * width : 8 * width + inner],
        grad_down_w,
        vector[4],
    )


def solution(mesh):
    rows = P("batch", "seq", None)
    return jax.shard_map(
        local,
        mesh=mesh,
        in_specs=(rows, rows, P("batch")) + (P(),) * 11,
        out_specs=(rows, rows) + (P(),) * 11,
        check_vma=False,
    )
```

```python
import functools

import jax
import jax.numpy as jnp
from jax import lax
from jax.experimental import pallas as pl
from jax.experimental.pallas import tpu as pltpu
from jax.sharding import PartitionSpec as P

WINDOW = 30
HEAD = 64
PAIR = 2 * HEAD
TILE = 64
EPS = 1e-05
NEG = -1e30
VMEM = 58 * 2**20
BF16 = jnp.bfloat16
F32 = jnp.float32


def layer_norm(field, gain, shift):
    center = field - jnp.mean(field, axis=-1, keepdims=True)
    spread = jnp.mean(center * center, axis=-1, keepdims=True)
    return center * lax.rsqrt(spread + EPS) * gain + shift


def rows_product(left, right):
    return lax.dot_general(
        left, right, (((0,), (0,)), ((), ())), preferred_element_type=F32
    )


def times_transposed(left, right):
    return lax.dot_general(
        left, right, (((1,), (1,)), ((), ())), preferred_element_type=F32
    )


def times(left, right):
    return lax.dot_general(
        left, right, (((1,), (0,)), ((), ())), preferred_element_type=F32
    )


def elu_feature(field):
    return jnp.where(field > 0, field + 1.0, jnp.exp(jnp.minimum(field, 0.0)))


def tanh_feature(field):
    return 1.0 + jnp.tanh(field)


def pair_lanes(p, part=0, width=PAIR):
    return slice(p * width + part * PAIR, p * width + (part + 1) * PAIR)


def store_split(ref, index, rows, block):
    lane = lax.broadcasted_iota(jnp.int32, (block.shape[0], PAIR), 1)
    for p in range(block.shape[1] // PAIR):
        pair = block[:, pair_lanes(p)]
        for h in range(2):
            mine = (lane < HEAD) if h == 0 else (lane >= HEAD)
            ref[index + (rows, pair_lanes(p, h, 2 * PAIR))] = jnp.where(mine, pair, 0.0).astype(
                BF16
            )


def load_split(ref, index, rows, p):
    return jnp.concatenate([ref[index + (rows, pair_lanes(p, h, 2 * PAIR))] for h in range(2)], 0)


def tall(block):
    return jnp.concatenate([block[:, :PAIR], block[:, PAIR:]], 0)


def fill_features(meta_ref, q_ref, k_ref, v_ref, halo_k, halo_v, keys, values, fq, fk, split):
    rows, width = q_ref.shape
    chunk = 2 * TILE
    front = pl.ds(0, TILE)
    zero = jnp.zeros((TILE, width), F32)
    store_split(keys, (), front, halo_k[...].astype(F32) * 0.125)
    store_split(values, (), front, halo_v[...].astype(F32))
    for c in range(2):
        store_split(fk, (c,), front, zero)

    def fill(step, carry):
        at = pl.multiple_of(step * chunk, chunk)
        here, there = pl.ds(at, chunk), pl.ds(at + TILE, chunk)
        q = q_ref[here, :].astype(F32)
        k = k_ref[here, :].astype(F32)
        store_split(keys, (), there, k * 0.125)
        store_split(values, (), there, v_ref[here, :].astype(F32))
        position = meta_ref[1] + at + lax.broadcasted_iota(jnp.int32, (chunk, width), 0)
        valid = position < meta_ref[0]
        for c, feature in enumerate((elu_feature, tanh_feature)):
            if split:
                store_split(fq, (c,), here, feature(q))
            else:
                fq[c, here, :] = feature(q).astype(BF16)
            store_split(fk, (c,), there, jnp.where(valid, feature(k), 0.0))
        return carry

    lax.fori_loop(0, rows // chunk, fill, 0)


def tile_masks(meta_ref, tile):
    shape = (TILE, 2 * PAIR)
    row = lax.broadcasted_iota(jnp.int32, shape, 0)
    lane = lax.broadcasted_iota(jnp.int32, shape, 1) % PAIR
    back = row + TILE - lane
    key = meta_ref[1] + (tile - 1) * TILE + lane
    known = (key >= 0) & (key < meta_ref[0])
    near = (back >= 0) & (back <= WINDOW) & (known | (back == 0))
    return near, back >= 0


def softmax_pair(scores):
    halves = []
    for h in range(2):
        part = scores[:, h * PAIR : (h + 1) * PAIR]
        part = jnp.exp(part - jnp.max(part, axis=1, keepdims=True))
        halves.append(part * (1.0 / jnp.sum(part, axis=1, keepdims=True)))
    return jnp.concatenate(halves, 1)


def tile_constants():
    row = lax.broadcasted_iota(jnp.int32, (2 * PAIR, PAIR), 0)
    lane = lax.broadcasted_iota(jnp.int32, (2 * PAIR, PAIR), 1)
    ones = jnp.where(row // PAIR == lane // HEAD, 1.0, 0.0).astype(BF16)
    row = lax.broadcasted_iota(jnp.int32, (PAIR, 2 * PAIR), 0)
    lane = lax.broadcasted_iota(jnp.int32, (PAIR, 2 * PAIR), 1)
    return ones, row // HEAD == (lane % PAIR) // HEAD


def whole(split):
    half = split.shape[0] // 2
    return split[:half] + split[half:]


def state_share(block, fks, vs):
    ones = jnp.ones((TILE, PAIR), BF16)
    share = rows_product(whole(fks), jnp.concatenate([whole(vs), ones], 1))
    return jnp.where(block, share, 0.0)


def attend_kernel(
    together, meta_ref, blend_ref, q_ref, k_ref, v_ref, halo_k, halo_v, state_ref,
    att_ref, total_ref, keys, values, fq, fk, state,
):
    rows, width = q_ref.shape
    pairs = range(width // PAIR)
    near_by = range(together)
    units = [(s, p) for s in near_by for p in pairs]
    fill_features(meta_ref, q_ref, k_ref, v_ref, halo_k, halo_v, keys, values, fq, fk, False)
    state[...] = state_ref[...]
    ones, block = tile_constants()

    def step(number, carry):
        first = number * together
        at = pl.multiple_of(first * TILE, TILE)
        here = [pl.ds(at + s * TILE, TILE) for s in near_by]
        window = [pl.ds(at + s * TILE, 2 * TILE) for s in near_by]
        masks = [tile_masks(meta_ref, first + s) for s in near_by]
        q = {(s, p): q_ref[here[s], pair_lanes(p)] for s, p in units}
        feats = {(s, p): [fq[c, here[s], pair_lanes(p)] for c in range(2)] for s, p in units}
        ks = {(s, p): load_split(keys, (), window[s], p) for s, p in units}
        fks = {(s, p): [load_split(fk, (c,), window[s], p) for c in range(2)] for s, p in units}
        wide = {
            (s, p): jnp.concatenate([load_split(values, (), window[s], p), ones], 1)
            for s, p in units
        }
        held = {(0, p): [state[c, p] for c in range(2)] for p in pairs}
        for s, p in units:
            vs = load_split(values, (), here[s], p)
            held[s + 1, p] = [
                held[s, p][c] + state_share(block, load_split(fk, (c,), here[s], p), vs)
                for c in range(2)
            ]
        near = {u: times_transposed(q[u], ks[u]) for u in units}
        far = {u: [times_transposed(feats[u][c], fks[u][c]) for c in range(2)] for u in units}
        old = {u: [times(feats[u][c], held[u][c].astype(BF16)) for c in range(2)] for u in units}
        near = {u: softmax_pair(jnp.where(masks[u[0]][0], near[u], NEG)) for u in units}
        far = {u: [jnp.where(masks[u[0]][1], f, 0.0) for f in far[u]] for u in units}
        stack = {u: jnp.concatenate([near[u]] + far[u], 0).astype(BF16) for u in units}
        sums = {u: times(stack[u], wide[u]) for u in units}
        for s, p in units:
            u, lanes = (s, p), pair_lanes(p)
            mixed = blend_ref[0:1, lanes] * sums[u][:TILE, :PAIR]
            for c in range(2):
                mine = sums[u][(c + 1) * TILE : (c + 2) * TILE] + old[u][c]
                mixed = mixed + blend_ref[c + 1 : c + 2, lanes] * (
                    mine[:, :PAIR] / mine[:, PAIR:]
                )
            att_ref[here[s], lanes] = mixed.astype(BF16)
        for p in pairs:
            for c in range(2):
                state[c, p] = held[together, p][c]
        return carry

    lax.fori_loop(0, rows // (together * TILE), step, 0)
    last = pl.ds(rows, TILE)
    for p in pairs:
        for c in range(2):
            total_ref[c, p] = state[c, p] + state_share(
                block, load_split(fk, (c,), last, p), load_split(values, (), last, p)
            )


def slopes_of(field):
    small = jnp.exp(jnp.minimum(field, 0.0))
    bent = jnp.tanh(field)
    return [jnp.where(field > 0, 1.0, small), 1.0 - bent * bent]


def split_heads(block):
    lane = lax.broadcasted_iota(jnp.int32, block.shape, 1)
    zero = jnp.zeros_like(block)
    return jnp.concatenate(
        [jnp.where(lane < HEAD, block, zero), jnp.where(lane < HEAD, zero, block)], 0
    )


def attend_back_kernel(
    together, meta_ref, blend_ref, q_ref, k_ref, v_ref, halo_k, halo_v, state_ref, later_ref,
    go_ref, gq_ref, gk_ref, gv_ref, hk_ref, hv_ref, mix_ref, total_ref,
    keys, values, fq, fk, state, gk, gv, gfk, gon,
):
    rows, width = q_ref.shape
    pairs = range(width // PAIR)
    tiles = rows // TILE
    near_by = range(together)
    units = [(s, p) for s in near_by for p in pairs]
    fill_features(meta_ref, q_ref, k_ref, v_ref, halo_k, halo_v, keys, values, fq, fk, True)
    state[...] = state_ref[...]
    mix_ref[...] = jnp.zeros_like(mix_ref)
    gk[:TILE, :] = jnp.zeros((TILE, width), F32)
    gv[:TILE, :] = jnp.zeros((TILE, width), F32)
    gfk[:, :TILE, :] = jnp.zeros((2, TILE, width), F32)
    ones, block = tile_constants()
    row = lax.broadcasted_iota(jnp.int32, (2 * PAIR, PAIR), 0) % PAIR
    lane = lax.broadcasted_iota(jnp.int32, (2 * PAIR, PAIR), 1)
    heads = jnp.where(row // HEAD == lane // HEAD, 1.0, 0.0).astype(BF16)
    plain_ones = jnp.ones((TILE, PAIR), BF16)
    high = (lax.broadcasted_iota(jnp.int32, (TILE, PAIR), 1) % HEAD) < HEAD // 2

    def step(number, carry):
        first = number * together
        at = pl.multiple_of(first * TILE, TILE)
        here = [pl.ds(at + s * TILE, TILE) for s in range(together + 1)]
        window = [pl.ds(at + s * TILE, 2 * TILE) for s in near_by]
        masks = [tile_masks(meta_ref, first + s) for s in near_by]
        q = {(s, p): q_ref[here[s], pair_lanes(p)] for s, p in units}
        go = {(s, p): go_ref[here[s], pair_lanes(p)] for s, p in units}
        blend = [[blend_ref[c : c + 1, pair_lanes(p)] for c in range(3)] for p in pairs]
        fqs = {(s, p): [load_split(fq, (c,), here[s], p) for c in range(2)] for s, p in units}
        feats = {u: [whole(f) for f in fqs[u]] for u in units}
        ks = {(s, p): load_split(keys, (), window[s], p) for s, p in units}
        fks = {(s, p): [load_split(fk, (c,), window[s], p) for c in range(2)] for s, p in units}
        wide = {
            (s, p): jnp.concatenate([load_split(values, (), window[s], p), ones], 1)
            for s, p in units
        }
        held = {(0, p): [state[c, p] for c in range(2)] for p in pairs}
        for s, p in units:
            vs = load_split(values, (), here[s], p)
            held[s + 1, p] = [
                held[s, p][c] + state_share(block, load_split(fk, (c,), here[s], p), vs)
                for c in range(2)
            ]
        past = {u: [h.astype(BF16) for h in held[u]] for u in units}
        old_k = [gk[here[0], pair_lanes(p)] for p in pairs]
        old_v = [gv[here[0], pair_lanes(p)] for p in pairs]
        old_f = [[gfk[c, here[0], pair_lanes(p)] for c in range(2)] for p in pairs]

        near = {u: times_transposed(q[u], ks[u]) for u in units}
        far = {u: [times_transposed(feats[u][c], fks[u][c]) for c in range(2)] for u in units}
        old = {u: [times(feats[u][c], past[u][c]) for c in range(2)] for u in units}
        near = {u: softmax_pair(jnp.where(masks[u[0]][0], near[u], NEG)) for u in units}
        far = {u: [jnp.where(masks[u[0]][1], f, 0.0).astype(BF16) for f in far[u]] for u in units}
        stack = {u: jnp.concatenate([near[u].astype(BF16)] + far[u], 0) for u in units}
        sums = {u: times(stack[u], wide[u]) for u in units}
        scales, prods = {}, {}
        for u in units:
            outs = [sums[u][:TILE, :PAIR]]
            scales[u] = [jnp.broadcast_to(blend[u[1]][0], (TILE, PAIR))]
            for c in range(2):
                mine = sums[u][(c + 1) * TILE : (c + 2) * TILE] + old[u][c]
                inverse = 1.0 / mine[:, PAIR:]
                outs.append(mine[:, :PAIR] * inverse)
                scales[u].append(blend[u[1]][c + 1] * inverse)
            prods[u] = jnp.concatenate([go[u] * out for out in outs], 0)
        deltas = {}
        for u in units:
            low = prods[u].astype(BF16)
            rest = (prods[u] - low.astype(F32)).astype(BF16)
            deltas[u] = times(jnp.concatenate([low, rest], 1), heads)
        grads = {}
        for u in units:
            grads[u] = []
            for c in range(3):
                delta = scales[u][c] * deltas[u][c * TILE : (c + 1) * TILE] * (-2.0 / HEAD)
                delta_low = delta.astype(BF16).astype(F32)
                delta = jnp.where(high, delta_low, delta - delta_low)
                grads[u].append(jnp.concatenate([scales[u][c] * go[u], delta], 1).astype(BF16))
        back = {u: times_transposed(jnp.concatenate(grads[u], 0), wide[u]) for u in units}
        late = {u: [times_transposed(grads[u][c + 1], past[u][c]) for c in range(2)] for u in units}
        ds = {u: (near[u] * back[u][:TILE]).astype(BF16) for u in units}
        gas = {
            u: [
                jnp.where(masks[u[0]][1], back[u][(c + 1) * TILE : (c + 2) * TILE], 0.0).astype(BF16)
                for c in range(2)
            ]
            for u in units
        }
        gq_near = {u: times(ds[u], ks[u]) for u in units}
        gq_far = {u: [times(gas[u][c], fks[u][c]) + late[u][c] for c in range(2)] for u in units}
        new_k = {u: rows_product(tall(ds[u]), split_heads(q[u] * 0.125)) for u in units}
        new_f = {u: [rows_product(tall(gas[u][c]), fqs[u][c]) for c in range(2)] for u in units}
        new_v = {
            u: rows_product(
                jnp.concatenate([tall(stack[u][c * TILE : (c + 1) * TILE]) for c in range(3)], 0),
                jnp.concatenate([split_heads(g[:, :PAIR]) for g in grads[u]], 0),
            )
            for u in units
        }

        def overlap(old, new, p):
            parts = [old + new(0, p)[:TILE]]
            parts += [new(s, p)[TILE:] + new(s + 1, p)[:TILE] for s in range(together - 1)]
            return parts + [new(together - 1, p)[TILE:]]

        for s, p in units:
            u, lanes = (s, p), pair_lanes(p)
            slopes = slopes_of(q[u].astype(F32))
            gq = gq_near[u] + slopes[0] * gq_far[u][0] + slopes[1] * gq_far[u][1]
            gq_ref[here[s], lanes] = gq.astype(BF16)
            for c in range(2):
                gon[c, here[s], p * 2 * PAIR : (p + 1) * 2 * PAIR] = grads[u][c + 1]
        for p in pairs:
            lanes = pair_lanes(p)
            for c in range(3):
                mix_ref[c : c + 1, lanes] += sum(
                    jnp.sum(prods[s, p][c * TILE : (c + 1) * TILE], axis=0, keepdims=True)
                    for s in near_by
                )
            for rows_at, part in zip(here, overlap(old_k[p], lambda s, p: new_k[s, p], p)):
                gk[rows_at, lanes] = part
            for rows_at, part in zip(here, overlap(old_v[p], lambda s, p: new_v[s, p], p)):
                gv[rows_at, lanes] = part
            for c in range(2):
                parts = overlap(old_f[p][c], lambda s, p: new_f[s, p][c], p)
                for rows_at, part in zip(here, parts):
                    gfk[c, rows_at, lanes] = part
                state[c, p] = held[together, p][c]
        return carry

    lax.fori_loop(0, tiles // together, step, 0)
    hk_ref[...] = gk[:TILE, :].astype(BF16)
    hv_ref[...] = gv[:TILE, :].astype(BF16)
    state[...] = later_ref[...]

    def come(at, c, p):
        here = pl.ds(at, TILE)
        grads = gon[c, here, p * 2 * PAIR : (p + 1) * 2 * PAIR]
        share = rows_product(whole(load_split(fq, (c,), here, p)), grads)
        return jnp.where(block, share, 0.0)

    def back_step(number, carry):
        first = tiles - 1 - number * together
        at = [pl.multiple_of((first - s) * TILE, TILE) for s in near_by]
        here = [pl.ds(a, TILE) for a in at]
        there = [pl.ds(a + TILE, TILE) for a in at]
        held = {(-1, p): [state[c, p] for c in range(2)] for p in pairs}
        for s, p in units:
            tile = first - s + 2
            nearer = pl.multiple_of(jnp.minimum(tile, tiles - 1) * TILE, TILE)
            held[s, p] = [
                held[s - 1, p][c] + jnp.where(tile < tiles, come(nearer, c, p), 0.0)
                for c in range(2)
            ]
        later = {u: [h.astype(BF16) for h in held[u]] for u in units}
        vs = {(s, p): whole(load_split(values, (), there[s], p)) for s, p in units}
        fks = {
            (s, p): jnp.concatenate([whole(load_split(fk, (c,), there[s], p)) for c in range(2)], 1)
            for s, p in units
        }
        wide = {u: jnp.concatenate([vs[u], plain_ones], 1) for u in units}
        far_k = {u: [times_transposed(wide[u], later[u][c]) for c in range(2)] for u in units}
        far_v = {
            u: times(fks[u], jnp.concatenate([g[:, :PAIR] for g in later[u]], 0)) for u in units
        }
        for s, p in units:
            u, lanes = (s, p), pair_lanes(p)
            position = meta_ref[1] + at[s] + lax.broadcasted_iota(jnp.int32, (TILE, PAIR), 0)
            slopes = slopes_of(k_ref[here[s], lanes].astype(F32))
            grad_f = [gfk[c, there[s], lanes] + far_k[u][c] for c in range(2)]
            bent = slopes[0] * grad_f[0] + slopes[1] * grad_f[1]
            grad_k = gk[there[s], lanes] + jnp.where(position < meta_ref[0], bent, 0.0)
            gk_ref[here[s], lanes] = grad_k.astype(BF16)
            gv_ref[here[s], lanes] = (gv[there[s], lanes] + far_v[u]).astype(BF16)
        for p in pairs:
            for c in range(2):
                state[c, p] = held[together - 1, p][c]
        return carry

    lax.fori_loop(0, tiles // together, back_step, 0)
    for p in pairs:
        for c in range(2):
            total_ref[c, p] = state[c, p] + come(0, c, p) + come(TILE, c, p)


def attention_specs(rows, width, lanes, number):
    calls = width // lanes

    def columns(height, part):
        return pl.BlockSpec((height, lanes), lambda i: (0, part * calls + number(i)))

    state = pl.BlockSpec(
        (2, lanes // PAIR, PAIR, 2 * PAIR), lambda i: (0, number(i), 0, 0)
    )
    ins = [pl.BlockSpec(memory_space=pltpu.SMEM), columns(3, 0)]
    ins += [columns(rows, part) for part in range(3)]
    ins += [columns(TILE, part) for part in range(2)]
    return columns, ins, state


def attention_scratch(rows, lanes, split):
    return [
        pltpu.VMEM((rows + TILE, 2 * lanes), BF16),
        pltpu.VMEM((rows + TILE, 2 * lanes), BF16),
        pltpu.VMEM((2, rows, (2 if split else 1) * lanes), BF16),
        pltpu.VMEM((2, rows + TILE, 2 * lanes), BF16),
        pltpu.VMEM((2, lanes // PAIR, PAIR, 2 * PAIR), F32),
    ]


def outcome(shape, dtype):
    return jax.ShapeDtypeStruct(shape, dtype), pl.BlockSpec(shape, lambda _: (0,) * len(shape))


UNITS = 8


def attend(meta, blend, qkv, halo, state):
    rows, width = qkv.shape[0], qkv.shape[1] // 3
    lanes = PAIR
    columns, ins, held = attention_specs(rows, width, lanes, lambda i: i)
    return pl.pallas_call(
        functools.partial(attend_kernel, UNITS * PAIR // lanes),
        grid=(width // lanes,),
        out_shape=(
            jax.ShapeDtypeStruct((rows, width), BF16),
            jax.ShapeDtypeStruct(state.shape, F32),
        ),
        in_specs=ins + [held],
        out_specs=(columns(rows, 0), held),
        scratch_shapes=attention_scratch(rows, lanes, False),
        compiler_params=pltpu.CompilerParams(vmem_limit_bytes=VMEM),
        cost_estimate=pl.CostEstimate(
            flops=rows * width * 44000, bytes_accessed=rows * width * 8, transcendentals=0
        ),
    )(meta, blend, qkv, qkv, qkv, halo, halo, state)


def attend_back(meta, blend, qkv, halo, state, later, go, calls, number):
    rows, width = qkv.shape[0], qkv.shape[1] // 3
    lanes = width // calls
    columns, ins, held = attention_specs(rows, width, lanes, lambda i: number)
    shapes, blocks = zip(
        *[outcome((rows, lanes), BF16)] * 3,
        *[outcome((TILE, lanes), BF16)] * 2,
        outcome((3, lanes), F32),
        outcome((2, lanes // PAIR, PAIR, 2 * PAIR), F32),
    )
    return pl.pallas_call(
        functools.partial(attend_back_kernel, UNITS * PAIR // lanes),
        grid=(1,),
        out_shape=shapes,
        in_specs=ins + [held, held, columns(rows, 0)],
        out_specs=blocks,
        scratch_shapes=attention_scratch(rows, lanes, True)
        + [
            pltpu.VMEM((rows + TILE, lanes), F32),
            pltpu.VMEM((rows + TILE, lanes), F32),
            pltpu.VMEM((2, rows + TILE, lanes), F32),
            pltpu.VMEM((2, rows, 2 * lanes), BF16),
        ],
        compiler_params=pltpu.CompilerParams(vmem_limit_bytes=VMEM),
        cost_estimate=pl.CostEstimate(
            flops=rows * lanes * 96000, bytes_accessed=rows * lanes * 16, transcendentals=0
        ),
    )(meta, blend, qkv, qkv, qkv, halo, halo, state, later, go)


CHUNK = 512
GELU_A, GELU_B = 0.7978845608028654, 0.044715


def normalized(field):
    center = field - jnp.mean(field, axis=-1, keepdims=True)
    scale = lax.rsqrt(jnp.mean(center * center, axis=-1, keepdims=True) + EPS)
    return center * scale, scale


def norm_back(grad, unit, scale):
    shared = jnp.mean(grad * unit, axis=-1, keepdims=True)
    return scale * (grad - jnp.mean(grad, axis=-1, keepdims=True) - unit * shared)


def gelu_pair(field):
    square = field * field
    bent = jnp.tanh(GELU_A * field * (1.0 + GELU_B * square))
    half = 0.5 + 0.5 * bent
    slope = half + 0.5 * field * (1.0 - bent * bent) * (GELU_A + 3.0 * GELU_A * GELU_B * square)
    return field * half, slope


def column_sum(block):
    return jnp.sum(block, axis=0, keepdims=True)


def deal(core_ref, rows, lanes, value, keep_ref, send_ref):
    half = value.shape[0] // 2

    @pl.when(core_ref[0] == 0)
    def _():
        keep_ref[rows, lanes] = value[:half]
        send_ref[rows, lanes] = value[half:]

    @pl.when(core_ref[0] != 0)
    def _():
        keep_ref[rows, lanes] = value[half:]
        send_ref[rows, lanes] = value[:half]


def feed_kernel(
    pieces, core_ref, x_ref, att_ref, grad_ref, out_w, gain_ref, bias_ref, in_w, in_b, down_w,
    down_b, result_ref, first_ref, go_ref, keep_ref, send_ref, small_ref, wide_ref,
    second, hidden, pre_low, att_low, att_all, grad_all,
):
    chunk, width = x_ref.shape
    inner = in_w.shape[1]
    number = pl.program_id(0)
    here = pl.ds(pl.multiple_of(number * chunk, chunk), chunk)

    @pl.when(number == 0)
    def _():
        small_ref[...] = jnp.zeros_like(small_ref)
        wide_ref[...] = jnp.zeros_like(wide_ref)

    att = att_ref[...]
    att_all[here, :] = att
    first = x_ref[...].astype(F32) + times(att, out_w[...])
    unit, scale = normalized(first)
    low = (unit * gain_ref[...] + bias_ref[...]).astype(BF16)
    second[here, :] = low
    grad = grad_ref[...]
    grad_all[here, :] = grad
    grad_f = grad.astype(F32)
    result = first + down_b[...]
    back = jnp.zeros((chunk, width), F32)
    for at in range(0, inner, width):
        lanes = slice(at, at + width)
        act, slope = gelu_pair(times(low, in_w[:, lanes]) + in_b[:, lanes])
        act = act.astype(BF16)
        hidden[here, lanes] = act
        result = result + times(act, down_w[lanes, :])
        pre = (times_transposed(grad, down_w[lanes, :]) * slope).astype(BF16)
        pre_low[here, lanes] = pre
        wide_ref[:, lanes] += column_sum(pre.astype(F32))
        back = back + times_transposed(pre, in_w[:, lanes])
    result_ref[...] = result.astype(BF16)
    small_ref[0:1, :] += column_sum(back * unit)
    small_ref[1:2, :] += column_sum(back)
    small_ref[2:3, :] += column_sum(grad_f)
    grad_first = grad_f + norm_back(back * gain_ref[...], unit, scale)
    first_ref[...] = grad_first
    grad_att = grad_first.astype(BF16)
    att_low[here, :] = grad_att
    go_ref[...] = times_transposed(grad_att, out_w[...])

    @pl.when(number == pl.num_programs(0) - 1)
    def _():
        every = slice(0, width // 2)
        for at in range(0, inner, width):
            lanes = slice(at, at + width)
            share = rows_product(second[...], pre_low[:, lanes]).astype(BF16)
            deal(core_ref, every, lanes, share, keep_ref, send_ref)
        share = rows_product(att_all[...], att_low[...]).astype(BF16)
        deal(core_ref, every, slice(inner, inner + width), share, keep_ref, send_ref)
        flat = width // pieces
        blocks = inner // width
        for block in range(blocks):
            lanes = slice(inner + (block + 1) * width, inner + (block + 2) * width)
            part = hidden[:, block * width : (block + 1) * width]
            share = rows_product(part, grad_all[...]).astype(BF16)
            each = width // flat
            for below in range(each):
                piece, side = divmod(block * each + below, blocks)
                lanes = slice(inner + (side + 1) * width, inner + (side + 2) * width)
                rows = slice(piece % (pieces // 2) * flat, (piece % (pieces // 2) + 1) * flat)
                mine = core_ref[0] == 2 * piece // pieces
                some = share[below * flat : (below + 1) * flat]

                @pl.when(mine)
                def _(rows=rows, lanes=lanes, some=some):
                    keep_ref[rows, lanes] = some

                @pl.when(jnp.logical_not(mine))
                def _(rows=rows, lanes=lanes, some=some):
                    send_ref[rows, lanes] = some


def by_rows(height, width):
    return pl.BlockSpec((height, width), lambda i: (i, 0))


def constant(shape):
    return pl.BlockSpec(shape, lambda i: (0, 0))


def feed_forward(pieces, core, x, att, grad, out_w, gain, bias, in_w, in_b, down_w, down_b):
    rows, width = x.shape
    inner = in_w.shape[1]
    packed = (width // 2, 2 * inner + width)
    block = by_rows(CHUNK, width)
    return pl.pallas_call(
        functools.partial(feed_kernel, pieces),
        grid=(rows // CHUNK,),
        out_shape=(
            jax.ShapeDtypeStruct((rows, width), BF16),
            jax.ShapeDtypeStruct((rows, width), F32),
            jax.ShapeDtypeStruct((rows, width), F32),
            jax.ShapeDtypeStruct(packed, BF16),
            jax.ShapeDtypeStruct(packed, BF16),
            jax.ShapeDtypeStruct((3, width), F32),
            jax.ShapeDtypeStruct((1, inner), F32),
        ),
        in_specs=[pl.BlockSpec(memory_space=pltpu.SMEM)]
        + [block] * 3
        + [constant(a.shape) for a in (out_w, gain[None], bias[None], in_w, in_b[None], down_w)]
        + [constant((1, width))],
        out_specs=(block, block, block, constant(packed), constant(packed))
        + (constant((3, width)), constant((1, inner))),
        scratch_shapes=[
            pltpu.VMEM((rows, width), BF16),
            pltpu.VMEM((rows, inner), BF16),
            pltpu.VMEM((rows, inner), BF16),
            pltpu.VMEM((rows, width), BF16),
            pltpu.VMEM((rows, width), BF16),
            pltpu.VMEM((rows, width), BF16),
        ],
        compiler_params=pltpu.CompilerParams(vmem_limit_bytes=VMEM),
        cost_estimate=pl.CostEstimate(
            flops=rows * width * inner * 24, bytes_accessed=rows * width * 20, transcendentals=0
        ),
    )(core, x, att, grad, out_w, gain[None], bias[None], in_w, in_b[None], down_w, down_b[None])


def project_back_kernel(
    calls, core_ref, x_ref, first_ref, w_ref, gain_ref, bias_ref, mix_ref, small2_ref, wide_ref,
    *refs,
):
    grads = refs[: 3 * calls]
    result_ref, keep_ref, send_ref, normed, gathered, sums, rows_of = refs[3 * calls :]
    chunk, width = x_ref.shape
    number = pl.program_id(0)
    here = pl.ds(pl.multiple_of(number * chunk, chunk), chunk)

    @pl.when(number == 0)
    def _():
        sums[...] = jnp.zeros_like(sums)

    unit, scale = normalized(x_ref[...].astype(F32))
    normed[here, :] = (unit * gain_ref[...] + bias_ref[...]).astype(BF16)
    grad = jnp.concatenate([ref[...] for ref in grads], 1)
    gathered[here, :] = grad
    back = times_transposed(grad, w_ref[...])
    sums[0:1, :] += column_sum(back * unit)
    sums[1:2, :] += column_sum(back)
    grad_x = first_ref[...] + norm_back(back * gain_ref[...], unit, scale)
    result_ref[...] = grad_x.astype(BF16)

    @pl.when(number == pl.num_programs(0) - 1)
    def _():
        every = slice(0, width // 2)
        for at in range(0, 3 * width, width):
            lanes = slice(at, at + width)
            share = rows_product(normed[...], gathered[:, lanes]).astype(BF16)
            deal(core_ref, every, lanes, share, keep_ref, send_ref)
        rows_of[...] = jnp.zeros_like(rows_of)
        at = 0
        for ref in (sums, small2_ref, mix_ref, wide_ref):
            for row in range(ref.shape[0]):
                for lane in range(0, ref.shape[1], PAIR):
                    rows_of[at : at + 1, :] = ref[row : row + 1, lane : lane + PAIR]
                    at += 1
        exact = rows_of[...]
        high = exact.astype(BF16)
        low = (exact - high.astype(F32)).astype(BF16)
        for part, value in enumerate((high, low)):
            lanes = slice(3 * width + part * PAIR, 3 * width + (part + 1) * PAIR)
            deal(core_ref, every, lanes, value, keep_ref, send_ref)


def project_back(core, x, grad_first, weight, gain, bias, mix, small2, wide, grads):
    rows, width = x.shape
    calls = len(grads) // 3
    packed = (width // 2, 3 * width + 2 * PAIR)
    block, chunk = by_rows(CHUNK, width), by_rows(CHUNK, width // calls)
    return pl.pallas_call(
        functools.partial(project_back_kernel, calls),
        grid=(rows // CHUNK,),
        out_shape=(
            jax.ShapeDtypeStruct((rows, width), BF16),
            jax.ShapeDtypeStruct(packed, BF16),
            jax.ShapeDtypeStruct(packed, BF16),
        ),
        in_specs=[pl.BlockSpec(memory_space=pltpu.SMEM), block, block]
        + [constant(a.shape) for a in (weight, gain[None], bias[None], mix, small2, wide)]
        + [chunk] * (3 * calls),
        out_specs=(block, constant(packed), constant(packed)),
        scratch_shapes=[
            pltpu.VMEM((rows, width), BF16),
            pltpu.VMEM((rows, 3 * width), BF16),
            pltpu.VMEM((2, width), F32),
            pltpu.VMEM((width, PAIR), F32),
        ],
        compiler_params=pltpu.CompilerParams(vmem_limit_bytes=VMEM),
        cost_estimate=pl.CostEstimate(
            flops=rows * width * width * 24, bytes_accessed=rows * width * 20, transcendentals=0
        ),
    )(core, x, grad_first, weight, gain[None], bias[None], mix, small2, wide, *grads)


def to_sequences(block, axis, groups):
    return lax.all_to_all(block, axis, 0, 0, axis_index_groups=groups)


def after(value, *others):
    return lax.optimization_barrier((value,) + others)[0]


def settle_kernel(source_ref, out_ref):
    out_ref[...] = source_ref[...]


def settle(value):
    vmem = pl.BlockSpec(memory_space=pltpu.VMEM)
    return pl.pallas_call(
        settle_kernel,
        out_shape=jax.ShapeDtypeStruct(value.shape, value.dtype),
        in_specs=[vmem],
        out_specs=vmem,
        compiler_params=pltpu.CompilerParams(vmem_limit_bytes=8 * 2**20),
        cost_estimate=pl.CostEstimate(flops=0, bytes_accessed=4 * value.size, transcendentals=0),
    )(value)


def from_parts(total, axis, parts, stride, forward):
    size = lax.axis_size(axis)
    low = total.astype(BF16)
    result = jnp.zeros_like(total)
    for hop in range(1, parts):
        distance = hop * stride
        route = [
            (i, i + distance) if forward else (i + distance, i) for i in range(size - distance)
        ]
        result = result + lax.ppermute(low, axis, route).astype(F32)
    return result


class Ring:
    def __init__(self, batch, seq):
        self.batch, self.seq = batch, seq
        self.low = 2 ** ((seq.bit_length() - 1) // 2)
        self.sizes = {"core": 2, "near": batch // 2 * self.low, "far": seq // self.low}
        self.pieces = batch * seq

    def place(self, s, b):
        return {"core": b % 2, "near": b // 2 * self.low + s % self.low, "far": s // self.low}

    def device(self, place):
        s = place["far"] * self.low + place["near"] % self.low
        return s * self.batch + place["near"] // self.low * 2 + place["core"]

    def mine(self):
        return self.place(lax.axis_index("seq"), lax.axis_index("batch"))

    def swap(self, value, level, k):
        route = []
        for s in range(self.seq):
            for b in range(self.batch):
                place = self.place(s, b)
                place[level] ^= k
                route.append((s * self.batch + b, self.device(place)))
        return lax.ppermute(value, ("seq", "batch"), route)

    def scatter(self, value, level, fine=0, beside=()):
        size, me = self.sizes[level], self.mine()[level]
        value = value.reshape((size, value.shape[0] // size) + value.shape[1:])
        parts = [
            self.swap(lax.dynamic_index_in_dim(value, me ^ k, 0, False), level, k)
            for k in range(1, size)
        ]
        return self.add(lax.dynamic_index_in_dim(value, me, 0, False), parts, fine, beside)

    def scatter_cores(self, keep, send, fine=0, beside=()):
        return self.add(self.to_pieces(keep), [self.swap(self.to_pieces(send), "core", 1)], fine, beside)

    def add(self, value, parts, fine, beside):
        total = after(value, *beside).astype(F32)
        for part in parts:
            total = total + part.astype(F32)
        if not fine:
            return total.astype(BF16)
        end = total.shape[-1] - 2 * fine
        exact = total[..., end : end + fine] + total[..., end + fine :]
        high = lax.reduce_precision(exact, 8, 7)
        return jnp.concatenate([total[..., :end], high, exact - high], -1).astype(BF16)

    def gather(self, value, level, beside=()):
        parts = [self.swap(value, level, k) for k in range(1, self.sizes[level])]
        return jnp.concatenate([after(value, *beside)] + parts, 0)

    def to_pieces(self, value):
        return value.reshape(self.pieces // 2, -1, value.shape[1])

    def order(self):
        me = self.mine()
        piece = jnp.arange(self.pieces, dtype=jnp.int32)
        far, near = self.sizes["far"], self.sizes["near"]
        core = (piece // (far * near)) ^ me["core"]
        near = ((piece // far) % near) ^ me["near"]
        return (core * self.sizes["near"] + near) * far + ((piece % far) ^ me["far"])


def unpack_kernel(write, order_ref, own_ref, other_ref, *out_refs):
    half = own_ref.shape[0]
    for piece in range(2 * half):
        at = order_ref[piece]

        @pl.when(at < half)
        def _(piece=piece, at=at):
            write(piece, own_ref[at].astype(F32), out_refs)

        @pl.when(at >= half)
        def _(piece=piece, at=at):
            write(piece, other_ref[at - half].astype(F32), out_refs)


def write_feed(piece, block, out_refs):
    in_ref, out_ref, down_ref = out_refs
    size, inner, width = block.shape[0], in_ref.shape[1], in_ref.shape[0]
    rows = slice(piece * size, (piece + 1) * size)
    in_ref[rows, :] = block[:, :inner]
    out_ref[rows, :] = block[:, inner : inner + width]
    tall_rows = inner // (width // size)
    for below in range(0, tall_rows, size):
        at = inner + width + below // size * width
        down_ref[piece * tall_rows + below : piece * tall_rows + below + size, :] = block[
            :, at : at + width
        ]


def write_project(piece, block, out_refs):
    w_ref, small_ref = out_refs
    size, end = block.shape[0], w_ref.shape[1]
    rows = slice(piece * size, (piece + 1) * size)
    w_ref[rows, :] = block[:, :end]
    small_ref[rows, :] = block[:, end : end + PAIR] + block[:, end + PAIR :]


def unpack(write, order, halves, shapes):
    vmem = pl.BlockSpec(memory_space=pltpu.VMEM)
    return pl.pallas_call(
        functools.partial(unpack_kernel, write),
        out_shape=[jax.ShapeDtypeStruct(shape, F32) for shape in shapes],
        in_specs=[pl.BlockSpec(memory_space=pltpu.SMEM), vmem, vmem],
        out_specs=[vmem] * len(shapes),
        compiler_params=pltpu.CompilerParams(vmem_limit_bytes=VMEM),
        cost_estimate=pl.CostEstimate(
            flops=0, bytes_accessed=8 * halves[0].size, transcendentals=0
        ),
    )(order, *halves)


def local(
    inputs,
    cotangent,
    lengths,
    norm1_gain,
    norm1_bias,
    qkv_weight,
    blend_weights,
    out_weight,
    norm2_gain,
    norm2_bias,
    in_weight,
    in_bias,
    down_weight,
    down_bias,
):
    seqs, span, width = inputs.shape
    heads = blend_weights.shape[1]
    devices = lax.axis_size("seq")
    parts = devices // seqs
    rows = seqs * span
    index = lax.axis_index("seq")
    groups = None
    if parts > 1:
        groups = [[r * seqs + s for s in range(seqs)] for r in range(parts)]
    mine, part = index % seqs, index // seqs
    meta = jnp.stack([lax.dynamic_index_in_dim(lengths, mine, 0, False), part * rows])
    blend = jnp.repeat(blend_weights, width // heads, axis=1)

    ring = Ring(lax.axis_size("batch"), devices)
    by_ring = width % (16 * ring.pieces) == 0
    inner = in_weight.shape[1]

    x = to_sequences(inputs, "seq", groups).reshape(rows, width)
    grad_out = to_sequences(cotangent, "seq", groups).reshape(rows, width)

    normed = layer_norm(x.astype(F32), norm1_gain, norm1_bias).astype(BF16)
    qkv = times(normed, qkv_weight).astype(BF16)
    halo = jnp.zeros((TILE, 2 * width), BF16)
    state = jnp.zeros((2, width // PAIR, PAIR, 2 * PAIR), F32)
    later = state
    if parts > 1:
        onward = [(i, i + seqs) for i in range(devices - seqs)]
        halo = lax.ppermute(qkv[rows - TILE :, width:], "seq", onward)
        total = attend(meta, blend, qkv, halo, state)[1]
        state = from_parts(total, "seq", parts, seqs, True)
    attended = attend(meta, blend, qkv, halo, state)[0]

    core = (lax.axis_index("batch") % 2)[None] if by_ring else jnp.zeros(1, jnp.int32)
    result, grad_first, grad_o, feed_keep, feed_send, small2, grad_in_b = feed_forward(
        ring.pieces if by_ring else 16,
        core, x, attended, grad_out, out_weight, norm2_gain, norm2_bias,
        in_weight, in_bias, down_weight, down_bias,
    )
    output = to_sequences(result.reshape(seqs, span, width), "seq", groups)
    def unpack_feed(order, halves):
        shapes = [(width, inner), (width, width), (inner, width)]
        return unpack(write_feed, order, halves, shapes)

    calls = 4

    def back(meta, number, later):
        return attend_back(meta, blend, qkv, halo, state, later, grad_o, calls, number)

    if parts > 1:
        total = jnp.concatenate([back(meta, number, later)[6] for number in range(calls)], 1)
        later = from_parts(total, "seq", parts, seqs, False)
    backs, turn = [], meta
    if by_ring:
        held = None
        for number in range(calls):
            if number == 1:
                held = ring.scatter_cores(feed_keep, feed_send)
                turn = after(turn, held)
            if number == 3:
                held = ring.scatter(held, "near")
                turn = after(turn, held)
            backs.append(back(turn, number, later))
            turn = after(turn, backs[-1][5])
        held = ring.scatter(held, "far")
        output = settle(after(output, backs[1][5]))
        grad_first = after(grad_first, held, output)
    else:
        backs = [back(meta, number, later) for number in range(calls)]
    grads = [[call[part] for call in backs] for part in range(3)]
    if parts > 1:
        homeward = [(i + seqs, i) for i in range(devices - seqs)]
        for part in (1, 2):
            for number in range(calls):
                received = lax.ppermute(backs[number][part + 2], "seq", homeward)
                grad = grads[part][number]
                tail = grad[rows - TILE :].astype(F32) + received.astype(F32)
                grads[part][number] = grad.at[rows - TILE :].set(tail.astype(BF16))
    mix = jnp.concatenate([call[5] for call in backs], 1)
    grad_x, project_keep, project_send = project_back(
        core, x, grad_first, qkv_weight, norm1_gain, norm1_bias, mix, small2, grad_in_b,
        grads[0] + grads[1] + grads[2],
    )
    if by_ring:
        order = ring.order()
        late = ring.scatter_cores(project_keep, project_send, PAIR)
        moved = to_sequences(after(grad_x, late).reshape(seqs, span, width), "seq", groups)
        held = ring.gather(held, "far")
        late = after(ring.scatter(late, "near", PAIR), moved)
        held = ring.gather(held, "near", (late,))
        other = ring.swap(held, "core", 1)
        late = ring.scatter(late, "far", PAIR, (held,))
        grad_in_w, grad_out_w, grad_down_w = unpack_feed(order, (held, after(other, late)))
        late = ring.gather(late, "far", (grad_out_w,))
        input_grad = settle(after(moved, late))
        late = ring.gather(late, "near", (input_grad,))
        project_halves = late, ring.swap(late, "core", 1)
    else:
        input_grad = to_sequences(grad_x.reshape(seqs, span, width), "seq", groups)
        order = jnp.arange(16, dtype=jnp.int32)
        halves = (feed_keep, feed_send, project_keep, project_send)
        halves = lax.psum([half.astype(F32) for half in halves], ("seq", "batch"))
        halves = [half.reshape(8, width // 16, -1) for half in halves]
        feed_halves, project_halves = halves[:2], halves[2:]
        grad_in_w, grad_out_w, grad_down_w = unpack_feed(order, feed_halves)
    grad_qkv_w, small = unpack(
        write_project, order, project_halves, [(width, 3 * width), (width, PAIR)]
    )
    vectors = small.reshape(-1)
    vector = [vectors[at : at + width] for at in range(0, 8 * width, width)]
    grad_blend = vectors[5 * width : 8 * width].reshape(3, heads, width // heads).sum(-1)
    return (
        output,
        input_grad,
        vector[0],
        vector[1],
        grad_qkv_w,
        grad_blend,
        grad_out_w,
        vector[2],
        vector[3],
        grad_in_w,
        vectors[8 * width : 8 * width + inner],
        grad_down_w,
        vector[4],
    )


def solution(mesh):
    rows = P("batch", "seq", None)
    return jax.shard_map(
        local,
        mesh=mesh,
        in_specs=(rows, rows, P("batch")) + (P(),) * 11,
        out_specs=(rows, rows) + (P(),) * 11,
        check_vma=False,
    )
```

```python
import functools

import jax
import jax.numpy as jnp
from jax import lax
from jax.experimental import pallas as pl
from jax.experimental.pallas import tpu as pltpu
from jax.sharding import PartitionSpec as P

WINDOW = 30
HEAD = 64
PAIR = 2 * HEAD
TILE = 64
EPS = 1e-05
NEG = -1e30
VMEM = 58 * 2**20
BRIEF = pl.CostEstimate(flops=1000, bytes_accessed=1000, transcendentals=0)
BF16 = jnp.bfloat16
F32 = jnp.float32


def layer_norm(field, gain, shift):
    center = field - jnp.mean(field, axis=-1, keepdims=True)
    spread = jnp.mean(center * center, axis=-1, keepdims=True)
    return center * lax.rsqrt(spread + EPS) * gain + shift


def rows_product(left, right):
    return lax.dot_general(
        left, right, (((0,), (0,)), ((), ())), preferred_element_type=F32
    )


def times_transposed(left, right):
    return lax.dot_general(
        left, right, (((1,), (1,)), ((), ())), preferred_element_type=F32
    )


def times(left, right):
    return lax.dot_general(
        left, right, (((1,), (0,)), ((), ())), preferred_element_type=F32
    )


def elu_feature(field):
    return jnp.where(field > 0, field + 1.0, jnp.exp(jnp.minimum(field, 0.0)))


def tanh_feature(field):
    return 1.0 + jnp.tanh(field)


def pair_lanes(p, part=0, width=PAIR):
    return slice(p * width + part * PAIR, p * width + (part + 1) * PAIR)


def store_split(ref, index, rows, block):
    lane = lax.broadcasted_iota(jnp.int32, (block.shape[0], PAIR), 1)
    for p in range(block.shape[1] // PAIR):
        pair = block[:, pair_lanes(p)]
        for h in range(2):
            mine = (lane < HEAD) if h == 0 else (lane >= HEAD)
            ref[index + (rows, pair_lanes(p, h, 2 * PAIR))] = jnp.where(mine, pair, 0.0).astype(
                BF16
            )


def load_split(ref, index, rows, p):
    return jnp.concatenate([ref[index + (rows, pair_lanes(p, h, 2 * PAIR))] for h in range(2)], 0)


def tall(block):
    return jnp.concatenate([block[:, :PAIR], block[:, PAIR:]], 0)


def fill_features(meta_ref, q_ref, k_ref, v_ref, halo_k, halo_v, keys, values, fq, fk, split):
    rows, width = q_ref.shape
    chunk = 2 * TILE
    front = pl.ds(0, TILE)
    keys[front, :] = jnp.zeros((TILE, 2 * width), BF16)
    values[front, :] = jnp.zeros((TILE, 2 * width), BF16)
    fk[:, front, :] = jnp.zeros((2, TILE, 2 * width), BF16)
    if halo_k is not None:
        store_split(keys, (), front, halo_k[...].astype(F32) * 0.125)
        store_split(values, (), front, halo_v[...].astype(F32))

    def fill(step, carry):
        at = pl.multiple_of(step * chunk, chunk)
        here, there = pl.ds(at, chunk), pl.ds(at + TILE, chunk)
        q = q_ref[here, :].astype(F32)
        k = k_ref[here, :].astype(F32)
        store_split(keys, (), there, k * 0.125)
        store_split(values, (), there, v_ref[here, :].astype(F32))
        position = meta_ref[1] + at + lax.broadcasted_iota(jnp.int32, (chunk, width), 0)
        valid = position < meta_ref[0]
        for c, feature in enumerate((elu_feature, tanh_feature)):
            if split:
                store_split(fq, (c,), here, feature(q))
            else:
                fq[c, here, :] = feature(q).astype(BF16)
            store_split(fk, (c,), there, jnp.where(valid, feature(k), 0.0))
        return carry

    lax.fori_loop(0, rows // chunk, fill, 0)


def tile_masks(meta_ref, tile):
    shape = (TILE, 2 * PAIR)
    row = lax.broadcasted_iota(jnp.int32, shape, 0)
    lane = lax.broadcasted_iota(jnp.int32, shape, 1) % PAIR
    back = row + TILE - lane
    key = meta_ref[1] + (tile - 1) * TILE + lane
    known = (key >= 0) & (key < meta_ref[0])
    near = (back >= 0) & (back <= WINDOW) & (known | (back == 0))
    return near, back >= 0


def softmax_pair(scores):
    halves = []
    for h in range(2):
        part = scores[:, h * PAIR : (h + 1) * PAIR]
        part = jnp.exp(part - jnp.max(part, axis=1, keepdims=True))
        halves.append(part * (1.0 / jnp.sum(part, axis=1, keepdims=True)))
    return jnp.concatenate(halves, 1)


def tile_constants():
    row = lax.broadcasted_iota(jnp.int32, (2 * PAIR, PAIR), 0)
    lane = lax.broadcasted_iota(jnp.int32, (2 * PAIR, PAIR), 1)
    ones = jnp.where(row // PAIR == lane // HEAD, 1.0, 0.0).astype(BF16)
    row = lax.broadcasted_iota(jnp.int32, (PAIR, 2 * PAIR), 0)
    lane = lax.broadcasted_iota(jnp.int32, (PAIR, 2 * PAIR), 1)
    return ones, row // HEAD == (lane % PAIR) // HEAD


def whole(split):
    half = split.shape[0] // 2
    return split[:half] + split[half:]


def state_share(block, fks, vs):
    ones = jnp.ones((TILE, PAIR), BF16)
    share = rows_product(whole(fks), jnp.concatenate([whole(vs), ones], 1))
    return jnp.where(block, share, 0.0)


def attend_kernel(
    together, whole_sequence, meta_ref, blend_ref, q_ref, k_ref, v_ref, *refs
):
    halo_k, halo_v, state_ref = (None,) * 3 if whole_sequence else refs[:3]
    att_ref, total_ref, keys, values, fq, fk, state = refs[-7:]
    rows, width = q_ref.shape
    pairs = range(width // PAIR)
    near_by = range(together)
    units = [(s, p) for s in near_by for p in pairs]
    fill_features(meta_ref, q_ref, k_ref, v_ref, halo_k, halo_v, keys, values, fq, fk, False)
    state[...] = jnp.zeros_like(state) if whole_sequence else state_ref[...]
    ones, block = tile_constants()

    def step(number, carry):
        first = number * together
        at = pl.multiple_of(first * TILE, TILE)
        here = [pl.ds(at + s * TILE, TILE) for s in near_by]
        window = [pl.ds(at + s * TILE, 2 * TILE) for s in near_by]
        masks = [tile_masks(meta_ref, first + s) for s in near_by]
        q = {(s, p): q_ref[here[s], pair_lanes(p)] for s, p in units}
        feats = {(s, p): [fq[c, here[s], pair_lanes(p)] for c in range(2)] for s, p in units}
        ks = {(s, p): load_split(keys, (), window[s], p) for s, p in units}
        fks = {(s, p): [load_split(fk, (c,), window[s], p) for c in range(2)] for s, p in units}
        wide = {
            (s, p): jnp.concatenate([load_split(values, (), window[s], p), ones], 1)
            for s, p in units
        }
        held = {(0, p): [state[c, p] for c in range(2)] for p in pairs}
        for s, p in units:
            vs = load_split(values, (), here[s], p)
            held[s + 1, p] = [
                held[s, p][c] + state_share(block, load_split(fk, (c,), here[s], p), vs)
                for c in range(2)
            ]
        near = {u: times_transposed(q[u], ks[u]) for u in units}
        far = {u: [times_transposed(feats[u][c], fks[u][c]) for c in range(2)] for u in units}
        old = {u: [times(feats[u][c], held[u][c].astype(BF16)) for c in range(2)] for u in units}
        near = {u: softmax_pair(jnp.where(masks[u[0]][0], near[u], NEG)) for u in units}
        far = {u: [jnp.where(masks[u[0]][1], f, 0.0) for f in far[u]] for u in units}
        stack = {u: jnp.concatenate([near[u]] + far[u], 0).astype(BF16) for u in units}
        sums = {u: times(stack[u], wide[u]) for u in units}
        for s, p in units:
            u, lanes = (s, p), pair_lanes(p)
            mixed = blend_ref[0:1, lanes] * sums[u][:TILE, :PAIR]
            for c in range(2):
                mine = sums[u][(c + 1) * TILE : (c + 2) * TILE] + old[u][c]
                mixed = mixed + blend_ref[c + 1 : c + 2, lanes] * (
                    mine[:, :PAIR] / mine[:, PAIR:]
                )
            att_ref[here[s], lanes] = mixed.astype(BF16)
        for p in pairs:
            for c in range(2):
                state[c, p] = held[together, p][c]
        return carry

    lax.fori_loop(0, rows // (together * TILE), step, 0)
    last = pl.ds(rows, TILE)
    for p in pairs:
        for c in range(2):
            total_ref[c, p] = state[c, p] + state_share(
                block, load_split(fk, (c,), last, p), load_split(values, (), last, p)
            )


def slopes_of(field):
    small = jnp.exp(jnp.minimum(field, 0.0))
    bent = jnp.tanh(field)
    return [jnp.where(field > 0, 1.0, small), 1.0 - bent * bent]


def split_heads(block):
    lane = lax.broadcasted_iota(jnp.int32, block.shape, 1)
    zero = jnp.zeros_like(block)
    return jnp.concatenate(
        [jnp.where(lane < HEAD, block, zero), jnp.where(lane < HEAD, zero, block)], 0
    )


def attend_back_kernel(
    together, whole_sequence, meta_ref, blend_ref, q_ref, k_ref, v_ref, go_ref, *refs
):
    halo_k, halo_v, state_ref, later_ref = (None,) * 4 if whole_sequence else refs[:4]
    gq_ref, gk_ref, gv_ref, hk_ref, hv_ref, mix_ref, total_ref = refs[-16:-9]
    keys, values, fq, fk, state, gk, gv, gfk, gon = refs[-9:]
    rows, width = q_ref.shape
    pairs = range(width // PAIR)
    tiles = rows // TILE
    near_by = range(together)
    units = [(s, p) for s in near_by for p in pairs]
    fill_features(meta_ref, q_ref, k_ref, v_ref, halo_k, halo_v, keys, values, fq, fk, True)
    state[...] = jnp.zeros_like(state) if whole_sequence else state_ref[...]
    mix_ref[...] = jnp.zeros_like(mix_ref)
    gk[:TILE, :] = jnp.zeros((TILE, width), F32)
    gv[:TILE, :] = jnp.zeros((TILE, width), F32)
    gfk[:, :TILE, :] = jnp.zeros((2, TILE, width), F32)
    ones, block = tile_constants()
    row = lax.broadcasted_iota(jnp.int32, (2 * PAIR, PAIR), 0) % PAIR
    lane = lax.broadcasted_iota(jnp.int32, (2 * PAIR, PAIR), 1)
    heads = jnp.where(row // HEAD == lane // HEAD, 1.0, 0.0).astype(BF16)
    plain_ones = jnp.ones((TILE, PAIR), BF16)
    high = (lax.broadcasted_iota(jnp.int32, (TILE, PAIR), 1) % HEAD) < HEAD // 2

    def step(number, carry):
        first = number * together
        at = pl.multiple_of(first * TILE, TILE)
        here = [pl.ds(at + s * TILE, TILE) for s in range(together + 1)]
        window = [pl.ds(at + s * TILE, 2 * TILE) for s in near_by]
        masks = [tile_masks(meta_ref, first + s) for s in near_by]
        q = {(s, p): q_ref[here[s], pair_lanes(p)] for s, p in units}
        go = {(s, p): go_ref[here[s], pair_lanes(p)] for s, p in units}
        blend = [[blend_ref[c : c + 1, pair_lanes(p)] for c in range(3)] for p in pairs]
        fqs = {(s, p): [load_split(fq, (c,), here[s], p) for c in range(2)] for s, p in units}
        feats = {u: [whole(f) for f in fqs[u]] for u in units}
        ks = {(s, p): load_split(keys, (), window[s], p) for s, p in units}
        fks = {(s, p): [load_split(fk, (c,), window[s], p) for c in range(2)] for s, p in units}
        wide = {
            (s, p): jnp.concatenate([load_split(values, (), window[s], p), ones], 1)
            for s, p in units
        }
        held = {(0, p): [state[c, p] for c in range(2)] for p in pairs}
        for s, p in units:
            vs = load_split(values, (), here[s], p)
            held[s + 1, p] = [
                held[s, p][c] + state_share(block, load_split(fk, (c,), here[s], p), vs)
                for c in range(2)
            ]
        past = {u: [h.astype(BF16) for h in held[u]] for u in units}
        old_k = [gk[here[0], pair_lanes(p)] for p in pairs]
        old_v = [gv[here[0], pair_lanes(p)] for p in pairs]
        old_f = [[gfk[c, here[0], pair_lanes(p)] for c in range(2)] for p in pairs]

        near = {u: times_transposed(q[u], ks[u]) for u in units}
        far = {u: [times_transposed(feats[u][c], fks[u][c]) for c in range(2)] for u in units}
        old = {u: [times(feats[u][c], past[u][c]) for c in range(2)] for u in units}
        near = {u: softmax_pair(jnp.where(masks[u[0]][0], near[u], NEG)) for u in units}
        far = {u: [jnp.where(masks[u[0]][1], f, 0.0).astype(BF16) for f in far[u]] for u in units}
        stack = {u: jnp.concatenate([near[u].astype(BF16)] + far[u], 0) for u in units}
        sums = {u: times(stack[u], wide[u]) for u in units}
        scales, prods = {}, {}
        for u in units:
            outs = [sums[u][:TILE, :PAIR]]
            scales[u] = [jnp.broadcast_to(blend[u[1]][0], (TILE, PAIR))]
            for c in range(2):
                mine = sums[u][(c + 1) * TILE : (c + 2) * TILE] + old[u][c]
                inverse = 1.0 / mine[:, PAIR:]
                outs.append(mine[:, :PAIR] * inverse)
                scales[u].append(blend[u[1]][c + 1] * inverse)
            prods[u] = jnp.concatenate([go[u] * out for out in outs], 0)
        deltas = {}
        for u in units:
            low = prods[u].astype(BF16)
            rest = (prods[u] - low.astype(F32)).astype(BF16)
            deltas[u] = times(jnp.concatenate([low, rest], 1), heads)
        grads = {}
        for u in units:
            grads[u] = []
            for c in range(3):
                delta = scales[u][c] * deltas[u][c * TILE : (c + 1) * TILE] * (-2.0 / HEAD)
                delta_low = delta.astype(BF16).astype(F32)
                delta = jnp.where(high, delta_low, delta - delta_low)
                grads[u].append(jnp.concatenate([scales[u][c] * go[u], delta], 1).astype(BF16))
        back = {u: times_transposed(jnp.concatenate(grads[u], 0), wide[u]) for u in units}
        late = {u: [times_transposed(grads[u][c + 1], past[u][c]) for c in range(2)] for u in units}
        ds = {u: (near[u] * back[u][:TILE]).astype(BF16) for u in units}
        gas = {
            u: [
                jnp.where(masks[u[0]][1], back[u][(c + 1) * TILE : (c + 2) * TILE], 0.0).astype(BF16)
                for c in range(2)
            ]
            for u in units
        }
        gq_near = {u: times(ds[u], ks[u]) for u in units}
        gq_far = {u: [times(gas[u][c], fks[u][c]) + late[u][c] for c in range(2)] for u in units}
        new_k = {u: rows_product(tall(ds[u]), split_heads(q[u] * 0.125)) for u in units}
        new_f = {u: [rows_product(tall(gas[u][c]), fqs[u][c]) for c in range(2)] for u in units}
        new_v = {
            u: rows_product(
                jnp.concatenate([tall(stack[u][c * TILE : (c + 1) * TILE]) for c in range(3)], 0),
                jnp.concatenate([split_heads(g[:, :PAIR]) for g in grads[u]], 0),
            )
            for u in units
        }

        def overlap(old, new, p):
            parts = [old + new(0, p)[:TILE]]
            parts += [new(s, p)[TILE:] + new(s + 1, p)[:TILE] for s in range(together - 1)]
            return parts + [new(together - 1, p)[TILE:]]

        for s, p in units:
            u, lanes = (s, p), pair_lanes(p)
            slopes = slopes_of(q[u].astype(F32))
            gq = gq_near[u] + slopes[0] * gq_far[u][0] + slopes[1] * gq_far[u][1]
            gq_ref[here[s], lanes] = gq.astype(BF16)
            for c in range(2):
                gon[c, here[s], p * 2 * PAIR : (p + 1) * 2 * PAIR] = grads[u][c + 1]
        for p in pairs:
            lanes = pair_lanes(p)
            for c in range(3):
                mix_ref[c : c + 1, lanes] += sum(
                    jnp.sum(prods[s, p][c * TILE : (c + 1) * TILE], axis=0, keepdims=True)
                    for s in near_by
                )
            for rows_at, part in zip(here, overlap(old_k[p], lambda s, p: new_k[s, p], p)):
                gk[rows_at, lanes] = part
            for rows_at, part in zip(here, overlap(old_v[p], lambda s, p: new_v[s, p], p)):
                gv[rows_at, lanes] = part
            for c in range(2):
                parts = overlap(old_f[p][c], lambda s, p: new_f[s, p][c], p)
                for rows_at, part in zip(here, parts):
                    gfk[c, rows_at, lanes] = part
                state[c, p] = held[together, p][c]
        return carry

    lax.fori_loop(0, tiles // together, step, 0)
    hk_ref[...] = gk[:TILE, :].astype(BF16)
    hv_ref[...] = gv[:TILE, :].astype(BF16)
    state[...] = jnp.zeros_like(state) if whole_sequence else later_ref[...]

    def come(at, c, p):
        here = pl.ds(at, TILE)
        grads = gon[c, here, p * 2 * PAIR : (p + 1) * 2 * PAIR]
        share = rows_product(whole(load_split(fq, (c,), here, p)), grads)
        return jnp.where(block, share, 0.0)

    def back_step(number, carry):
        first = tiles - 1 - number * together
        at = [pl.multiple_of((first - s) * TILE, TILE) for s in near_by]
        here = [pl.ds(a, TILE) for a in at]
        there = [pl.ds(a + TILE, TILE) for a in at]
        held = {(-1, p): [state[c, p] for c in range(2)] for p in pairs}
        for s, p in units:
            tile = first - s + 2
            nearer = pl.multiple_of(jnp.minimum(tile, tiles - 1) * TILE, TILE)
            held[s, p] = [
                held[s - 1, p][c] + jnp.where(tile < tiles, come(nearer, c, p), 0.0)
                for c in range(2)
            ]
        later = {u: [h.astype(BF16) for h in held[u]] for u in units}
        vs = {(s, p): whole(load_split(values, (), there[s], p)) for s, p in units}
        fks = {
            (s, p): jnp.concatenate([whole(load_split(fk, (c,), there[s], p)) for c in range(2)], 1)
            for s, p in units
        }
        wide = {u: jnp.concatenate([vs[u], plain_ones], 1) for u in units}
        far_k = {u: [times_transposed(wide[u], later[u][c]) for c in range(2)] for u in units}
        far_v = {
            u: times(fks[u], jnp.concatenate([g[:, :PAIR] for g in later[u]], 0)) for u in units
        }
        for s, p in units:
            u, lanes = (s, p), pair_lanes(p)
            position = meta_ref[1] + at[s] + lax.broadcasted_iota(jnp.int32, (TILE, PAIR), 0)
            slopes = slopes_of(k_ref[here[s], lanes].astype(F32))
            grad_f = [gfk[c, there[s], lanes] + far_k[u][c] for c in range(2)]
            bent = slopes[0] * grad_f[0] + slopes[1] * grad_f[1]
            grad_k = gk[there[s], lanes] + jnp.where(position < meta_ref[0], bent, 0.0)
            gk_ref[here[s], lanes] = grad_k.astype(BF16)
            gv_ref[here[s], lanes] = (gv[there[s], lanes] + far_v[u]).astype(BF16)
        for p in pairs:
            for c in range(2):
                state[c, p] = held[together - 1, p][c]
        return carry

    lax.fori_loop(0, tiles // together, back_step, 0)
    for p in pairs:
        for c in range(2):
            total_ref[c, p] = state[c, p] + come(0, c, p) + come(TILE, c, p)


def attention_specs(rows, width, lanes, number):
    calls = width // lanes

    def columns(height, part):
        return pl.BlockSpec((height, lanes), lambda i: (0, part * calls + number(i)))

    state = pl.BlockSpec(
        (2, lanes // PAIR, PAIR, 2 * PAIR), lambda i: (0, number(i), 0, 0)
    )
    ins = [pl.BlockSpec(memory_space=pltpu.SMEM), columns(3, 0)]
    ins += [columns(rows, part) for part in range(3)]
    return columns, ins, [columns(TILE, part) for part in range(2)] + [state]


def attention_scratch(rows, lanes, split):
    return [
        pltpu.VMEM((rows + TILE, 2 * lanes), BF16),
        pltpu.VMEM((rows + TILE, 2 * lanes), BF16),
        pltpu.VMEM((2, rows, (2 if split else 1) * lanes), BF16),
        pltpu.VMEM((2, rows + TILE, 2 * lanes), BF16),
        pltpu.VMEM((2, lanes // PAIR, PAIR, 2 * PAIR), F32),
    ]


def outcome(shape, dtype):
    return jax.ShapeDtypeStruct(shape, dtype), pl.BlockSpec(shape, lambda _: (0,) * len(shape))


UNITS = 8


def attend(meta, blend, qkv, halo, state):
    rows, width = qkv.shape[0], qkv.shape[1] // 3
    lanes = PAIR
    columns, ins, before = attention_specs(rows, width, lanes, lambda i: i)
    held = before[-1]
    share = (2, width // PAIR, PAIR, 2 * PAIR)
    earlier = () if state is None else (halo, halo, state)
    return pl.pallas_call(
        functools.partial(attend_kernel, UNITS * PAIR // lanes, state is None),
        grid=(width // lanes,),
        out_shape=(
            jax.ShapeDtypeStruct((rows, width), BF16),
            jax.ShapeDtypeStruct(share, F32),
        ),
        in_specs=ins + before[: len(earlier)],
        out_specs=(columns(rows, 0), held),
        scratch_shapes=attention_scratch(rows, lanes, False),
        compiler_params=pltpu.CompilerParams(vmem_limit_bytes=VMEM),
        cost_estimate=BRIEF,
    )(meta, blend, qkv, qkv, qkv, *earlier)


def attend_back(meta, blend, qkv, halo, state, later, go, calls, number):
    rows, width = qkv.shape[0], qkv.shape[1] // 3
    lanes = width // calls
    columns, ins, before = attention_specs(rows, width, lanes, lambda i: number)
    others = () if state is None else (halo, halo, state, later)
    shapes, blocks = zip(
        *[outcome((rows, lanes), BF16)] * 3,
        *[outcome((TILE, lanes), BF16)] * 2,
        outcome((3, lanes), F32),
        outcome((2, lanes // PAIR, PAIR, 2 * PAIR), F32),
    )
    return pl.pallas_call(
        functools.partial(attend_back_kernel, UNITS * PAIR // lanes, state is None),
        grid=(1,),
        out_shape=shapes,
        in_specs=ins + [columns(rows, 0)] + (before + before[-1:])[: len(others)],
        out_specs=blocks,
        scratch_shapes=attention_scratch(rows, lanes, True)
        + [
            pltpu.VMEM((rows + TILE, lanes), F32),
            pltpu.VMEM((rows + TILE, lanes), F32),
            pltpu.VMEM((2, rows + TILE, lanes), F32),
            pltpu.VMEM((2, rows, 2 * lanes), BF16),
        ],
        compiler_params=pltpu.CompilerParams(vmem_limit_bytes=VMEM),
        cost_estimate=BRIEF,
    )(meta, blend, qkv, qkv, qkv, go, *others)


CHUNK = 512
GELU_A, GELU_B = 0.7978845608028654, 0.044715


def normalized(field):
    center = field - jnp.mean(field, axis=-1, keepdims=True)
    scale = lax.rsqrt(jnp.mean(center * center, axis=-1, keepdims=True) + EPS)
    return center * scale, scale


def norm_back(grad, unit, scale):
    shared = jnp.mean(grad * unit, axis=-1, keepdims=True)
    return scale * (grad - jnp.mean(grad, axis=-1, keepdims=True) - unit * shared)


def gelu_pair(field):
    square = field * field
    bent = jnp.tanh(GELU_A * field * (1.0 + GELU_B * square))
    half = 0.5 + 0.5 * bent
    slope = half + 0.5 * field * (1.0 - bent * bent) * (GELU_A + 3.0 * GELU_A * GELU_B * square)
    return field * half, slope


def column_sum(block):
    return jnp.sum(block, axis=0, keepdims=True)


def deal(core_ref, rows, lanes, value, keep_ref, send_ref):
    half = value.shape[0] // 2

    @pl.when(core_ref[0] == 0)
    def _():
        keep_ref[rows, lanes] = value[:half]
        send_ref[rows, lanes] = value[half:]

    @pl.when(core_ref[0] != 0)
    def _():
        keep_ref[rows, lanes] = value[half:]
        send_ref[rows, lanes] = value[:half]


def feed_kernel(
    pieces, core_ref, x_ref, att_ref, grad_ref, out_from, gain_ref, bias_ref, in_from, in_b,
    down_from, down_b, result_ref, first_ref, go_ref, keep_to, send_to, small_ref, wide_ref,
    second, hidden, pre_low, att_low, att_all, grad_all, out_w, in_w, down_w, keep_ref, send_ref,
    in_sems, out_sems,
):
    chunk, width = x_ref.shape
    inner = in_w.shape[1]
    number = pl.program_id(0)
    here = pl.ds(pl.multiple_of(number * chunk, chunk), chunk)
    tiles = [slice(at, at + width) for at in range(0, inner, width)]
    copies = [pltpu.make_async_copy(out_from, out_w, in_sems.at[0])]
    for i, lanes in enumerate(tiles):
        copies += [
            pltpu.make_async_copy(in_from.at[:, lanes], in_w.at[:, lanes], in_sems.at[2 * i + 1]),
            pltpu.make_async_copy(down_from.at[lanes, :], down_w.at[lanes, :], in_sems.at[2 * i + 2]),
        ]

    def arrived(i):
        @pl.when(number == 0)
        def _():
            copies[i].wait()

    @pl.when(number == 0)
    def _():
        for copy in copies:
            copy.start()
        small_ref[...] = jnp.zeros_like(small_ref)
        wide_ref[...] = jnp.zeros_like(wide_ref)

    att = att_ref[...]
    att_all[here, :] = att
    arrived(0)
    first = x_ref[...].astype(F32) + times(att, out_w[...])
    unit, scale = normalized(first)
    low = (unit * gain_ref[...] + bias_ref[...]).astype(BF16)
    second[here, :] = low
    grad = grad_ref[...]
    grad_all[here, :] = grad
    grad_f = grad.astype(F32)
    result = first + down_b[...]
    back = jnp.zeros((chunk, width), F32)
    for i, lanes in enumerate(tiles):
        arrived(2 * i + 1)
        arrived(2 * i + 2)
        act, slope = gelu_pair(times(low, in_w[:, lanes]) + in_b[:, lanes])
        act = act.astype(BF16)
        hidden[here, lanes] = act
        result = result + times(act, down_w[lanes, :])
        pre = (times_transposed(grad, down_w[lanes, :]) * slope).astype(BF16)
        pre_low[here, lanes] = pre
        wide_ref[:, lanes] += column_sum(pre.astype(F32))
        back = back + times_transposed(pre, in_w[:, lanes])
    result_ref[...] = result.astype(BF16)
    small_ref[0:1, :] += column_sum(back * unit)
    small_ref[1:2, :] += column_sum(back)
    small_ref[2:3, :] += column_sum(grad_f)
    grad_first = grad_f + norm_back(back * gain_ref[...], unit, scale)
    first_ref[...] = grad_first
    grad_att = grad_first.astype(BF16)
    att_low[here, :] = grad_att
    go_ref[...] = times_transposed(grad_att, out_w[...])

    @pl.when(number == pl.num_programs(0) - 1)
    def _():
        every = slice(0, width // 2)
        leaving = []

        def leave(lanes):
            for here, there in ((keep_ref, keep_to), (send_ref, send_to)):
                sem = out_sems.at[len(leaving)]
                copy = pltpu.make_async_copy(here.at[:, lanes], there.at[:, lanes], sem)
                copy.start()
                leaving.append(copy)

        flat, each, after_out = width // pieces, pieces, inner + width
        for block, lanes in enumerate(tiles):
            share = rows_product(hidden[:, lanes], grad_all[...]).astype(BF16)
            for below in range(each):
                piece, side = divmod(block * each + below, len(tiles))
                to = slice(after_out + side * width, after_out + (side + 1) * width)
                rows = slice(piece % (pieces // 2) * flat, (piece % (pieces // 2) + 1) * flat)
                mine = core_ref[0] == 2 * piece // pieces
                some = share[below * flat : (below + 1) * flat]

                @pl.when(mine)
                def _(rows=rows, to=to, some=some):
                    keep_ref[rows, to] = some

                @pl.when(jnp.logical_not(mine))
                def _(rows=rows, to=to, some=some):
                    send_ref[rows, to] = some

        leave(slice(after_out, after_out + inner))
        for lanes in tiles:
            share = rows_product(second[...], pre_low[:, lanes]).astype(BF16)
            deal(core_ref, every, lanes, share, keep_ref, send_ref)
            leave(lanes)
        share = rows_product(att_all[...], att_low[...]).astype(BF16)
        deal(core_ref, every, slice(inner, after_out), share, keep_ref, send_ref)
        leave(slice(inner, after_out))
        for copy in leaving:
            copy.wait()


def by_rows(height, width):
    return pl.BlockSpec((height, width), lambda i: (i, 0))


def constant(shape):
    return pl.BlockSpec(shape, lambda i: (0, 0))


def feed_forward(pieces, core, x, att, grad, out_w, gain, bias, in_w, in_b, down_w, down_b):
    rows, width = x.shape
    inner = in_w.shape[1]
    packed = (width // 2, 2 * inner + width)
    block, far = by_rows(CHUNK, width), pl.BlockSpec(memory_space=pl.ANY)
    return pl.pallas_call(
        functools.partial(feed_kernel, pieces),
        grid=(rows // CHUNK,),
        out_shape=(
            jax.ShapeDtypeStruct((rows, width), BF16),
            jax.ShapeDtypeStruct((rows, width), F32),
            jax.ShapeDtypeStruct((rows, width), F32),
            jax.ShapeDtypeStruct(packed, BF16),
            jax.ShapeDtypeStruct(packed, BF16),
            jax.ShapeDtypeStruct((3, width), F32),
            jax.ShapeDtypeStruct((1, inner), F32),
        ),
        in_specs=[pl.BlockSpec(memory_space=pltpu.SMEM)]
        + [block] * 3
        + [far, constant((1, width)), constant((1, width)), far, constant((1, inner)), far]
        + [constant((1, width))],
        out_specs=(block, block, block, far, far)
        + (constant((3, width)), constant((1, inner))),
        scratch_shapes=[
            pltpu.VMEM((rows, width), BF16),
            pltpu.VMEM((rows, inner), BF16),
            pltpu.VMEM((rows, inner), BF16),
            pltpu.VMEM((rows, width), BF16),
            pltpu.VMEM((rows, width), BF16),
            pltpu.VMEM((rows, width), BF16),
            pltpu.VMEM(out_w.shape, BF16),
            pltpu.VMEM(in_w.shape, BF16),
            pltpu.VMEM(down_w.shape, BF16),
            pltpu.VMEM(packed, BF16),
            pltpu.VMEM(packed, BF16),
            pltpu.SemaphoreType.DMA((1 + 2 * inner // width,)),
            pltpu.SemaphoreType.DMA((4 + 2 * inner // width,)),
        ],
        compiler_params=pltpu.CompilerParams(vmem_limit_bytes=VMEM),
        cost_estimate=BRIEF,
    )(core, x, att, grad, out_w, gain[None], bias[None], in_w, in_b[None], down_w, down_b[None])


def project_back_kernel(
    calls, core_ref, x_ref, first_ref, w_ref, gain_ref, bias_ref, small2_ref, wide_ref, *refs
):
    grads, mixes = refs[: 3 * calls], refs[3 * calls : 4 * calls]
    result_ref, keep_ref, send_ref, normed, gathered, sums, rows_of = refs[4 * calls :]
    chunk, width = x_ref.shape
    number = pl.program_id(0)
    here = pl.ds(pl.multiple_of(number * chunk, chunk), chunk)

    @pl.when(number == 0)
    def _():
        sums[...] = jnp.zeros_like(sums)

    unit, scale = normalized(x_ref[...].astype(F32))
    normed[here, :] = (unit * gain_ref[...] + bias_ref[...]).astype(BF16)
    grad = jnp.concatenate([ref[...] for ref in grads], 1)
    gathered[here, :] = grad
    back = times_transposed(grad, w_ref[...])
    sums[0:1, :] += column_sum(back * unit)
    sums[1:2, :] += column_sum(back)
    grad_x = first_ref[...] + norm_back(back * gain_ref[...], unit, scale)
    result_ref[...] = grad_x.astype(BF16)

    @pl.when(number == pl.num_programs(0) - 1)
    def _():
        every = slice(0, width // 2)
        rows_of[...] = jnp.zeros_like(rows_of)
        at = 0
        for ref in (sums, small2_ref, wide_ref):
            for row in range(ref.shape[0]):
                for lane in range(0, ref.shape[1], PAIR):
                    rows_of[at : at + 1, :] = ref[row : row + 1, lane : lane + PAIR]
                    at += 1
        lane = lax.broadcasted_iota(jnp.int32, (3, PAIR), 1)
        blend = jnp.zeros((3, PAIR), F32)
        head = 0
        for mix in mixes:
            for first in range(0, mix.shape[1], HEAD):
                mine = jnp.sum(mix[:, first : first + HEAD], axis=1, keepdims=True)
                blend = blend + jnp.where(lane == head, mine, 0.0)
                head += 1
        rows_of[at : at + 3, :] = blend
        exact = rows_of[...]
        high = exact.astype(BF16)
        low = (exact - high.astype(F32)).astype(BF16)
        for part, value in enumerate((high, low)):
            lanes = slice(3 * width + part * PAIR, 3 * width + (part + 1) * PAIR)
            deal(core_ref, every, lanes, value, keep_ref, send_ref)
        for at in range(0, 3 * width, width):
            lanes = slice(at, at + width)
            share = rows_product(normed[...], gathered[:, lanes]).astype(BF16)
            deal(core_ref, every, lanes, share, keep_ref, send_ref)


def project_back(core, x, grad_first, weight, gain, bias, small2, wide, grads, mixes):
    rows, width = x.shape
    calls = len(mixes)
    packed = (width // 2, 3 * width + 2 * PAIR)
    block, chunk = by_rows(CHUNK, width), by_rows(CHUNK, width // calls)
    return pl.pallas_call(
        functools.partial(project_back_kernel, calls),
        grid=(rows // CHUNK,),
        out_shape=(jax.ShapeDtypeStruct((rows, width), BF16),)
        + (jax.ShapeDtypeStruct(packed, BF16),) * 2,
        in_specs=[pl.BlockSpec(memory_space=pltpu.SMEM), block, block]
        + [constant(a.shape) for a in (weight, gain[None], bias[None], small2, wide)]
        + [chunk] * (3 * calls)
        + [constant(mix.shape) for mix in mixes],
        out_specs=(block, constant(packed), constant(packed)),
        scratch_shapes=[
            pltpu.VMEM((rows, width), BF16),
            pltpu.VMEM((rows, 3 * width), BF16),
            pltpu.VMEM((2, width), F32),
            pltpu.VMEM((width, PAIR), F32),
        ],
        compiler_params=pltpu.CompilerParams(vmem_limit_bytes=VMEM),
        cost_estimate=BRIEF,
    )(core, x, grad_first, weight, gain[None], bias[None], small2, wide, *grads, *mixes)


def to_sequences(block, axis, groups):
    return lax.all_to_all(block, axis, 0, 0, axis_index_groups=groups)


def after(value, *others):
    return lax.optimization_barrier((value,) + others)[0]


def settle_kernel(source_ref, out_ref):
    out_ref[...] = source_ref[...]


def settle(value):
    vmem = pl.BlockSpec(memory_space=pltpu.VMEM)
    return pl.pallas_call(
        settle_kernel,
        out_shape=jax.ShapeDtypeStruct(value.shape, value.dtype),
        in_specs=[vmem],
        out_specs=vmem,
        compiler_params=pltpu.CompilerParams(vmem_limit_bytes=8 * 2**20),
        cost_estimate=BRIEF,
    )(value)


def from_parts(total, axis, parts, stride, forward):
    size = lax.axis_size(axis)
    low = total.astype(BF16)
    result = jnp.zeros_like(total)
    for hop in range(1, parts):
        distance = hop * stride
        route = [
            (i, i + distance) if forward else (i + distance, i) for i in range(size - distance)
        ]
        result = result + lax.ppermute(low, axis, route).astype(F32)
    return result


class Ring:
    def __init__(self, batch, seq):
        self.batch, self.seq = batch, seq
        self.low = 2 ** ((seq.bit_length() - 1) // 2)
        self.sizes = {"core": 2, "near": batch // 2 * self.low, "far": seq // self.low}
        self.pieces = batch * seq

    def place(self, s, b):
        return {"core": b % 2, "near": b // 2 * self.low + s % self.low, "far": s // self.low}

    def device(self, place):
        s = place["far"] * self.low + place["near"] % self.low
        return s * self.batch + place["near"] // self.low * 2 + place["core"]

    def mine(self):
        return self.place(lax.axis_index("seq"), lax.axis_index("batch"))

    def swap(self, value, level, k):
        route = []
        for s in range(self.seq):
            for b in range(self.batch):
                place = self.place(s, b)
                place[level] ^= k
                route.append((s * self.batch + b, self.device(place)))
        return lax.ppermute(value, ("seq", "batch"), route)

    def scatter(self, value, level, fine=0, beside=()):
        size, me = self.sizes[level], self.mine()[level]
        value = value.reshape((size, value.shape[0] // size) + value.shape[1:])
        parts = [
            self.swap(lax.dynamic_index_in_dim(value, me ^ k, 0, False), level, k)
            for k in range(1, size)
        ]
        return self.add(lax.dynamic_index_in_dim(value, me, 0, False), parts, fine, beside)

    def scatter_cores(self, keep, send, fine=0, beside=()):
        return self.add(self.to_pieces(keep), [self.swap(self.to_pieces(send), "core", 1)], fine, beside)

    def add(self, value, parts, fine, beside):
        total = after(value, *beside).astype(F32)
        for part in parts:
            total = total + part.astype(F32)
        if not fine:
            return total.astype(BF16)
        end = total.shape[-1] - 2 * fine
        exact = total[..., end : end + fine] + total[..., end + fine :]
        high = lax.reduce_precision(exact, 8, 7)
        return jnp.concatenate([total[..., :end], high, exact - high], -1).astype(BF16)

    def gather(self, value, level, beside=()):
        parts = [self.swap(value, level, k) for k in range(1, self.sizes[level])]
        return jnp.concatenate([after(value, *beside)] + parts, 0)

    def to_pieces(self, value):
        return value.reshape(self.pieces // 2, -1, value.shape[1])

    def order(self):
        me = self.mine()
        piece = jnp.arange(self.pieces, dtype=jnp.int32)
        far, near = self.sizes["far"], self.sizes["near"]
        core = (piece // (far * near)) ^ me["core"]
        near = ((piece // far) % near) ^ me["near"]
        return (core * self.sizes["near"] + near) * far + ((piece % far) ^ me["far"])


def unpack_kernel(write, finish, order_ref, own_ref, other_ref, *out_refs):
    half = own_ref.shape[0]
    for piece in range(2 * half):
        at = order_ref[piece]

        @pl.when(at < half)
        def _(piece=piece, at=at):
            write(piece, own_ref[at].astype(F32), out_refs)

        @pl.when(at >= half)
        def _(piece=piece, at=at):
            write(piece, other_ref[at - half].astype(F32), out_refs)

    finish(out_refs)


def write_feed(piece, block, out_refs):
    in_ref, out_ref, down_ref = out_refs
    size, inner, width = block.shape[0], in_ref.shape[1], in_ref.shape[0]
    rows = slice(piece * size, (piece + 1) * size)
    in_ref[rows, :] = block[:, :inner]
    out_ref[rows, :] = block[:, inner : inner + width]
    tall_rows = inner // (width // size)
    for below in range(0, tall_rows, size):
        at = inner + width + below // size * width
        down_ref[piece * tall_rows + below : piece * tall_rows + below + size, :] = block[
            :, at : at + width
        ]


def write_project(piece, block, out_refs):
    w_ref, small = out_refs[0], out_refs[-1]
    size, end = block.shape[0], w_ref.shape[1]
    rows = slice(piece * size, (piece + 1) * size)
    w_ref[rows, :] = block[:, :end]
    if piece * size < small.shape[0]:
        small[rows, :] = block[:, end : end + PAIR] + block[:, end + PAIR :]


def finish_project(out_refs):
    small, at = out_refs[-1], 0
    for vector in out_refs[1:-2]:
        for lane in range(0, vector.shape[0], PAIR):
            vector[lane : lane + PAIR] = small[at, :]
            at += 1
    blend = out_refs[-2]
    blend[...] = small[at : at + 3, : blend.shape[1]]


def unpack(write, order, halves, shapes, finish=lambda refs: None, scratch=()):
    vmem = pl.BlockSpec(memory_space=pltpu.VMEM)
    return pl.pallas_call(
        functools.partial(unpack_kernel, write, finish),
        out_shape=[jax.ShapeDtypeStruct(shape, F32) for shape in shapes],
        in_specs=[pl.BlockSpec(memory_space=pltpu.SMEM), vmem, vmem],
        out_specs=[vmem] * len(shapes),
        scratch_shapes=scratch,
        compiler_params=pltpu.CompilerParams(vmem_limit_bytes=VMEM),
        cost_estimate=BRIEF,
    )(order, *halves)


def local(
    inputs,
    cotangent,
    lengths,
    norm1_gain,
    norm1_bias,
    qkv_weight,
    blend_weights,
    out_weight,
    norm2_gain,
    norm2_bias,
    in_weight,
    in_bias,
    down_weight,
    down_bias,
):
    seqs, span, width = inputs.shape
    heads = blend_weights.shape[1]
    devices = lax.axis_size("seq")
    parts = devices // seqs
    rows = seqs * span
    index = lax.axis_index("seq")
    groups = None
    if parts > 1:
        groups = [[r * seqs + s for s in range(seqs)] for r in range(parts)]
    mine, part = index % seqs, index // seqs
    meta = jnp.stack([lax.dynamic_index_in_dim(lengths, mine, 0, False), part * rows])
    blend = jnp.repeat(blend_weights, width // heads, axis=1)

    ring = Ring(lax.axis_size("batch"), devices)
    by_ring = width % (16 * ring.pieces) == 0
    inner = in_weight.shape[1]

    x = to_sequences(inputs, "seq", groups).reshape(rows, width)
    grad_out = to_sequences(cotangent, "seq", groups).reshape(rows, width)

    normed = layer_norm(x.astype(F32), norm1_gain, norm1_bias).astype(BF16)
    qkv = times(normed, qkv_weight).astype(BF16)
    halo = state = later = None
    if parts > 1:
        state = later = jnp.zeros((2, width // PAIR, PAIR, 2 * PAIR), F32)
        onward = [(i, i + seqs) for i in range(devices - seqs)]
        halo = lax.ppermute(qkv[rows - TILE :, width:], "seq", onward)
        total = attend(meta, blend, qkv, halo, state)[1]
        state = from_parts(total, "seq", parts, seqs, True)
    attended = attend(meta, blend, qkv, halo, state)[0]

    core = (lax.axis_index("batch") % 2)[None] if by_ring else jnp.zeros(1, jnp.int32)
    result, grad_first, grad_o, feed_keep, feed_send, small2, grad_in_b = feed_forward(
        ring.pieces if by_ring else 16,
        core, x, attended, grad_out, out_weight, norm2_gain, norm2_bias,
        in_weight, in_bias, down_weight, down_bias,
    )
    output = to_sequences(result.reshape(seqs, span, width), "seq", groups)
    def unpack_feed(order, halves):
        shapes = [(width, inner), (width, width), (inner, width)]
        return unpack(write_feed, order, halves, shapes)

    calls = 4

    def back(meta, number, later):
        return attend_back(meta, blend, qkv, halo, state, later, grad_o, calls, number)

    if parts > 1:
        total = jnp.concatenate([back(meta, number, later)[6] for number in range(calls)], 1)
        later = from_parts(total, "seq", parts, seqs, False)
    backs, turn = [], meta
    if by_ring:
        held = None
        for number in range(calls):
            if number == 1:
                held = ring.scatter_cores(feed_keep, feed_send, 0, (backs[0][5],))
                turn = after(turn, held)
            if number == 3:
                held = ring.scatter(held, "near", 0, (backs[2][5],))
                turn = after(turn, held)
            backs.append(back(turn, number, later))
            turn = after(turn, backs[-1][5])
        held = ring.scatter(held, "far", 0, (backs[3][5],))
        output = settle(after(output, backs[2][5]))
        grad_first = after(grad_first, held, output)
    else:
        backs = [back(meta, number, later) for number in range(calls)]
    grads = [[call[part] for call in backs] for part in range(3)]
    if parts > 1:
        homeward = [(i + seqs, i) for i in range(devices - seqs)]
        for part in (1, 2):
            for number in range(calls):
                received = lax.ppermute(backs[number][part + 2], "seq", homeward)
                grad = grads[part][number]
                tail = grad[rows - TILE :].astype(F32) + received.astype(F32)
                grads[part][number] = grad.at[rows - TILE :].set(tail.astype(BF16))
    grads = grads[0] + grads[1] + grads[2]
    grad_x, project_keep, project_send = project_back(
        core, x, grad_first, qkv_weight, norm1_gain, norm1_bias, small2, grad_in_b, grads,
        [call[5] for call in backs],
    )
    moved = to_sequences(grad_x.reshape(seqs, span, width), "seq", groups)

    if by_ring:
        order = ring.order()
        held = ring.gather(held, "far", (project_keep,))
        late = ring.scatter_cores(project_keep, project_send, PAIR, (held,))
        near = [ring.swap(held, "near", k) for k in range(1, ring.sizes["near"])]
        late = after(ring.scatter(late, "near", PAIR), moved)
        late = ring.scatter(late, "far", PAIR)
        held = jnp.concatenate([after(held, late)] + near, 0)
        other = ring.swap(held, "core", 1)
        late = ring.gather(late, "far", (held,))
        grad_in_w, grad_out_w, grad_down_w = unpack_feed(order, (held, after(other, late)))
        input_grad = settle(after(moved, late))
        late = ring.gather(late, "near", (input_grad, grad_out_w))
        project_halves = late, ring.swap(late, "core", 1)
    else:
        input_grad = moved
        order = jnp.arange(16, dtype=jnp.int32)
        halves = (feed_keep, feed_send, project_keep, project_send)
        halves = lax.psum([half.astype(F32) for half in halves], ("seq", "batch"))
        halves = [half.reshape(8, width // 16, -1) for half in halves]
        feed_halves, project_halves = halves[:2], halves[2:]
        grad_in_w, grad_out_w, grad_down_w = unpack_feed(order, feed_halves)
    vectors = [(width,)] * 5 + [(inner,)]
    lines = sum(size for (size,) in vectors) // PAIR + 3
    lines += -lines % (width // order.shape[0])
    grad_qkv_w, gain1, bias1, gain2, bias2, grad_down_b, grad_in_b, grad_blend = unpack(
        write_project, order, project_halves, [(width, 3 * width)] + vectors + [(3, heads)],
        finish_project, [pltpu.VMEM((lines, PAIR), F32)],
    )
    return (
        output,
        input_grad,
        gain1,
        bias1,
        grad_qkv_w,
        grad_blend,
        grad_out_w,
        gain2,
        bias2,
        grad_in_w,
        grad_in_b,
        grad_down_w,
        grad_down_b,
    )


def solution(mesh):
    rows = P("batch", "seq", None)
    return jax.shard_map(
        local,
        mesh=mesh,
        in_specs=(rows, rows, P("batch")) + (P(),) * 11,
        out_specs=(rows, rows) + (P(),) * 11,
        check_vma=False,
    )
```

```python
import functools

import jax
import jax.numpy as jnp
from jax import lax
from jax.experimental import pallas as pl
from jax.experimental.pallas import tpu as pltpu
from jax.sharding import PartitionSpec as P

WINDOW = 30
HEAD = 64
PAIR = 2 * HEAD
TILE = 64
EPS = 1e-05
NEG = -1e30
VMEM = 58 * 2**20
BRIEF = pl.CostEstimate(flops=1000, bytes_accessed=1000, transcendentals=0)
BF16 = jnp.bfloat16
F32 = jnp.float32


def layer_norm(field, gain, shift):
    center = field - jnp.mean(field, axis=-1, keepdims=True)
    spread = jnp.mean(center * center, axis=-1, keepdims=True)
    return center * lax.rsqrt(spread + EPS) * gain + shift


def rows_product(left, right):
    return lax.dot_general(
        left, right, (((0,), (0,)), ((), ())), preferred_element_type=F32
    )


def times_transposed(left, right):
    return lax.dot_general(
        left, right, (((1,), (1,)), ((), ())), preferred_element_type=F32
    )


def times(left, right):
    return lax.dot_general(
        left, right, (((1,), (0,)), ((), ())), preferred_element_type=F32
    )


def elu_feature(field):
    return jnp.where(field > 0, field + 1.0, jnp.exp(jnp.minimum(field, 0.0)))


def tanh_feature(field):
    return 1.0 + jnp.tanh(field)


def pair_lanes(p, part=0, width=PAIR):
    return slice(p * width + part * PAIR, p * width + (part + 1) * PAIR)


def store_split(ref, index, rows, block):
    lane = lax.broadcasted_iota(jnp.int32, (block.shape[0], PAIR), 1)
    for p in range(block.shape[1] // PAIR):
        pair = block[:, pair_lanes(p)]
        for h in range(2):
            mine = (lane < HEAD) if h == 0 else (lane >= HEAD)
            ref[index + (rows, pair_lanes(p, h, 2 * PAIR))] = jnp.where(mine, pair, 0.0).astype(
                BF16
            )


def load_split(ref, index, rows, p):
    return jnp.concatenate([ref[index + (rows, pair_lanes(p, h, 2 * PAIR))] for h in range(2)], 0)


def tall(block):
    return jnp.concatenate([block[:, :PAIR], block[:, PAIR:]], 0)


def fill_features(meta_ref, q_ref, k_ref, v_ref, halo_k, halo_v, keys, values, fq, fk, split):
    rows, width = q_ref.shape
    chunk = 2 * TILE
    front = pl.ds(0, TILE)
    keys[front, :] = jnp.zeros((TILE, 2 * width), BF16)
    values[front, :] = jnp.zeros((TILE, 2 * width), BF16)
    fk[:, front, :] = jnp.zeros((2, TILE, 2 * width), BF16)
    if halo_k is not None:
        store_split(keys, (), front, halo_k[...].astype(F32) * 0.125)
        store_split(values, (), front, halo_v[...].astype(F32))

    def fill(step, carry):
        at = pl.multiple_of(step * chunk, chunk)
        here, there = pl.ds(at, chunk), pl.ds(at + TILE, chunk)
        q = q_ref[here, :].astype(F32)
        k = k_ref[here, :].astype(F32)
        store_split(keys, (), there, k * 0.125)
        store_split(values, (), there, v_ref[here, :].astype(F32))
        position = meta_ref[1] + at + lax.broadcasted_iota(jnp.int32, (chunk, width), 0)
        valid = position < meta_ref[0]
        for c, feature in enumerate((elu_feature, tanh_feature)):
            if split:
                store_split(fq, (c,), here, feature(q))
            else:
                fq[c, here, :] = feature(q).astype(BF16)
            store_split(fk, (c,), there, jnp.where(valid, feature(k), 0.0))
        return carry

    lax.fori_loop(0, rows // chunk, fill, 0)


def tile_masks(meta_ref, tile):
    shape = (TILE, 2 * PAIR)
    row = lax.broadcasted_iota(jnp.int32, shape, 0)
    lane = lax.broadcasted_iota(jnp.int32, shape, 1) % PAIR
    back = row + TILE - lane
    key = meta_ref[1] + (tile - 1) * TILE + lane
    known = (key >= 0) & (key < meta_ref[0])
    near = (back >= 0) & (back <= WINDOW) & (known | (back == 0))
    return near, back >= 0


def softmax_pair(scores):
    halves = []
    for h in range(2):
        part = scores[:, h * PAIR : (h + 1) * PAIR]
        part = jnp.exp(part - jnp.max(part, axis=1, keepdims=True))
        halves.append(part * (1.0 / jnp.sum(part, axis=1, keepdims=True)))
    return jnp.concatenate(halves, 1)


def tile_constants():
    row = lax.broadcasted_iota(jnp.int32, (2 * PAIR, PAIR), 0)
    lane = lax.broadcasted_iota(jnp.int32, (2 * PAIR, PAIR), 1)
    ones = jnp.where(row // PAIR == lane // HEAD, 1.0, 0.0).astype(BF16)
    row = lax.broadcasted_iota(jnp.int32, (PAIR, 2 * PAIR), 0)
    lane = lax.broadcasted_iota(jnp.int32, (PAIR, 2 * PAIR), 1)
    return ones, row // HEAD == (lane % PAIR) // HEAD


def whole(split):
    half = split.shape[0] // 2
    return split[:half] + split[half:]


def state_share(block, fks, vs):
    ones = jnp.ones((TILE, PAIR), BF16)
    share = rows_product(whole(fks), jnp.concatenate([whole(vs), ones], 1))
    return jnp.where(block, share, 0.0)


def attend_kernel(
    together, whole_sequence, meta_ref, blend_ref, q_ref, k_ref, v_ref, *refs
):
    halo_k, halo_v, state_ref = (None,) * 3 if whole_sequence else refs[:3]
    att_ref, keys, values, fq, fk, state = refs[-6:] if whole_sequence else refs[3:4] + refs[-5:]
    total_ref = None if whole_sequence else refs[4]
    rows, width = q_ref.shape
    pairs = range(width // PAIR)
    near_by = range(together)
    units = [(s, p) for s in near_by for p in pairs]
    fill_features(meta_ref, q_ref, k_ref, v_ref, halo_k, halo_v, keys, values, fq, fk, False)
    state[...] = jnp.zeros_like(state) if whole_sequence else state_ref[...]
    ones, block = tile_constants()

    def step(number, carry):
        first = number * together
        at = pl.multiple_of(first * TILE, TILE)
        here = [pl.ds(at + s * TILE, TILE) for s in near_by]
        window = [pl.ds(at + s * TILE, 2 * TILE) for s in near_by]
        masks = [tile_masks(meta_ref, first + s) for s in near_by]
        q = {(s, p): q_ref[here[s], pair_lanes(p)] for s, p in units}
        feats = {(s, p): [fq[c, here[s], pair_lanes(p)] for c in range(2)] for s, p in units}
        ks = {(s, p): load_split(keys, (), window[s], p) for s, p in units}
        fks = {(s, p): [load_split(fk, (c,), window[s], p) for c in range(2)] for s, p in units}
        wide = {
            (s, p): jnp.concatenate([load_split(values, (), window[s], p), ones], 1)
            for s, p in units
        }
        held = {(0, p): [state[c, p] for c in range(2)] for p in pairs}
        for s, p in units:
            vs = load_split(values, (), here[s], p)
            held[s + 1, p] = [
                held[s, p][c] + state_share(block, load_split(fk, (c,), here[s], p), vs)
                for c in range(2)
            ]
        near = {u: times_transposed(q[u], ks[u]) for u in units}
        far = {u: [times_transposed(feats[u][c], fks[u][c]) for c in range(2)] for u in units}
        old = {u: [times(feats[u][c], held[u][c].astype(BF16)) for c in range(2)] for u in units}
        near = {u: softmax_pair(jnp.where(masks[u[0]][0], near[u], NEG)) for u in units}
        far = {u: [jnp.where(masks[u[0]][1], f, 0.0) for f in far[u]] for u in units}
        stack = {u: jnp.concatenate([near[u]] + far[u], 0).astype(BF16) for u in units}
        sums = {u: times(stack[u], wide[u]) for u in units}
        for s, p in units:
            u, lanes = (s, p), pair_lanes(p)
            mixed = blend_ref[0:1, lanes] * sums[u][:TILE, :PAIR]
            for c in range(2):
                mine = sums[u][(c + 1) * TILE : (c + 2) * TILE] + old[u][c]
                mixed = mixed + blend_ref[c + 1 : c + 2, lanes] * (
                    mine[:, :PAIR] / mine[:, PAIR:]
                )
            att_ref[here[s], lanes] = mixed.astype(BF16)
        for p in pairs:
            for c in range(2):
                state[c, p] = held[together, p][c]
        return carry

    lax.fori_loop(0, rows // (together * TILE), step, 0)
    if whole_sequence:
        return
    last = pl.ds(rows, TILE)
    for p in pairs:
        for c in range(2):
            total_ref[c, p] = state[c, p] + state_share(
                block, load_split(fk, (c,), last, p), load_split(values, (), last, p)
            )


def slopes_of(field):
    small = jnp.exp(jnp.minimum(field, 0.0))
    bent = jnp.tanh(field)
    return [jnp.where(field > 0, 1.0, small), 1.0 - bent * bent]


def split_heads(block):
    lane = lax.broadcasted_iota(jnp.int32, block.shape, 1)
    zero = jnp.zeros_like(block)
    return jnp.concatenate(
        [jnp.where(lane < HEAD, block, zero), jnp.where(lane < HEAD, zero, block)], 0
    )


def attend_back_kernel(
    together, whole_sequence, meta_ref, blend_ref, q_ref, k_ref, v_ref, go_ref, *refs
):
    halo_k, halo_v, state_ref, later_ref = (None,) * 4 if whole_sequence else refs[:4]
    if whole_sequence:
        gq_ref, gk_ref, gv_ref, mix_ref = refs[:4]
    else:
        gq_ref, gk_ref, gv_ref, mix_ref, hk_ref, hv_ref, total_ref = refs[4:11]
    keys, values, fq, fk, state, gk, gv, gfk, gon = refs[-9:]
    rows, width = q_ref.shape
    pairs = range(width // PAIR)
    tiles = rows // TILE
    near_by = range(together)
    units = [(s, p) for s in near_by for p in pairs]
    fill_features(meta_ref, q_ref, k_ref, v_ref, halo_k, halo_v, keys, values, fq, fk, True)
    state[...] = jnp.zeros_like(state) if whole_sequence else state_ref[...]
    mix_ref[...] = jnp.zeros_like(mix_ref)
    gk[:TILE, :] = jnp.zeros((TILE, width), F32)
    gv[:TILE, :] = jnp.zeros((TILE, width), F32)
    gfk[:, :TILE, :] = jnp.zeros((2, TILE, width), F32)
    ones, block = tile_constants()
    row = lax.broadcasted_iota(jnp.int32, (2 * PAIR, PAIR), 0) % PAIR
    lane = lax.broadcasted_iota(jnp.int32, (2 * PAIR, PAIR), 1)
    heads = jnp.where(row // HEAD == lane // HEAD, 1.0, 0.0).astype(BF16)
    plain_ones = jnp.ones((TILE, PAIR), BF16)
    high = (lax.broadcasted_iota(jnp.int32, (TILE, PAIR), 1) % HEAD) < HEAD // 2

    def step(number, carry):
        first = number * together
        at = pl.multiple_of(first * TILE, TILE)
        here = [pl.ds(at + s * TILE, TILE) for s in range(together + 1)]
        window = [pl.ds(at + s * TILE, 2 * TILE) for s in near_by]
        masks = [tile_masks(meta_ref, first + s) for s in near_by]
        q = {(s, p): q_ref[here[s], pair_lanes(p)] for s, p in units}
        go = {(s, p): go_ref[here[s], pair_lanes(p)] for s, p in units}
        blend = [[blend_ref[c : c + 1, pair_lanes(p)] for c in range(3)] for p in pairs]
        fqs = {(s, p): [load_split(fq, (c,), here[s], p) for c in range(2)] for s, p in units}
        feats = {u: [whole(f) for f in fqs[u]] for u in units}
        ks = {(s, p): load_split(keys, (), window[s], p) for s, p in units}
        fks = {(s, p): [load_split(fk, (c,), window[s], p) for c in range(2)] for s, p in units}
        wide = {
            (s, p): jnp.concatenate([load_split(values, (), window[s], p), ones], 1)
            for s, p in units
        }
        held = {(0, p): [state[c, p] for c in range(2)] for p in pairs}
        for s, p in units:
            vs = load_split(values, (), here[s], p)
            held[s + 1, p] = [
                held[s, p][c] + state_share(block, load_split(fk, (c,), here[s], p), vs)
                for c in range(2)
            ]
        past = {u: [h.astype(BF16) for h in held[u]] for u in units}
        old_k = [gk[here[0], pair_lanes(p)] for p in pairs]
        old_v = [gv[here[0], pair_lanes(p)] for p in pairs]
        old_f = [[gfk[c, here[0], pair_lanes(p)] for c in range(2)] for p in pairs]

        near = {u: times_transposed(q[u], ks[u]) for u in units}
        far = {u: [times_transposed(feats[u][c], fks[u][c]) for c in range(2)] for u in units}
        old = {u: [times(feats[u][c], past[u][c]) for c in range(2)] for u in units}
        near = {u: softmax_pair(jnp.where(masks[u[0]][0], near[u], NEG)) for u in units}
        far = {u: [jnp.where(masks[u[0]][1], f, 0.0).astype(BF16) for f in far[u]] for u in units}
        stack = {u: jnp.concatenate([near[u].astype(BF16)] + far[u], 0) for u in units}
        sums = {u: times(stack[u], wide[u]) for u in units}
        scales, prods = {}, {}
        for u in units:
            outs = [sums[u][:TILE, :PAIR]]
            scales[u] = [jnp.broadcast_to(blend[u[1]][0], (TILE, PAIR))]
            for c in range(2):
                mine = sums[u][(c + 1) * TILE : (c + 2) * TILE] + old[u][c]
                inverse = 1.0 / mine[:, PAIR:]
                outs.append(mine[:, :PAIR] * inverse)
                scales[u].append(blend[u[1]][c + 1] * inverse)
            prods[u] = jnp.concatenate([go[u] * out for out in outs], 0)
        deltas = {}
        for u in units:
            low = prods[u].astype(BF16)
            rest = (prods[u] - low.astype(F32)).astype(BF16)
            deltas[u] = times(jnp.concatenate([low, rest], 1), heads)
        grads = {}
        for u in units:
            grads[u] = []
            for c in range(3):
                delta = scales[u][c] * deltas[u][c * TILE : (c + 1) * TILE] * (-2.0 / HEAD)
                delta_low = delta.astype(BF16).astype(F32)
                delta = jnp.where(high, delta_low, delta - delta_low)
                grads[u].append(jnp.concatenate([scales[u][c] * go[u], delta], 1).astype(BF16))
        back = {u: times_transposed(jnp.concatenate(grads[u], 0), wide[u]) for u in units}
        late = {u: [times_transposed(grads[u][c + 1], past[u][c]) for c in range(2)] for u in units}
        ds = {u: (near[u] * back[u][:TILE]).astype(BF16) for u in units}
        gas = {
            u: [
                jnp.where(masks[u[0]][1], back[u][(c + 1) * TILE : (c + 2) * TILE], 0.0).astype(BF16)
                for c in range(2)
            ]
            for u in units
        }
        gq_near = {u: times(ds[u], ks[u]) for u in units}
        gq_far = {u: [times(gas[u][c], fks[u][c]) + late[u][c] for c in range(2)] for u in units}
        new_k = {u: rows_product(tall(ds[u]), split_heads(q[u] * 0.125)) for u in units}
        new_f = {u: [rows_product(tall(gas[u][c]), fqs[u][c]) for c in range(2)] for u in units}
        new_v = {
            u: rows_product(
                jnp.concatenate([tall(stack[u][c * TILE : (c + 1) * TILE]) for c in range(3)], 0),
                jnp.concatenate([split_heads(g[:, :PAIR]) for g in grads[u]], 0),
            )
            for u in units
        }

        def overlap(old, new, p):
            parts = [old + new(0, p)[:TILE]]
            parts += [new(s, p)[TILE:] + new(s + 1, p)[:TILE] for s in range(together - 1)]
            return parts + [new(together - 1, p)[TILE:]]

        for s, p in units:
            u, lanes = (s, p), pair_lanes(p)
            slopes = slopes_of(q[u].astype(F32))
            gq = gq_near[u] + slopes[0] * gq_far[u][0] + slopes[1] * gq_far[u][1]
            gq_ref[here[s], lanes] = gq.astype(BF16)
            for c in range(2):
                gon[c, here[s], p * 2 * PAIR : (p + 1) * 2 * PAIR] = grads[u][c + 1]
        for p in pairs:
            lanes = pair_lanes(p)
            for c in range(3):
                mix_ref[c : c + 1, lanes] += sum(
                    jnp.sum(prods[s, p][c * TILE : (c + 1) * TILE], axis=0, keepdims=True)
                    for s in near_by
                )
            for rows_at, part in zip(here, overlap(old_k[p], lambda s, p: new_k[s, p], p)):
                gk[rows_at, lanes] = part
            for rows_at, part in zip(here, overlap(old_v[p], lambda s, p: new_v[s, p], p)):
                gv[rows_at, lanes] = part
            for c in range(2):
                parts = overlap(old_f[p][c], lambda s, p: new_f[s, p][c], p)
                for rows_at, part in zip(here, parts):
                    gfk[c, rows_at, lanes] = part
                state[c, p] = held[together, p][c]
        return carry

    lax.fori_loop(0, tiles // together, step, 0)
    if not whole_sequence:
        hk_ref[...] = gk[:TILE, :].astype(BF16)
        hv_ref[...] = gv[:TILE, :].astype(BF16)
    state[...] = jnp.zeros_like(state) if whole_sequence else later_ref[...]

    def come(at, c, p):
        here = pl.ds(at, TILE)
        grads = gon[c, here, p * 2 * PAIR : (p + 1) * 2 * PAIR]
        share = rows_product(whole(load_split(fq, (c,), here, p)), grads)
        return jnp.where(block, share, 0.0)

    def back_step(number, carry):
        first = tiles - 1 - number * together
        at = [pl.multiple_of((first - s) * TILE, TILE) for s in near_by]
        here = [pl.ds(a, TILE) for a in at]
        there = [pl.ds(a + TILE, TILE) for a in at]
        held = {(-1, p): [state[c, p] for c in range(2)] for p in pairs}
        for s, p in units:
            tile = first - s + 2
            nearer = pl.multiple_of(jnp.minimum(tile, tiles - 1) * TILE, TILE)
            held[s, p] = [
                held[s - 1, p][c] + jnp.where(tile < tiles, come(nearer, c, p), 0.0)
                for c in range(2)
            ]
        later = {u: [h.astype(BF16) for h in held[u]] for u in units}
        vs = {(s, p): whole(load_split(values, (), there[s], p)) for s, p in units}
        fks = {
            (s, p): jnp.concatenate([whole(load_split(fk, (c,), there[s], p)) for c in range(2)], 1)
            for s, p in units
        }
        wide = {u: jnp.concatenate([vs[u], plain_ones], 1) for u in units}
        far_k = {u: [times_transposed(wide[u], later[u][c]) for c in range(2)] for u in units}
        far_v = {
            u: times(fks[u], jnp.concatenate([g[:, :PAIR] for g in later[u]], 0)) for u in units
        }
        for s, p in units:
            u, lanes = (s, p), pair_lanes(p)
            position = meta_ref[1] + at[s] + lax.broadcasted_iota(jnp.int32, (TILE, PAIR), 0)
            slopes = slopes_of(k_ref[here[s], lanes].astype(F32))
            grad_f = [gfk[c, there[s], lanes] + far_k[u][c] for c in range(2)]
            bent = slopes[0] * grad_f[0] + slopes[1] * grad_f[1]
            grad_k = gk[there[s], lanes] + jnp.where(position < meta_ref[0], bent, 0.0)
            gk_ref[here[s], lanes] = grad_k.astype(BF16)
            gv_ref[here[s], lanes] = (gv[there[s], lanes] + far_v[u]).astype(BF16)
        for p in pairs:
            for c in range(2):
                state[c, p] = held[together - 1, p][c]
        return carry

    lax.fori_loop(0, tiles // together, back_step, 0)
    if whole_sequence:
        return
    for p in pairs:
        for c in range(2):
            total_ref[c, p] = state[c, p] + come(0, c, p) + come(TILE, c, p)


def attention_specs(rows, width, lanes, number):
    calls = width // lanes

    def columns(height, part):
        return pl.BlockSpec((height, lanes), lambda i: (0, part * calls + number(i)))

    state = pl.BlockSpec(
        (2, lanes // PAIR, PAIR, 2 * PAIR), lambda i: (0, number(i), 0, 0)
    )
    ins = [pl.BlockSpec(memory_space=pltpu.SMEM), columns(3, 0)]
    ins += [columns(rows, part) for part in range(3)]
    return columns, ins, [columns(TILE, part) for part in range(2)] + [state]


def attention_scratch(rows, lanes, split):
    return [
        pltpu.VMEM((rows + TILE, 2 * lanes), BF16),
        pltpu.VMEM((rows + TILE, 2 * lanes), BF16),
        pltpu.VMEM((2, rows, (2 if split else 1) * lanes), BF16),
        pltpu.VMEM((2, rows + TILE, 2 * lanes), BF16),
        pltpu.VMEM((2, lanes // PAIR, PAIR, 2 * PAIR), F32),
    ]


def outcome(shape, dtype):
    return jax.ShapeDtypeStruct(shape, dtype), pl.BlockSpec(shape, lambda _: (0,) * len(shape))


UNITS = 16


def attend(meta, blend, qkv, halo, state):
    rows, width = qkv.shape[0], qkv.shape[1] // 3
    lanes = PAIR
    columns, ins, before = attention_specs(rows, width, lanes, lambda i: i)
    held = before[-1]
    share = (2, width // PAIR, PAIR, 2 * PAIR)
    earlier = () if state is None else (halo, halo, state)
    return pl.pallas_call(
        functools.partial(attend_kernel, UNITS * PAIR // lanes, state is None),
        grid=(width // lanes,),
        out_shape=(
            jax.ShapeDtypeStruct((rows, width), BF16),
            jax.ShapeDtypeStruct(share, F32),
        )[: 1 if state is None else 2],
        in_specs=ins + before[: len(earlier)],
        out_specs=(columns(rows, 0), held)[: 1 if state is None else 2],
        scratch_shapes=attention_scratch(rows, lanes, False),
        compiler_params=pltpu.CompilerParams(vmem_limit_bytes=VMEM),
        cost_estimate=BRIEF,
    )(meta, blend, qkv, qkv, qkv, *earlier)


def attend_back(meta, blend, qkv, halo, state, later, go, calls, number):
    rows, width = qkv.shape[0], qkv.shape[1] // 3
    lanes = width // calls
    columns, ins, before = attention_specs(rows, width, lanes, lambda i: number)
    others = () if state is None else (halo, halo, state, later)
    outs = [outcome((rows, lanes), BF16)] * 3 + [outcome((3, lanes), F32)]
    if state is not None:
        outs += [outcome((TILE, lanes), BF16)] * 2
        outs += [outcome((2, lanes // PAIR, PAIR, 2 * PAIR), F32)]
    shapes, blocks = zip(*outs)
    return pl.pallas_call(
        functools.partial(attend_back_kernel, UNITS * PAIR // lanes, state is None),
        grid=(1,),
        out_shape=shapes,
        in_specs=ins + [columns(rows, 0)] + (before + before[-1:])[: len(others)],
        out_specs=blocks,
        scratch_shapes=attention_scratch(rows, lanes, True)
        + [
            pltpu.VMEM((rows + TILE, lanes), F32),
            pltpu.VMEM((rows + TILE, lanes), F32),
            pltpu.VMEM((2, rows + TILE, lanes), F32),
            pltpu.VMEM((2, rows, 2 * lanes), BF16),
        ],
        compiler_params=pltpu.CompilerParams(vmem_limit_bytes=VMEM),
        cost_estimate=BRIEF,
    )(meta, blend, qkv, qkv, qkv, go, *others)


CHUNK = 512
GELU_A, GELU_B = 0.7978845608028654, 0.044715


def normalized(field):
    center = field - jnp.mean(field, axis=-1, keepdims=True)
    scale = lax.rsqrt(jnp.mean(center * center, axis=-1, keepdims=True) + EPS)
    return center * scale, scale


def norm_back(grad, unit, scale):
    shared = jnp.mean(grad * unit, axis=-1, keepdims=True)
    return scale * (grad - jnp.mean(grad, axis=-1, keepdims=True) - unit * shared)


def gelu_pair(field):
    square = field * field
    bent = jnp.tanh(GELU_A * field * (1.0 + GELU_B * square))
    half = 0.5 + 0.5 * bent
    slope = half + 0.5 * field * (1.0 - bent * bent) * (GELU_A + 3.0 * GELU_A * GELU_B * square)
    return field * half, slope


def column_sum(block):
    return jnp.sum(block, axis=0, keepdims=True)


def deal(core_ref, rows, lanes, value, keep_ref, send_ref):
    half = value.shape[0] // 2

    @pl.when(core_ref[0] == 0)
    def _():
        keep_ref[rows, lanes] = value[:half]
        send_ref[rows, lanes] = value[half:]

    @pl.when(core_ref[0] != 0)
    def _():
        keep_ref[rows, lanes] = value[half:]
        send_ref[rows, lanes] = value[:half]


def feed_kernel(
    pieces, core_ref, x_ref, att_ref, grad_ref, out_from, gain_ref, bias_ref, in_from, in_b,
    down_from, down_b, result_ref, first_ref, go_ref, keep_to, send_to, small_ref, wide_ref,
    second, hidden, pre_low, att_low, att_all, grad_all, out_w, in_w, down_w, keep_ref, send_ref,
    in_sems, out_sems,
):
    chunk, width = x_ref.shape
    inner = in_w.shape[1]
    number = pl.program_id(0)
    here = pl.ds(pl.multiple_of(number * chunk, chunk), chunk)
    tiles = [slice(at, at + width) for at in range(0, inner, width)]
    copies = [pltpu.make_async_copy(out_from, out_w, in_sems.at[0])]
    for i, lanes in enumerate(tiles):
        copies += [
            pltpu.make_async_copy(in_from.at[:, lanes], in_w.at[:, lanes], in_sems.at[2 * i + 1]),
            pltpu.make_async_copy(down_from.at[lanes, :], down_w.at[lanes, :], in_sems.at[2 * i + 2]),
        ]

    def arrived(i):
        @pl.when(number == 0)
        def _():
            copies[i].wait()

    @pl.when(number == 0)
    def _():
        for copy in copies:
            copy.start()
        small_ref[...] = jnp.zeros_like(small_ref)
        wide_ref[...] = jnp.zeros_like(wide_ref)

    att = att_ref[...]
    att_all[here, :] = att
    arrived(0)
    first = x_ref[...].astype(F32) + times(att, out_w[...])
    unit, scale = normalized(first)
    low = (unit * gain_ref[...] + bias_ref[...]).astype(BF16)
    second[here, :] = low
    grad = grad_ref[...]
    grad_all[here, :] = grad
    grad_f = grad.astype(F32)
    result = first + down_b[...]
    back = jnp.zeros((chunk, width), F32)
    for i, lanes in enumerate(tiles):
        arrived(2 * i + 1)
        arrived(2 * i + 2)
        act, slope = gelu_pair(times(low, in_w[:, lanes]) + in_b[:, lanes])
        act = act.astype(BF16)
        hidden[here, lanes] = act
        result = result + times(act, down_w[lanes, :])
        pre = (times_transposed(grad, down_w[lanes, :]) * slope).astype(BF16)
        pre_low[here, lanes] = pre
        wide_ref[:, lanes] += column_sum(pre.astype(F32))
        back = back + times_transposed(pre, in_w[:, lanes])
    result_ref[...] = result.astype(BF16)
    small_ref[0:1, :] += column_sum(back * unit)
    small_ref[1:2, :] += column_sum(back)
    small_ref[2:3, :] += column_sum(grad_f)
    grad_first = grad_f + norm_back(back * gain_ref[...], unit, scale)
    first_ref[...] = grad_first
    grad_att = grad_first.astype(BF16)
    att_low[here, :] = grad_att
    go_ref[...] = times_transposed(grad_att, out_w[...])

    @pl.when(number == pl.num_programs(0) - 1)
    def _():
        every = slice(0, width // 2)
        leaving = []

        def leave(lanes):
            for here, there in ((keep_ref, keep_to), (send_ref, send_to)):
                sem = out_sems.at[len(leaving)]
                copy = pltpu.make_async_copy(here.at[:, lanes], there.at[:, lanes], sem)
                copy.start()
                leaving.append(copy)

        flat, each, after_out = width // pieces, pieces, inner + width
        for block, lanes in enumerate(tiles):
            share = rows_product(hidden[:, lanes], grad_all[...]).astype(BF16)
            for below in range(each):
                piece, side = divmod(block * each + below, len(tiles))
                to = slice(after_out + side * width, after_out + (side + 1) * width)
                rows = slice(piece % (pieces // 2) * flat, (piece % (pieces // 2) + 1) * flat)
                mine = core_ref[0] == 2 * piece // pieces
                some = share[below * flat : (below + 1) * flat]

                @pl.when(mine)
                def _(rows=rows, to=to, some=some):
                    keep_ref[rows, to] = some

                @pl.when(jnp.logical_not(mine))
                def _(rows=rows, to=to, some=some):
                    send_ref[rows, to] = some

        leave(slice(after_out, after_out + inner))
        for lanes in tiles:
            share = rows_product(second[...], pre_low[:, lanes]).astype(BF16)
            deal(core_ref, every, lanes, share, keep_ref, send_ref)
            leave(lanes)
        share = rows_product(att_all[...], att_low[...]).astype(BF16)
        deal(core_ref, every, slice(inner, after_out), share, keep_ref, send_ref)
        leave(slice(inner, after_out))
        for copy in leaving:
            copy.wait()


def by_rows(height, width):
    return pl.BlockSpec((height, width), lambda i: (i, 0))


def constant(shape):
    return pl.BlockSpec(shape, lambda i: (0, 0))


def feed_forward(pieces, core, x, att, grad, out_w, gain, bias, in_w, in_b, down_w, down_b):
    rows, width = x.shape
    inner = in_w.shape[1]
    packed = (width // 2, 2 * inner + width)
    block, far = by_rows(CHUNK, width), pl.BlockSpec(memory_space=pl.ANY)
    return pl.pallas_call(
        functools.partial(feed_kernel, pieces),
        grid=(rows // CHUNK,),
        out_shape=(
            jax.ShapeDtypeStruct((rows, width), BF16),
            jax.ShapeDtypeStruct((rows, width), F32),
            jax.ShapeDtypeStruct((rows, width), F32),
            jax.ShapeDtypeStruct(packed, BF16),
            jax.ShapeDtypeStruct(packed, BF16),
            jax.ShapeDtypeStruct((3, width), F32),
            jax.ShapeDtypeStruct((1, inner), F32),
        ),
        in_specs=[pl.BlockSpec(memory_space=pltpu.SMEM)]
        + [block] * 3
        + [far, constant((1, width)), constant((1, width)), far, constant((1, inner)), far]
        + [constant((1, width))],
        out_specs=(block, block, block, far, far)
        + (constant((3, width)), constant((1, inner))),
        scratch_shapes=[
            pltpu.VMEM((rows, width), BF16),
            pltpu.VMEM((rows, inner), BF16),
            pltpu.VMEM((rows, inner), BF16),
            pltpu.VMEM((rows, width), BF16),
            pltpu.VMEM((rows, width), BF16),
            pltpu.VMEM((rows, width), BF16),
            pltpu.VMEM(out_w.shape, BF16),
            pltpu.VMEM(in_w.shape, BF16),
            pltpu.VMEM(down_w.shape, BF16),
            pltpu.VMEM(packed, BF16),
            pltpu.VMEM(packed, BF16),
            pltpu.SemaphoreType.DMA((1 + 2 * inner // width,)),
            pltpu.SemaphoreType.DMA((4 + 2 * inner // width,)),
        ],
        compiler_params=pltpu.CompilerParams(vmem_limit_bytes=VMEM),
        cost_estimate=BRIEF,
    )(core, x, att, grad, out_w, gain[None], bias[None], in_w, in_b[None], down_w, down_b[None])


def project_back_kernel(
    calls, core_ref, x_ref, first_ref, w_ref, gain_ref, bias_ref, small2_ref, wide_ref, *refs
):
    grads, mixes = refs[: 3 * calls], refs[3 * calls : 4 * calls]
    result_ref, keep_ref, send_ref, normed, gathered, sums, rows_of = refs[4 * calls :]
    chunk, width = x_ref.shape
    number = pl.program_id(0)
    here = pl.ds(pl.multiple_of(number * chunk, chunk), chunk)

    @pl.when(number == 0)
    def _():
        sums[...] = jnp.zeros_like(sums)

    unit, scale = normalized(x_ref[...].astype(F32))
    normed[here, :] = (unit * gain_ref[...] + bias_ref[...]).astype(BF16)
    grad = jnp.concatenate([ref[...] for ref in grads], 1)
    gathered[here, :] = grad
    back = times_transposed(grad, w_ref[...])
    sums[0:1, :] += column_sum(back * unit)
    sums[1:2, :] += column_sum(back)
    grad_x = first_ref[...] + norm_back(back * gain_ref[...], unit, scale)
    result_ref[...] = grad_x.astype(BF16)

    @pl.when(number == pl.num_programs(0) - 1)
    def _():
        every = slice(0, width // 2)
        rows_of[...] = jnp.zeros_like(rows_of)
        at = 0
        for ref in (sums, small2_ref, wide_ref):
            for row in range(ref.shape[0]):
                for lane in range(0, ref.shape[1], PAIR):
                    rows_of[at : at + 1, :] = ref[row : row + 1, lane : lane + PAIR]
                    at += 1
        lane = lax.broadcasted_iota(jnp.int32, (3, PAIR), 1)
        blend = jnp.zeros((3, PAIR), F32)
        head = 0
        for mix in mixes:
            for first in range(0, mix.shape[1], HEAD):
                mine = jnp.sum(mix[:, first : first + HEAD], axis=1, keepdims=True)
                blend = blend + jnp.where(lane == head, mine, 0.0)
                head += 1
        rows_of[at : at + 3, :] = blend
        exact = rows_of[...]
        high = exact.astype(BF16)
        low = (exact - high.astype(F32)).astype(BF16)
        for part, value in enumerate((high, low)):
            lanes = slice(3 * width + part * PAIR, 3 * width + (part + 1) * PAIR)
            deal(core_ref, every, lanes, value, keep_ref, send_ref)
        for at in range(0, 3 * width, width):
            lanes = slice(at, at + width)
            share = rows_product(normed[...], gathered[:, lanes]).astype(BF16)
            deal(core_ref, every, lanes, share, keep_ref, send_ref)


def project_back(core, x, grad_first, weight, gain, bias, small2, wide, grads, mixes):
    rows, width = x.shape
    calls = len(mixes)
    packed = (width // 2, 3 * width + 2 * PAIR)
    block, chunk = by_rows(CHUNK, width), by_rows(CHUNK, width // calls)
    return pl.pallas_call(
        functools.partial(project_back_kernel, calls),
        grid=(rows // CHUNK,),
        out_shape=(jax.ShapeDtypeStruct((rows, width), BF16),)
        + (jax.ShapeDtypeStruct(packed, BF16),) * 2,
        in_specs=[pl.BlockSpec(memory_space=pltpu.SMEM), block, block]
        + [constant(a.shape) for a in (weight, gain[None], bias[None], small2, wide)]
        + [chunk] * (3 * calls)
        + [constant(mix.shape) for mix in mixes],
        out_specs=(block, constant(packed), constant(packed)),
        scratch_shapes=[
            pltpu.VMEM((rows, width), BF16),
            pltpu.VMEM((rows, 3 * width), BF16),
            pltpu.VMEM((2, width), F32),
            pltpu.VMEM((width, PAIR), F32),
        ],
        compiler_params=pltpu.CompilerParams(vmem_limit_bytes=VMEM),
        cost_estimate=BRIEF,
    )(core, x, grad_first, weight, gain[None], bias[None], small2, wide, *grads, *mixes)


def to_sequences(block, axis, groups):
    return lax.all_to_all(block, axis, 0, 0, axis_index_groups=groups)


def after(value, *others):
    return lax.optimization_barrier((value,) + others)[0]


def join_kernel(*refs):
    out_ref = refs[-1]
    size = refs[0].shape[0]
    for k, part in enumerate(refs[:-1]):
        out_ref[k * size : (k + 1) * size] = part[...]


def join(parts):
    vmem, part = pl.BlockSpec(memory_space=pltpu.VMEM), parts[0]
    return pl.pallas_call(
        join_kernel,
        out_shape=jax.ShapeDtypeStruct((len(parts) * part.shape[0],) + part.shape[1:], part.dtype),
        in_specs=[vmem] * len(parts),
        out_specs=vmem,
        compiler_params=pltpu.CompilerParams(vmem_limit_bytes=16 * 2**20),
        cost_estimate=BRIEF,
    )(*parts)


def settle_kernel(source_ref, out_ref):
    out_ref[...] = source_ref[...]


def settle(value):
    vmem = pl.BlockSpec(memory_space=pltpu.VMEM)
    return pl.pallas_call(
        settle_kernel,
        out_shape=jax.ShapeDtypeStruct(value.shape, value.dtype),
        in_specs=[vmem],
        out_specs=vmem,
        compiler_params=pltpu.CompilerParams(vmem_limit_bytes=8 * 2**20),
        cost_estimate=BRIEF,
    )(value)


def from_parts(total, axis, parts, stride, forward):
    size = lax.axis_size(axis)
    low = total.astype(BF16)
    result = jnp.zeros_like(total)
    for hop in range(1, parts):
        distance = hop * stride
        route = [
            (i, i + distance) if forward else (i + distance, i) for i in range(size - distance)
        ]
        result = result + lax.ppermute(low, axis, route).astype(F32)
    return result


class Ring:
    def __init__(self, batch, seq):
        self.batch, self.seq = batch, seq
        self.low = 2 ** ((seq.bit_length() - 1) // 2)
        self.sizes = {"core": 2, "near": batch // 2 * self.low, "far": seq // self.low}
        self.pieces = batch * seq

    def place(self, s, b):
        return {"core": b % 2, "near": b // 2 * self.low + s % self.low, "far": s // self.low}

    def device(self, place):
        s = place["far"] * self.low + place["near"] % self.low
        return s * self.batch + place["near"] // self.low * 2 + place["core"]

    def mine(self):
        return self.place(lax.axis_index("seq"), lax.axis_index("batch"))

    def swap(self, value, level, k):
        route = []
        for s in range(self.seq):
            for b in range(self.batch):
                place = self.place(s, b)
                place[level] ^= k
                route.append((s * self.batch + b, self.device(place)))
        return lax.ppermute(value, ("seq", "batch"), route)

    def scatter(self, value, level, fine=0, beside=()):
        size, me = self.sizes[level], self.mine()[level]
        value = value.reshape((size, value.shape[0] // size) + value.shape[1:])
        parts = [
            self.swap(lax.dynamic_index_in_dim(value, me ^ k, 0, False), level, k)
            for k in range(1, size)
        ]
        return self.add(lax.dynamic_index_in_dim(value, me, 0, False), parts, fine, beside)

    def scatter_cores(self, keep, send, fine=0, beside=()):
        return self.add(self.to_pieces(keep), [self.swap(self.to_pieces(send), "core", 1)], fine, beside)

    def add(self, value, parts, fine, beside):
        total = after(value, *beside).astype(F32)
        for part in parts:
            total = total + part.astype(F32)
        if not fine:
            return total.astype(BF16)
        end = total.shape[-1] - 2 * fine
        exact = total[..., end : end + fine] + total[..., end + fine :]
        high = lax.reduce_precision(exact, 8, 7)
        return jnp.concatenate([total[..., :end], high, exact - high], -1).astype(BF16)

    def gather(self, value, level, beside=()):
        parts = [self.swap(value, level, k) for k in range(1, self.sizes[level])]
        return join([after(value, *beside)] + parts)

    def to_pieces(self, value):
        return value.reshape(self.pieces // 2, -1, value.shape[1])

    def order(self):
        me = self.mine()
        piece = jnp.arange(self.pieces, dtype=jnp.int32)
        far, near = self.sizes["far"], self.sizes["near"]
        core = (piece // (far * near)) ^ me["core"]
        near = ((piece // far) % near) ^ me["near"]
        return (core * self.sizes["near"] + near) * far + ((piece % far) ^ me["far"])


def unpack_kernel(write, finish, order_ref, own_ref, other_ref, *out_refs):
    half = own_ref.shape[0]
    for piece in range(2 * half):
        at = order_ref[piece]

        @pl.when(at < half)
        def _(piece=piece, at=at):
            write(piece, own_ref[at].astype(F32), out_refs)

        @pl.when(at >= half)
        def _(piece=piece, at=at):
            write(piece, other_ref[at - half].astype(F32), out_refs)

    finish(out_refs)


def write_feed(piece, block, out_refs):
    in_ref, out_ref, down_ref = out_refs
    size, inner, width = block.shape[0], in_ref.shape[1], in_ref.shape[0]
    rows = slice(piece * size, (piece + 1) * size)
    in_ref[rows, :] = block[:, :inner]
    out_ref[rows, :] = block[:, inner : inner + width]
    tall_rows = inner // (width // size)
    for below in range(0, tall_rows, size):
        at = inner + width + below // size * width
        down_ref[piece * tall_rows + below : piece * tall_rows + below + size, :] = block[
            :, at : at + width
        ]


def write_project(piece, block, out_refs):
    w_ref, small = out_refs[0], out_refs[-1]
    size, end = block.shape[0], w_ref.shape[1]
    rows = slice(piece * size, (piece + 1) * size)
    w_ref[rows, :] = block[:, :end]
    if piece * size < small.shape[0]:
        small[rows, :] = block[:, end : end + PAIR] + block[:, end + PAIR :]


def finish_project(out_refs):
    small, at = out_refs[-1], 0
    for vector in out_refs[1:-2]:
        for lane in range(0, vector.shape[0], PAIR):
            vector[lane : lane + PAIR] = small[at, :]
            at += 1
    blend = out_refs[-2]
    blend[...] = small[at : at + 3, : blend.shape[1]]


def unpack(write, order, halves, shapes, finish=lambda refs: None, scratch=()):
    vmem = pl.BlockSpec(memory_space=pltpu.VMEM)
    return pl.pallas_call(
        functools.partial(unpack_kernel, write, finish),
        out_shape=[jax.ShapeDtypeStruct(shape, F32) for shape in shapes],
        in_specs=[pl.BlockSpec(memory_space=pltpu.SMEM), vmem, vmem],
        out_specs=[vmem] * len(shapes),
        scratch_shapes=scratch,
        compiler_params=pltpu.CompilerParams(vmem_limit_bytes=VMEM),
        cost_estimate=BRIEF,
    )(order, *halves)


def local(
    inputs,
    cotangent,
    lengths,
    norm1_gain,
    norm1_bias,
    qkv_weight,
    blend_weights,
    out_weight,
    norm2_gain,
    norm2_bias,
    in_weight,
    in_bias,
    down_weight,
    down_bias,
):
    seqs, span, width = inputs.shape
    heads = blend_weights.shape[1]
    devices = lax.axis_size("seq")
    parts = devices // seqs
    rows = seqs * span
    index = lax.axis_index("seq")
    groups = None
    if parts > 1:
        groups = [[r * seqs + s for s in range(seqs)] for r in range(parts)]
    mine, part = index % seqs, index // seqs
    meta = jnp.stack([lax.dynamic_index_in_dim(lengths, mine, 0, False), part * rows])
    blend = jnp.repeat(blend_weights, width // heads, axis=1)

    ring = Ring(lax.axis_size("batch"), devices)
    by_ring = width % (16 * ring.pieces) == 0
    inner = in_weight.shape[1]

    x = to_sequences(inputs, "seq", groups).reshape(rows, width)
    grad_out = to_sequences(cotangent, "seq", groups).reshape(rows, width)

    normed = layer_norm(x.astype(F32), norm1_gain, norm1_bias).astype(BF16)
    qkv = times(normed, qkv_weight).astype(BF16)
    halo = state = later = None
    if parts > 1:
        state = later = jnp.zeros((2, width // PAIR, PAIR, 2 * PAIR), F32)
        onward = [(i, i + seqs) for i in range(devices - seqs)]
        halo = lax.ppermute(qkv[rows - TILE :, width:], "seq", onward)
        total = attend(meta, blend, qkv, halo, state)[1]
        state = from_parts(total, "seq", parts, seqs, True)
    attended = attend(meta, blend, qkv, halo, state)[0]

    core = (lax.axis_index("batch") % 2)[None] if by_ring else jnp.zeros(1, jnp.int32)
    result, grad_first, grad_o, feed_keep, feed_send, small2, grad_in_b = feed_forward(
        ring.pieces if by_ring else 16,
        core, x, attended, grad_out, out_weight, norm2_gain, norm2_bias,
        in_weight, in_bias, down_weight, down_bias,
    )
    output = to_sequences(result.reshape(seqs, span, width), "seq", groups)
    def unpack_feed(order, halves):
        shapes = [(width, inner), (width, width), (inner, width)]
        return unpack(write_feed, order, halves, shapes)

    calls = 4

    def back(meta, number, later):
        return attend_back(meta, blend, qkv, halo, state, later, grad_o, calls, number)

    if parts > 1:
        total = jnp.concatenate([back(meta, number, later)[6] for number in range(calls)], 1)
        later = from_parts(total, "seq", parts, seqs, False)
    backs, turn = [], meta
    if by_ring:
        held = None
        for number in range(calls):
            if number == 1:
                held = ring.scatter_cores(feed_keep, feed_send, 0, (backs[0][3],))
                turn = after(turn, held)
            backs.append(back(turn, number, later))
            turn = after(turn, backs[-1][3])
        held = ring.scatter(held, "near", 0, (backs[3][3],))
        output = settle(after(output, backs[2][3]))
        grad_first = after(grad_first, held, output)
    else:
        backs = [back(meta, number, later) for number in range(calls)]
    grads = [[call[part] for call in backs] for part in range(3)]
    if parts > 1:
        homeward = [(i + seqs, i) for i in range(devices - seqs)]
        for part in (1, 2):
            for number in range(calls):
                received = lax.ppermute(backs[number][part + 3], "seq", homeward)
                grad = grads[part][number]
                tail = grad[rows - TILE :].astype(F32) + received.astype(F32)
                grads[part][number] = grad.at[rows - TILE :].set(tail.astype(BF16))
    grads = grads[0] + grads[1] + grads[2]
    grad_x, project_keep, project_send = project_back(
        core, x, grad_first, qkv_weight, norm1_gain, norm1_bias, small2, grad_in_b, grads,
        [call[3] for call in backs],
    )

    def move(grad_x):
        return to_sequences(grad_x.reshape(seqs, span, width), "seq", groups)

    if by_ring:
        order = ring.order()
        held = ring.scatter(held, "far", 0, (project_keep,))
        late = ring.scatter_cores(project_keep, project_send, PAIR, (held,))
        held = ring.gather(held, "far")
        moved = move(after(grad_x, late))
        near = [ring.swap(held, "near", k) for k in range(1, ring.sizes["near"])]
        late = ring.scatter(late, "near", PAIR, (held,))
        late = ring.scatter(late, "far", PAIR)
        late = ring.gather(late, "far")
        last = [ring.swap(late, "near", k) for k in range(1, ring.sizes["near"])]
        input_grad = settle(after(moved, late))
        held = join([after(held, late, input_grad)] + near)
        other = ring.swap(held, "core", 1)
        late = join([after(late, held)] + last)
        rest = ring.swap(late, "core", 1)
        grad_in_w, grad_out_w, grad_down_w = unpack_feed(order, (held, after(other, late)))
        project_halves = after(late, grad_out_w), rest
    else:
        input_grad = move(grad_x)
        order = jnp.arange(16, dtype=jnp.int32)
        halves = (feed_keep, feed_send, project_keep, project_send)
        halves = lax.psum([half.astype(F32) for half in halves], ("seq", "batch"))
        halves = [half.reshape(8, width // 16, -1) for half in halves]
        feed_halves, project_halves = halves[:2], halves[2:]
        grad_in_w, grad_out_w, grad_down_w = unpack_feed(order, feed_halves)
    vectors = [(width,)] * 5 + [(inner,)]
    lines = sum(size for (size,) in vectors) // PAIR + 3
    lines += -lines % (width // order.shape[0])
    grad_qkv_w, gain1, bias1, gain2, bias2, grad_down_b, grad_in_b, grad_blend = unpack(
        write_project, order, project_halves, [(width, 3 * width)] + vectors + [(3, heads)],
        finish_project, [pltpu.VMEM((lines, PAIR), F32)],
    )
    return (
        output,
        input_grad,
        gain1,
        bias1,
        grad_qkv_w,
        grad_blend,
        grad_out_w,
        gain2,
        bias2,
        grad_in_w,
        grad_in_b,
        grad_down_w,
        grad_down_b,
    )


def solution(mesh):
    rows = P("batch", "seq", None)
    return jax.shard_map(
        local,
        mesh=mesh,
        in_specs=(rows, rows, P("batch")) + (P(),) * 11,
        out_specs=(rows, rows) + (P(),) * 11,
        check_vma=False,
    )
```

```python
import functools

import jax
import jax.numpy as jnp
from jax import lax
from jax.experimental import pallas as pl
from jax.experimental.pallas import tpu as pltpu
from jax.sharding import PartitionSpec as P

WINDOW = 30
HEAD = 64
PAIR = 2 * HEAD
TILE = 64
EPS = 1e-05
NEG = -1e30
VMEM = 58 * 2**20
BRIEF = pl.CostEstimate(flops=1000, bytes_accessed=1000, transcendentals=0)
BF16 = jnp.bfloat16
F32 = jnp.float32


def layer_norm(field, gain, shift):
    center = field - jnp.mean(field, axis=-1, keepdims=True)
    spread = jnp.mean(center * center, axis=-1, keepdims=True)
    return center * lax.rsqrt(spread + EPS) * gain + shift


def rows_product(left, right):
    return lax.dot_general(
        left, right, (((0,), (0,)), ((), ())), preferred_element_type=F32
    )


def times_transposed(left, right):
    return lax.dot_general(
        left, right, (((1,), (1,)), ((), ())), preferred_element_type=F32
    )


def times(left, right):
    return lax.dot_general(
        left, right, (((1,), (0,)), ((), ())), preferred_element_type=F32
    )


def elu_feature(field):
    return jnp.where(field > 0, field + 1.0, jnp.exp(jnp.minimum(field, 0.0)))


def tanh_feature(field):
    return 1.0 + jnp.tanh(field)


def pair_lanes(p, part=0, width=PAIR):
    return slice(p * width + part * PAIR, p * width + (part + 1) * PAIR)


def store_split(ref, index, rows, block):
    lane = lax.broadcasted_iota(jnp.int32, (block.shape[0], PAIR), 1)
    for p in range(block.shape[1] // PAIR):
        pair = block[:, pair_lanes(p)]
        for h in range(2):
            mine = (lane < HEAD) if h == 0 else (lane >= HEAD)
            ref[index + (rows, pair_lanes(p, h, 2 * PAIR))] = jnp.where(mine, pair, 0.0).astype(
                BF16
            )


def load_split(ref, index, rows, p):
    return jnp.concatenate([ref[index + (rows, pair_lanes(p, h, 2 * PAIR))] for h in range(2)], 0)


def tall(block):
    return jnp.concatenate([block[:, :PAIR], block[:, PAIR:]], 0)


def width_of(ref):
    return ref.shape[1]


def blend_rows(blend_ref, first):
    lane = lax.broadcasted_iota(jnp.int32, (1, PAIR), 1)

    def row(branch, pair):
        head = 2 * (first + pair)
        return jnp.where(lane < HEAD, blend_ref[branch, head], blend_ref[branch, head + 1])

    return row


def fill_features(meta_ref, q_ref, k_ref, v_ref, halo_k, halo_v, keys, values, fq, fk, split):
    rows, width = q_ref.shape
    chunk = 2 * TILE
    front = pl.ds(0, TILE)
    keys[front, :] = jnp.zeros((TILE, 2 * width), BF16)
    values[front, :] = jnp.zeros((TILE, 2 * width), BF16)
    fk[:, front, :] = jnp.zeros((2, TILE, 2 * width), BF16)
    if halo_k is not None:
        store_split(keys, (), front, halo_k[...].astype(F32) * 0.125)
        store_split(values, (), front, halo_v[...].astype(F32))

    def fill(step, carry):
        at = pl.multiple_of(step * chunk, chunk)
        here, there = pl.ds(at, chunk), pl.ds(at + TILE, chunk)
        q = q_ref[here, :].astype(F32)
        k = k_ref[here, :].astype(F32)
        store_split(keys, (), there, k * 0.125)
        store_split(values, (), there, v_ref[here, :].astype(F32))
        position = meta_ref[1] + at + lax.broadcasted_iota(jnp.int32, (chunk, width), 0)
        valid = position < meta_ref[0]
        for c, feature in enumerate((elu_feature, tanh_feature)):
            if split:
                store_split(fq, (c,), here, feature(q))
            else:
                fq[c, here, :] = feature(q).astype(BF16)
            store_split(fk, (c,), there, jnp.where(valid, feature(k), 0.0))
        return carry

    lax.fori_loop(0, rows // chunk, fill, 0)


def tile_masks(meta_ref, tile):
    shape = (TILE, 2 * PAIR)
    row = lax.broadcasted_iota(jnp.int32, shape, 0)
    lane = lax.broadcasted_iota(jnp.int32, shape, 1) % PAIR
    back = row + TILE - lane
    key = meta_ref[1] + (tile - 1) * TILE + lane
    known = (key >= 0) & (key < meta_ref[0])
    near = (back >= 0) & (back <= WINDOW) & (known | (back == 0))
    return near, back >= 0


def softmax_pair(scores):
    halves = []
    for h in range(2):
        part = scores[:, h * PAIR : (h + 1) * PAIR]
        part = jnp.exp(part - jnp.max(part, axis=1, keepdims=True))
        halves.append(part * (1.0 / jnp.sum(part, axis=1, keepdims=True)))
    return jnp.concatenate(halves, 1)


def tile_constants():
    row = lax.broadcasted_iota(jnp.int32, (2 * PAIR, PAIR), 0)
    lane = lax.broadcasted_iota(jnp.int32, (2 * PAIR, PAIR), 1)
    ones = jnp.where(row // PAIR == lane // HEAD, 1.0, 0.0).astype(BF16)
    row = lax.broadcasted_iota(jnp.int32, (PAIR, 2 * PAIR), 0)
    lane = lax.broadcasted_iota(jnp.int32, (PAIR, 2 * PAIR), 1)
    return ones, row // HEAD == (lane % PAIR) // HEAD


def whole(split):
    half = split.shape[0] // 2
    return split[:half] + split[half:]


def state_share(block, fks, vs):
    ones = jnp.ones((TILE, PAIR), BF16)
    share = rows_product(whole(fks), jnp.concatenate([whole(vs), ones], 1))
    return jnp.where(block, share, 0.0)


def attend_kernel(
    together, whole_sequence, place_ref, lengths_ref, blend_ref, q_ref, k_ref, v_ref, *refs
):
    halo_k, halo_v, state_ref = (None,) * 3 if whole_sequence else refs[:3]
    meta_ref = lengths_ref[place_ref[0]], place_ref[1]
    blend_at = blend_rows(blend_ref, pl.program_id(0) * (width_of(q_ref) // PAIR))
    att_ref, keys, values, fq, fk, state = refs[-6:] if whole_sequence else refs[3:4] + refs[-5:]
    total_ref = None if whole_sequence else refs[4]
    rows, width = q_ref.shape
    pairs = range(width // PAIR)
    near_by = range(together)
    units = [(s, p) for s in near_by for p in pairs]
    fill_features(meta_ref, q_ref, k_ref, v_ref, halo_k, halo_v, keys, values, fq, fk, False)
    state[...] = jnp.zeros_like(state) if whole_sequence else state_ref[...]
    ones, block = tile_constants()

    def step(number, carry):
        first = number * together
        at = pl.multiple_of(first * TILE, TILE)
        here = [pl.ds(at + s * TILE, TILE) for s in near_by]
        window = [pl.ds(at + s * TILE, 2 * TILE) for s in near_by]
        masks = [tile_masks(meta_ref, first + s) for s in near_by]
        q = {(s, p): q_ref[here[s], pair_lanes(p)] for s, p in units}
        feats = {(s, p): [fq[c, here[s], pair_lanes(p)] for c in range(2)] for s, p in units}
        ks = {(s, p): load_split(keys, (), window[s], p) for s, p in units}
        fks = {(s, p): [load_split(fk, (c,), window[s], p) for c in range(2)] for s, p in units}
        wide = {
            (s, p): jnp.concatenate([load_split(values, (), window[s], p), ones], 1)
            for s, p in units
        }
        held = {(0, p): [state[c, p] for c in range(2)] for p in pairs}
        for s, p in units:
            vs = load_split(values, (), here[s], p)
            held[s + 1, p] = [
                held[s, p][c] + state_share(block, load_split(fk, (c,), here[s], p), vs)
                for c in range(2)
            ]
        near = {u: times_transposed(q[u], ks[u]) for u in units}
        far = {u: [times_transposed(feats[u][c], fks[u][c]) for c in range(2)] for u in units}
        old = {u: [times(feats[u][c], held[u][c].astype(BF16)) for c in range(2)] for u in units}
        near = {u: softmax_pair(jnp.where(masks[u[0]][0], near[u], NEG)) for u in units}
        far = {u: [jnp.where(masks[u[0]][1], f, 0.0) for f in far[u]] for u in units}
        stack = {u: jnp.concatenate([near[u]] + far[u], 0).astype(BF16) for u in units}
        sums = {u: times(stack[u], wide[u]) for u in units}
        for s, p in units:
            u, lanes = (s, p), pair_lanes(p)
            mixed = blend_at(0, p) * sums[u][:TILE, :PAIR]
            for c in range(2):
                mine = sums[u][(c + 1) * TILE : (c + 2) * TILE] + old[u][c]
                mixed = mixed + blend_at(c + 1, p) * (
                    mine[:, :PAIR] / mine[:, PAIR:]
                )
            att_ref[here[s], lanes] = mixed.astype(BF16)
        for p in pairs:
            for c in range(2):
                state[c, p] = held[together, p][c]
        return carry

    lax.fori_loop(0, rows // (together * TILE), step, 0)
    if whole_sequence:
        return
    last = pl.ds(rows, TILE)
    for p in pairs:
        for c in range(2):
            total_ref[c, p] = state[c, p] + state_share(
                block, load_split(fk, (c,), last, p), load_split(values, (), last, p)
            )


def slopes_of(field):
    small = jnp.exp(jnp.minimum(field, 0.0))
    bent = jnp.tanh(field)
    return [jnp.where(field > 0, 1.0, small), 1.0 - bent * bent]


def split_heads(block):
    lane = lax.broadcasted_iota(jnp.int32, block.shape, 1)
    zero = jnp.zeros_like(block)
    return jnp.concatenate(
        [jnp.where(lane < HEAD, block, zero), jnp.where(lane < HEAD, zero, block)], 0
    )


def attend_back_kernel(
    together, number, whole_sequence, place_ref, lengths_ref, blend_ref, q_ref, k_ref, v_ref, go_ref, *refs
):
    meta_ref = lengths_ref[place_ref[0]], place_ref[1]
    blend_at = blend_rows(blend_ref, number * (width_of(q_ref) // PAIR))
    halo_k, halo_v, state_ref, later_ref = (None,) * 4 if whole_sequence else refs[:4]
    if whole_sequence:
        gq_ref, gk_ref, gv_ref, mix_ref = refs[:4]
    else:
        gq_ref, gk_ref, gv_ref, mix_ref, hk_ref, hv_ref, total_ref = refs[4:11]
    keys, values, fq, fk, state, gk, gv, gfk, gon = refs[-9:]
    rows, width = q_ref.shape
    pairs = range(width // PAIR)
    tiles = rows // TILE
    near_by = range(together)
    units = [(s, p) for s in near_by for p in pairs]
    fill_features(meta_ref, q_ref, k_ref, v_ref, halo_k, halo_v, keys, values, fq, fk, True)
    state[...] = jnp.zeros_like(state) if whole_sequence else state_ref[...]
    mix_ref[...] = jnp.zeros_like(mix_ref)
    gk[:TILE, :] = jnp.zeros((TILE, width), F32)
    gv[:TILE, :] = jnp.zeros((TILE, width), F32)
    gfk[:, :TILE, :] = jnp.zeros((2, TILE, width), F32)
    ones, block = tile_constants()
    row = lax.broadcasted_iota(jnp.int32, (2 * PAIR, PAIR), 0) % PAIR
    lane = lax.broadcasted_iota(jnp.int32, (2 * PAIR, PAIR), 1)
    heads = jnp.where(row // HEAD == lane // HEAD, 1.0, 0.0).astype(BF16)
    plain_ones = jnp.ones((TILE, PAIR), BF16)
    high = (lax.broadcasted_iota(jnp.int32, (TILE, PAIR), 1) % HEAD) < HEAD // 2

    def step(turn, carry):
        first = turn * together
        at = pl.multiple_of(first * TILE, TILE)
        here = [pl.ds(at + s * TILE, TILE) for s in range(together + 1)]
        window = [pl.ds(at + s * TILE, 2 * TILE) for s in near_by]
        masks = [tile_masks(meta_ref, first + s) for s in near_by]
        q = {(s, p): q_ref[here[s], pair_lanes(p)] for s, p in units}
        go = {(s, p): go_ref[here[s], pair_lanes(p)] for s, p in units}
        blend = [[blend_at(c, p) for c in range(3)] for p in pairs]
        fqs = {(s, p): [load_split(fq, (c,), here[s], p) for c in range(2)] for s, p in units}
        feats = {u: [whole(f) for f in fqs[u]] for u in units}
        ks = {(s, p): load_split(keys, (), window[s], p) for s, p in units}
        fks = {(s, p): [load_split(fk, (c,), window[s], p) for c in range(2)] for s, p in units}
        wide = {
            (s, p): jnp.concatenate([load_split(values, (), window[s], p), ones], 1)
            for s, p in units
        }
        held = {(0, p): [state[c, p] for c in range(2)] for p in pairs}
        for s, p in units:
            vs = load_split(values, (), here[s], p)
            held[s + 1, p] = [
                held[s, p][c] + state_share(block, load_split(fk, (c,), here[s], p), vs)
                for c in range(2)
            ]
        past = {u: [h.astype(BF16) for h in held[u]] for u in units}
        old_k = [gk[here[0], pair_lanes(p)] for p in pairs]
        old_v = [gv[here[0], pair_lanes(p)] for p in pairs]
        old_f = [[gfk[c, here[0], pair_lanes(p)] for c in range(2)] for p in pairs]

        near = {u: times_transposed(q[u], ks[u]) for u in units}
        far = {u: [times_transposed(feats[u][c], fks[u][c]) for c in range(2)] for u in units}
        old = {u: [times(feats[u][c], past[u][c]) for c in range(2)] for u in units}
        near = {u: softmax_pair(jnp.where(masks[u[0]][0], near[u], NEG)) for u in units}
        far = {u: [jnp.where(masks[u[0]][1], f, 0.0).astype(BF16) for f in far[u]] for u in units}
        stack = {u: jnp.concatenate([near[u].astype(BF16)] + far[u], 0) for u in units}
        sums = {u: times(stack[u], wide[u]) for u in units}
        scales, prods = {}, {}
        for u in units:
            outs = [sums[u][:TILE, :PAIR]]
            scales[u] = [jnp.broadcast_to(blend[u[1]][0], (TILE, PAIR))]
            for c in range(2):
                mine = sums[u][(c + 1) * TILE : (c + 2) * TILE] + old[u][c]
                inverse = 1.0 / mine[:, PAIR:]
                outs.append(mine[:, :PAIR] * inverse)
                scales[u].append(blend[u[1]][c + 1] * inverse)
            prods[u] = jnp.concatenate([go[u] * out for out in outs], 0)
        deltas = {}
        for u in units:
            low = prods[u].astype(BF16)
            rest = (prods[u] - low.astype(F32)).astype(BF16)
            deltas[u] = times(jnp.concatenate([low, rest], 1), heads)
        grads = {}
        for u in units:
            grads[u] = []
            for c in range(3):
                delta = scales[u][c] * deltas[u][c * TILE : (c + 1) * TILE] * (-2.0 / HEAD)
                delta_low = delta.astype(BF16).astype(F32)
                delta = jnp.where(high, delta_low, delta - delta_low)
                grads[u].append(jnp.concatenate([scales[u][c] * go[u], delta], 1).astype(BF16))
        back = {u: times_transposed(jnp.concatenate(grads[u], 0), wide[u]) for u in units}
        late = {u: [times_transposed(grads[u][c + 1], past[u][c]) for c in range(2)] for u in units}
        ds = {u: (near[u] * back[u][:TILE]).astype(BF16) for u in units}
        gas = {
            u: [
                jnp.where(masks[u[0]][1], back[u][(c + 1) * TILE : (c + 2) * TILE], 0.0).astype(BF16)
                for c in range(2)
            ]
            for u in units
        }
        gq_near = {u: times(ds[u], ks[u]) for u in units}
        gq_far = {u: [times(gas[u][c], fks[u][c]) + late[u][c] for c in range(2)] for u in units}
        new_k = {u: rows_product(tall(ds[u]), split_heads(q[u] * 0.125)) for u in units}
        new_f = {u: [rows_product(tall(gas[u][c]), fqs[u][c]) for c in range(2)] for u in units}
        new_v = {
            u: rows_product(
                jnp.concatenate([tall(stack[u][c * TILE : (c + 1) * TILE]) for c in range(3)], 0),
                jnp.concatenate([split_heads(g[:, :PAIR]) for g in grads[u]], 0),
            )
            for u in units
        }

        def overlap(old, new, p):
            parts = [old + new(0, p)[:TILE]]
            parts += [new(s, p)[TILE:] + new(s + 1, p)[:TILE] for s in range(together - 1)]
            return parts + [new(together - 1, p)[TILE:]]

        for s, p in units:
            u, lanes = (s, p), pair_lanes(p)
            slopes = slopes_of(q[u].astype(F32))
            gq = gq_near[u] + slopes[0] * gq_far[u][0] + slopes[1] * gq_far[u][1]
            gq_ref[here[s], lanes] = gq.astype(BF16)
            for c in range(2):
                gon[c, here[s], p * 2 * PAIR : (p + 1) * 2 * PAIR] = grads[u][c + 1]
        for p in pairs:
            lanes = pair_lanes(p)
            for c in range(3):
                mix_ref[c : c + 1, lanes] += sum(
                    jnp.sum(prods[s, p][c * TILE : (c + 1) * TILE], axis=0, keepdims=True)
                    for s in near_by
                )
            for rows_at, part in zip(here, overlap(old_k[p], lambda s, p: new_k[s, p], p)):
                gk[rows_at, lanes] = part
            for rows_at, part in zip(here, overlap(old_v[p], lambda s, p: new_v[s, p], p)):
                gv[rows_at, lanes] = part
            for c in range(2):
                parts = overlap(old_f[p][c], lambda s, p: new_f[s, p][c], p)
                for rows_at, part in zip(here, parts):
                    gfk[c, rows_at, lanes] = part
                state[c, p] = held[together, p][c]
        return carry

    lax.fori_loop(0, tiles // together, step, 0)
    if not whole_sequence:
        hk_ref[...] = gk[:TILE, :].astype(BF16)
        hv_ref[...] = gv[:TILE, :].astype(BF16)
    state[...] = jnp.zeros_like(state) if whole_sequence else later_ref[...]

    def come(at, c, p):
        here = pl.ds(at, TILE)
        grads = gon[c, here, p * 2 * PAIR : (p + 1) * 2 * PAIR]
        share = rows_product(whole(load_split(fq, (c,), here, p)), grads)
        return jnp.where(block, share, 0.0)

    def back_step(turn, carry):
        first = tiles - 1 - turn * together
        at = [pl.multiple_of((first - s) * TILE, TILE) for s in near_by]
        here = [pl.ds(a, TILE) for a in at]
        there = [pl.ds(a + TILE, TILE) for a in at]
        held = {(-1, p): [state[c, p] for c in range(2)] for p in pairs}
        for s, p in units:
            tile = first - s + 2
            nearer = pl.multiple_of(jnp.minimum(tile, tiles - 1) * TILE, TILE)
            held[s, p] = [
                held[s - 1, p][c] + jnp.where(tile < tiles, come(nearer, c, p), 0.0)
                for c in range(2)
            ]
        later = {u: [h.astype(BF16) for h in held[u]] for u in units}
        vs = {(s, p): whole(load_split(values, (), there[s], p)) for s, p in units}
        fks = {
            (s, p): jnp.concatenate([whole(load_split(fk, (c,), there[s], p)) for c in range(2)], 1)
            for s, p in units
        }
        wide = {u: jnp.concatenate([vs[u], plain_ones], 1) for u in units}
        far_k = {u: [times_transposed(wide[u], later[u][c]) for c in range(2)] for u in units}
        far_v = {
            u: times(fks[u], jnp.concatenate([g[:, :PAIR] for g in later[u]], 0)) for u in units
        }
        for s, p in units:
            u, lanes = (s, p), pair_lanes(p)
            position = meta_ref[1] + at[s] + lax.broadcasted_iota(jnp.int32, (TILE, PAIR), 0)
            slopes = slopes_of(k_ref[here[s], lanes].astype(F32))
            grad_f = [gfk[c, there[s], lanes] + far_k[u][c] for c in range(2)]
            bent = slopes[0] * grad_f[0] + slopes[1] * grad_f[1]
            grad_k = gk[there[s], lanes] + jnp.where(position < meta_ref[0], bent, 0.0)
            gk_ref[here[s], lanes] = grad_k.astype(BF16)
            gv_ref[here[s], lanes] = (gv[there[s], lanes] + far_v[u]).astype(BF16)
        for p in pairs:
            for c in range(2):
                state[c, p] = held[together - 1, p][c]
        return carry

    lax.fori_loop(0, tiles // together, back_step, 0)
    if whole_sequence:
        return
    for p in pairs:
        for c in range(2):
            total_ref[c, p] = state[c, p] + come(0, c, p) + come(TILE, c, p)


def attention_specs(rows, width, lanes, number):
    calls = width // lanes

    def columns(height, part):
        return pl.BlockSpec((height, lanes), lambda i: (0, part * calls + number(i)))

    state = pl.BlockSpec(
        (2, lanes // PAIR, PAIR, 2 * PAIR), lambda i: (0, number(i), 0, 0)
    )
    ins = [pl.BlockSpec(memory_space=pltpu.SMEM)] * 3
    ins += [columns(rows, part) for part in range(3)]
    return columns, ins, [columns(TILE, part) for part in range(2)] + [state]


def attention_scratch(rows, lanes, split):
    return [
        pltpu.VMEM((rows + TILE, 2 * lanes), BF16),
        pltpu.VMEM((rows + TILE, 2 * lanes), BF16),
        pltpu.VMEM((2, rows, (2 if split else 1) * lanes), BF16),
        pltpu.VMEM((2, rows + TILE, 2 * lanes), BF16),
        pltpu.VMEM((2, lanes // PAIR, PAIR, 2 * PAIR), F32),
    ]


def outcome(shape, dtype):
    return jax.ShapeDtypeStruct(shape, dtype), pl.BlockSpec(shape, lambda _: (0,) * len(shape))


UNITS = 16


def together(rows, lanes):
    return min(UNITS * PAIR // lanes, rows // TILE)


def attend(place, lengths, blend, qkv, halo, state):
    rows, width = qkv.shape[0], qkv.shape[1] // 3
    lanes = PAIR
    columns, ins, before = attention_specs(rows, width, lanes, lambda i: i)
    held = before[-1]
    share = (2, width // PAIR, PAIR, 2 * PAIR)
    earlier = () if state is None else (halo, halo, state)
    return pl.pallas_call(
        functools.partial(attend_kernel, together(rows, lanes), state is None),
        grid=(width // lanes,),
        out_shape=(
            jax.ShapeDtypeStruct((rows, width), BF16),
            jax.ShapeDtypeStruct(share, F32),
        )[: 1 if state is None else 2],
        in_specs=ins + before[: len(earlier)],
        out_specs=(columns(rows, 0), held)[: 1 if state is None else 2],
        scratch_shapes=attention_scratch(rows, lanes, False),
        compiler_params=pltpu.CompilerParams(vmem_limit_bytes=VMEM),
        cost_estimate=BRIEF,
    )(place, lengths, blend, qkv, qkv, qkv, *earlier)


def attend_back(place, lengths, blend, qkv, halo, state, later, go, calls, number):
    rows, width = qkv.shape[0], qkv.shape[1] // 3
    lanes = width // calls
    columns, ins, before = attention_specs(rows, width, lanes, lambda i: number)
    others = () if state is None else (halo, halo, state, later)
    outs = [outcome((rows, lanes), BF16)] * 3 + [outcome((3, lanes), F32)]
    if state is not None:
        outs += [outcome((TILE, lanes), BF16)] * 2
        outs += [outcome((2, lanes // PAIR, PAIR, 2 * PAIR), F32)]
    shapes, blocks = zip(*outs)
    return pl.pallas_call(
        functools.partial(attend_back_kernel, together(rows, lanes), number, state is None),
        grid=(1,),
        out_shape=shapes,
        in_specs=ins + [columns(rows, 0)] + (before + before[-1:])[: len(others)],
        out_specs=blocks,
        scratch_shapes=attention_scratch(rows, lanes, True)
        + [
            pltpu.VMEM((rows + TILE, lanes), F32),
            pltpu.VMEM((rows + TILE, lanes), F32),
            pltpu.VMEM((2, rows + TILE, lanes), F32),
            pltpu.VMEM((2, rows, 2 * lanes), BF16),
        ],
        compiler_params=pltpu.CompilerParams(vmem_limit_bytes=VMEM),
        cost_estimate=BRIEF,
    )(place, lengths, blend, qkv, qkv, qkv, go, *others)


CHUNK = 512
GELU_A, GELU_B = 0.7978845608028654, 0.044715


def normalized(field):
    center = field - jnp.mean(field, axis=-1, keepdims=True)
    scale = lax.rsqrt(jnp.mean(center * center, axis=-1, keepdims=True) + EPS)
    return center * scale, scale


def norm_back(grad, unit, scale):
    shared = jnp.mean(grad * unit, axis=-1, keepdims=True)
    return scale * (grad - jnp.mean(grad, axis=-1, keepdims=True) - unit * shared)


def gelu_pair(field):
    square = field * field
    bent = jnp.tanh(GELU_A * field * (1.0 + GELU_B * square))
    half = 0.5 + 0.5 * bent
    slope = half + 0.5 * field * (1.0 - bent * bent) * (GELU_A + 3.0 * GELU_A * GELU_B * square)
    return field * half, slope


def column_sum(block):
    return jnp.sum(block, axis=0, keepdims=True)


def enter_kernel(place_ref, w_ref, gain_ref, bias_ref, *refs):
    parts, x_ref, qkv_ref, whole_x = refs[:-3], refs[-3], refs[-2], refs[-1]
    span, chunk = parts[0].shape[0], x_ref.shape[0]

    @pl.when(pl.program_id(0) == 0)
    def _():
        for k, part in enumerate(parts):
            at = lax.rem(place_ref[0] + len(parts) - k, len(parts)) * span
            whole_x[pl.ds(pl.multiple_of(at, span), span), :] = part[...]

    x = whole_x[pl.ds(pl.multiple_of(pl.program_id(0) * chunk, chunk), chunk), :]
    x_ref[...] = x
    unit, _ = normalized(x.astype(F32))
    low = (unit * gain_ref[...] + bias_ref[...]).astype(BF16)
    qkv_ref[...] = times(low, w_ref[...]).astype(BF16)


def enter(place, parts, weight, gain, bias):
    span, width = parts[0].shape
    rows, lanes = span * len(parts), weight.shape[1]
    size = min(CHUNK, rows)
    return pl.pallas_call(
        enter_kernel,
        grid=(rows // size,),
        out_shape=(
            jax.ShapeDtypeStruct((rows, width), BF16),
            jax.ShapeDtypeStruct((rows, lanes), BF16),
        ),
        in_specs=[pl.BlockSpec(memory_space=pltpu.SMEM)]
        + [constant(a.shape) for a in (weight, gain[None], bias[None], *parts)],
        out_specs=(by_rows(size, width), by_rows(size, lanes)),
        scratch_shapes=[pltpu.VMEM((rows, width), BF16)],
        compiler_params=pltpu.CompilerParams(vmem_limit_bytes=VMEM),
        cost_estimate=BRIEF,
    )(place, weight, gain[None], bias[None], *parts)


def deal(place_ref, rows, lanes, value, keep_ref, send_ref):
    half = value.shape[0] // 2

    @pl.when(place_ref[2] == 0)
    def _():
        keep_ref[rows, lanes] = value[:half]
        send_ref[rows, lanes] = value[half:]

    @pl.when(place_ref[2] != 0)
    def _():
        keep_ref[rows, lanes] = value[half:]
        send_ref[rows, lanes] = value[:half]


def feed_kernel(
    pieces, place_ref, x_ref, att_ref, grad_ref, out_from, gain_ref, bias_ref, in_from, in_b,
    down_from, down_b, result_to, first_to, go_to, keep_to, send_to, small_ref, wide_ref,
    second, hidden, pre_low, att_low, att_all, grad_all, out_w, in_w, down_w, keep_ref, send_ref,
    result_ref, first_ref, go_ref, in_sems, out_sems, row_sems,
):
    chunk, width = x_ref.shape
    inner = in_w.shape[1]
    number = pl.program_id(0)
    here = pl.ds(pl.multiple_of(number * chunk, chunk), chunk)
    tiles = [slice(at, at + width) for at in range(0, inner, width)]
    copies = [pltpu.make_async_copy(out_from, out_w, in_sems.at[0])]
    for i, lanes in enumerate(tiles):
        copies += [
            pltpu.make_async_copy(in_from.at[:, lanes], in_w.at[:, lanes], in_sems.at[2 * i + 1]),
            pltpu.make_async_copy(down_from.at[lanes, :], down_w.at[lanes, :], in_sems.at[2 * i + 2]),
        ]

    def arrived(i):
        @pl.when(number == 0)
        def _():
            copies[i].wait()

    @pl.when(number == 0)
    def _():
        for copy in copies:
            copy.start()
        small_ref[...] = jnp.zeros_like(small_ref)
        wide_ref[...] = jnp.zeros_like(wide_ref)

    att = att_ref[...]
    att_all[here, :] = att
    arrived(0)
    first = x_ref[...].astype(F32) + times(att, out_w[...])
    unit, scale = normalized(first)
    low = (unit * gain_ref[...] + bias_ref[...]).astype(BF16)
    second[here, :] = low
    grad = grad_ref[...]
    grad_all[here, :] = grad
    grad_f = grad.astype(F32)
    result = first + down_b[...]
    back = jnp.zeros((chunk, width), F32)
    for i, lanes in enumerate(tiles):
        arrived(2 * i + 1)
        arrived(2 * i + 2)
        act, slope = gelu_pair(times(low, in_w[:, lanes]) + in_b[:, lanes])
        act = act.astype(BF16)
        hidden[here, lanes] = act
        result = result + times(act, down_w[lanes, :])
        pre = (times_transposed(grad, down_w[lanes, :]) * slope).astype(BF16)
        pre_low[here, lanes] = pre
        wide_ref[:, lanes] += column_sum(pre.astype(F32))
        back = back + times_transposed(pre, in_w[:, lanes])
    result_ref[here, :] = result.astype(BF16)
    small_ref[0:1, :] += column_sum(back * unit)
    small_ref[1:2, :] += column_sum(back)
    small_ref[2:3, :] += column_sum(grad_f)
    grad_first = grad_f + norm_back(back * gain_ref[...], unit, scale)
    first_ref[here, :] = grad_first
    grad_att = grad_first.astype(BF16)
    att_low[here, :] = grad_att
    go_ref[here, :] = times_transposed(grad_att, out_w[...])
    pairs = ((result_ref, result_to), (first_ref, first_to), (go_ref, go_to))
    done = [
        pltpu.make_async_copy(inside.at[here, :], outside.at[here, :], row_sems.at[number, i])
        for i, (inside, outside) in enumerate(pairs)
    ]
    for copy in done:
        copy.start()

    @pl.when(number == pl.num_programs(0) - 1)
    def _():
        every = slice(0, width // 2)
        leaving = []

        def leave(lanes):
            for here, there in ((keep_ref, keep_to), (send_ref, send_to)):
                sem = out_sems.at[len(leaving)]
                copy = pltpu.make_async_copy(here.at[:, lanes], there.at[:, lanes], sem)
                copy.start()
                leaving.append(copy)

        flat, each, after_out = width // pieces, pieces, inner + width
        for block, lanes in enumerate(tiles):
            share = rows_product(hidden[:, lanes], grad_all[...]).astype(BF16)
            for below in range(each):
                piece, side = divmod(block * each + below, len(tiles))
                to = slice(after_out + side * width, after_out + (side + 1) * width)
                rows = slice(piece % (pieces // 2) * flat, (piece % (pieces // 2) + 1) * flat)
                mine = place_ref[2] == 2 * piece // pieces
                some = share[below * flat : (below + 1) * flat]

                @pl.when(mine)
                def _(rows=rows, to=to, some=some):
                    keep_ref[rows, to] = some

                @pl.when(jnp.logical_not(mine))
                def _(rows=rows, to=to, some=some):
                    send_ref[rows, to] = some

        leave(slice(after_out, after_out + inner))
        for lanes in tiles:
            share = rows_product(second[...], pre_low[:, lanes]).astype(BF16)
            deal(place_ref, every, lanes, share, keep_ref, send_ref)
            leave(lanes)
        share = rows_product(att_all[...], att_low[...]).astype(BF16)
        deal(place_ref, every, slice(inner, after_out), share, keep_ref, send_ref)
        leave(slice(inner, after_out))
        for copy in leaving:
            copy.wait()
        for step in range(att_all.shape[0] // chunk):
            rows = slice(step * chunk, (step + 1) * chunk)
            for i, (inside, outside) in enumerate(pairs):
                sem = row_sems.at[step, i]
                pltpu.make_async_copy(inside.at[rows, :], outside.at[rows, :], sem).wait()


def by_rows(height, width):
    return pl.BlockSpec((height, width), lambda i: (i, 0))


def constant(shape):
    return pl.BlockSpec(shape, lambda i: (0, 0))


def feed_forward(pieces, place, x, att, grad, out_w, gain, bias, in_w, in_b, down_w, down_b):
    rows, width = x.shape
    inner = in_w.shape[1]
    packed = (width // 2, 2 * inner + width)
    size = min(CHUNK, rows)
    block, far = by_rows(size, width), pl.BlockSpec(memory_space=pl.ANY)
    return pl.pallas_call(
        functools.partial(feed_kernel, pieces),
        grid=(rows // size,),
        out_shape=(
            jax.ShapeDtypeStruct((rows, width), BF16),
            jax.ShapeDtypeStruct((rows, width), F32),
            jax.ShapeDtypeStruct((rows, width), F32),
            jax.ShapeDtypeStruct(packed, BF16),
            jax.ShapeDtypeStruct(packed, BF16),
            jax.ShapeDtypeStruct((3, width), F32),
            jax.ShapeDtypeStruct((1, inner), F32),
        ),
        in_specs=[pl.BlockSpec(memory_space=pltpu.SMEM)]
        + [block] * 3
        + [far, constant((1, width)), constant((1, width)), far, constant((1, inner)), far]
        + [constant((1, width))],
        out_specs=(far,) * 5
        + (constant((3, width)), constant((1, inner))),
        scratch_shapes=[
            pltpu.VMEM((rows, width), BF16),
            pltpu.VMEM((rows, inner), BF16),
            pltpu.VMEM((rows, inner), BF16),
            pltpu.VMEM((rows, width), BF16),
            pltpu.VMEM((rows, width), BF16),
            pltpu.VMEM((rows, width), BF16),
            pltpu.VMEM(out_w.shape, BF16),
            pltpu.VMEM(in_w.shape, BF16),
            pltpu.VMEM(down_w.shape, BF16),
            pltpu.VMEM(packed, BF16),
            pltpu.VMEM(packed, BF16),
            pltpu.VMEM((rows, width), BF16),
            pltpu.VMEM((rows, width), F32),
            pltpu.VMEM((rows, width), F32),
            pltpu.SemaphoreType.DMA((1 + 2 * inner // width,)),
            pltpu.SemaphoreType.DMA((4 + 2 * inner // width,)),
            pltpu.SemaphoreType.DMA((rows // size, 3)),
        ],
        compiler_params=pltpu.CompilerParams(vmem_limit_bytes=VMEM),
        cost_estimate=BRIEF,
    )(place, x, att, grad, out_w, gain[None], bias[None], in_w, in_b[None], down_w, down_b[None])


def project_back_kernel(
    calls, place_ref, x_ref, first_ref, w_ref, gain_ref, bias_ref, small2_ref, wide_ref, *refs
):
    grads, mixes = refs[: 3 * calls], refs[3 * calls : 4 * calls]
    result_ref, keep_ref, send_ref, normed, gathered, sums, rows_of = refs[4 * calls :]
    chunk, width = x_ref.shape
    number = pl.program_id(0)
    here = pl.ds(pl.multiple_of(number * chunk, chunk), chunk)

    @pl.when(number == 0)
    def _():
        sums[...] = jnp.zeros_like(sums)

    unit, scale = normalized(x_ref[...].astype(F32))
    normed[here, :] = (unit * gain_ref[...] + bias_ref[...]).astype(BF16)
    grad = jnp.concatenate([ref[...] for ref in grads], 1)
    gathered[here, :] = grad
    back = times_transposed(grad, w_ref[...])
    sums[0:1, :] += column_sum(back * unit)
    sums[1:2, :] += column_sum(back)
    grad_x = first_ref[...] + norm_back(back * gain_ref[...], unit, scale)
    result_ref[...] = grad_x.astype(BF16)

    @pl.when(number == pl.num_programs(0) - 1)
    def _():
        every = slice(0, width // 2)
        rows_of[...] = jnp.zeros_like(rows_of)
        at = 0
        for ref in (sums, small2_ref, wide_ref):
            for row in range(ref.shape[0]):
                for lane in range(0, ref.shape[1], PAIR):
                    rows_of[at : at + 1, :] = ref[row : row + 1, lane : lane + PAIR]
                    at += 1
        lane = lax.broadcasted_iota(jnp.int32, (3, PAIR), 1)
        blend = jnp.zeros((3, PAIR), F32)
        head = 0
        for mix in mixes:
            for first in range(0, mix.shape[1], HEAD):
                mine = jnp.sum(mix[:, first : first + HEAD], axis=1, keepdims=True)
                blend = blend + jnp.where(lane == head, mine, 0.0)
                head += 1
        rows_of[at : at + 3, :] = blend
        exact = rows_of[...]
        high = exact.astype(BF16)
        low = (exact - high.astype(F32)).astype(BF16)
        for part, value in enumerate((high, low)):
            lanes = slice(3 * width + part * PAIR, 3 * width + (part + 1) * PAIR)
            deal(place_ref, every, lanes, value, keep_ref, send_ref)
        for at in range(0, 3 * width, width):
            lanes = slice(at, at + width)
            share = rows_product(normed[...], gathered[:, lanes]).astype(BF16)
            deal(place_ref, every, lanes, share, keep_ref, send_ref)


def project_back(place, x, grad_first, weight, gain, bias, small2, wide, grads, mixes):
    rows, width = x.shape
    calls = len(mixes)
    packed = (width // 2, 3 * width + 2 * PAIR)
    size = min(CHUNK, rows)
    block, chunk = by_rows(size, width), by_rows(size, width // calls)
    return pl.pallas_call(
        functools.partial(project_back_kernel, calls),
        grid=(rows // size,),
        out_shape=(jax.ShapeDtypeStruct((rows, width), BF16),)
        + (jax.ShapeDtypeStruct(packed, BF16),) * 2,
        in_specs=[pl.BlockSpec(memory_space=pltpu.SMEM), block, block]
        + [constant(a.shape) for a in (weight, gain[None], bias[None], small2, wide)]
        + [chunk] * (3 * calls)
        + [constant(mix.shape) for mix in mixes],
        out_specs=(block, constant(packed), constant(packed)),
        scratch_shapes=[
            pltpu.VMEM((rows, width), BF16),
            pltpu.VMEM((rows, 3 * width), BF16),
            pltpu.VMEM((2, width), F32),
            pltpu.VMEM((width, PAIR), F32),
        ],
        compiler_params=pltpu.CompilerParams(vmem_limit_bytes=VMEM),
        cost_estimate=BRIEF,
    )(place, x, grad_first, weight, gain[None], bias[None], small2, wide, *grads, *mixes)


def to_sequences(block, axis, groups):
    return lax.all_to_all(block, axis, 0, 0, axis_index_groups=groups)


def spans_of(block, axis, mine):
    seqs, devices = block.shape[0], lax.axis_size(axis)
    spans = []
    for k in range(seqs):
        span = lax.dynamic_index_in_dim(block, lax.rem(mine + k, seqs), 0, False)
        route = [(i, i // seqs * seqs + (i + k) % seqs) for i in range(devices)]
        spans.append(lax.ppermute(span, axis, route) if k else span)
    return spans


def after(value, *others):
    return lax.optimization_barrier((value,) + others)[0]


def join_kernel(placed, *refs):
    parts, outs = refs[: len(placed)], refs[len(placed) :]
    for part, places in zip(parts, placed):
        for source, out, to, lanes in places:
            outs[out][to, :, lanes] = part[source]


def join_to(parts, placed, shapes):
    vmem = pl.BlockSpec(memory_space=pltpu.VMEM)
    return pl.pallas_call(
        functools.partial(join_kernel, placed),
        out_shape=[jax.ShapeDtypeStruct(shape, parts[0].dtype) for shape in shapes],
        in_specs=[vmem] * len(parts),
        out_specs=[vmem] * len(shapes),
        compiler_params=pltpu.CompilerParams(vmem_limit_bytes=16 * 2**20),
        cost_estimate=BRIEF,
    )(*parts)


def split_kernel(count, *refs):
    first, second = refs[count:]
    size, _, lanes = refs[0].shape
    for k, part in enumerate(refs[:count]):
        first[k * size : (k + 1) * size] = part[:, :, : lanes // 2]
        second[k * size : (k + 1) * size] = part[:, :, lanes // 2 :]


def split_to(parts, shapes):
    vmem = pl.BlockSpec(memory_space=pltpu.VMEM)
    return pl.pallas_call(
        functools.partial(split_kernel, len(parts)),
        out_shape=[jax.ShapeDtypeStruct(shape, parts[0].dtype) for shape in shapes],
        in_specs=[vmem] * len(parts),
        out_specs=[vmem] * 2,
        compiler_params=pltpu.CompilerParams(vmem_limit_bytes=16 * 2**20),
        cost_estimate=BRIEF,
    )(*parts)


def join(parts):
    size, height, lanes = parts[0].shape
    placed = [
        [(slice(0, size), 0, slice(k * size, (k + 1) * size), slice(0, lanes))]
        for k in range(len(parts))
    ]
    return join_to(parts, placed, [(len(parts) * size, height, lanes)])[0]


def settle_kernel(source_ref, out_ref):
    out_ref[...] = source_ref[...]


def settle(value):
    vmem = pl.BlockSpec(memory_space=pltpu.VMEM)
    return pl.pallas_call(
        settle_kernel,
        out_shape=jax.ShapeDtypeStruct(value.shape, value.dtype),
        in_specs=[vmem],
        out_specs=vmem,
        compiler_params=pltpu.CompilerParams(vmem_limit_bytes=8 * 2**20),
        cost_estimate=BRIEF,
    )(value)


def from_parts(total, axis, parts, stride, forward):
    size = lax.axis_size(axis)
    low = total.astype(BF16)
    result = jnp.zeros_like(total)
    for hop in range(1, parts):
        distance = hop * stride
        route = [
            (i, i + distance) if forward else (i + distance, i) for i in range(size - distance)
        ]
        result = result + lax.ppermute(low, axis, route).astype(F32)
    return result


class Ring:
    def __init__(self, batch, seq):
        self.batch, self.seq = batch, seq
        self.low = 2 ** ((seq.bit_length() - 1) // 2)
        self.sizes = {"core": 2, "near": batch // 2 * self.low, "far": seq // self.low}
        self.pieces = batch * seq

    def place(self, s, b):
        return {"core": b % 2, "near": b // 2 * self.low + s % self.low, "far": s // self.low}

    def device(self, place):
        s = place["far"] * self.low + place["near"] % self.low
        return s * self.batch + place["near"] // self.low * 2 + place["core"]

    def mine(self):
        return self.place(lax.axis_index("seq"), lax.axis_index("batch"))

    def swap(self, value, level, k):
        route = []
        for s in range(self.seq):
            for b in range(self.batch):
                place = self.place(s, b)
                place[level] ^= k
                route.append((s * self.batch + b, self.device(place)))
        return lax.ppermute(value, ("seq", "batch"), route)

    def slices(self, value, level):
        size, me = self.sizes[level], self.mine()[level]
        value = value.reshape((size, value.shape[0] // size) + value.shape[1:])
        return [lax.dynamic_index_in_dim(value, me ^ k, 0, False) for k in range(size)]

    def scatter(self, value, level, fine=0, beside=()):
        slices = value if isinstance(value, list) else self.slices(value, level)
        parts = [self.swap(part, level, k) for k, part in enumerate(slices) if k]
        return self.add(slices[0], parts, fine, beside)

    def scatter_cores(self, keep, send, fine=0, beside=()):
        return self.add(self.to_pieces(keep), [self.swap(self.to_pieces(send), "core", 1)], fine, beside)

    def add(self, value, parts, fine, beside):
        total = after(value, *beside).astype(F32)
        for part in parts:
            total = total + part.astype(F32)
        if not fine:
            return total.astype(BF16)
        end = total.shape[-1] - 2 * fine
        exact = total[..., end : end + fine] + total[..., end + fine :]
        high = lax.reduce_precision(exact, 8, 7)
        return jnp.concatenate([total[..., :end], high, exact - high], -1).astype(BF16)

    def gather(self, value, level, beside=()):
        parts = [self.swap(value, level, k) for k in range(1, self.sizes[level])]
        return join([after(value, *beside)] + parts)

    def to_pieces(self, value):
        return value.reshape(self.pieces // 2, -1, value.shape[1])

    def gather_split(self, value, level, beside=()):
        parts = [after(value, *beside)]
        parts += [self.swap(value, level, k) for k in range(1, self.sizes[level])]
        size, height, lanes = value.shape
        shape = (len(parts) * size, height, lanes // 2)
        return split_to(parts, [shape, shape])

    def join_ways(self, halves, ways):
        size, height, half = halves[0].shape
        size //= 2
        placed = []
        for out_lanes, order in ((0, (0, 2)), (0, (1, 3)), (half, (0, 1)), (half, (2, 3))):
            lanes = slice(out_lanes, out_lanes + half)
            placed.append(
                [
                    (slice(i * size, (i + 1) * size), 0, slice(k * size, (k + 1) * size), lanes)
                    for i, k in enumerate(order)
                ]
            )
        parts = [halves[0], ways[0], halves[1], ways[1]]
        return join_to(parts, placed, [(4 * size, height, 2 * half)])[0]

    def code(self):
        me = self.mine()
        return (me["core"] * self.sizes["near"] + me["near"]) * self.sizes["far"] + me["far"]


def unpack_kernel(write, finish, place_ref, own_ref, other_ref, *out_refs):
    half = own_ref.shape[0]
    for piece in range(2 * half):
        at = place_ref[3] ^ piece

        @pl.when(at < half)
        def _(piece=piece, at=at):
            write(piece, own_ref[at].astype(F32), out_refs)

        @pl.when(at >= half)
        def _(piece=piece, at=at):
            write(piece, other_ref[at - half].astype(F32), out_refs)

    finish(out_refs)


def write_feed(piece, block, out_refs):
    in_ref, out_ref, down_ref = out_refs
    size, inner, width = block.shape[0], in_ref.shape[1], in_ref.shape[0]
    rows = slice(piece * size, (piece + 1) * size)
    in_ref[rows, :] = block[:, :inner]
    out_ref[rows, :] = block[:, inner : inner + width]
    tall_rows = inner // (width // size)
    for below in range(0, tall_rows, size):
        at = inner + width + below // size * width
        down_ref[piece * tall_rows + below : piece * tall_rows + below + size, :] = block[
            :, at : at + width
        ]


def write_project(piece, block, out_refs):
    w_ref, small = out_refs[0], out_refs[-1]
    size, end = block.shape[0], w_ref.shape[1]
    rows = slice(piece * size, (piece + 1) * size)
    w_ref[rows, :] = block[:, :end]
    if piece * size < small.shape[0]:
        small[rows, :] = block[:, end : end + PAIR] + block[:, end + PAIR :]


def finish_project(out_refs):
    small, at = out_refs[-1], 0
    for vector in out_refs[1:-2]:
        for lane in range(0, vector.shape[0], PAIR):
            vector[lane : lane + PAIR] = small[at, :]
            at += 1
    blend = out_refs[-2]
    blend[...] = small[at : at + 3, : blend.shape[1]]


def unpack(write, place, halves, shapes, finish=lambda refs: None, scratch=()):
    vmem = pl.BlockSpec(memory_space=pltpu.VMEM)
    return pl.pallas_call(
        functools.partial(unpack_kernel, write, finish),
        out_shape=[jax.ShapeDtypeStruct(shape, F32) for shape in shapes],
        in_specs=[pl.BlockSpec(memory_space=pltpu.SMEM), vmem, vmem],
        out_specs=[vmem] * len(shapes),
        scratch_shapes=scratch,
        compiler_params=pltpu.CompilerParams(vmem_limit_bytes=24 * 2**20),
        cost_estimate=BRIEF,
    )(place, *halves)


def local(
    inputs,
    cotangent,
    lengths,
    norm1_gain,
    norm1_bias,
    qkv_weight,
    blend_weights,
    out_weight,
    norm2_gain,
    norm2_bias,
    in_weight,
    in_bias,
    down_weight,
    down_bias,
):
    seqs, span, width = inputs.shape
    heads = blend_weights.shape[1]
    devices = lax.axis_size("seq")
    parts = devices // seqs
    rows = seqs * span
    index = lax.axis_index("seq")
    groups = None
    if parts > 1:
        groups = [[r * seqs + s for s in range(seqs)] for r in range(parts)]
    mine, part = index % seqs, index // seqs
    ring = Ring(lax.axis_size("batch"), devices)
    by_ring = width % (16 * ring.pieces) == 0
    inner = in_weight.shape[1]
    numbers = [mine, part * rows, 0, 0]
    if by_ring:
        numbers[2:] = [lax.axis_index("batch") % 2, ring.code()]
    place = jnp.stack([jnp.asarray(number, jnp.int32) for number in numbers])

    spans = spans_of(inputs, "seq", mine)
    x, qkv = enter(place, spans, qkv_weight, norm1_gain, norm1_bias)
    grad_out = to_sequences(after(cotangent, *spans), "seq", groups).reshape(rows, width)
    halo = state = later = None
    if parts > 1:
        state = later = jnp.zeros((2, width // PAIR, PAIR, 2 * PAIR), F32)
        onward = [(i, i + seqs) for i in range(devices - seqs)]
        halo = lax.ppermute(qkv[rows - TILE :, width:], "seq", onward)
        total = attend(place, lengths, blend_weights, qkv, halo, state)[1]
        state = from_parts(total, "seq", parts, seqs, True)
    attended = attend(place, lengths, blend_weights, qkv, halo, state)[0]

    result, grad_first, grad_o, feed_keep, feed_send, small2, grad_in_b = feed_forward(
        ring.pieces if by_ring else 16,
        place, x, attended, grad_out, out_weight, norm2_gain, norm2_bias,
        in_weight, in_bias, down_weight, down_bias,
    )

    def move(rows):
        return to_sequences(rows.reshape(seqs, span, width), "seq", groups)

    feed_shapes = [(width, inner), (width, width), (inner, width)]
    calls = 4

    def back(place, number, later):
        return attend_back(
            place, lengths, blend_weights, qkv, halo, state, later, grad_o, calls, number
        )

    if parts > 1:
        total = jnp.concatenate([back(place, number, later)[6] for number in range(calls)], 1)
        later = from_parts(total, "seq", parts, seqs, False)
    backs, turn = [], place
    if by_ring:
        held, output = None, move(result)
        for number in range(calls):
            if number == 1:
                held = ring.scatter_cores(feed_keep, feed_send, 0, (backs[0][3],))
                turn = after(turn, held)
            backs.append(back(turn, number, later))
            turn = after(turn, backs[-1][3])
        held = ring.scatter(held, "near", 0, (backs[3][3],))
        output = settle(after(output, backs[2][3]))
        grad_first = after(grad_first, held, output)
    else:
        backs = [back(place, number, later) for number in range(calls)]
        output = move(result)
    grads = [[call[part] for call in backs] for part in range(3)]
    if parts > 1:
        homeward = [(i + seqs, i) for i in range(devices - seqs)]
        for part in (1, 2):
            for number in range(calls):
                received = lax.ppermute(backs[number][part + 3], "seq", homeward)
                grad = grads[part][number]
                tail = grad[rows - TILE :].astype(F32) + received.astype(F32)
                grads[part][number] = grad.at[rows - TILE :].set(tail.astype(BF16))
    grads = grads[0] + grads[1] + grads[2]
    grad_x, project_keep, project_send = project_back(
        place, x, grad_first, qkv_weight, norm1_gain, norm1_bias, small2, grad_in_b, grads,
        [call[3] for call in backs],
    )

    if by_ring:
        held = ring.scatter(held, "far", 0, (project_keep,))
        late = ring.scatter_cores(project_keep, project_send, PAIR, (held,))
        late = ring.slices(late, "near")
        halves = ring.gather_split(held, "far", late)
        ways = [ring.swap(half, "near", k) for half, k in zip(halves, (2, 1))]
        late = ring.scatter(late, "near", PAIR)
        halves = [join([half, way]) for half, way in zip(halves, ways)]
        ways = [ring.swap(half, "near", k) for half, k in zip(halves, (1, 2))]
        late = ring.scatter(late, "far", PAIR, halves)
        late = ring.gather(late, "far")
        moved = move(after(grad_x, late))
        held = ring.join_ways([after(halves[0], late), halves[1]], ways)
        other = ring.swap(held, "core", 1)
        feed_grads = unpack(write_feed, place, (held, other), feed_shapes)
        late = ring.gather(late, "near", feed_grads)
        input_grad = settle(after(moved, late))
        halves = after(late, input_grad), ring.swap(late, "core", 1)
    else:
        input_grad = move(grad_x)
        halves = (feed_keep, feed_send, project_keep, project_send)
        halves = lax.psum([half.astype(F32) for half in halves], ("seq", "batch"))
        halves = [half.reshape(8, width // 16, -1) for half in halves]
        feed_grads = unpack(write_feed, place, halves[:2], feed_shapes)
        halves = halves[2:]
    grad_in_w, grad_out_w, grad_down_w = feed_grads
    vectors = [(width,)] * 5 + [(inner,)]
    lines = sum(size for (size,) in vectors) // PAIR + 3
    lines += -lines % (width // (2 * halves[0].shape[0]))
    grad_qkv_w, gain1, bias1, gain2, bias2, grad_down_b, grad_in_b, grad_blend = unpack(
        write_project, place, halves, [(width, 3 * width)] + vectors + [(3, heads)],
        finish_project, [pltpu.VMEM((lines, PAIR), F32)],
    )
    return (
        output,
        input_grad,
        gain1,
        bias1,
        grad_qkv_w,
        grad_blend,
        grad_out_w,
        gain2,
        bias2,
        grad_in_w,
        grad_in_b,
        grad_down_w,
        grad_down_b,
    )


def solution(mesh):
    rows = P("batch", "seq", None)
    return jax.shard_map(
        local,
        mesh=mesh,
        in_specs=(rows, rows, P("batch")) + (P(),) * 11,
        out_specs=(rows, rows) + (P(),) * 11,
        check_vma=False,
    )
```

```python
import functools

import jax
import jax.numpy as jnp
from jax import lax
from jax.experimental import pallas as pl
from jax.experimental.pallas import tpu as pltpu
from jax.sharding import PartitionSpec as P

WINDOW = 30
HEAD = 64
PAIR = 2 * HEAD
TILE = 64
EPS = 1e-05
NEG = -1e30
VMEM = 58 * 2**20
BRIEF = pl.CostEstimate(flops=1000, bytes_accessed=1000, transcendentals=0)
BF16 = jnp.bfloat16
F32 = jnp.float32


def layer_norm(field, gain, shift):
    center = field - jnp.mean(field, axis=-1, keepdims=True)
    spread = jnp.mean(center * center, axis=-1, keepdims=True)
    return center * lax.rsqrt(spread + EPS) * gain + shift


def rows_product(left, right):
    return lax.dot_general(
        left, right, (((0,), (0,)), ((), ())), preferred_element_type=F32
    )


def times_transposed(left, right):
    return lax.dot_general(
        left, right, (((1,), (1,)), ((), ())), preferred_element_type=F32
    )


def times(left, right):
    return lax.dot_general(
        left, right, (((1,), (0,)), ((), ())), preferred_element_type=F32
    )


def elu_feature(field):
    return jnp.where(field > 0, field + 1.0, jnp.exp(jnp.minimum(field, 0.0)))


def tanh_feature(field):
    return 1.0 + jnp.tanh(field)


def pair_lanes(p, part=0, width=PAIR):
    return slice(p * width + part * PAIR, p * width + (part + 1) * PAIR)


def store_split(ref, index, rows, block):
    lane = lax.broadcasted_iota(jnp.int32, (block.shape[0], PAIR), 1)
    for p in range(block.shape[1] // PAIR):
        pair = block[:, pair_lanes(p)]
        for h in range(2):
            mine = (lane < HEAD) if h == 0 else (lane >= HEAD)
            ref[index + (rows, pair_lanes(p, h, 2 * PAIR))] = jnp.where(mine, pair, 0.0).astype(
                BF16
            )


def load_split(ref, index, rows, p):
    return jnp.concatenate([ref[index + (rows, pair_lanes(p, h, 2 * PAIR))] for h in range(2)], 0)


def tall(block):
    return jnp.concatenate([block[:, :PAIR], block[:, PAIR:]], 0)


def width_of(ref):
    return ref.shape[1]


def blend_rows(blend_ref, first):
    lane = lax.broadcasted_iota(jnp.int32, (1, PAIR), 1)

    def row(branch, pair):
        head = 2 * (first + pair)
        return jnp.where(lane < HEAD, blend_ref[branch, head], blend_ref[branch, head + 1])

    return row


def fill_features(meta_ref, q_ref, k_ref, v_ref, halo_k, halo_v, keys, values, fq, fk, split):
    rows, width = q_ref.shape
    chunk = 2 * TILE
    front = pl.ds(0, TILE)
    keys[front, :] = jnp.zeros((TILE, 2 * width), BF16)
    values[front, :] = jnp.zeros((TILE, 2 * width), BF16)
    fk[:, front, :] = jnp.zeros((2, TILE, 2 * width), BF16)
    if halo_k is not None:
        store_split(keys, (), front, halo_k[...].astype(F32) * 0.125)
        store_split(values, (), front, halo_v[...].astype(F32))

    def fill(step, carry):
        at = pl.multiple_of(step * chunk, chunk)
        here, there = pl.ds(at, chunk), pl.ds(at + TILE, chunk)
        q = q_ref[here, :].astype(F32)
        k = k_ref[here, :].astype(F32)
        store_split(keys, (), there, k * 0.125)
        store_split(values, (), there, v_ref[here, :].astype(F32))
        position = meta_ref[1] + at + lax.broadcasted_iota(jnp.int32, (chunk, width), 0)
        valid = position < meta_ref[0]
        for c, feature in enumerate((elu_feature, tanh_feature)):
            if split:
                store_split(fq, (c,), here, feature(q))
            else:
                fq[c, here, :] = feature(q).astype(BF16)
            store_split(fk, (c,), there, jnp.where(valid, feature(k), 0.0))
        return carry

    lax.fori_loop(0, rows // chunk, fill, 0)


def tile_masks(meta_ref, tile):
    shape = (TILE, 2 * PAIR)
    row = lax.broadcasted_iota(jnp.int32, shape, 0)
    lane = lax.broadcasted_iota(jnp.int32, shape, 1) % PAIR
    back = row + TILE - lane
    key = meta_ref[1] + (tile - 1) * TILE + lane
    known = (key >= 0) & (key < meta_ref[0])
    near = (back >= 0) & (back <= WINDOW) & (known | (back == 0))
    return near, back >= 0


def softmax_pair(scores):
    halves = []
    for h in range(2):
        part = scores[:, h * PAIR : (h + 1) * PAIR]
        part = jnp.exp(part - jnp.max(part, axis=1, keepdims=True))
        halves.append(part * (1.0 / jnp.sum(part, axis=1, keepdims=True)))
    return jnp.concatenate(halves, 1)


def tile_constants():
    row = lax.broadcasted_iota(jnp.int32, (2 * PAIR, PAIR), 0)
    lane = lax.broadcasted_iota(jnp.int32, (2 * PAIR, PAIR), 1)
    ones = jnp.where(row // PAIR == lane // HEAD, 1.0, 0.0).astype(BF16)
    row = lax.broadcasted_iota(jnp.int32, (PAIR, 2 * PAIR), 0)
    lane = lax.broadcasted_iota(jnp.int32, (PAIR, 2 * PAIR), 1)
    return ones, row // HEAD == (lane % PAIR) // HEAD


def whole(split):
    half = split.shape[0] // 2
    return split[:half] + split[half:]


def state_share(block, fks, vs):
    ones = jnp.ones((TILE, PAIR), BF16)
    share = rows_product(whole(fks), jnp.concatenate([whole(vs), ones], 1))
    return jnp.where(block, share, 0.0)


def attend_kernel(
    together, whole_sequence, place_ref, lengths_ref, blend_ref, q_ref, k_ref, v_ref, *refs
):
    halo_k, halo_v, state_ref = (None,) * 3 if whole_sequence else refs[:3]
    meta_ref = lengths_ref[place_ref[0]], place_ref[1]
    blend_at = blend_rows(blend_ref, pl.program_id(0) * (width_of(q_ref) // PAIR))
    att_ref, keys, values, fq, fk, state = refs[-6:] if whole_sequence else refs[3:4] + refs[-5:]
    total_ref = None if whole_sequence else refs[4]
    rows, width = q_ref.shape
    pairs = range(width // PAIR)
    near_by = range(together)
    units = [(s, p) for s in near_by for p in pairs]
    fill_features(meta_ref, q_ref, k_ref, v_ref, halo_k, halo_v, keys, values, fq, fk, False)
    state[...] = jnp.zeros_like(state) if whole_sequence else state_ref[...]
    ones, block = tile_constants()

    def step(number, carry):
        first = number * together
        at = pl.multiple_of(first * TILE, TILE)
        here = [pl.ds(at + s * TILE, TILE) for s in near_by]
        window = [pl.ds(at + s * TILE, 2 * TILE) for s in near_by]
        masks = [tile_masks(meta_ref, first + s) for s in near_by]
        q = {(s, p): q_ref[here[s], pair_lanes(p)] for s, p in units}
        feats = {(s, p): [fq[c, here[s], pair_lanes(p)] for c in range(2)] for s, p in units}
        ks = {(s, p): load_split(keys, (), window[s], p) for s, p in units}
        fks = {(s, p): [load_split(fk, (c,), window[s], p) for c in range(2)] for s, p in units}
        wide = {
            (s, p): jnp.concatenate([load_split(values, (), window[s], p), ones], 1)
            for s, p in units
        }
        held = {(0, p): [state[c, p] for c in range(2)] for p in pairs}
        for s, p in units:
            vs = load_split(values, (), here[s], p)
            held[s + 1, p] = [
                held[s, p][c] + state_share(block, load_split(fk, (c,), here[s], p), vs)
                for c in range(2)
            ]
        near = {u: times_transposed(q[u], ks[u]) for u in units}
        far = {u: [times_transposed(feats[u][c], fks[u][c]) for c in range(2)] for u in units}
        old = {u: [times(feats[u][c], held[u][c].astype(BF16)) for c in range(2)] for u in units}
        near = {u: softmax_pair(jnp.where(masks[u[0]][0], near[u], NEG)) for u in units}
        far = {u: [jnp.where(masks[u[0]][1], f, 0.0) for f in far[u]] for u in units}
        stack = {u: jnp.concatenate([near[u]] + far[u], 0).astype(BF16) for u in units}
        sums = {u: times(stack[u], wide[u]) for u in units}
        for s, p in units:
            u, lanes = (s, p), pair_lanes(p)
            mixed = blend_at(0, p) * sums[u][:TILE, :PAIR]
            for c in range(2):
                mine = sums[u][(c + 1) * TILE : (c + 2) * TILE] + old[u][c]
                mixed = mixed + blend_at(c + 1, p) * (
                    mine[:, :PAIR] / mine[:, PAIR:]
                )
            att_ref[here[s], lanes] = mixed.astype(BF16)
        for p in pairs:
            for c in range(2):
                state[c, p] = held[together, p][c]
        return carry

    lax.fori_loop(0, rows // (together * TILE), step, 0)
    if whole_sequence:
        return
    last = pl.ds(rows, TILE)
    for p in pairs:
        for c in range(2):
            total_ref[c, p] = state[c, p] + state_share(
                block, load_split(fk, (c,), last, p), load_split(values, (), last, p)
            )


def slopes_of(field):
    small = jnp.exp(jnp.minimum(field, 0.0))
    bent = jnp.tanh(field)
    return [jnp.where(field > 0, 1.0, small), 1.0 - bent * bent]


def split_heads(block):
    lane = lax.broadcasted_iota(jnp.int32, block.shape, 1)
    zero = jnp.zeros_like(block)
    return jnp.concatenate(
        [jnp.where(lane < HEAD, block, zero), jnp.where(lane < HEAD, zero, block)], 0
    )


def attend_back_kernel(
    together, number, whole_sequence, place_ref, lengths_ref, blend_ref, q_ref, k_ref, v_ref, go_ref, *refs
):
    meta_ref = lengths_ref[place_ref[0]], place_ref[1]
    blend_at = blend_rows(blend_ref, (number + pl.program_id(0)) * (width_of(q_ref) // PAIR))
    halo_k, halo_v, state_ref, later_ref = (None,) * 4 if whole_sequence else refs[:4]
    if whole_sequence:
        gq_ref, gk_ref, gv_ref, mix_ref = refs[:4]
    else:
        gq_ref, gk_ref, gv_ref, mix_ref, hk_ref, hv_ref, total_ref = refs[4:11]
    keys, values, fq, fk, state, gk, gv, gfk, gon = refs[-9:]
    rows, width = q_ref.shape
    pairs = range(width // PAIR)
    tiles = rows // TILE
    near_by = range(together)
    units = [(s, p) for s in near_by for p in pairs]
    fill_features(meta_ref, q_ref, k_ref, v_ref, halo_k, halo_v, keys, values, fq, fk, True)
    state[...] = jnp.zeros_like(state) if whole_sequence else state_ref[...]
    mix_ref[...] = jnp.zeros_like(mix_ref)
    gk[:TILE, :] = jnp.zeros((TILE, width), F32)
    gv[:TILE, :] = jnp.zeros((TILE, width), F32)
    gfk[:, :TILE, :] = jnp.zeros((2, TILE, width), F32)
    ones, block = tile_constants()
    row = lax.broadcasted_iota(jnp.int32, (2 * PAIR, PAIR), 0) % PAIR
    lane = lax.broadcasted_iota(jnp.int32, (2 * PAIR, PAIR), 1)
    heads = jnp.where(row // HEAD == lane // HEAD, 1.0, 0.0).astype(BF16)
    plain_ones = jnp.ones((TILE, PAIR), BF16)
    high = (lax.broadcasted_iota(jnp.int32, (TILE, PAIR), 1) % HEAD) < HEAD // 2

    def step(turn, carry):
        first = turn * together
        at = pl.multiple_of(first * TILE, TILE)
        here = [pl.ds(at + s * TILE, TILE) for s in range(together + 1)]
        window = [pl.ds(at + s * TILE, 2 * TILE) for s in near_by]
        masks = [tile_masks(meta_ref, first + s) for s in near_by]
        q = {(s, p): q_ref[here[s], pair_lanes(p)] for s, p in units}
        go = {(s, p): go_ref[here[s], pair_lanes(p)] for s, p in units}
        blend = [[blend_at(c, p) for c in range(3)] for p in pairs]
        fqs = {(s, p): [load_split(fq, (c,), here[s], p) for c in range(2)] for s, p in units}
        feats = {u: [whole(f) for f in fqs[u]] for u in units}
        ks = {(s, p): load_split(keys, (), window[s], p) for s, p in units}
        fks = {(s, p): [load_split(fk, (c,), window[s], p) for c in range(2)] for s, p in units}
        wide = {
            (s, p): jnp.concatenate([load_split(values, (), window[s], p), ones], 1)
            for s, p in units
        }
        held = {(0, p): [state[c, p] for c in range(2)] for p in pairs}
        for s, p in units:
            vs = load_split(values, (), here[s], p)
            held[s + 1, p] = [
                held[s, p][c] + state_share(block, load_split(fk, (c,), here[s], p), vs)
                for c in range(2)
            ]
        past = {u: [h.astype(BF16) for h in held[u]] for u in units}
        old_k = [gk[here[0], pair_lanes(p)] for p in pairs]
        old_v = [gv[here[0], pair_lanes(p)] for p in pairs]
        old_f = [[gfk[c, here[0], pair_lanes(p)] for c in range(2)] for p in pairs]

        near = {u: times_transposed(q[u], ks[u]) for u in units}
        far = {u: [times_transposed(feats[u][c], fks[u][c]) for c in range(2)] for u in units}
        old = {u: [times(feats[u][c], past[u][c]) for c in range(2)] for u in units}
        near = {u: softmax_pair(jnp.where(masks[u[0]][0], near[u], NEG)) for u in units}
        far = {u: [jnp.where(masks[u[0]][1], f, 0.0).astype(BF16) for f in far[u]] for u in units}
        stack = {u: jnp.concatenate([near[u].astype(BF16)] + far[u], 0) for u in units}
        sums = {u: times(stack[u], wide[u]) for u in units}
        scales, prods = {}, {}
        for u in units:
            outs = [sums[u][:TILE, :PAIR]]
            scales[u] = [jnp.broadcast_to(blend[u[1]][0], (TILE, PAIR))]
            for c in range(2):
                mine = sums[u][(c + 1) * TILE : (c + 2) * TILE] + old[u][c]
                inverse = 1.0 / mine[:, PAIR:]
                outs.append(mine[:, :PAIR] * inverse)
                scales[u].append(blend[u[1]][c + 1] * inverse)
            prods[u] = jnp.concatenate([go[u] * out for out in outs], 0)
        deltas = {}
        for u in units:
            low = prods[u].astype(BF16)
            rest = (prods[u] - low.astype(F32)).astype(BF16)
            deltas[u] = times(jnp.concatenate([low, rest], 1), heads)
        grads = {}
        for u in units:
            grads[u] = []
            for c in range(3):
                delta = scales[u][c] * deltas[u][c * TILE : (c + 1) * TILE] * (-2.0 / HEAD)
                delta_low = delta.astype(BF16).astype(F32)
                delta = jnp.where(high, delta_low, delta - delta_low)
                grads[u].append(jnp.concatenate([scales[u][c] * go[u], delta], 1).astype(BF16))
        back = {u: times_transposed(jnp.concatenate(grads[u], 0), wide[u]) for u in units}
        late = {u: [times_transposed(grads[u][c + 1], past[u][c]) for c in range(2)] for u in units}
        ds = {u: (near[u] * back[u][:TILE]).astype(BF16) for u in units}
        gas = {
            u: [
                jnp.where(masks[u[0]][1], back[u][(c + 1) * TILE : (c + 2) * TILE], 0.0).astype(BF16)
                for c in range(2)
            ]
            for u in units
        }
        gq_near = {u: times(ds[u], ks[u]) for u in units}
        gq_far = {u: [times(gas[u][c], fks[u][c]) + late[u][c] for c in range(2)] for u in units}
        new_k = {u: rows_product(tall(ds[u]), split_heads(q[u] * 0.125)) for u in units}
        new_f = {u: [rows_product(tall(gas[u][c]), fqs[u][c]) for c in range(2)] for u in units}
        new_v = {
            u: rows_product(
                jnp.concatenate([tall(stack[u][c * TILE : (c + 1) * TILE]) for c in range(3)], 0),
                jnp.concatenate([split_heads(g[:, :PAIR]) for g in grads[u]], 0),
            )
            for u in units
        }

        def overlap(old, new, p):
            parts = [old + new(0, p)[:TILE]]
            parts += [new(s, p)[TILE:] + new(s + 1, p)[:TILE] for s in range(together - 1)]
            return parts + [new(together - 1, p)[TILE:]]

        for s, p in units:
            u, lanes = (s, p), pair_lanes(p)
            slopes = slopes_of(q[u].astype(F32))
            gq = gq_near[u] + slopes[0] * gq_far[u][0] + slopes[1] * gq_far[u][1]
            gq_ref[here[s], lanes] = gq.astype(BF16)
            for c in range(2):
                gon[c, here[s], p * 2 * PAIR : (p + 1) * 2 * PAIR] = grads[u][c + 1]
        for p in pairs:
            lanes = pair_lanes(p)
            for c in range(3):
                mix_ref[c : c + 1, lanes] += sum(
                    jnp.sum(prods[s, p][c * TILE : (c + 1) * TILE], axis=0, keepdims=True)
                    for s in near_by
                )
            for rows_at, part in zip(here, overlap(old_k[p], lambda s, p: new_k[s, p], p)):
                gk[rows_at, lanes] = part
            for rows_at, part in zip(here, overlap(old_v[p], lambda s, p: new_v[s, p], p)):
                gv[rows_at, lanes] = part
            for c in range(2):
                parts = overlap(old_f[p][c], lambda s, p: new_f[s, p][c], p)
                for rows_at, part in zip(here, parts):
                    gfk[c, rows_at, lanes] = part
                state[c, p] = held[together, p][c]
        return carry

    lax.fori_loop(0, tiles // together, step, 0)
    if not whole_sequence:
        hk_ref[...] = gk[:TILE, :].astype(BF16)
        hv_ref[...] = gv[:TILE, :].astype(BF16)
    state[...] = jnp.zeros_like(state) if whole_sequence else later_ref[...]

    def come(at, c, p):
        here = pl.ds(at, TILE)
        grads = gon[c, here, p * 2 * PAIR : (p + 1) * 2 * PAIR]
        share = rows_product(whole(load_split(fq, (c,), here, p)), grads)
        return jnp.where(block, share, 0.0)

    def back_step(turn, carry):
        first = tiles - 1 - turn * together
        at = [pl.multiple_of((first - s) * TILE, TILE) for s in near_by]
        here = [pl.ds(a, TILE) for a in at]
        there = [pl.ds(a + TILE, TILE) for a in at]
        held = {(-1, p): [state[c, p] for c in range(2)] for p in pairs}
        for s, p in units:
            tile = first - s + 2
            nearer = pl.multiple_of(jnp.minimum(tile, tiles - 1) * TILE, TILE)
            held[s, p] = [
                held[s - 1, p][c] + jnp.where(tile < tiles, come(nearer, c, p), 0.0)
                for c in range(2)
            ]
        later = {u: [h.astype(BF16) for h in held[u]] for u in units}
        vs = {(s, p): whole(load_split(values, (), there[s], p)) for s, p in units}
        fks = {
            (s, p): jnp.concatenate([whole(load_split(fk, (c,), there[s], p)) for c in range(2)], 1)
            for s, p in units
        }
        wide = {u: jnp.concatenate([vs[u], plain_ones], 1) for u in units}
        far_k = {u: [times_transposed(wide[u], later[u][c]) for c in range(2)] for u in units}
        far_v = {
            u: times(fks[u], jnp.concatenate([g[:, :PAIR] for g in later[u]], 0)) for u in units
        }
        for s, p in units:
            u, lanes = (s, p), pair_lanes(p)
            position = meta_ref[1] + at[s] + lax.broadcasted_iota(jnp.int32, (TILE, PAIR), 0)
            slopes = slopes_of(k_ref[here[s], lanes].astype(F32))
            grad_f = [gfk[c, there[s], lanes] + far_k[u][c] for c in range(2)]
            bent = slopes[0] * grad_f[0] + slopes[1] * grad_f[1]
            grad_k = gk[there[s], lanes] + jnp.where(position < meta_ref[0], bent, 0.0)
            gk_ref[here[s], lanes] = grad_k.astype(BF16)
            gv_ref[here[s], lanes] = (gv[there[s], lanes] + far_v[u]).astype(BF16)
        for p in pairs:
            for c in range(2):
                state[c, p] = held[together - 1, p][c]
        return carry

    lax.fori_loop(0, tiles // together, back_step, 0)
    if whole_sequence:
        return
    for p in pairs:
        for c in range(2):
            total_ref[c, p] = state[c, p] + come(0, c, p) + come(TILE, c, p)


def attention_specs(rows, width, lanes, number):
    calls = width // lanes

    def columns(height, part):
        return pl.BlockSpec((height, lanes), lambda i: (0, part * calls + number(i)))

    state = pl.BlockSpec(
        (2, lanes // PAIR, PAIR, 2 * PAIR), lambda i: (0, number(i), 0, 0)
    )
    ins = [pl.BlockSpec(memory_space=pltpu.SMEM)] * 3
    ins += [columns(rows, part) for part in range(3)]
    return columns, ins, [columns(TILE, part) for part in range(2)] + [state]


def attention_scratch(rows, lanes, split):
    return [
        pltpu.VMEM((rows + TILE, 2 * lanes), BF16),
        pltpu.VMEM((rows + TILE, 2 * lanes), BF16),
        pltpu.VMEM((2, rows, (2 if split else 1) * lanes), BF16),
        pltpu.VMEM((2, rows + TILE, 2 * lanes), BF16),
        pltpu.VMEM((2, lanes // PAIR, PAIR, 2 * PAIR), F32),
    ]


def outcome(shape, dtype):
    return jax.ShapeDtypeStruct(shape, dtype), pl.BlockSpec(shape, lambda _: (0,) * len(shape))


UNITS = 16


def together(rows, lanes):
    return min(UNITS * PAIR // lanes, rows // TILE)


def attend(place, lengths, blend, qkv, halo, state):
    rows, width = qkv.shape[0], qkv.shape[1] // 3
    lanes = PAIR
    columns, ins, before = attention_specs(rows, width, lanes, lambda i: i)
    held = before[-1]
    share = (2, width // PAIR, PAIR, 2 * PAIR)
    earlier = () if state is None else (halo, halo, state)
    return pl.pallas_call(
        functools.partial(attend_kernel, together(rows, lanes), state is None),
        grid=(width // lanes,),
        out_shape=(
            jax.ShapeDtypeStruct((rows, width), BF16),
            jax.ShapeDtypeStruct(share, F32),
        )[: 1 if state is None else 2],
        in_specs=ins + before[: len(earlier)],
        out_specs=(columns(rows, 0), held)[: 1 if state is None else 2],
        scratch_shapes=attention_scratch(rows, lanes, False),
        compiler_params=pltpu.CompilerParams(vmem_limit_bytes=VMEM),
        cost_estimate=BRIEF,
    )(place, lengths, blend, qkv, qkv, qkv, *earlier)


def attend_back(place, lengths, blend, qkv, halo, state, later, go, first, count):
    rows, width = qkv.shape[0], qkv.shape[1] // 3
    lanes = PAIR
    columns, ins, before = attention_specs(rows, width, lanes, lambda i: first + i)
    others = () if state is None else (halo, halo, state, later)

    def side_by_side(height, dtype):
        shape = jax.ShapeDtypeStruct((height, count * lanes), dtype)
        return shape, pl.BlockSpec((height, lanes), lambda i: (0, i))

    outs = [side_by_side(rows, BF16)] * 3 + [side_by_side(3, F32)]
    if state is not None:
        share = (2, 1, PAIR, 2 * PAIR)
        outs += [side_by_side(TILE, BF16)] * 2
        outs += [
            (
                jax.ShapeDtypeStruct((2, count) + share[2:], F32),
                pl.BlockSpec(share, lambda i: (0, i, 0, 0)),
            )
        ]
    shapes, blocks = zip(*outs)
    return pl.pallas_call(
        functools.partial(attend_back_kernel, together(rows, lanes), first, state is None),
        grid=(count,),
        out_shape=shapes,
        in_specs=ins + [columns(rows, 0)] + (before + before[-1:])[: len(others)],
        out_specs=blocks,
        scratch_shapes=attention_scratch(rows, lanes, True)
        + [
            pltpu.VMEM((rows + TILE, lanes), F32),
            pltpu.VMEM((rows + TILE, lanes), F32),
            pltpu.VMEM((2, rows + TILE, lanes), F32),
            pltpu.VMEM((2, rows, 2 * lanes), BF16),
        ],
        compiler_params=pltpu.CompilerParams(vmem_limit_bytes=VMEM),
        cost_estimate=BRIEF,
    )(place, lengths, blend, qkv, qkv, qkv, go, *others)


CHUNK = 512
GELU_A, GELU_B = 0.7978845608028654, 0.044715


def normalized(field):
    center = field - jnp.mean(field, axis=-1, keepdims=True)
    scale = lax.rsqrt(jnp.mean(center * center, axis=-1, keepdims=True) + EPS)
    return center * scale, scale


def norm_back(grad, unit, scale):
    shared = jnp.mean(grad * unit, axis=-1, keepdims=True)
    return scale * (grad - jnp.mean(grad, axis=-1, keepdims=True) - unit * shared)


def gelu_pair(field):
    square = field * field
    half = 0.5 + 0.5 * jnp.tanh(field * (GELU_A + GELU_A * GELU_B * square))
    act = field * half
    return act, half + act * (1.0 - half) * (2.0 * GELU_A + 6.0 * GELU_A * GELU_B * square)


def column_sum(block):
    return jnp.sum(block, axis=0, keepdims=True)


def enter_kernel(place_ref, w_ref, gain_ref, bias_ref, *refs):
    parts, x_ref, qkv_ref, whole_x = refs[:-3], refs[-3], refs[-2], refs[-1]
    span, chunk = parts[0].shape[0], x_ref.shape[0]

    @pl.when(pl.program_id(0) == 0)
    def _():
        for k, part in enumerate(parts):
            at = (place_ref[0] ^ k) * span
            whole_x[pl.ds(pl.multiple_of(at, span), span), :] = part[...]

    x = whole_x[pl.ds(pl.multiple_of(pl.program_id(0) * chunk, chunk), chunk), :]
    x_ref[...] = x
    unit, _ = normalized(x.astype(F32))
    low = (unit * gain_ref[...] + bias_ref[...]).astype(BF16)
    qkv_ref[...] = times(low, w_ref[...]).astype(BF16)


def enter(place, parts, weight, gain, bias):
    span, width = parts[0].shape
    rows, lanes = span * len(parts), weight.shape[1]
    size = min(CHUNK, rows)
    return pl.pallas_call(
        enter_kernel,
        grid=(rows // size,),
        out_shape=(
            jax.ShapeDtypeStruct((rows, width), BF16),
            jax.ShapeDtypeStruct((rows, lanes), BF16),
        ),
        in_specs=[pl.BlockSpec(memory_space=pltpu.SMEM)]
        + [constant(a.shape) for a in (weight, gain[None], bias[None], *parts)],
        out_specs=(by_rows(size, width), by_rows(size, lanes)),
        scratch_shapes=[pltpu.VMEM((rows, width), BF16)],
        compiler_params=pltpu.CompilerParams(vmem_limit_bytes=VMEM),
        cost_estimate=BRIEF,
    )(place, weight, gain[None], bias[None], *parts)


def deal(place_ref, rows, lanes, value, keep_ref, send_ref):
    half = value.shape[0] // 2

    @pl.when(place_ref[2] == 0)
    def _():
        keep_ref[rows, lanes] = value[:half]
        send_ref[rows, lanes] = value[half:]

    @pl.when(place_ref[2] != 0)
    def _():
        keep_ref[rows, lanes] = value[half:]
        send_ref[rows, lanes] = value[:half]


def feed_kernel(
    pieces, place_ref, x_ref, att_ref, grad_ref, out_from, gain_ref, bias_ref, in_from, in_b,
    down_from, down_b, result_to, first_to, go_to, keep_to, send_to, small_ref, wide_ref,
    second, hidden, pre_low, att_low, att_all, grad_all, out_w, in_w, down_w, keep_ref, send_ref,
    result_ref, first_ref, go_ref, in_sems, out_sems, row_sems,
):
    chunk, width = x_ref.shape
    inner = in_w.shape[1]
    number = pl.program_id(0)
    here = pl.ds(pl.multiple_of(number * chunk, chunk), chunk)
    tiles = [slice(at, at + width) for at in range(0, inner, width)]
    copies = [pltpu.make_async_copy(out_from, out_w, in_sems.at[0])]
    for i, lanes in enumerate(tiles):
        copies += [
            pltpu.make_async_copy(in_from.at[:, lanes], in_w.at[:, lanes], in_sems.at[2 * i + 1]),
            pltpu.make_async_copy(down_from.at[lanes, :], down_w.at[lanes, :], in_sems.at[2 * i + 2]),
        ]

    def arrived(i):
        @pl.when(number == 0)
        def _():
            copies[i].wait()

    @pl.when(number == 0)
    def _():
        for copy in copies:
            copy.start()
        small_ref[...] = jnp.zeros_like(small_ref)
        wide_ref[...] = jnp.zeros_like(wide_ref)

    att = att_ref[...]
    att_all[here, :] = att
    arrived(0)
    first = x_ref[...].astype(F32) + times(att, out_w[...])
    unit, scale = normalized(first)
    low = (unit * gain_ref[...] + bias_ref[...]).astype(BF16)
    second[here, :] = low
    grad = grad_ref[...]
    grad_all[here, :] = grad
    grad_f = grad.astype(F32)
    result = first + down_b[...]
    back = jnp.zeros((chunk, width), F32)
    for i, lanes in enumerate(tiles):
        arrived(2 * i + 1)
        arrived(2 * i + 2)
        act, slope = gelu_pair(times(low, in_w[:, lanes]) + in_b[:, lanes])
        act = act.astype(BF16)
        hidden[here, lanes] = act
        result = result + times(act, down_w[lanes, :])
        pre = (times_transposed(grad, down_w[lanes, :]) * slope).astype(BF16)
        pre_low[here, lanes] = pre
        wide_ref[:, lanes] += column_sum(pre.astype(F32))
        back = back + times_transposed(pre, in_w[:, lanes])
    result_ref[here, :] = result.astype(BF16)
    small_ref[0:1, :] += column_sum(back * unit)
    small_ref[1:2, :] += column_sum(back)
    small_ref[2:3, :] += column_sum(grad_f)
    grad_first = grad_f + norm_back(back * gain_ref[...], unit, scale)
    first_ref[here, :] = grad_first
    grad_att = grad_first.astype(BF16)
    att_low[here, :] = grad_att
    go_ref[here, :] = times_transposed(grad_att, out_w[...])
    pairs = ((result_ref, result_to), (first_ref, first_to), (go_ref, go_to))
    done = [
        pltpu.make_async_copy(inside.at[here, :], outside.at[here, :], row_sems.at[number, i])
        for i, (inside, outside) in enumerate(pairs)
    ]
    for copy in done:
        copy.start()

    @pl.when(number == pl.num_programs(0) - 1)
    def _():
        every = slice(0, width // 2)
        leaving = []

        def leave(lanes):
            for here, there in ((keep_ref, keep_to), (send_ref, send_to)):
                sem = out_sems.at[len(leaving)]
                copy = pltpu.make_async_copy(here.at[:, lanes], there.at[:, lanes], sem)
                copy.start()
                leaving.append(copy)

        flat, after_out = width // pieces, inner + width

        def spread(block, share, ref):
            for below in range(pieces):
                piece, side = divmod(block * pieces + below, len(tiles))
                rows = slice(piece % (pieces // 2) * flat, (piece % (pieces // 2) + 1) * flat)
                lanes = slice(after_out + side * width, after_out + (side + 1) * width)
                ref[rows, lanes] = share[below * flat : (below + 1) * flat]

        for block, lanes in enumerate(tiles):
            share = rows_product(hidden[:, lanes], grad_all[...]).astype(BF16)
            mine = place_ref[2] == 2 * block // len(tiles)

            @pl.when(mine)
            def _(block=block, share=share):
                spread(block, share, keep_ref)

            @pl.when(jnp.logical_not(mine))
            def _(block=block, share=share):
                spread(block, share, send_ref)

        leave(slice(after_out, after_out + inner))
        for lanes in tiles:
            share = rows_product(second[...], pre_low[:, lanes]).astype(BF16)
            deal(place_ref, every, lanes, share, keep_ref, send_ref)
            leave(lanes)
        share = rows_product(att_all[...], att_low[...]).astype(BF16)
        deal(place_ref, every, slice(inner, after_out), share, keep_ref, send_ref)
        leave(slice(inner, after_out))
        for copy in leaving:
            copy.wait()
        for step in range(att_all.shape[0] // chunk):
            rows = slice(step * chunk, (step + 1) * chunk)
            for i, (inside, outside) in enumerate(pairs):
                sem = row_sems.at[step, i]
                pltpu.make_async_copy(inside.at[rows, :], outside.at[rows, :], sem).wait()


def by_rows(height, width):
    return pl.BlockSpec((height, width), lambda i: (i, 0))


def constant(shape):
    return pl.BlockSpec(shape, lambda i: (0, 0))


def feed_forward(pieces, place, x, att, grad, out_w, gain, bias, in_w, in_b, down_w, down_b):
    rows, width = x.shape
    inner = in_w.shape[1]
    packed = (width // 2, 2 * inner + width)
    size = min(CHUNK, rows)
    block, far = by_rows(size, width), pl.BlockSpec(memory_space=pl.ANY)
    return pl.pallas_call(
        functools.partial(feed_kernel, pieces),
        grid=(rows // size,),
        out_shape=(
            jax.ShapeDtypeStruct((rows, width), BF16),
            jax.ShapeDtypeStruct((rows, width), F32),
            jax.ShapeDtypeStruct((rows, width), F32),
            jax.ShapeDtypeStruct(packed, BF16),
            jax.ShapeDtypeStruct(packed, BF16),
            jax.ShapeDtypeStruct((3, width), F32),
            jax.ShapeDtypeStruct((1, inner), F32),
        ),
        in_specs=[pl.BlockSpec(memory_space=pltpu.SMEM)]
        + [block] * 3
        + [far, constant((1, width)), constant((1, width)), far, constant((1, inner)), far]
        + [constant((1, width))],
        out_specs=(far,) * 5
        + (constant((3, width)), constant((1, inner))),
        scratch_shapes=[
            pltpu.VMEM((rows, width), BF16),
            pltpu.VMEM((rows, inner), BF16),
            pltpu.VMEM((rows, inner), BF16),
            pltpu.VMEM((rows, width), BF16),
            pltpu.VMEM((rows, width), BF16),
            pltpu.VMEM((rows, width), BF16),
            pltpu.VMEM(out_w.shape, BF16),
            pltpu.VMEM(in_w.shape, BF16),
            pltpu.VMEM(down_w.shape, BF16),
            pltpu.VMEM(packed, BF16),
            pltpu.VMEM(packed, BF16),
            pltpu.VMEM((rows, width), BF16),
            pltpu.VMEM((rows, width), F32),
            pltpu.VMEM((rows, width), F32),
            pltpu.SemaphoreType.DMA((1 + 2 * inner // width,)),
            pltpu.SemaphoreType.DMA((4 + 2 * inner // width,)),
            pltpu.SemaphoreType.DMA((rows // size, 3)),
        ],
        compiler_params=pltpu.CompilerParams(vmem_limit_bytes=VMEM),
        cost_estimate=BRIEF,
    )(place, x, att, grad, out_w, gain[None], bias[None], in_w, in_b[None], down_w, down_b[None])


def project_back_kernel(
    calls, place_ref, x_ref, first_ref, w_ref, gain_ref, bias_ref, small2_ref, wide_ref, *refs
):
    grads, mixes = refs[: 3 * calls], refs[3 * calls : 4 * calls]
    result_ref, keep_ref, send_ref, normed, gathered, sums, rows_of = refs[4 * calls :]
    chunk, width = x_ref.shape
    number = pl.program_id(0)
    here = pl.ds(pl.multiple_of(number * chunk, chunk), chunk)

    @pl.when(number == 0)
    def _():
        sums[...] = jnp.zeros_like(sums)

    unit, scale = normalized(x_ref[...].astype(F32))
    normed[here, :] = (unit * gain_ref[...] + bias_ref[...]).astype(BF16)
    grad = jnp.concatenate([ref[...] for ref in grads], 1)
    gathered[here, :] = grad
    back = times_transposed(grad, w_ref[...])
    sums[0:1, :] += column_sum(back * unit)
    sums[1:2, :] += column_sum(back)
    grad_x = first_ref[...] + norm_back(back * gain_ref[...], unit, scale)
    result_ref[...] = grad_x.astype(BF16)

    @pl.when(number == pl.num_programs(0) - 1)
    def _():
        every = slice(0, width // 2)
        rows_of[...] = jnp.zeros_like(rows_of)
        at = 0
        for ref in (sums, small2_ref, wide_ref):
            for row in range(ref.shape[0]):
                for lane in range(0, ref.shape[1], PAIR):
                    rows_of[at : at + 1, :] = ref[row : row + 1, lane : lane + PAIR]
                    at += 1
        lane = lax.broadcasted_iota(jnp.int32, (3, PAIR), 1)
        blend = jnp.zeros((3, PAIR), F32)
        head = 0
        for mix in mixes:
            for first in range(0, mix.shape[1], HEAD):
                mine = jnp.sum(mix[:, first : first + HEAD], axis=1, keepdims=True)
                blend = blend + jnp.where(lane == head, mine, 0.0)
                head += 1
        rows_of[at : at + 3, :] = blend
        exact = rows_of[...]
        high = exact.astype(BF16)
        low = (exact - high.astype(F32)).astype(BF16)
        for part, value in enumerate((high, low)):
            lanes = slice(3 * width + part * PAIR, 3 * width + (part + 1) * PAIR)
            deal(place_ref, every, lanes, value, keep_ref, send_ref)
        for at in range(0, 3 * width, width):
            lanes = slice(at, at + width)
            share = rows_product(normed[...], gathered[:, lanes]).astype(BF16)
            deal(place_ref, every, lanes, share, keep_ref, send_ref)


def project_back(place, x, grad_first, weight, gain, bias, small2, wide, grads, mixes):
    rows, width = x.shape
    calls = len(mixes)
    packed = (width // 2, 3 * width + 2 * PAIR)
    size = min(CHUNK, rows)
    block = by_rows(size, width)
    return pl.pallas_call(
        functools.partial(project_back_kernel, calls),
        grid=(rows // size,),
        out_shape=(jax.ShapeDtypeStruct((rows, width), BF16),)
        + (jax.ShapeDtypeStruct(packed, BF16),) * 2,
        in_specs=[pl.BlockSpec(memory_space=pltpu.SMEM), block, block]
        + [constant(a.shape) for a in (weight, gain[None], bias[None], small2, wide)]
        + [by_rows(size, grad.shape[1]) for grad in grads]
        + [constant(mix.shape) for mix in mixes],
        out_specs=(block, constant(packed), constant(packed)),
        scratch_shapes=[
            pltpu.VMEM((rows, width), BF16),
            pltpu.VMEM((rows, 3 * width), BF16),
            pltpu.VMEM((2, width), F32),
            pltpu.VMEM((width, PAIR), F32),
        ],
        compiler_params=pltpu.CompilerParams(vmem_limit_bytes=VMEM),
        cost_estimate=BRIEF,
    )(place, x, grad_first, weight, gain[None], bias[None], small2, wide, *grads, *mixes)


def to_sequences(block, axis, groups):
    return lax.all_to_all(block, axis, 0, 0, axis_index_groups=groups)


def spans_of(block, axis, mine):
    seqs, devices = block.shape[0], lax.axis_size(axis)
    spans = []
    for k in range(seqs):
        span = lax.dynamic_index_in_dim(block, mine ^ k, 0, False)
        route = [(i, i ^ k) for i in range(devices)]
        spans.append(lax.ppermute(span, axis, route) if k else span)
    return spans


def after(value, *others):
    return lax.optimization_barrier((value,) + others)[0]


def join_kernel(placed, *refs):
    parts, outs = refs[: len(placed)], refs[len(placed) :]
    for part, places in zip(parts, placed):
        for source, out, to, lanes in places:
            outs[out][to, :, lanes] = part[source]


def join_to(parts, placed, shapes):
    vmem = pl.BlockSpec(memory_space=pltpu.VMEM)
    return pl.pallas_call(
        functools.partial(join_kernel, placed),
        out_shape=[jax.ShapeDtypeStruct(shape, parts[0].dtype) for shape in shapes],
        in_specs=[vmem] * len(parts),
        out_specs=[vmem] * len(shapes),
        compiler_params=pltpu.CompilerParams(vmem_limit_bytes=16 * 2**20),
        cost_estimate=BRIEF,
    )(*parts)


def split_kernel(count, *refs):
    first, second = refs[count:]
    size, _, lanes = refs[0].shape
    for k, part in enumerate(refs[:count]):
        first[k * size : (k + 1) * size] = part[:, :, : lanes // 2]
        second[k * size : (k + 1) * size] = part[:, :, lanes // 2 :]


def split_to(parts, shapes):
    vmem = pl.BlockSpec(memory_space=pltpu.VMEM)
    return pl.pallas_call(
        functools.partial(split_kernel, len(parts)),
        out_shape=[jax.ShapeDtypeStruct(shape, parts[0].dtype) for shape in shapes],
        in_specs=[vmem] * len(parts),
        out_specs=[vmem] * 2,
        compiler_params=pltpu.CompilerParams(vmem_limit_bytes=16 * 2**20),
        cost_estimate=BRIEF,
    )(*parts)


def join(parts):
    size, height, lanes = parts[0].shape
    placed = [
        [(slice(0, size), 0, slice(k * size, (k + 1) * size), slice(0, lanes))]
        for k in range(len(parts))
    ]
    return join_to(parts, placed, [(len(parts) * size, height, lanes)])[0]


def settle_kernel(source_ref, out_ref):
    out_ref[...] = source_ref[...]


def settle(value):
    vmem = pl.BlockSpec(memory_space=pltpu.VMEM)
    return pl.pallas_call(
        settle_kernel,
        out_shape=jax.ShapeDtypeStruct(value.shape, value.dtype),
        in_specs=[vmem],
        out_specs=vmem,
        compiler_params=pltpu.CompilerParams(vmem_limit_bytes=8 * 2**20),
        cost_estimate=BRIEF,
    )(value)


def from_parts(total, axis, parts, stride, forward):
    size = lax.axis_size(axis)
    low = total.astype(BF16)
    result = jnp.zeros_like(total)
    for hop in range(1, parts):
        distance = hop * stride
        route = [
            (i, i + distance) if forward else (i + distance, i) for i in range(size - distance)
        ]
        result = result + lax.ppermute(low, axis, route).astype(F32)
    return result


class Ring:
    def __init__(self, batch, seq):
        self.batch, self.seq = batch, seq
        self.low = 2 ** ((seq.bit_length() - 1) // 2)
        self.sizes = {"core": 2, "near": batch // 2 * self.low, "far": seq // self.low}
        self.pieces = batch * seq

    def place(self, s, b):
        return {"core": b % 2, "near": b // 2 * self.low + s % self.low, "far": s // self.low}

    def device(self, place):
        s = place["far"] * self.low + place["near"] % self.low
        return s * self.batch + place["near"] // self.low * 2 + place["core"]

    def mine(self):
        return self.place(lax.axis_index("seq"), lax.axis_index("batch"))

    def swap(self, value, level, k):
        route = []
        for s in range(self.seq):
            for b in range(self.batch):
                place = self.place(s, b)
                place[level] ^= k
                route.append((s * self.batch + b, self.device(place)))
        return lax.ppermute(value, ("seq", "batch"), route)

    def slices(self, value, level):
        size, me = self.sizes[level], self.mine()[level]
        value = value.reshape((size, value.shape[0] // size) + value.shape[1:])
        return [lax.dynamic_index_in_dim(value, me ^ k, 0, False) for k in range(size)]

    def scatter(self, value, level, fine=0, beside=()):
        slices = value if isinstance(value, list) else self.slices(value, level)
        parts = [self.swap(part, level, k) for k, part in enumerate(slices) if k]
        return self.add(slices[0], parts, fine, beside)

    def scatter_cores(self, keep, send, fine=0, beside=()):
        return self.add(self.to_pieces(keep), [self.swap(self.to_pieces(send), "core", 1)], fine, beside)

    def add(self, value, parts, fine, beside):
        total = after(value, *beside).astype(F32)
        for part in parts:
            total = total + part.astype(F32)
        if not fine:
            return total.astype(BF16)
        end = total.shape[-1] - 2 * fine
        exact = total[..., end : end + fine] + total[..., end + fine :]
        high = lax.reduce_precision(exact, 8, 7)
        return jnp.concatenate([total[..., :end], high, exact - high], -1).astype(BF16)

    def gather(self, value, level, beside=()):
        parts = [self.swap(value, level, k) for k in range(1, self.sizes[level])]
        return join([after(value, *beside)] + parts)

    def to_pieces(self, value):
        return value.reshape(self.pieces // 2, -1, value.shape[1])

    def gather_split(self, value, level, beside=()):
        parts = [after(value, *beside)]
        parts += [self.swap(value, level, k) for k in range(1, self.sizes[level])]
        size, height, lanes = value.shape
        shape = (len(parts) * size, height, lanes // 2)
        return split_to(parts, [shape, shape])

    def join_ways(self, halves, ways):
        size, height, half = halves[0].shape
        size //= 2
        placed = []
        for out_lanes, order in ((0, (0, 2)), (0, (1, 3)), (half, (0, 1)), (half, (2, 3))):
            lanes = slice(out_lanes, out_lanes + half)
            placed.append(
                [
                    (slice(i * size, (i + 1) * size), 0, slice(k * size, (k + 1) * size), lanes)
                    for i, k in enumerate(order)
                ]
            )
        parts = [halves[0], ways[0], halves[1], ways[1]]
        return join_to(parts, placed, [(4 * size, height, 2 * half)])[0]

    def code(self):
        me = self.mine()
        return (me["core"] * self.sizes["near"] + me["near"]) * self.sizes["far"] + me["far"]


def unpack_kernel(write, finish, place_ref, own_ref, other_ref, *out_refs):
    half = own_ref.shape[0]
    for piece in range(2 * half):
        at = place_ref[3] ^ piece

        @pl.when(at < half)
        def _(piece=piece, at=at):
            write(piece, own_ref[at].astype(F32), out_refs)

        @pl.when(at >= half)
        def _(piece=piece, at=at):
            write(piece, other_ref[at - half].astype(F32), out_refs)

    finish(out_refs)


def write_feed(piece, block, out_refs):
    in_ref, out_ref, down_ref = out_refs
    size, inner, width = block.shape[0], in_ref.shape[1], in_ref.shape[0]
    rows = slice(piece * size, (piece + 1) * size)
    in_ref[rows, :] = block[:, :inner]
    out_ref[rows, :] = block[:, inner : inner + width]
    tall_rows = inner // (width // size)
    for below in range(0, tall_rows, size):
        at = inner + width + below // size * width
        down_ref[piece * tall_rows + below : piece * tall_rows + below + size, :] = block[
            :, at : at + width
        ]


def write_project(piece, block, out_refs):
    w_ref, small = out_refs[0], out_refs[-1]
    size, end = block.shape[0], w_ref.shape[1]
    rows = slice(piece * size, (piece + 1) * size)
    w_ref[rows, :] = block[:, :end]
    if piece * size < small.shape[0]:
        small[rows, :] = block[:, end : end + PAIR] + block[:, end + PAIR :]


def finish_project(out_refs):
    small, at = out_refs[-1], 0
    for vector in out_refs[1:-2]:
        for lane in range(0, vector.shape[0], PAIR):
            vector[lane : lane + PAIR] = small[at, :]
            at += 1
    blend = out_refs[-2]
    blend[...] = small[at : at + 3, : blend.shape[1]]


def unpack(write, place, halves, shapes, finish=lambda refs: None, scratch=()):
    vmem = pl.BlockSpec(memory_space=pltpu.VMEM)
    return pl.pallas_call(
        functools.partial(unpack_kernel, write, finish),
        out_shape=[jax.ShapeDtypeStruct(shape, F32) for shape in shapes],
        in_specs=[pl.BlockSpec(memory_space=pltpu.SMEM), vmem, vmem],
        out_specs=[vmem] * len(shapes),
        scratch_shapes=scratch,
        compiler_params=pltpu.CompilerParams(vmem_limit_bytes=24 * 2**20),
        cost_estimate=BRIEF,
    )(place, *halves)


def local(
    inputs,
    cotangent,
    lengths,
    norm1_gain,
    norm1_bias,
    qkv_weight,
    blend_weights,
    out_weight,
    norm2_gain,
    norm2_bias,
    in_weight,
    in_bias,
    down_weight,
    down_bias,
):
    seqs, span, width = inputs.shape
    heads = blend_weights.shape[1]
    devices = lax.axis_size("seq")
    parts = devices // seqs
    rows = seqs * span
    index = lax.axis_index("seq")
    groups = None
    if parts > 1:
        groups = [[r * seqs + s for s in range(seqs)] for r in range(parts)]
    mine, part = index % seqs, index // seqs
    ring = Ring(lax.axis_size("batch"), devices)
    by_ring = width % (16 * ring.pieces) == 0 and ring.sizes["near"] == 4
    inner = in_weight.shape[1]
    numbers = [mine, part * rows, 0, 0]
    if by_ring:
        numbers[2:] = [lax.axis_index("batch") % 2, ring.code()]
    place = jnp.stack([jnp.asarray(number, jnp.int32) for number in numbers])

    spans = spans_of(inputs, "seq", mine)
    x, qkv = enter(place, spans, qkv_weight, norm1_gain, norm1_bias)
    grad_out = to_sequences(after(cotangent, *spans), "seq", groups).reshape(rows, width)
    halo = state = later = None
    if parts > 1:
        state = later = jnp.zeros((2, width // PAIR, PAIR, 2 * PAIR), F32)
        onward = [(i, i + seqs) for i in range(devices - seqs)]
        halo = lax.ppermute(qkv[rows - TILE :, width:], "seq", onward)
        total = attend(place, lengths, blend_weights, qkv, halo, state)[1]
        state = from_parts(total, "seq", parts, seqs, True)
    attended = attend(place, lengths, blend_weights, qkv, halo, state)[0]

    result, grad_first, grad_o, feed_keep, feed_send, small2, grad_in_b = feed_forward(
        ring.pieces if by_ring else 16,
        place, x, attended, grad_out, out_weight, norm2_gain, norm2_bias,
        in_weight, in_bias, down_weight, down_bias,
    )

    def move(rows):
        return to_sequences(rows.reshape(seqs, span, width), "seq", groups)

    feed_shapes = [(width, inner), (width, width), (inner, width)]
    calls = ((0, 1), (1, width // PAIR - 1))

    def back(place, pairs, later):
        return attend_back(
            place, lengths, blend_weights, qkv, halo, state, later, grad_o, *pairs
        )

    if parts > 1:
        total = jnp.concatenate([back(place, pairs, later)[6] for pairs in calls], 1)
        later = from_parts(total, "seq", parts, seqs, False)
    if by_ring:
        output = move(result)
        backs = [back(place, calls[0], later)]
        held = ring.scatter_cores(feed_keep, feed_send, 0, (backs[0][3],))
        backs.append(back(after(place, held), calls[1], later))
        held = ring.scatter(held, "near", 0, (backs[1][3],))
        output = settle(after(output, backs[1][3]))
        grad_first = after(grad_first, held, output)
    else:
        backs = [back(place, pairs, later) for pairs in calls]
        output = move(result)
    grads = [[call[part] for call in backs] for part in range(3)]
    if parts > 1:
        homeward = [(i + seqs, i) for i in range(devices - seqs)]
        for part in (1, 2):
            for number in range(len(calls)):
                received = lax.ppermute(backs[number][part + 3], "seq", homeward)
                grad = grads[part][number]
                tail = grad[rows - TILE :].astype(F32) + received.astype(F32)
                grads[part][number] = grad.at[rows - TILE :].set(tail.astype(BF16))
    grads = grads[0] + grads[1] + grads[2]
    grad_x, project_keep, project_send = project_back(
        place, x, grad_first, qkv_weight, norm1_gain, norm1_bias, small2, grad_in_b, grads,
        [call[3] for call in backs],
    )

    if by_ring:
        held = ring.scatter(held, "far", 0, (project_keep,))
        late = ring.scatter_cores(project_keep, project_send, PAIR, (held,))
        late = ring.scatter(late, "near", PAIR)
        halves = ring.gather_split(held, "far", (late,))
        ways = [ring.swap(half, "near", k) for half, k in zip(halves, (2, 1))]
        halves = [join([half, way]) for half, way in zip(halves, ways)]
        ways = [ring.swap(half, "near", k) for half, k in zip(halves, (1, 2))]
        late = ring.scatter(late, "far", PAIR, halves)
        late = ring.gather(late, "far")
        moved = move(after(grad_x, late))
        held = ring.join_ways([after(halves[0], late), halves[1]], ways)
        other = ring.swap(held, "core", 1)
        feed_grads = unpack(write_feed, place, (held, other), feed_shapes)
        late = ring.gather(late, "near", feed_grads)
        input_grad = settle(after(moved, late))
        halves = after(late, input_grad), ring.swap(late, "core", 1)
    else:
        input_grad = move(grad_x)
        halves = (feed_keep, feed_send, project_keep, project_send)
        halves = lax.psum([half.astype(F32) for half in halves], ("seq", "batch"))
        halves = [half.reshape(8, width // 16, -1) for half in halves]
        feed_grads = unpack(write_feed, place, halves[:2], feed_shapes)
        halves = halves[2:]
    grad_in_w, grad_out_w, grad_down_w = feed_grads
    vectors = [(width,)] * 5 + [(inner,)]
    lines = sum(size for (size,) in vectors) // PAIR + 3
    lines += -lines % (width // (2 * halves[0].shape[0]))
    grad_qkv_w, gain1, bias1, gain2, bias2, grad_down_b, grad_in_b, grad_blend = unpack(
        write_project, place, halves, [(width, 3 * width)] + vectors + [(3, heads)],
        finish_project, [pltpu.VMEM((lines, PAIR), F32)],
    )
    return (
        output,
        input_grad,
        gain1,
        bias1,
        grad_qkv_w,
        grad_blend,
        grad_out_w,
        gain2,
        bias2,
        grad_in_w,
        grad_in_b,
        grad_down_w,
        grad_down_b,
    )


def solution(mesh):
    rows = P("batch", "seq", None)
    return jax.shard_map(
        local,
        mesh=mesh,
        in_specs=(rows, rows, P("batch")) + (P(),) * 11,
        out_specs=(rows, rows) + (P(),) * 11,
        check_vma=False,
    )
```

```python
import functools

import jax
import jax.numpy as jnp
from jax import lax
from jax.experimental import pallas as pl
from jax.experimental.pallas import tpu as pltpu
from jax.sharding import PartitionSpec as P

WINDOW = 30
HEAD = 64
PAIR = 2 * HEAD
TILE = 64
EPS = 1e-05
NEG = -1e30
VMEM = 58 * 2**20
BRIEF = pl.CostEstimate(flops=1000, bytes_accessed=1000, transcendentals=0)
BF16 = jnp.bfloat16
F32 = jnp.float32


def layer_norm(field, gain, shift):
    center = field - jnp.mean(field, axis=-1, keepdims=True)
    spread = jnp.mean(center * center, axis=-1, keepdims=True)
    return center * lax.rsqrt(spread + EPS) * gain + shift


def rows_product(left, right):
    return lax.dot_general(
        left, right, (((0,), (0,)), ((), ())), preferred_element_type=F32
    )


def times_transposed(left, right):
    return lax.dot_general(
        left, right, (((1,), (1,)), ((), ())), preferred_element_type=F32
    )


def times(left, right):
    return lax.dot_general(
        left, right, (((1,), (0,)), ((), ())), preferred_element_type=F32
    )


def elu_feature(field):
    return jnp.where(field > 0, field + 1.0, jnp.exp(jnp.minimum(field, 0.0)))


def tanh_feature(field):
    return 1.0 + jnp.tanh(field)


def pair_lanes(p, part=0, width=PAIR):
    return slice(p * width + part * PAIR, p * width + (part + 1) * PAIR)


def store_split(ref, index, rows, block):
    lane = lax.broadcasted_iota(jnp.int32, (block.shape[0], PAIR), 1)
    for p in range(block.shape[1] // PAIR):
        pair = block[:, pair_lanes(p)]
        for h in range(2):
            mine = (lane < HEAD) if h == 0 else (lane >= HEAD)
            ref[index + (rows, pair_lanes(p, h, 2 * PAIR))] = jnp.where(mine, pair, 0.0).astype(
                BF16
            )


def load_split(ref, index, rows, p):
    return jnp.concatenate([ref[index + (rows, pair_lanes(p, h, 2 * PAIR))] for h in range(2)], 0)


def tall(block):
    return jnp.concatenate([block[:, :PAIR], block[:, PAIR:]], 0)


def width_of(ref):
    return ref.shape[1]


def blend_rows(blend_ref, first):
    lane = lax.broadcasted_iota(jnp.int32, (1, PAIR), 1)

    def row(branch, pair):
        head = 2 * (first + pair)
        return jnp.where(lane < HEAD, blend_ref[branch, head], blend_ref[branch, head + 1])

    return row


def fill_features(meta_ref, q_ref, k_ref, v_ref, halo_k, halo_v, keys, values, fq, fk, split):
    rows, width = q_ref.shape
    chunk = 2 * TILE
    front = pl.ds(0, TILE)
    keys[front, :] = jnp.zeros((TILE, 2 * width), BF16)
    values[front, :] = jnp.zeros((TILE, 2 * width), BF16)
    fk[:, front, :] = jnp.zeros((2, TILE, 2 * width), BF16)
    if halo_k is not None:
        store_split(keys, (), front, halo_k[...].astype(F32) * 0.125)
        store_split(values, (), front, halo_v[...].astype(F32))

    def fill(step, carry):
        at = pl.multiple_of(step * chunk, chunk)
        here, there = pl.ds(at, chunk), pl.ds(at + TILE, chunk)
        q = q_ref[here, :].astype(F32)
        k = k_ref[here, :].astype(F32)
        store_split(keys, (), there, k * 0.125)
        store_split(values, (), there, v_ref[here, :].astype(F32))
        position = meta_ref[1] + at + lax.broadcasted_iota(jnp.int32, (chunk, width), 0)
        valid = position < meta_ref[0]
        for c, feature in enumerate((elu_feature, tanh_feature)):
            if split:
                store_split(fq, (c,), here, feature(q))
            else:
                fq[c, here, :] = feature(q).astype(BF16)
            store_split(fk, (c,), there, jnp.where(valid, feature(k), 0.0))
        return carry

    lax.fori_loop(0, rows // chunk, fill, 0)


def tile_masks(meta_ref, tile):
    shape = (TILE, 2 * PAIR)
    row = lax.broadcasted_iota(jnp.int32, shape, 0)
    lane = lax.broadcasted_iota(jnp.int32, shape, 1) % PAIR
    back = row + TILE - lane
    key = meta_ref[1] + (tile - 1) * TILE + lane
    known = (key >= 0) & (key < meta_ref[0])
    near = (back >= 0) & (back <= WINDOW) & (known | (back == 0))
    return near, back >= 0


def softmax_pair(scores):
    halves = []
    for h in range(2):
        part = scores[:, h * PAIR : (h + 1) * PAIR]
        part = jnp.exp(part - jnp.max(part, axis=1, keepdims=True))
        halves.append(part * (1.0 / jnp.sum(part, axis=1, keepdims=True)))
    return jnp.concatenate(halves, 1)


def tile_constants():
    row = lax.broadcasted_iota(jnp.int32, (2 * PAIR, PAIR), 0)
    lane = lax.broadcasted_iota(jnp.int32, (2 * PAIR, PAIR), 1)
    ones = jnp.where(row // PAIR == lane // HEAD, 1.0, 0.0).astype(BF16)
    row = lax.broadcasted_iota(jnp.int32, (PAIR, 2 * PAIR), 0)
    lane = lax.broadcasted_iota(jnp.int32, (PAIR, 2 * PAIR), 1)
    return ones, row // HEAD == (lane % PAIR) // HEAD


def whole(split):
    half = split.shape[0] // 2
    return split[:half] + split[half:]


def state_share(block, fks, vs):
    ones = jnp.ones((TILE, PAIR), BF16)
    share = rows_product(whole(fks), jnp.concatenate([whole(vs), ones], 1))
    return jnp.where(block, share, 0.0)


def attend_kernel(
    together, whole_sequence, place_ref, lengths_ref, blend_ref, q_ref, k_ref, v_ref, *refs
):
    halo_k, halo_v, state_ref = (None,) * 3 if whole_sequence else refs[:3]
    meta_ref = lengths_ref[place_ref[0]], place_ref[1]
    blend_at = blend_rows(blend_ref, pl.program_id(0) * (width_of(q_ref) // PAIR))
    att_ref, keys, values, fq, fk, state = refs[-6:] if whole_sequence else refs[3:4] + refs[-5:]
    total_ref = None if whole_sequence else refs[4]
    rows, width = q_ref.shape
    pairs = range(width // PAIR)
    near_by = range(together)
    units = [(s, p) for s in near_by for p in pairs]
    fill_features(meta_ref, q_ref, k_ref, v_ref, halo_k, halo_v, keys, values, fq, fk, False)
    state[...] = jnp.zeros_like(state) if whole_sequence else state_ref[...]
    ones, block = tile_constants()

    def step(number, carry):
        first = number * together
        at = pl.multiple_of(first * TILE, TILE)
        here = [pl.ds(at + s * TILE, TILE) for s in near_by]
        window = [pl.ds(at + s * TILE, 2 * TILE) for s in near_by]
        masks = [tile_masks(meta_ref, first + s) for s in near_by]
        q = {(s, p): q_ref[here[s], pair_lanes(p)] for s, p in units}
        feats = {(s, p): [fq[c, here[s], pair_lanes(p)] for c in range(2)] for s, p in units}
        ks = {(s, p): load_split(keys, (), window[s], p) for s, p in units}
        fks = {(s, p): [load_split(fk, (c,), window[s], p) for c in range(2)] for s, p in units}
        wide = {
            (s, p): jnp.concatenate([load_split(values, (), window[s], p), ones], 1)
            for s, p in units
        }
        held = {(0, p): [state[c, p] for c in range(2)] for p in pairs}
        for s, p in units:
            vs = load_split(values, (), here[s], p)
            held[s + 1, p] = [
                held[s, p][c] + state_share(block, load_split(fk, (c,), here[s], p), vs)
                for c in range(2)
            ]
        near = {u: times_transposed(q[u], ks[u]) for u in units}
        far = {u: [times_transposed(feats[u][c], fks[u][c]) for c in range(2)] for u in units}
        old = {u: [times(feats[u][c], held[u][c].astype(BF16)) for c in range(2)] for u in units}
        near = {u: softmax_pair(jnp.where(masks[u[0]][0], near[u], NEG)) for u in units}
        far = {u: [jnp.where(masks[u[0]][1], f, 0.0) for f in far[u]] for u in units}
        stack = {u: jnp.concatenate([near[u]] + far[u], 0).astype(BF16) for u in units}
        sums = {u: times(stack[u], wide[u]) for u in units}
        for s, p in units:
            u, lanes = (s, p), pair_lanes(p)
            mixed = blend_at(0, p) * sums[u][:TILE, :PAIR]
            for c in range(2):
                mine = sums[u][(c + 1) * TILE : (c + 2) * TILE] + old[u][c]
                mixed = mixed + blend_at(c + 1, p) * (
                    mine[:, :PAIR] / mine[:, PAIR:]
                )
            att_ref[here[s], lanes] = mixed.astype(BF16)
        for p in pairs:
            for c in range(2):
                state[c, p] = held[together, p][c]
        return carry

    lax.fori_loop(0, rows // (together * TILE), step, 0)
    if whole_sequence:
        return
    last = pl.ds(rows, TILE)
    for p in pairs:
        for c in range(2):
            total_ref[c, p] = state[c, p] + state_share(
                block, load_split(fk, (c,), last, p), load_split(values, (), last, p)
            )


def slopes_of(field):
    small = jnp.exp(jnp.minimum(field, 0.0))
    bent = jnp.tanh(field)
    return [jnp.where(field > 0, 1.0, small), 1.0 - bent * bent]


def split_heads(block):
    lane = lax.broadcasted_iota(jnp.int32, block.shape, 1)
    zero = jnp.zeros_like(block)
    return jnp.concatenate(
        [jnp.where(lane < HEAD, block, zero), jnp.where(lane < HEAD, zero, block)], 0
    )


def attend_back_kernel(
    together, number, whole_sequence, place_ref, lengths_ref, blend_ref, q_ref, k_ref, v_ref, go_ref, *refs
):
    meta_ref = lengths_ref[place_ref[0]], place_ref[1]
    blend_at = blend_rows(blend_ref, (number + pl.program_id(0)) * (width_of(q_ref) // PAIR))
    halo_k, halo_v, state_ref, later_ref = (None,) * 4 if whole_sequence else refs[:4]
    if whole_sequence:
        gq_ref, gk_ref, gv_ref, mix_ref = refs[:4]
    else:
        gq_ref, gk_ref, gv_ref, mix_ref, hk_ref, hv_ref, total_ref = refs[4:11]
    keys, values, fq, fk, state, gk, gv, gfk, gon = refs[-9:]
    rows, width = q_ref.shape
    pairs = range(width // PAIR)
    tiles = rows // TILE
    near_by = range(together)
    units = [(s, p) for s in near_by for p in pairs]
    fill_features(meta_ref, q_ref, k_ref, v_ref, halo_k, halo_v, keys, values, fq, fk, True)
    state[...] = jnp.zeros_like(state) if whole_sequence else state_ref[...]
    mix_ref[...] = jnp.zeros_like(mix_ref)
    gk[:TILE, :] = jnp.zeros((TILE, width), F32)
    gv[:TILE, :] = jnp.zeros((TILE, width), F32)
    gfk[:, :TILE, :] = jnp.zeros((2, TILE, width), F32)
    ones, block = tile_constants()
    row = lax.broadcasted_iota(jnp.int32, (2 * PAIR, PAIR), 0) % PAIR
    lane = lax.broadcasted_iota(jnp.int32, (2 * PAIR, PAIR), 1)
    heads = jnp.where(row // HEAD == lane // HEAD, 1.0, 0.0).astype(BF16)
    plain_ones = jnp.ones((TILE, PAIR), BF16)
    high = (lax.broadcasted_iota(jnp.int32, (TILE, PAIR), 1) % HEAD) < HEAD // 2

    def step(turn, carry):
        first = turn * together
        at = pl.multiple_of(first * TILE, TILE)
        here = [pl.ds(at + s * TILE, TILE) for s in range(together + 1)]
        window = [pl.ds(at + s * TILE, 2 * TILE) for s in near_by]
        masks = [tile_masks(meta_ref, first + s) for s in near_by]
        q = {(s, p): q_ref[here[s], pair_lanes(p)] for s, p in units}
        go = {(s, p): go_ref[here[s], pair_lanes(p)].astype(F32) for s, p in units}
        blend = [[blend_at(c, p) for c in range(3)] for p in pairs]
        fqs = {(s, p): [load_split(fq, (c,), here[s], p) for c in range(2)] for s, p in units}
        feats = {u: [whole(f) for f in fqs[u]] for u in units}
        ks = {(s, p): load_split(keys, (), window[s], p) for s, p in units}
        fks = {(s, p): [load_split(fk, (c,), window[s], p) for c in range(2)] for s, p in units}
        wide = {
            (s, p): jnp.concatenate([load_split(values, (), window[s], p), ones], 1)
            for s, p in units
        }
        held = {(0, p): [state[c, p] for c in range(2)] for p in pairs}
        for s, p in units:
            vs = load_split(values, (), here[s], p)
            held[s + 1, p] = [
                held[s, p][c] + state_share(block, load_split(fk, (c,), here[s], p), vs)
                for c in range(2)
            ]
        past = {u: [h.astype(BF16) for h in held[u]] for u in units}
        old_k = [gk[here[0], pair_lanes(p)] for p in pairs]
        old_v = [gv[here[0], pair_lanes(p)] for p in pairs]
        old_f = [[gfk[c, here[0], pair_lanes(p)] for c in range(2)] for p in pairs]

        near = {u: times_transposed(q[u], ks[u]) for u in units}
        far = {u: [times_transposed(feats[u][c], fks[u][c]) for c in range(2)] for u in units}
        old = {u: [times(feats[u][c], past[u][c]) for c in range(2)] for u in units}
        near = {u: softmax_pair(jnp.where(masks[u[0]][0], near[u], NEG)) for u in units}
        far = {u: [jnp.where(masks[u[0]][1], f, 0.0).astype(BF16) for f in far[u]] for u in units}
        stack = {u: jnp.concatenate([near[u].astype(BF16)] + far[u], 0) for u in units}
        sums = {u: times(stack[u], wide[u]) for u in units}
        scales, prods = {}, {}
        for u in units:
            outs = [sums[u][:TILE, :PAIR]]
            scales[u] = [jnp.broadcast_to(blend[u[1]][0], (TILE, PAIR))]
            for c in range(2):
                mine = sums[u][(c + 1) * TILE : (c + 2) * TILE] + old[u][c]
                inverse = 1.0 / mine[:, PAIR:]
                outs.append(mine[:, :PAIR] * inverse)
                scales[u].append(blend[u[1]][c + 1] * inverse)
            prods[u] = jnp.concatenate([go[u] * out for out in outs], 0)
        deltas = {}
        for u in units:
            low = prods[u].astype(BF16)
            rest = (prods[u] - low.astype(F32)).astype(BF16)
            deltas[u] = times(jnp.concatenate([low, rest], 1), heads)
        grads = {}
        for u in units:
            grads[u] = []
            for c in range(3):
                delta = scales[u][c] * deltas[u][c * TILE : (c + 1) * TILE] * (-2.0 / HEAD)
                delta_low = delta.astype(BF16).astype(F32)
                delta = jnp.where(high, delta_low, delta - delta_low)
                grads[u].append(jnp.concatenate([scales[u][c] * go[u], delta], 1).astype(BF16))
        back = {u: times_transposed(jnp.concatenate(grads[u], 0), wide[u]) for u in units}
        late = {u: [times_transposed(grads[u][c + 1], past[u][c]) for c in range(2)] for u in units}
        ds = {u: (near[u] * back[u][:TILE]).astype(BF16) for u in units}
        gas = {
            u: [
                jnp.where(masks[u[0]][1], back[u][(c + 1) * TILE : (c + 2) * TILE], 0.0).astype(BF16)
                for c in range(2)
            ]
            for u in units
        }
        gq_near = {u: times(ds[u], ks[u]) for u in units}
        gq_far = {u: [times(gas[u][c], fks[u][c]) + late[u][c] for c in range(2)] for u in units}
        new_k = {u: rows_product(tall(ds[u]), split_heads(q[u] * 0.125)) for u in units}
        new_f = {u: [rows_product(tall(gas[u][c]), fqs[u][c]) for c in range(2)] for u in units}
        new_v = {
            u: rows_product(
                jnp.concatenate([tall(stack[u][c * TILE : (c + 1) * TILE]) for c in range(3)], 0),
                jnp.concatenate([split_heads(g[:, :PAIR]) for g in grads[u]], 0),
            )
            for u in units
        }

        def overlap(old, new, p):
            parts = [old + new(0, p)[:TILE]]
            parts += [new(s, p)[TILE:] + new(s + 1, p)[:TILE] for s in range(together - 1)]
            return parts + [new(together - 1, p)[TILE:]]

        for s, p in units:
            u, lanes = (s, p), pair_lanes(p)
            slopes = slopes_of(q[u].astype(F32))
            gq = gq_near[u] + slopes[0] * gq_far[u][0] + slopes[1] * gq_far[u][1]
            gq_ref[here[s], lanes] = gq.astype(BF16)
            for c in range(2):
                gon[c, here[s], p * 2 * PAIR : (p + 1) * 2 * PAIR] = grads[u][c + 1]
        for p in pairs:
            lanes = pair_lanes(p)
            for c in range(3):
                mix_ref[c : c + 1, lanes] += sum(
                    jnp.sum(prods[s, p][c * TILE : (c + 1) * TILE], axis=0, keepdims=True)
                    for s in near_by
                )
            for rows_at, part in zip(here, overlap(old_k[p], lambda s, p: new_k[s, p], p)):
                gk[rows_at, lanes] = part
            for rows_at, part in zip(here, overlap(old_v[p], lambda s, p: new_v[s, p], p)):
                gv[rows_at, lanes] = part
            for c in range(2):
                parts = overlap(old_f[p][c], lambda s, p: new_f[s, p][c], p)
                for rows_at, part in zip(here, parts):
                    gfk[c, rows_at, lanes] = part
                state[c, p] = held[together, p][c]
        return carry

    lax.fori_loop(0, tiles // together, step, 0)
    if not whole_sequence:
        hk_ref[...] = gk[:TILE, :].astype(BF16)
        hv_ref[...] = gv[:TILE, :].astype(BF16)
    state[...] = jnp.zeros_like(state) if whole_sequence else later_ref[...]

    def come(at, c, p):
        here = pl.ds(at, TILE)
        grads = gon[c, here, p * 2 * PAIR : (p + 1) * 2 * PAIR]
        share = rows_product(whole(load_split(fq, (c,), here, p)), grads)
        return jnp.where(block, share, 0.0)

    def back_step(turn, carry):
        first = tiles - 1 - turn * together
        at = [pl.multiple_of((first - s) * TILE, TILE) for s in near_by]
        here = [pl.ds(a, TILE) for a in at]
        there = [pl.ds(a + TILE, TILE) for a in at]
        held = {(-1, p): [state[c, p] for c in range(2)] for p in pairs}
        for s, p in units:
            tile = first - s + 2
            nearer = pl.multiple_of(jnp.minimum(tile, tiles - 1) * TILE, TILE)
            held[s, p] = [
                held[s - 1, p][c] + jnp.where(tile < tiles, come(nearer, c, p), 0.0)
                for c in range(2)
            ]
        later = {u: [h.astype(BF16) for h in held[u]] for u in units}
        vs = {(s, p): whole(load_split(values, (), there[s], p)) for s, p in units}
        fks = {
            (s, p): jnp.concatenate([whole(load_split(fk, (c,), there[s], p)) for c in range(2)], 1)
            for s, p in units
        }
        wide = {u: jnp.concatenate([vs[u], plain_ones], 1) for u in units}
        far_k = {u: [times_transposed(wide[u], later[u][c]) for c in range(2)] for u in units}
        far_v = {
            u: times(fks[u], jnp.concatenate([g[:, :PAIR] for g in later[u]], 0)) for u in units
        }
        for s, p in units:
            u, lanes = (s, p), pair_lanes(p)
            position = meta_ref[1] + at[s] + lax.broadcasted_iota(jnp.int32, (TILE, PAIR), 0)
            slopes = slopes_of(k_ref[here[s], lanes].astype(F32))
            grad_f = [gfk[c, there[s], lanes] + far_k[u][c] for c in range(2)]
            bent = slopes[0] * grad_f[0] + slopes[1] * grad_f[1]
            grad_k = gk[there[s], lanes] + jnp.where(position < meta_ref[0], bent, 0.0)
            gk_ref[here[s], lanes] = grad_k.astype(BF16)
            gv_ref[here[s], lanes] = (gv[there[s], lanes] + far_v[u]).astype(BF16)
        for p in pairs:
            for c in range(2):
                state[c, p] = held[together - 1, p][c]
        return carry

    lax.fori_loop(0, tiles // together, back_step, 0)
    if whole_sequence:
        return
    for p in pairs:
        for c in range(2):
            total_ref[c, p] = state[c, p] + come(0, c, p) + come(TILE, c, p)


def attention_specs(rows, width, lanes, number):
    calls = width // lanes

    def columns(height, part):
        return pl.BlockSpec((height, lanes), lambda i: (0, part * calls + number(i)))

    state = pl.BlockSpec(
        (2, lanes // PAIR, PAIR, 2 * PAIR), lambda i: (0, number(i), 0, 0)
    )
    ins = [pl.BlockSpec(memory_space=pltpu.SMEM)] * 3
    ins += [columns(rows, part) for part in range(3)]
    return columns, ins, [columns(TILE, part) for part in range(2)] + [state]


def attention_scratch(rows, lanes, split):
    return [
        pltpu.VMEM((rows + TILE, 2 * lanes), BF16),
        pltpu.VMEM((rows + TILE, 2 * lanes), BF16),
        pltpu.VMEM((2, rows, (2 if split else 1) * lanes), BF16),
        pltpu.VMEM((2, rows + TILE, 2 * lanes), BF16),
        pltpu.VMEM((2, lanes // PAIR, PAIR, 2 * PAIR), F32),
    ]


def outcome(shape, dtype):
    return jax.ShapeDtypeStruct(shape, dtype), pl.BlockSpec(shape, lambda _: (0,) * len(shape))


UNITS = 16


def together(rows, lanes):
    return min(UNITS * PAIR // lanes, rows // TILE)


def attend(place, lengths, blend, qkv, halo, state):
    rows, width = qkv.shape[0], qkv.shape[1] // 3
    lanes = PAIR
    columns, ins, before = attention_specs(rows, width, lanes, lambda i: i)
    held = before[-1]
    share = (2, width // PAIR, PAIR, 2 * PAIR)
    earlier = () if state is None else (halo, halo, state)
    return pl.pallas_call(
        functools.partial(attend_kernel, together(rows, lanes), state is None),
        grid=(width // lanes,),
        out_shape=(
            jax.ShapeDtypeStruct((rows, width), BF16),
            jax.ShapeDtypeStruct(share, F32),
        )[: 1 if state is None else 2],
        in_specs=ins + before[: len(earlier)],
        out_specs=(columns(rows, 0), held)[: 1 if state is None else 2],
        scratch_shapes=attention_scratch(rows, lanes, False),
        compiler_params=pltpu.CompilerParams(vmem_limit_bytes=VMEM),
        cost_estimate=BRIEF,
    )(place, lengths, blend, qkv, qkv, qkv, *earlier)


def attend_back(place, lengths, blend, qkv, halo, state, later, go, first, count):
    rows, width = qkv.shape[0], qkv.shape[1] // 3
    lanes = PAIR
    columns, ins, before = attention_specs(rows, width, lanes, lambda i: first + i)
    others = () if state is None else (halo, halo, state, later)

    def side_by_side(height, dtype):
        shape = jax.ShapeDtypeStruct((height, count * lanes), dtype)
        return shape, pl.BlockSpec((height, lanes), lambda i: (0, i))

    outs = [side_by_side(rows, BF16)] * 3 + [side_by_side(3, F32)]
    if state is not None:
        share = (2, 1, PAIR, 2 * PAIR)
        outs += [side_by_side(TILE, BF16)] * 2
        outs += [
            (
                jax.ShapeDtypeStruct((2, count) + share[2:], F32),
                pl.BlockSpec(share, lambda i: (0, i, 0, 0)),
            )
        ]
    shapes, blocks = zip(*outs)
    return pl.pallas_call(
        functools.partial(attend_back_kernel, together(rows, lanes), first, state is None),
        grid=(count,),
        out_shape=shapes,
        in_specs=ins + [columns(rows, 0)] + (before + before[-1:])[: len(others)],
        out_specs=blocks,
        scratch_shapes=attention_scratch(rows, lanes, True)
        + [
            pltpu.VMEM((rows + TILE, lanes), F32),
            pltpu.VMEM((rows + TILE, lanes), F32),
            pltpu.VMEM((2, rows + TILE, lanes), F32),
            pltpu.VMEM((2, rows, 2 * lanes), BF16),
        ],
        compiler_params=pltpu.CompilerParams(vmem_limit_bytes=VMEM),
        cost_estimate=BRIEF,
    )(place, lengths, blend, qkv, qkv, qkv, go, *others)


CHUNK = 512
GELU_A, GELU_B = 0.7978845608028654, 0.044715


def normalized(field):
    center = field - jnp.mean(field, axis=-1, keepdims=True)
    scale = lax.rsqrt(jnp.mean(center * center, axis=-1, keepdims=True) + EPS)
    return center * scale, scale


def norm_back(grad, unit, scale):
    shared = jnp.mean(grad * unit, axis=-1, keepdims=True)
    return scale * (grad - jnp.mean(grad, axis=-1, keepdims=True) - unit * shared)


def gelu_pair(field):
    square = field * field
    half = 0.5 + 0.5 * jnp.tanh(field * (GELU_A + GELU_A * GELU_B * square))
    act = field * half
    return act, half + act * (1.0 - half) * (2.0 * GELU_A + 6.0 * GELU_A * GELU_B * square)


def column_sum(block):
    return jnp.sum(block, axis=0, keepdims=True)


def enter_kernel(place_ref, w_ref, gain_ref, bias_ref, *refs):
    parts, x_ref, qkv_ref, whole_x = refs[:-3], refs[-3], refs[-2], refs[-1]
    span, chunk = parts[0].shape[0], x_ref.shape[0]

    @pl.when(pl.program_id(0) == 0)
    def _():
        for k, part in enumerate(parts):
            at = (place_ref[0] ^ k) * span
            whole_x[pl.ds(pl.multiple_of(at, span), span), :] = part[...]

    x = whole_x[pl.ds(pl.multiple_of(pl.program_id(0) * chunk, chunk), chunk), :]
    x_ref[...] = x
    unit, _ = normalized(x.astype(F32))
    low = (unit * gain_ref[...] + bias_ref[...]).astype(BF16)
    qkv_ref[...] = times(low, w_ref[...]).astype(BF16)


def enter(place, parts, weight, gain, bias):
    span, width = parts[0].shape
    rows, lanes = span * len(parts), weight.shape[1]
    size = min(CHUNK, rows)
    return pl.pallas_call(
        enter_kernel,
        grid=(rows // size,),
        out_shape=(
            jax.ShapeDtypeStruct((rows, width), BF16),
            jax.ShapeDtypeStruct((rows, lanes), BF16),
        ),
        in_specs=[pl.BlockSpec(memory_space=pltpu.SMEM)]
        + [constant(a.shape) for a in (weight, gain[None], bias[None], *parts)],
        out_specs=(by_rows(size, width), by_rows(size, lanes)),
        scratch_shapes=[pltpu.VMEM((rows, width), BF16)],
        compiler_params=pltpu.CompilerParams(vmem_limit_bytes=VMEM),
        cost_estimate=BRIEF,
    )(place, weight, gain[None], bias[None], *parts)


def deal(place_ref, rows, lanes, value, keep_ref, send_ref):
    half = value.shape[0] // 2

    @pl.when(place_ref[2] == 0)
    def _():
        keep_ref[rows, lanes] = value[:half]
        send_ref[rows, lanes] = value[half:]

    @pl.when(place_ref[2] != 0)
    def _():
        keep_ref[rows, lanes] = value[half:]
        send_ref[rows, lanes] = value[:half]


def feed_kernel(
    pieces, place_ref, x_ref, att_ref, grad_ref, out_from, gain_ref, bias_ref, in_from, in_b,
    down_from, down_b, result_to, first_to, go_to, keep_to, send_to, small_ref, wide_ref,
    second, hidden, pre_low, att_low, att_all, grad_all, out_w, in_w, down_w, keep_ref, send_ref,
    result_ref, go_ref, in_sems, out_sems, row_sems,
):
    chunk, width = x_ref.shape
    inner = in_w.shape[1]
    number = pl.program_id(0)
    here = pl.ds(pl.multiple_of(number * chunk, chunk), chunk)
    tiles = [slice(at, at + width) for at in range(0, inner, width)]
    copies = [pltpu.make_async_copy(out_from, out_w, in_sems.at[0])]
    for i, lanes in enumerate(tiles):
        copies += [
            pltpu.make_async_copy(in_from.at[:, lanes], in_w.at[:, lanes], in_sems.at[2 * i + 1]),
            pltpu.make_async_copy(down_from.at[lanes, :], down_w.at[lanes, :], in_sems.at[2 * i + 2]),
        ]

    def arrived(i):
        @pl.when(number == 0)
        def _():
            copies[i].wait()

    @pl.when(number == 0)
    def _():
        for copy in copies:
            copy.start()
        small_ref[...] = jnp.zeros_like(small_ref)
        wide_ref[...] = jnp.zeros_like(wide_ref)

    att = att_ref[...]
    att_all[here, :] = att
    arrived(0)
    first = x_ref[...].astype(F32) + times(att, out_w[...])
    unit, scale = normalized(first)
    low = (unit * gain_ref[...] + bias_ref[...]).astype(BF16)
    second[here, :] = low
    grad = grad_ref[...]
    grad_all[here, :] = grad
    grad_f = grad.astype(F32)
    result = first + down_b[...]
    back = jnp.zeros((chunk, width), F32)
    for i, lanes in enumerate(tiles):
        arrived(2 * i + 1)
        arrived(2 * i + 2)
        act, slope = gelu_pair(times(low, in_w[:, lanes]) + in_b[:, lanes])
        act = act.astype(BF16)
        hidden[here, lanes] = act
        result = result + times(act, down_w[lanes, :])
        pre = (times_transposed(grad, down_w[lanes, :]) * slope).astype(BF16)
        pre_low[here, lanes] = pre
        wide_ref[:, lanes] += column_sum(pre.astype(F32))
        back = back + times_transposed(pre, in_w[:, lanes])
    result_ref[here, :] = result.astype(BF16)
    small_ref[0:1, :] += column_sum(back * unit)
    small_ref[1:2, :] += column_sum(back)
    small_ref[2:3, :] += column_sum(grad_f)
    grad_first = grad_f + norm_back(back * gain_ref[...], unit, scale)
    grad_att = grad_first.astype(BF16)
    att_low[here, :] = grad_att
    go_ref[here, :] = times_transposed(grad_att, out_w[...]).astype(BF16)
    pairs = ((result_ref, result_to), (att_low, first_to), (go_ref, go_to))
    done = [
        pltpu.make_async_copy(inside.at[here, :], outside.at[here, :], row_sems.at[number, i])
        for i, (inside, outside) in enumerate(pairs)
    ]
    for copy in done:
        copy.start()

    @pl.when(number == pl.num_programs(0) - 1)
    def _():
        every = slice(0, width // 2)
        leaving = []

        def leave(lanes):
            for here, there in ((keep_ref, keep_to), (send_ref, send_to)):
                sem = out_sems.at[len(leaving)]
                copy = pltpu.make_async_copy(here.at[:, lanes], there.at[:, lanes], sem)
                copy.start()
                leaving.append(copy)

        flat, after_out = width // pieces, inner + width

        def spread(block, share, ref):
            for below in range(pieces):
                piece, side = divmod(block * pieces + below, len(tiles))
                rows = slice(piece % (pieces // 2) * flat, (piece % (pieces // 2) + 1) * flat)
                lanes = slice(after_out + side * width, after_out + (side + 1) * width)
                ref[rows, lanes] = share[below * flat : (below + 1) * flat]

        for block, lanes in enumerate(tiles):
            share = rows_product(hidden[:, lanes], grad_all[...]).astype(BF16)
            mine = place_ref[2] == 2 * block // len(tiles)

            @pl.when(mine)
            def _(block=block, share=share):
                spread(block, share, keep_ref)

            @pl.when(jnp.logical_not(mine))
            def _(block=block, share=share):
                spread(block, share, send_ref)

        leave(slice(after_out, after_out + inner))
        for lanes in tiles:
            share = rows_product(second[...], pre_low[:, lanes]).astype(BF16)
            deal(place_ref, every, lanes, share, keep_ref, send_ref)
            leave(lanes)
        share = rows_product(att_all[...], att_low[...]).astype(BF16)
        deal(place_ref, every, slice(inner, after_out), share, keep_ref, send_ref)
        leave(slice(inner, after_out))
        for copy in leaving:
            copy.wait()
        for step in range(att_all.shape[0] // chunk):
            rows = slice(step * chunk, (step + 1) * chunk)
            for i, (inside, outside) in enumerate(pairs):
                sem = row_sems.at[step, i]
                pltpu.make_async_copy(inside.at[rows, :], outside.at[rows, :], sem).wait()


def by_rows(height, width):
    return pl.BlockSpec((height, width), lambda i: (i, 0))


def constant(shape):
    return pl.BlockSpec(shape, lambda i: (0, 0))


def feed_forward(pieces, place, x, att, grad, out_w, gain, bias, in_w, in_b, down_w, down_b):
    rows, width = x.shape
    inner = in_w.shape[1]
    packed = (width // 2, 2 * inner + width)
    size = min(2 * CHUNK, rows)
    block, far = by_rows(size, width), pl.BlockSpec(memory_space=pl.ANY)
    return pl.pallas_call(
        functools.partial(feed_kernel, pieces),
        grid=(rows // size,),
        out_shape=(
            jax.ShapeDtypeStruct((rows, width), BF16),
            jax.ShapeDtypeStruct((rows, width), BF16),
            jax.ShapeDtypeStruct((rows, width), BF16),
            jax.ShapeDtypeStruct(packed, BF16),
            jax.ShapeDtypeStruct(packed, BF16),
            jax.ShapeDtypeStruct((3, width), F32),
            jax.ShapeDtypeStruct((1, inner), F32),
        ),
        in_specs=[pl.BlockSpec(memory_space=pltpu.SMEM)]
        + [block] * 3
        + [far, constant((1, width)), constant((1, width)), far, constant((1, inner)), far]
        + [constant((1, width))],
        out_specs=(far,) * 5
        + (constant((3, width)), constant((1, inner))),
        scratch_shapes=[
            pltpu.VMEM((rows, width), BF16),
            pltpu.VMEM((rows, inner), BF16),
            pltpu.VMEM((rows, inner), BF16),
            pltpu.VMEM((rows, width), BF16),
            pltpu.VMEM((rows, width), BF16),
            pltpu.VMEM((rows, width), BF16),
            pltpu.VMEM(out_w.shape, BF16),
            pltpu.VMEM(in_w.shape, BF16),
            pltpu.VMEM(down_w.shape, BF16),
            pltpu.VMEM(packed, BF16),
            pltpu.VMEM(packed, BF16),
            pltpu.VMEM((rows, width), BF16),
            pltpu.VMEM((rows, width), BF16),
            pltpu.SemaphoreType.DMA((1 + 2 * inner // width,)),
            pltpu.SemaphoreType.DMA((4 + 2 * inner // width,)),
            pltpu.SemaphoreType.DMA((rows // size, 3)),
        ],
        compiler_params=pltpu.CompilerParams(vmem_limit_bytes=VMEM),
        cost_estimate=BRIEF,
    )(place, x, att, grad, out_w, gain[None], bias[None], in_w, in_b[None], down_w, down_b[None])


def project_back_kernel(
    calls, place_ref, x_ref, first_ref, w_ref, gain_ref, bias_ref, small2_ref, wide_ref, *refs
):
    grads, mixes = refs[: 3 * calls], refs[3 * calls : 4 * calls]
    result_ref, keep_ref, send_ref, normed, gathered, sums, rows_of = refs[4 * calls :]
    chunk, width = x_ref.shape
    number = pl.program_id(0)
    here = pl.ds(pl.multiple_of(number * chunk, chunk), chunk)

    @pl.when(number == 0)
    def _():
        sums[...] = jnp.zeros_like(sums)

    unit, scale = normalized(x_ref[...].astype(F32))
    normed[here, :] = (unit * gain_ref[...] + bias_ref[...]).astype(BF16)
    grad = jnp.concatenate([ref[...] for ref in grads], 1)
    gathered[here, :] = grad
    back = times_transposed(grad, w_ref[...])
    sums[0:1, :] += column_sum(back * unit)
    sums[1:2, :] += column_sum(back)
    grad_x = first_ref[...].astype(F32) + norm_back(back * gain_ref[...], unit, scale)
    result_ref[...] = grad_x.astype(BF16)

    @pl.when(number == pl.num_programs(0) - 1)
    def _():
        every = slice(0, width // 2)
        rows_of[...] = jnp.zeros_like(rows_of)
        at = 0
        for ref in (sums, small2_ref, wide_ref):
            for row in range(ref.shape[0]):
                for lane in range(0, ref.shape[1], PAIR):
                    rows_of[at : at + 1, :] = ref[row : row + 1, lane : lane + PAIR]
                    at += 1
        lane = lax.broadcasted_iota(jnp.int32, (3, PAIR), 1)
        blend = jnp.zeros((3, PAIR), F32)
        head = 0
        for mix in mixes:
            for first in range(0, mix.shape[1], HEAD):
                mine = jnp.sum(mix[:, first : first + HEAD], axis=1, keepdims=True)
                blend = blend + jnp.where(lane == head, mine, 0.0)
                head += 1
        rows_of[at : at + 3, :] = blend
        exact = rows_of[...]
        high = exact.astype(BF16)
        low = (exact - high.astype(F32)).astype(BF16)
        for part, value in enumerate((high, low)):
            lanes = slice(3 * width + part * PAIR, 3 * width + (part + 1) * PAIR)
            deal(place_ref, every, lanes, value, keep_ref, send_ref)
        for at in range(0, 3 * width, width):
            lanes = slice(at, at + width)
            share = rows_product(normed[...], gathered[:, lanes]).astype(BF16)
            deal(place_ref, every, lanes, share, keep_ref, send_ref)


def project_back(place, x, grad_first, weight, gain, bias, small2, wide, grads, mixes):
    rows, width = x.shape
    calls = len(mixes)
    packed = (width // 2, 3 * width + 2 * PAIR)
    size = min(CHUNK, rows)
    block = by_rows(size, width)
    return pl.pallas_call(
        functools.partial(project_back_kernel, calls),
        grid=(rows // size,),
        out_shape=(jax.ShapeDtypeStruct((rows, width), BF16),)
        + (jax.ShapeDtypeStruct(packed, BF16),) * 2,
        in_specs=[pl.BlockSpec(memory_space=pltpu.SMEM), block, block]
        + [constant(a.shape) for a in (weight, gain[None], bias[None], small2, wide)]
        + [by_rows(size, grad.shape[1]) for grad in grads]
        + [constant(mix.shape) for mix in mixes],
        out_specs=(block, constant(packed), constant(packed)),
        scratch_shapes=[
            pltpu.VMEM((rows, width), BF16),
            pltpu.VMEM((rows, 3 * width), BF16),
            pltpu.VMEM((2, width), F32),
            pltpu.VMEM((width, PAIR), F32),
        ],
        compiler_params=pltpu.CompilerParams(vmem_limit_bytes=VMEM),
        cost_estimate=BRIEF,
    )(place, x, grad_first, weight, gain[None], bias[None], small2, wide, *grads, *mixes)


def to_sequences(block, axis, groups):
    return lax.all_to_all(block, axis, 0, 0, axis_index_groups=groups)


def spans_of(block, axis, mine):
    seqs, devices = block.shape[0], lax.axis_size(axis)
    spans = []
    for k in range(seqs):
        span = lax.dynamic_index_in_dim(block, mine ^ k, 0, False)
        route = [(i, i ^ k) for i in range(devices)]
        spans.append(lax.ppermute(span, axis, route) if k else span)
    return spans


def after(value, *others):
    return lax.optimization_barrier((value,) + others)[0]


def join_kernel(placed, *refs):
    parts, outs = refs[: len(placed)], refs[len(placed) :]
    for part, places in zip(parts, placed):
        for source, out, to, lanes in places:
            outs[out][to, :, lanes] = part[source]


def join_to(parts, placed, shapes):
    vmem = pl.BlockSpec(memory_space=pltpu.VMEM)
    return pl.pallas_call(
        functools.partial(join_kernel, placed),
        out_shape=[jax.ShapeDtypeStruct(shape, parts[0].dtype) for shape in shapes],
        in_specs=[vmem] * len(parts),
        out_specs=[vmem] * len(shapes),
        compiler_params=pltpu.CompilerParams(vmem_limit_bytes=16 * 2**20),
        cost_estimate=BRIEF,
    )(*parts)


def split_kernel(count, *refs):
    first, second = refs[count:]
    size, _, lanes = refs[0].shape
    for k, part in enumerate(refs[:count]):
        first[k * size : (k + 1) * size] = part[:, :, : lanes // 2]
        second[k * size : (k + 1) * size] = part[:, :, lanes // 2 :]


def split_to(parts, shapes):
    vmem = pl.BlockSpec(memory_space=pltpu.VMEM)
    return pl.pallas_call(
        functools.partial(split_kernel, len(parts)),
        out_shape=[jax.ShapeDtypeStruct(shape, parts[0].dtype) for shape in shapes],
        in_specs=[vmem] * len(parts),
        out_specs=[vmem] * 2,
        compiler_params=pltpu.CompilerParams(vmem_limit_bytes=16 * 2**20),
        cost_estimate=BRIEF,
    )(*parts)


def join(parts):
    size, height, lanes = parts[0].shape
    placed = [
        [(slice(0, size), 0, slice(k * size, (k + 1) * size), slice(0, lanes))]
        for k in range(len(parts))
    ]
    return join_to(parts, placed, [(len(parts) * size, height, lanes)])[0]


def settle_kernel(source_ref, out_ref):
    out_ref[...] = source_ref[...]


def settle(value):
    vmem = pl.BlockSpec(memory_space=pltpu.VMEM)
    return pl.pallas_call(
        settle_kernel,
        out_shape=jax.ShapeDtypeStruct(value.shape, value.dtype),
        in_specs=[vmem],
        out_specs=vmem,
        compiler_params=pltpu.CompilerParams(vmem_limit_bytes=8 * 2**20),
        cost_estimate=BRIEF,
    )(value)


def from_parts(total, axis, parts, stride, forward):
    size = lax.axis_size(axis)
    low = total.astype(BF16)
    result = jnp.zeros_like(total)
    for hop in range(1, parts):
        distance = hop * stride
        route = [
            (i, i + distance) if forward else (i + distance, i) for i in range(size - distance)
        ]
        result = result + lax.ppermute(low, axis, route).astype(F32)
    return result


class Ring:
    def __init__(self, batch, seq):
        self.batch, self.seq = batch, seq
        self.low = 2 ** ((seq.bit_length() - 1) // 2)
        self.sizes = {"core": 2, "near": batch // 2 * self.low, "far": seq // self.low}
        self.pieces = batch * seq

    def place(self, s, b):
        return {"core": b % 2, "near": b // 2 * self.low + s % self.low, "far": s // self.low}

    def device(self, place):
        s = place["far"] * self.low + place["near"] % self.low
        return s * self.batch + place["near"] // self.low * 2 + place["core"]

    def mine(self):
        return self.place(lax.axis_index("seq"), lax.axis_index("batch"))

    def swap(self, value, level, k):
        route = []
        for s in range(self.seq):
            for b in range(self.batch):
                place = self.place(s, b)
                place[level] ^= k
                route.append((s * self.batch + b, self.device(place)))
        return lax.ppermute(value, ("seq", "batch"), route)

    def slices(self, value, level):
        size, me = self.sizes[level], self.mine()[level]
        value = value.reshape((size, value.shape[0] // size) + value.shape[1:])
        return [lax.dynamic_index_in_dim(value, me ^ k, 0, False) for k in range(size)]

    def scatter(self, value, level, fine=0, beside=()):
        slices = value if isinstance(value, list) else self.slices(value, level)
        parts = [self.swap(part, level, k) for k, part in enumerate(slices) if k]
        return self.add(slices[0], parts, fine, beside)

    def scatter_cores(self, keep, send, fine=0, beside=()):
        return self.add(self.to_pieces(keep), [self.swap(self.to_pieces(send), "core", 1)], fine, beside)

    def add(self, value, parts, fine, beside):
        total = after(value, *beside).astype(F32)
        for part in parts:
            total = total + part.astype(F32)
        if not fine:
            return total.astype(BF16)
        end = total.shape[-1] - 2 * fine
        exact = total[..., end : end + fine] + total[..., end + fine :]
        high = lax.reduce_precision(exact, 8, 7)
        return jnp.concatenate([total[..., :end], high, exact - high], -1).astype(BF16)

    def gather(self, value, level, beside=()):
        parts = [self.swap(value, level, k) for k in range(1, self.sizes[level])]
        return join([after(value, *beside)] + parts)

    def to_pieces(self, value):
        return value.reshape(self.pieces // 2, -1, value.shape[1])

    def gather_split(self, value, level, beside=()):
        parts = [after(value, *beside)]
        parts += [self.swap(value, level, k) for k in range(1, self.sizes[level])]
        size, height, lanes = value.shape
        shape = (len(parts) * size, height, lanes // 2)
        return split_to(parts, [shape, shape])

    def join_ways(self, halves, ways):
        size, height, half = halves[0].shape
        size //= 2
        placed = []
        for out_lanes, order in ((0, (0, 2)), (0, (1, 3)), (half, (0, 1)), (half, (2, 3))):
            lanes = slice(out_lanes, out_lanes + half)
            placed.append(
                [
                    (slice(i * size, (i + 1) * size), 0, slice(k * size, (k + 1) * size), lanes)
                    for i, k in enumerate(order)
                ]
            )
        parts = [halves[0], ways[0], halves[1], ways[1]]
        return join_to(parts, placed, [(4 * size, height, 2 * half)])[0]

    def code(self):
        me = self.mine()
        return (me["core"] * self.sizes["near"] + me["near"]) * self.sizes["far"] + me["far"]


def unpack_kernel(write, finish, place_ref, own_ref, other_ref, *out_refs):
    half = own_ref.shape[0]
    for piece in range(2 * half):
        at = place_ref[3] ^ piece

        @pl.when(at < half)
        def _(piece=piece, at=at):
            write(piece, own_ref[at].astype(F32), out_refs)

        @pl.when(at >= half)
        def _(piece=piece, at=at):
            write(piece, other_ref[at - half].astype(F32), out_refs)

    finish(out_refs)


def write_feed(piece, block, out_refs):
    in_ref, out_ref, down_ref = out_refs
    size, inner, width = block.shape[0], in_ref.shape[1], in_ref.shape[0]
    rows = slice(piece * size, (piece + 1) * size)
    in_ref[rows, :] = block[:, :inner]
    out_ref[rows, :] = block[:, inner : inner + width]
    tall_rows = inner // (width // size)
    for below in range(0, tall_rows, size):
        at = inner + width + below // size * width
        down_ref[piece * tall_rows + below : piece * tall_rows + below + size, :] = block[
            :, at : at + width
        ]


def write_project(piece, block, out_refs):
    w_ref, small = out_refs[0], out_refs[-1]
    size, end = block.shape[0], w_ref.shape[1]
    rows = slice(piece * size, (piece + 1) * size)
    w_ref[rows, :] = block[:, :end]
    if piece * size < small.shape[0]:
        small[rows, :] = block[:, end : end + PAIR] + block[:, end + PAIR :]


def finish_project(out_refs):
    small, at = out_refs[-1], 0
    for vector in out_refs[1:-2]:
        for lane in range(0, vector.shape[0], PAIR):
            vector[lane : lane + PAIR] = small[at, :]
            at += 1
    blend = out_refs[-2]
    blend[...] = small[at : at + 3, : blend.shape[1]]


def unpack(write, place, halves, shapes, finish=lambda refs: None, scratch=()):
    vmem = pl.BlockSpec(memory_space=pltpu.VMEM)
    return pl.pallas_call(
        functools.partial(unpack_kernel, write, finish),
        out_shape=[jax.ShapeDtypeStruct(shape, F32) for shape in shapes],
        in_specs=[pl.BlockSpec(memory_space=pltpu.SMEM), vmem, vmem],
        out_specs=[vmem] * len(shapes),
        scratch_shapes=scratch,
        compiler_params=pltpu.CompilerParams(vmem_limit_bytes=24 * 2**20),
        cost_estimate=BRIEF,
    )(place, *halves)


def local(
    inputs,
    cotangent,
    lengths,
    norm1_gain,
    norm1_bias,
    qkv_weight,
    blend_weights,
    out_weight,
    norm2_gain,
    norm2_bias,
    in_weight,
    in_bias,
    down_weight,
    down_bias,
):
    seqs, span, width = inputs.shape
    heads = blend_weights.shape[1]
    devices = lax.axis_size("seq")
    parts = devices // seqs
    rows = seqs * span
    index = lax.axis_index("seq")
    groups = None
    if parts > 1:
        groups = [[r * seqs + s for s in range(seqs)] for r in range(parts)]
    mine, part = index % seqs, index // seqs
    ring = Ring(lax.axis_size("batch"), devices)
    by_ring = width % (16 * ring.pieces) == 0 and ring.sizes["near"] == 4
    inner = in_weight.shape[1]
    numbers = [mine, part * rows, 0, 0]
    if by_ring:
        numbers[2:] = [lax.axis_index("batch") % 2, ring.code()]
    place = jnp.stack([jnp.asarray(number, jnp.int32) for number in numbers])

    spans = spans_of(inputs, "seq", mine)
    x, qkv = enter(place, spans, qkv_weight, norm1_gain, norm1_bias)
    grad_out = to_sequences(after(cotangent, *spans), "seq", groups).reshape(rows, width)
    halo = state = later = None
    if parts > 1:
        state = later = jnp.zeros((2, width // PAIR, PAIR, 2 * PAIR), F32)
        onward = [(i, i + seqs) for i in range(devices - seqs)]
        halo = lax.ppermute(qkv[rows - TILE :, width:], "seq", onward)
        total = attend(place, lengths, blend_weights, qkv, halo, state)[1]
        state = from_parts(total, "seq", parts, seqs, True)
    attended = attend(place, lengths, blend_weights, qkv, halo, state)[0]

    result, grad_first, grad_o, feed_keep, feed_send, small2, grad_in_b = feed_forward(
        ring.pieces if by_ring else 16,
        place, x, attended, grad_out, out_weight, norm2_gain, norm2_bias,
        in_weight, in_bias, down_weight, down_bias,
    )

    def move(rows):
        return to_sequences(rows.reshape(seqs, span, width), "seq", groups)

    feed_shapes = [(width, inner), (width, width), (inner, width)]
    calls = ((0, 1), (1, width // PAIR - 1))

    def back(place, pairs, later):
        return attend_back(
            place, lengths, blend_weights, qkv, halo, state, later, grad_o, *pairs
        )

    if parts > 1:
        total = jnp.concatenate([back(place, pairs, later)[6] for pairs in calls], 1)
        later = from_parts(total, "seq", parts, seqs, False)
    if by_ring:
        output = move(result)
        backs = [back(place, calls[0], later)]
        held = ring.scatter_cores(feed_keep, feed_send, 0, (backs[0][3],))
        backs.append(back(after(place, held), calls[1], later))
        held = ring.scatter(held, "near", 0, (backs[1][3],))
        output = settle(after(output, backs[1][3]))
        grad_first = after(grad_first, held, output)
    else:
        backs = [back(place, pairs, later) for pairs in calls]
        output = move(result)
    grads = [[call[part] for call in backs] for part in range(3)]
    if parts > 1:
        homeward = [(i + seqs, i) for i in range(devices - seqs)]
        for part in (1, 2):
            for number in range(len(calls)):
                received = lax.ppermute(backs[number][part + 3], "seq", homeward)
                grad = grads[part][number]
                tail = grad[rows - TILE :].astype(F32) + received.astype(F32)
                grads[part][number] = grad.at[rows - TILE :].set(tail.astype(BF16))
    grads = grads[0] + grads[1] + grads[2]
    grad_x, project_keep, project_send = project_back(
        place, x, grad_first, qkv_weight, norm1_gain, norm1_bias, small2, grad_in_b, grads,
        [call[3] for call in backs],
    )

    if by_ring:
        held = ring.scatter(held, "far", 0, (project_keep,))
        late = ring.scatter_cores(project_keep, project_send, PAIR, (held,))
        late = ring.scatter(late, "near", PAIR)
        halves = ring.gather_split(held, "far", (late,))
        ways = [ring.swap(half, "near", k) for half, k in zip(halves, (2, 1))]
        halves = [join([half, way]) for half, way in zip(halves, ways)]
        ways = [ring.swap(half, "near", k) for half, k in zip(halves, (1, 2))]
        late = ring.scatter(late, "far", PAIR, halves)
        late = ring.gather(late, "far")
        moved = move(after(grad_x, late))
        held = ring.join_ways([after(halves[0], late), halves[1]], ways)
        other = ring.swap(held, "core", 1)
        feed_grads = unpack(write_feed, place, (held, other), feed_shapes)
        late = ring.gather(late, "near", feed_grads)
        input_grad = settle(after(moved, late))
        halves = after(late, input_grad), ring.swap(late, "core", 1)
    else:
        input_grad = move(grad_x)
        halves = (feed_keep, feed_send, project_keep, project_send)
        halves = lax.psum([half.astype(F32) for half in halves], ("seq", "batch"))
        halves = [half.reshape(8, width // 16, -1) for half in halves]
        feed_grads = unpack(write_feed, place, halves[:2], feed_shapes)
        halves = halves[2:]
    grad_in_w, grad_out_w, grad_down_w = feed_grads
    vectors = [(width,)] * 5 + [(inner,)]
    lines = sum(size for (size,) in vectors) // PAIR + 3
    lines += -lines % (width // (2 * halves[0].shape[0]))
    grad_qkv_w, gain1, bias1, gain2, bias2, grad_down_b, grad_in_b, grad_blend = unpack(
        write_project, place, halves, [(width, 3 * width)] + vectors + [(3, heads)],
        finish_project, [pltpu.VMEM((lines, PAIR), F32)],
    )
    return (
        output,
        input_grad,
        gain1,
        bias1,
        grad_qkv_w,
        grad_blend,
        grad_out_w,
        gain2,
        bias2,
        grad_in_w,
        grad_in_b,
        grad_down_w,
        grad_down_b,
    )


def solution(mesh):
    rows = P("batch", "seq", None)
    return jax.shard_map(
        local,
        mesh=mesh,
        in_specs=(rows, rows, P("batch")) + (P(),) * 11,
        out_specs=(rows, rows) + (P(),) * 11,
        check_vma=False,
    )
```
